32 devices in a mesh: parts: 2 (over y), row: 4 (over z), col: 2 (over x), depth: 2 (over core).
Axes of the slice: x: 2, y: 2, z: 4, core: 2. Of those that a mesh axis runs over, the one named last changes fastest.
Arguments:
- homolog_ensemble: bfloat16 [128, 64, 64], P(('parts', 'depth'), 'row'), parts along dimension 0, may hold values from -6 to 6
- duplex_embedding: bfloat16 [128, 64, 128], P(('parts', 'row'), 'col'), parts along dimension 0, may hold values from -6 to 6
- homolog_present_flags: int32 [128], P('parts'), parts along dimension 0, may hold values 0 or 1
- resolved_position_flags: int32 [128], P(('parts', 'col')), parts along dimension 0, may hold values 0 or 1
- payload_weights: bfloat16 [64, 256], replicated, may hold values from -0.75 to 0.75
- sigmoid_weights: bfloat16 [64, 256], replicated, may hold values from -0.75 to 0.75
- averager_final_weights: bfloat16 [256, 64], replicated, may hold values from -0.375 to 0.375
- first_operand_weights: bfloat16 [64, 32], replicated, may hold values from -0.75 to 0.75
- second_operand_weights: bfloat16 [64, 32], replicated, may hold values from -0.75 to 0.75
- duplex_logit_weights: bfloat16 [128, 8], replicated, may hold values from -20 to 20
- tensor_product_weights: bfloat16 [1024, 128], replicated, may hold values from -0.1875 to 0.1875
- averager_upstream_adjoint: bfloat16 [128, 64, 64], P(('parts', 'depth'), 'row'), parts along dimension 0, may hold values from -6 to 6
- duplex_upstream_adjoint: bfloat16 [128, 64, 128], P(('parts', 'row'), 'col'), parts along dimension 0, may hold values from -2.5 to 2.5
Outputs:
- ensemble_derivative: bfloat16 [128, 64, 64], P(('parts', 'depth'), 'row'), parts along dimension 0
- pairwise_gradient: bfloat16 [128, 64, 128], P(('parts', 'row'), 'col'), parts along dimension 0
- outer_matrix_gradient: float32 [2048, 128], P('parts'), parts along dimension 0
The draws below stay inside these ranges and needn't reach their ends.
There are 2 independent parts, one for each index of `parts`. The reference program is written for one: setup_inputs(seed, part) draws one part's arguments, and reference() takes and returns one part's arrays. A program takes and returns all parts, laid end to end along the dimension named above; an argument that names none is the same for every part. Nothing has to cross between parts.
All inputs are finite; a program needn't handle non-finite values. No bound on the sum of `resolved_position_flags` on one device may be relied on, other than what follows from the above.
Results may differ from the reference program's by a relative error of at most 0.013.
The reference program's roundings to bfloat16 on the way count: a program that leaves them out, or rounds other values in their place, can miss the bound.
Values may be sent and summed in bfloat16 or wider, within the bound.
No kernel may reach another device: no remote copies, remote signals or barrier semaphores. Data moves between devices by JAX's collectives and lax.ppermute only.
A program may use at most 64 MiB of HBM per device.

```python
import jax
import jax.numpy as jnp
from jax import lax

ALIGNED_FEATURES = 64
ATTENDER_NUMBER = 8
PER_ATTEND_SIZE = 32
DUAL_WIDTH = 128
PRODUCT_FEATURES = 32
POSITIONS = 64
ALIGNED_SEQS = 64


def alternating(width):
    return jnp.where(jnp.arange(width) % 2 == 0, 1.0, -1.0).astype(jnp.float32)


def balanced_signs(width):
    return jnp.where(jnp.arange(width) // 2 % 2 == 0, 1.0, -1.0).astype(jnp.float32)


def lower_regions(keys, base, amplitude):
    region_size = POSITIONS // 8
    depths = jax.random.uniform(keys[5], (POSITIONS, 8), jnp.float32, 1.5, 5.5)
    home = jax.random.randint(keys[6], (POSITIONS,), 0, 8)
    region = jnp.arange(POSITIONS) // region_size
    per_cell = depths[:, region]
    per_cell = jnp.where(region[None, :] == home[:, None], 0.0, per_cell)
    fraction = per_cell / amplitude
    along = -fraction / jnp.sqrt(1.0 - fraction * fraction)
    return base + along[:, :, None] * alternating(DUAL_WIDTH)[None, None, :]


def place_aligned(keys, base):
    chosen = jax.random.randint(keys[1], (POSITIONS,), 0, 16) == 0
    first_col = jax.random.randint(keys[2], (POSITIONS,), 0, POSITIONS)
    second_col = (first_col + 1 + jax.random.randint(keys[3], (POSITIONS,), 0, POSITIONS - 1)) % POSITIONS
    columns = jnp.arange(POSITIONS)
    hit_first = chosen[:, None] & (columns[None, :] == first_col[:, None])
    hit_second = chosen[:, None] & (columns[None, :] == second_col[:, None])
    aligned = 1.5 * alternating(DUAL_WIDTH)[None, None, :]
    spread = 0.11 + 0.015 * jax.random.randint(keys[4], (POSITIONS,), 0, 3).astype(jnp.float32)
    second = aligned * (1.0 + spread[:, None, None] * balanced_signs(DUAL_WIDTH)[None, None, :])
    base = jnp.where(hit_first[:, :, None], aligned, base)
    base = jnp.where(hit_second[:, :, None], second, base)
    return base


def draw_duplex_embedding(key, part):
    key = jax.random.fold_in(key, 11)
    keys = jax.random.split(key, 8)
    base = jnp.clip(jax.random.normal(keys[0], (POSITIONS, POSITIONS, DUAL_WIDTH), jnp.float32), -4.0, 4.0)
    amplitude = 13.0
    base = lower_regions(keys, base, amplitude)
    return place_aligned(keys, base).astype(jnp.bfloat16)


def draw_duplex_logit_weights(key, part):
    key = jax.random.fold_in(key, 23)
    noise = jnp.clip(jax.random.normal(key, (DUAL_WIDTH, ATTENDER_NUMBER), jnp.float32), -4.0, 4.0) * (0.8 / DUAL_WIDTH ** 0.5)
    amplitude = 13.0
    pattern = amplitude / DUAL_WIDTH * alternating(DUAL_WIDTH)[:, None]
    return (pattern + noise).astype(jnp.bfloat16)


def draw_homolog_ensemble(key, part):
    key = jax.random.fold_in(key, 31)
    keys = jax.random.split(key, 1)
    return jnp.clip(jax.random.normal(keys[0], (ALIGNED_SEQS, POSITIONS, ALIGNED_FEATURES), jnp.float32), -6.0, 6.0).astype(jnp.bfloat16)


def touch_ends(result, key, least, top_value):
    longest = result.shape.index(max(result.shape))
    spots = []
    for shift in (0, 1):
        where = [jax.random.randint(jax.random.fold_in(key, axis), (), 0, length) for axis, length in enumerate(result.shape)]
        where[longest] = (where[longest] + shift) % result.shape[longest]
        spots.append(tuple(where))
    return result.at[spots[0]].set(least).at[spots[1]].set(top_value)


def steps_of(own_key, dims, shards, least, top_value):
    level = 1.0
    for position, blocks in shards:
        draws = jax.random.uniform(jax.random.fold_in(jax.random.fold_in(own_key, 6), position), (blocks,), jnp.float32, least / len(shards), top_value / len(shards))
        level = level * jnp.repeat(jnp.exp(draws), dims[position] // blocks).reshape((-1,) + (1,) * (len(dims) - 1 - position))
    return level


def scatter_about(key, shape, scale, limit, shards=(), kind=jnp.bfloat16):
    entries = jax.random.normal(key, shape, jnp.float32) * scale
    if len(shards) > 0:
        entries = steps_of(key, shape, shards, -0.22, 0.18) * entries
    return jnp.clip(entries, min=-limit, max=limit).astype(kind)


def setup_inputs(seed: int = 0, part: int = 0) -> dict:
    key_of = jax.random.split(jax.random.key(seed), 14)
    part_splits = jax.random.split(jax.random.fold_in(key_of[13], part), 14)
    homolog_ensemble = draw_homolog_ensemble(jax.random.fold_in(jax.random.fold_in(key_of[13], part), 71), part)
    duplex_embedding = draw_duplex_embedding(jax.random.fold_in(jax.random.fold_in(key_of[13], part), 71), part)
    homolog_present_flags = touch_ends((jax.random.randint(part_splits[2], (ALIGNED_SEQS,), 0, 4) < 3).astype(jnp.int32), jax.random.fold_in(part_splits[2], 1), 0, 1)
    resolved_position_flags = touch_ends((jax.random.randint(part_splits[3], (POSITIONS,), 0, 8) < 7).astype(jnp.int32), jax.random.fold_in(part_splits[3], 1), 0, 1)
    payload_weights = scatter_about(key_of[4], (ALIGNED_FEATURES, ATTENDER_NUMBER * PER_ATTEND_SIZE), ALIGNED_FEATURES ** -0.5, 0.75)
    sigmoid_weights = scatter_about(key_of[5], (ALIGNED_FEATURES, ATTENDER_NUMBER * PER_ATTEND_SIZE), ALIGNED_FEATURES ** -0.5, 0.75)
    averager_final_weights = scatter_about(key_of[6], (ATTENDER_NUMBER * PER_ATTEND_SIZE, ALIGNED_FEATURES), (ATTENDER_NUMBER * PER_ATTEND_SIZE) ** -0.5, 0.375)
    first_operand_weights = scatter_about(key_of[7], (ALIGNED_FEATURES, PRODUCT_FEATURES), ALIGNED_FEATURES ** -0.5, 0.75)
    second_operand_weights = scatter_about(key_of[8], (ALIGNED_FEATURES, PRODUCT_FEATURES), ALIGNED_FEATURES ** -0.5, 0.75)
    duplex_logit_weights = draw_duplex_logit_weights(jax.random.fold_in(key_of[13], 71), part)
    tensor_product_weights = scatter_about(key_of[10], (PRODUCT_FEATURES * PRODUCT_FEATURES, DUAL_WIDTH), (PRODUCT_FEATURES * PRODUCT_FEATURES) ** -0.5, 0.1875)
    averager_upstream_adjoint = scatter_about(part_splits[11], (ALIGNED_SEQS, POSITIONS, ALIGNED_FEATURES), 1.0, 6.0, ((0, 2), (1, 4)))
    duplex_upstream_adjoint = scatter_about(part_splits[12], (POSITIONS, POSITIONS, DUAL_WIDTH), 0.25, 2.5, ((0, 4), (1, 2)))
    return dict(homolog_ensemble=homolog_ensemble, duplex_embedding=duplex_embedding, homolog_present_flags=homolog_present_flags, resolved_position_flags=resolved_position_flags, payload_weights=payload_weights, sigmoid_weights=sigmoid_weights, averager_final_weights=averager_final_weights, first_operand_weights=first_operand_weights, second_operand_weights=second_operand_weights, duplex_logit_weights=duplex_logit_weights, tensor_product_weights=tensor_product_weights, averager_upstream_adjoint=averager_upstream_adjoint, duplex_upstream_adjoint=duplex_upstream_adjoint)


EPS = 1e-05
PENALTY = 10000.0

def standardize_features(inputs):
    inputs = inputs.astype(jnp.float32)
    row_mean = lax.optimization_barrier(jnp.mean(inputs, -1, keepdims=True))
    centred = inputs - row_mean
    inverse = lax.rsqrt(lax.optimization_barrier(jnp.mean(centred * centred, -1, keepdims=True)) + EPS)
    return (centred * inverse, inverse)

def standardizer_derivative(inputs, upstream):
    scaled, inverse = standardize_features(inputs)
    mean_grad = lax.optimization_barrier(jnp.mean(upstream, -1, keepdims=True))
    mean_cross = lax.optimization_barrier(jnp.mean(upstream * scaled, -1, keepdims=True))
    return (upstream - mean_grad - scaled * mean_cross) * inverse

def reference(homolog_ensemble, duplex_embedding, homolog_present_flags, resolved_position_flags, payload_weights, sigmoid_weights, averager_final_weights, first_operand_weights, second_operand_weights, duplex_logit_weights, tensor_product_weights, averager_upstream_adjoint, duplex_upstream_adjoint):
    highest = lax.Precision.HIGHEST
    ensemble_standardized = standardize_features(homolog_ensemble)[0].astype(jnp.bfloat16)
    normed_broadcast = ensemble_standardized.astype(jnp.float32)
    payload_vectors = jnp.einsum('snm,mv->snv', normed_broadcast, payload_weights.astype(jnp.float32)).astype(jnp.bfloat16)
    gates = jax.nn.sigmoid(jnp.einsum('snm,mv->snv', normed_broadcast, sigmoid_weights.astype(jnp.float32)))
    present_flags = homolog_present_flags.astype(jnp.float32)
    left_projected = (jnp.einsum('snm,mp->snp', normed_broadcast, first_operand_weights.astype(jnp.float32)) * present_flags[:, None, None]).astype(jnp.bfloat16)
    right_proj = (jnp.einsum('snm,mp->snp', normed_broadcast, second_operand_weights.astype(jnp.float32)) * present_flags[:, None, None]).astype(jnp.bfloat16)
    pair_norm = standardize_features(duplex_embedding)[0].astype(jnp.bfloat16)
    logits = jnp.einsum('ijz,zh->hij', pair_norm.astype(jnp.float32), duplex_logit_weights.astype(jnp.float32))
    logits = logits + (resolved_position_flags.astype(jnp.float32)[None, None, :] - 1.0) * PENALTY
    peak = lax.optimization_barrier(jnp.max(logits, -1, keepdims=True))
    shifted = jnp.exp(logits - peak)
    soft = shifted / lax.optimization_barrier(jnp.sum(shifted, -1, keepdims=True))
    reduced_precision_softmax = soft.astype(jnp.bfloat16).astype(jnp.float32)
    payload_per_attender = payload_vectors.astype(jnp.float32).reshape(ALIGNED_SEQS, POSITIONS, ATTENDER_NUMBER, PER_ATTEND_SIZE)
    blended_payload = jnp.einsum('wgp,tpwb->tgwb', reduced_precision_softmax, payload_per_attender).reshape(ALIGNED_SEQS, POSITIONS, ATTENDER_NUMBER * PER_ATTEND_SIZE)
    gated_gradient = jnp.einsum('rlu,gu->rlg', averager_upstream_adjoint.astype(jnp.float32), averager_final_weights.astype(jnp.float32))
    derivative_blended = (gated_gradient * gates).astype(jnp.bfloat16)
    grad_gate = (gated_gradient * blended_payload * gates * (1.0 - gates)).astype(jnp.bfloat16)
    derivative_per_attender = derivative_blended.astype(jnp.float32).reshape(ALIGNED_SEQS, POSITIONS, ATTENDER_NUMBER, PER_ATTEND_SIZE)
    grad_soft = jnp.einsum('sihc,sjhc->hij', derivative_per_attender, payload_per_attender)
    derivative_payload = jnp.einsum('aqd,zqar->zdar', reduced_precision_softmax, derivative_per_attender).reshape(ALIGNED_SEQS, POSITIONS, ATTENDER_NUMBER * PER_ATTEND_SIZE)
    row_count = 0.001 + jnp.sum(present_flags)
    block_rows = 8 if POSITIONS % 8 == 0 else 1
    left_wide = left_projected.astype(jnp.float32)
    right_wide = right_proj.astype(jnp.float32)
    outer_wide = tensor_product_weights.astype(jnp.float32)

    def outer_step(carry, block_index):
        right_acc, weight_acc = carry
        first_row = block_index * block_rows
        cot_block = lax.dynamic_slice_in_dim(duplex_upstream_adjoint, first_row, block_rows, 0).astype(jnp.float32)
        grad_outer = (jnp.einsum('ijz,kz->ijk', cot_block, outer_wide) / row_count).astype(jnp.bfloat16)
        grad_outer = grad_outer.astype(jnp.float32).reshape(block_rows, POSITIONS, PRODUCT_FEATURES, PRODUCT_FEATURES)
        left_block = lax.dynamic_slice_in_dim(left_wide, first_row, block_rows, 1)
        first_operand_derivative = jnp.einsum('ijpq,sjq->sip', grad_outer, right_wide)
        right_acc = right_acc + jnp.einsum('ijpq,sip->sjq', grad_outer, left_block)
        outer_block = (jnp.einsum('sip,sjq->ijpq', left_block, right_wide) / row_count).astype(jnp.bfloat16).astype(jnp.float32)
        weight_acc = weight_acc + jnp.einsum('ak,az->kz', outer_block.reshape(block_rows * POSITIONS, PRODUCT_FEATURES * PRODUCT_FEATURES), cot_block.reshape(block_rows * POSITIONS, DUAL_WIDTH), precision=highest)
        return ((right_acc, weight_acc), first_operand_derivative)
    initial_accumulator = (jnp.zeros((ALIGNED_SEQS, POSITIONS, PRODUCT_FEATURES), jnp.float32), jnp.zeros((PRODUCT_FEATURES * PRODUCT_FEATURES, DUAL_WIDTH), jnp.float32))
    (right_grad, outer_matrix_gradient), first_operand_pieces = lax.scan(outer_step, initial_accumulator, jnp.arange(POSITIONS // block_rows))
    first_operand_derivative = jnp.transpose(first_operand_pieces, (1, 0, 2, 3)).reshape(ALIGNED_SEQS, POSITIONS, PRODUCT_FEATURES) * present_flags[:, None, None]
    right_grad = right_grad * present_flags[:, None, None]
    standardized_derivative = jnp.einsum('snv,mv->snm', grad_gate.astype(jnp.float32), sigmoid_weights.astype(jnp.float32))
    standardized_derivative = standardized_derivative + jnp.einsum('snv,mv->snm', derivative_payload, payload_weights.astype(jnp.float32), precision=highest)
    standardized_derivative = standardized_derivative + jnp.einsum('snp,mp->snm', first_operand_derivative, first_operand_weights.astype(jnp.float32), precision=highest)
    standardized_derivative = standardized_derivative + jnp.einsum('snp,mp->snm', right_grad, second_operand_weights.astype(jnp.float32), precision=highest)
    ensemble_derivative = standardizer_derivative(homolog_ensemble, standardized_derivative).astype(jnp.bfloat16)
    row_dot = lax.optimization_barrier(jnp.sum(soft * grad_soft, -1, keepdims=True))
    grad_logits = soft * (grad_soft - row_dot)
    grad_pair_norm = jnp.einsum('hij,zh->ijz', grad_logits, duplex_logit_weights.astype(jnp.float32), precision=highest)
    pairwise_gradient = standardizer_derivative(duplex_embedding, grad_pair_norm).astype(jnp.bfloat16)
    return (ensemble_derivative, pairwise_gradient, outer_matrix_gradient)
```

```python
import functools
import math

import jax
import jax.numpy as jnp
from jax import lax
from jax.experimental import pallas as pl
from jax.experimental.pallas import tpu as pltpu
from jax.sharding import PartitionSpec as P

EPS = 1e-05
PENALTY = 10000.0
F32 = jnp.float32
BF16 = jnp.bfloat16
LANES = 128
NN = (((1,), (0,)), ((), ()))
NT = (((1,), (1,)), ((), ()))
VMEM = pl.BlockSpec(memory_space=pltpu.VMEM)
SMEM = pl.BlockSpec(memory_space=pltpu.SMEM)


def mm(a, b, dims=NN):
    return lax.dot_general(a, b, dims, preferred_element_type=F32)


def split_high_low(value):
    high = value.astype(BF16)
    return high, (value - high.astype(F32)).astype(BF16)


def iota(shape, dim):
    return lax.broadcasted_iota(jnp.int32, shape, dim)


def lanes_of(pieces):
    return pieces[0] if len(pieces) == 1 else jnp.concatenate(pieces, axis=-1)


def rows_of(pieces):
    return pieces[0] if len(pieces) == 1 else jnp.concatenate(pieces, axis=0)


def standardize(values):
    centred = values - jnp.mean(values, -1, keepdims=True)
    inverse = lax.rsqrt(jnp.mean(centred * centred, -1, keepdims=True) + EPS)
    return centred * inverse, inverse


def standardize_backward(values, upstream):
    scaled, inverse = standardize(values)
    mean_grad = jnp.mean(upstream, -1, keepdims=True)
    mean_cross = jnp.mean(upstream * scaled, -1, keepdims=True)
    return (upstream - mean_grad - scaled * mean_cross) * inverse


def on_diagonal(block, width):
    rows, lanes = block.shape
    same = iota(block.shape, 0) // (rows // 2) == iota(block.shape, 1) // width
    return jnp.where(same, block, jnp.zeros_like(block))


def live_masks(live_ref, first, pairs, width):
    lane = iota((1, 2 * width), 1)
    return [
        jnp.where(lane < width, live_ref[first + 2 * k], live_ref[first + 2 * k + 1]).astype(F32)
        for k in range(pairs)
    ]


def inverse_count(live_ref):
    total = live_ref[0]
    for s in range(1, live_ref.shape[0]):
        total = total + live_ref[s]
    return 1.0 / (0.001 + jnp.full((1, LANES), total, jnp.int32).astype(F32))


def normalise_kernel(g, x_ref, e_ref, flag_ref, wl_ref, xn_ref, *rest):
    logit_refs, (rows_ref, heads_ref) = rest[: g.C], rest[g.C :]
    normed = standardize(x_ref[...].astype(F32))[0].reshape(g.SP, 2, g.I, g.M)
    xn_ref[...] = jnp.concatenate([normed[:, 0], normed[:, 1]], axis=-1).astype(BF16)
    pair = standardize(e_ref[...].astype(F32).reshape(g.I * g.JC, g.Z))[0].astype(BF16)
    eye = (iota((g.H, g.H), 0) == iota((g.H, g.H), 1)).astype(BF16)
    weights = mm(eye, wl_ref[...], NT).astype(BF16)
    penalty = (flag_ref[...].astype(F32) - 1.0) * PENALTY
    for i in range(g.I):
        rows_ref[i * g.H : (i + 1) * g.H, : g.JC] = (
            mm(weights, pair[i * g.JC : (i + 1) * g.JC], NT) + penalty
        )
    for h in range(g.H):
        heads_ref[h] = rows_ref[pl.ds(h, g.I, stride=g.H), :][:, : g.JC]
    col = lax.axis_index("col")
    for k in range(g.C):
        first = lax.rem(col + k, g.C) * g.HL
        logit_refs[k][...] = heads_ref[pl.ds(first, g.HL)].reshape(g.HL * g.I, g.JC)


def local_kernel(
    g, xn_ref, u_ref, sg_ref, wf_ref, w1_ref, t_ref, live_ref,
    gm_ref, gate_ref, left_ref, ts_ref, lt_ref, wide_ref, half_ref,
):
    col, depth = lax.axis_index("col"), lax.axis_index("depth")
    rows = g.SP * g.I
    xn = xn_ref[...]
    pick = (iota((g.HW * g.H // g.HL, 2 * g.HW), 0) == col * g.HW + iota((g.HW * g.H // g.HL, 2 * g.HW), 1) % g.HW).astype(BF16)
    sg = sg_ref[...]
    gate_weights = on_diagonal(mm(rows_of([sg, sg]), pick), g.HW).astype(BF16)
    gates = jax.nn.sigmoid(mm(xn.reshape(rows, 2 * g.M), gate_weights))
    u = u_ref[...].reshape(g.SP, 2, g.I, g.M)
    packed_u = jnp.concatenate([u[:, 0], u[:, 1]], axis=-1).reshape(rows, 2 * g.M)
    wf = wf_ref[pl.ds(pl.multiple_of(col * g.HW, g.HW), g.HW), :]
    zero = jnp.zeros_like(wf)
    final_weights = rows_of([lanes_of([wf, zero]), lanes_of([zero, wf])])
    gated = mm(packed_u, final_weights, NT)
    blended = gated * gates
    gm_ref[...] = blended.astype(BF16)
    gate_ref[...] = blended * (1.0 - gates)
    masks = live_masks(live_ref, depth * g.S, g.SP, g.M)
    live_xn = rows_of([(xn[k].astype(F32) * masks[k]).astype(BF16) for k in range(g.SP)])
    w1 = lanes_of([w1_ref[...], jnp.zeros((g.M, LANES - g.Q), BF16)])
    zero = jnp.zeros_like(w1)
    half_ref[0] = mm(live_xn, rows_of([w1, zero]))
    half_ref[1] = mm(live_xn, rows_of([zero, w1]))
    for half in range(2):
        for i in range(g.I):
            first = (half * g.I + i) * g.SP
            left_ref[first : first + g.SP, :] = half_ref[half, pl.ds(i, g.SP, stride=g.I), :][
                :, : g.Q
            ].astype(BF16)
    wide_ref[...] = t_ref[...].astype(F32)
    for q in range(g.QL):
        ts_ref[q] = wide_ref[pl.ds(col * g.QL + q, g.Q, stride=g.Q), :].astype(BF16)
    left = left_ref[...]
    for q in range(0, g.QL, 2):
        product = mm(left, lanes_of([ts_ref[q], ts_ref[q + 1]]))
        for k in range(2):
            for half in range(2):
                block = product[half * g.I * g.SP : (half + 1) * g.I * g.SP, k * g.Z : (k + 1) * g.Z]
                first = (q + k) * g.S + half * g.SP
                lt_ref[:, first : first + g.SP, :] = block.reshape(g.I, g.SP, g.Z).astype(BF16)


def outer_kernel(g, *refs):
    refs = list(refs)
    x_refs, refs = refs[: g.R], refs[g.R :]
    d_refs, refs = refs[: g.C], refs[g.C :]
    left_ref, ts_ref, lt_ref, w1_ref, w2_ref, live_ref = refs[:6]
    refs = refs[6:]
    xall_ref, w_refs, refs = refs[0], refs[1 : 1 + g.D], refs[1 + g.D :]
    go_ref, gl_ref, d_ref, spread_ref, rt_ref, ds_ref, all_ref, turn_ref, rg_ref = refs
    row, col, depth = (lax.axis_index(a) for a in ("row", "col", "depth"))
    masks = live_masks(live_ref, depth * g.S, g.SP, g.M)
    scale = inverse_count(live_ref)
    for k in range(g.R):
        xall_ref[:, pl.ds(g.place(lax.rem(row - k + g.R, g.R), col), g.I), :] = x_refs[k][...]
    for k in range(g.C):
        spot = (g.C - k) % g.C
        d_ref[:, spot * g.JC : (spot + 1) * g.JC, :] = d_refs[k][...]
    w2 = w2_ref[...]
    doubled = rows_of([w2, w2])
    pick = (iota((2 * g.QL, g.Q), 1) == col * g.QL + iota((2 * g.QL, g.Q), 0) % g.QL).astype(BF16)
    second = on_diagonal(mm(pick, doubled, NT), g.M).astype(BF16)
    for k in range(g.SP):
        live_x = (xall_ref[k].astype(F32) * masks[k]).astype(BF16)
        part = mm(second, live_x, NT)
        for t in range(g.NT):
            lanes = min(LANES, g.N - t * LANES)
            spread_ref[t, k * 2 * g.QL : (k + 1) * 2 * g.QL, :lanes] = part[
                :, t * LANES : t * LANES + lanes
            ]
    for q in range(g.QL):
        for half in range(2):
            first = q * g.S + half * g.SP
            for t in range(g.NT):
                lanes = min(LANES, g.N - t * LANES)
                piece = spread_ref[t, pl.ds(half * g.QL + q, g.SP, stride=2 * g.QL), :]
                rt_ref[first : first + g.SP, t * LANES : t * LANES + lanes] = piece[
                    :, :lanes
                ].astype(BF16)
    rt = rt_ref[...]
    for i in range(0, g.I, 2):
        product = mm(rt, lanes_of([d_ref[i], d_ref[i + 1]]))
        for k in range(2):
            block = product[:, k * g.Z : (k + 1) * g.Z]
            ds_ref[:, :, i + k] = block.reshape(g.QL, 2, g.SP, g.Z).astype(BF16)
    left = left_ref[...]
    eye = (iota((g.Q, g.Q), 0) == iota((g.Q, g.Q), 1)).astype(BF16)
    left_t = mm(eye, left, NT).astype(BF16)
    entries = g.S * g.I
    left_grad = jnp.zeros((entries, g.Q), F32)
    for q in range(0, g.QL, 2):
        both = lanes_of([ds_ref[q].reshape(entries, g.Z), ds_ref[q + 1].reshape(entries, g.Z)])
        part = mm(left_t, both)
        all_ref[q] = part[:, : g.Z] * scale
        all_ref[q + 1] = part[:, g.Z :] * scale
        left_grad = left_grad + mm(both, lanes_of([ts_ref[q], ts_ref[q + 1]]), NT)
    share = g.QL // g.D
    for k in range(g.D):
        first = lax.rem(depth + k, g.D) * share
        w_refs[k][...] = all_ref[pl.ds(first, share)].reshape(share * g.Q, g.Z)
    w1 = w1_ref[...]
    zero = jnp.zeros_like(w1)
    first_term = jnp.zeros((entries // 2, 2 * g.M), F32)
    for half in range(2):
        weights = rows_of([w1, zero] if half == 0 else [zero, w1])
        block = left_grad[half * (entries // 2) : (half + 1) * (entries // 2)] * scale[:, : g.Q]
        for piece in split_high_low(block):
            first_term = first_term + mm(piece, weights, NT)
    turn_ref[...] = first_term
    for k in range(g.SP):
        gl_ref[k] = turn_ref[pl.ds(k, g.I, stride=g.SP), :] * masks[k]
    right_grad = jnp.zeros((g.QL * g.S, g.N), F32)
    for i in range(0, g.I, 2):
        right_grad = right_grad + mm(
            lanes_of([lt_ref[i], lt_ref[i + 1]]), lanes_of([d_ref[i], d_ref[i + 1]]), NT
        )
    for t in range(g.NT):
        lanes = min(LANES, g.N - t * LANES)
        piece = right_grad[:, t * LANES : t * LANES + lanes]
        if lanes < LANES:
            piece = lanes_of([piece, jnp.zeros((g.QL * g.S, LANES - lanes), F32)])
        rg_ref[t] = piece
    deep = 2 * g.QL
    group = min(g.SP, LANES // deep)
    order = iota((group * deep, g.Q), 0) % deep // 2
    pick = (iota((group * deep, g.Q), 1) == col * g.QL + order).astype(BF16)
    base = mm(pick, doubled, NT)
    which = iota(base.shape, 0)
    base = jnp.where(which % 2 == iota(base.shape, 1) // g.M, base, 0.0)
    weights = lanes_of([jnp.where(which // deep == k, base, 0.0) for k in range(group)]).astype(BF16)
    for k in range(0, g.SP, group):
        for t in range(g.NT):
            lanes = min(LANES, g.N - t * LANES)
            tall = rows_of(
                [rg_ref[t, pl.ds(k + m, deep, stride=g.SP), :] for m in range(group)]
            )
            tall = (tall * scale).T[:lanes]
            high, low = split_high_low(tall)
            part = mm(high, weights) + mm(low, weights)
            for m in range(group):
                go_ref[k + m, t * LANES : t * LANES + lanes, :] = (
                    part[:, m * 2 * g.M : (m + 1) * 2 * g.M] * masks[k + m]
                )


def attend_kernel(g, *refs):
    refs = list(refs)
    xall_ref, refs = refs[0], refs[1:]
    logit_refs, refs = refs[: g.C], refs[g.C :]
    gm_ref, gate_ref, p_ref, sg_ref, go_ref, gl_ref = refs[:6]
    soft_ref, gs_ref, own_ref, send_refs, refs = refs[6], refs[7], refs[8], refs[9 : 8 + g.R], refs[8 + g.R :]
    total_ref, gg_ref = refs
    row, col = lax.axis_index("row"), lax.axis_index("col")
    logits = lanes_of([logit_refs[(g.C - k) % g.C][...] for k in range(g.C)])
    shifted = jnp.exp(logits - jnp.max(logits, -1, keepdims=True))
    soft = shifted / jnp.sum(shifted, -1, keepdims=True)
    soft_ref[...] = soft
    low = soft.astype(BF16)
    eye = (iota((g.N, g.N), 0) == iota((g.N, g.N), 1)).astype(BF16)
    low_t = mm(eye, low, NT).astype(BF16)
    wide = g.HW * g.H // g.HL
    pick = (iota((wide, 2 * g.HW), 0) == col * g.HW + iota((wide, 2 * g.HW), 1) % g.HW).astype(BF16)
    p, sg = p_ref[...], sg_ref[...]
    value_weights = on_diagonal(mm(rows_of([p, p]), pick), g.HW).astype(BF16)
    gate_weights = on_diagonal(mm(rows_of([sg, sg]), pick), g.HW).astype(BF16)
    values = mm(xall_ref[...].reshape(g.SP * g.N, 2 * g.M), value_weights).astype(BF16)
    head = iota((1, 2 * g.HW), 1) % g.HW // (g.HW // g.HL)
    grad_soft = jnp.zeros((g.HL * g.I, g.N), F32)
    for k in range(g.SP):
        v = values[k * g.N : (k + 1) * g.N]
        crossed = mm(low, v)
        mixed = jnp.zeros((g.I, 2 * g.HW), F32)
        for h in range(g.HL):
            mixed = mixed + jnp.where(head == h, crossed[h * g.I : (h + 1) * g.I], 0.0)
        rows = slice(k * g.I, (k + 1) * g.I)
        gg_ref[rows, :] = (gate_ref[rows, :] * mixed).astype(BF16)
        blended = gm_ref[rows, :]
        by_head = rows_of(
            [jnp.where(head == h, blended, jnp.zeros_like(blended)) for h in range(g.HL)]
        )
        grad_soft = grad_soft + mm(by_head, v, NT)
        part = go_ref[k]
        for piece in split_high_low(mm(low_t, by_head)):
            part = part + mm(piece, value_weights, NT)
        total_ref[k] = part
    gs_ref[...] = grad_soft
    own = total_ref[:, pl.ds(g.place(row, col), g.I), :]
    gate_term = mm(gg_ref[...], gate_weights, NT).reshape(g.SP, g.I, 2 * g.M)
    own_ref[...] = own + gate_term + gl_ref[...]
    for k in range(1, g.R):
        spot = g.place(lax.rem(row + k, g.R), col)
        send_refs[k - 1][...] = total_ref[:, pl.ds(spot, g.I), :].astype(BF16)


def row_sum_kernel(g, *refs):
    total = refs[0][...]
    for ref in refs[1:-1]:
        total = total + ref[...].astype(F32)
    refs[-1][...] = total.astype(BF16)


def ensemble_kernel(g, x_ref, *refs):
    parts, (out_ref, order_ref) = refs[: g.C], refs[g.C :]
    col = lax.axis_index("col")
    for k in range(g.C):
        order_ref[lax.rem(col - k + g.C, g.C)] = parts[k][...]
    total = order_ref[0].astype(F32)
    for k in range(1, g.C):
        total = total + order_ref[k].astype(F32)
    pieces = [total[:, :, : g.M].reshape(g.SP, 1, g.I, g.M), total[:, :, g.M :].reshape(g.SP, 1, g.I, g.M)]
    upstream = jnp.concatenate(pieces, axis=1).reshape(g.S, g.I, g.M)
    out_ref[...] = standardize_backward(x_ref[...].astype(F32), upstream).astype(BF16)


def logit_grad_kernel(g, soft_ref, *refs):
    parts, outs, order_ref = refs[: g.D], refs[g.D : g.D + g.C], refs[g.D + g.C]
    depth = lax.axis_index("depth")
    for k in range(g.D):
        order_ref[lax.rem(depth - k + g.D, g.D)] = parts[k][...]
    grad_soft = order_ref[0]
    for k in range(1, g.D):
        grad_soft = grad_soft + order_ref[k]
    soft = soft_ref[...]
    grad = soft * (grad_soft - jnp.sum(soft * grad_soft, -1, keepdims=True))
    for k in range(g.C):
        outs[k][...] = grad[:, k * g.JC : (k + 1) * g.JC]


def pair_kernel(g, e_ref, wl_ref, *refs):
    parts, (out_ref, order_ref) = refs[: g.C], refs[g.C :]
    col = lax.axis_index("col")
    for k in range(g.C):
        first = pl.multiple_of(lax.rem(col - k + g.C, g.C) * g.HL * g.I, g.HL * g.I)
        order_ref[pl.ds(first, g.HL * g.I), : g.JC] = parts[k][...]
    count = g.H * g.I
    order_ref[:, g.JC :] = jnp.zeros((count, LANES - g.JC), F32)
    high, low = split_high_low(order_ref[...].T[: g.JC])
    grads = lanes_of([high, low])
    pick = (iota((count, g.H), 0) // g.I == iota((count, g.H), 1)).astype(BF16)
    base = mm(pick, wl_ref[...], NT).astype(BF16)
    token = iota((count, 1), 0) % g.I
    for i in range(0, g.I, 2):
        weights = lanes_of(
            [jnp.where(token == i + k, base, jnp.zeros_like(base)) for k in range(2)]
        )
        upstream = mm(grads, rows_of([weights, weights]))
        for k in range(2):
            out_ref[i + k] = standardize_backward(
                e_ref[i + k].astype(F32), upstream[:, k * g.Z : (k + 1) * g.Z]
            ).astype(BF16)


def half_sum_kernel(g, *refs):
    parts, outs, sum_ref = refs[: g.D], refs[g.D : g.D + g.R], refs[-1]
    total = parts[0][...]
    for ref in parts[1:]:
        total = total + ref[...]
    sum_ref[...] = total
    row = lax.axis_index("row")
    for k in range(g.R):
        outs[k][...] = sum_ref[lax.rem(row + k, g.R)]


def gather_kernel(g, *refs):
    parts, out_ref = refs[:-1], refs[-1]
    row, col = lax.axis_index("row"), lax.axis_index("col")
    for k in range(g.C):
        for m in range(g.R):
            out_ref[lax.rem(col - k + g.C, g.C), lax.rem(row - m + g.R, g.R)] = parts[
                k * g.R + m
            ][...]


def matrix_kernel(g, *refs):
    parts, (out_ref, order_ref) = refs[: g.D], refs[g.D :]
    depth = lax.axis_index("depth")
    for k in range(g.D):
        order_ref[lax.rem(depth - k + g.D, g.D)] = parts[k][...]
    share = g.QL // g.D
    for c in range(g.C):
        for d in range(g.D):
            for q in range(share):
                out_ref[pl.ds(c * g.QL + d * share + q, g.Q, stride=g.Q), :] = order_ref[
                    d, c, q
                ].astype(F32)


class Sizes:
    def __init__(self, x, e, wl, p, w1):
        self.R, self.C, self.D = (lax.axis_size(a) for a in ("row", "col", "depth"))
        self.S, self.I, self.M = x.shape
        self.JC, self.Z = e.shape[1:]
        self.H, self.Q = wl.shape[1], w1.shape[1]
        self.SP, self.N = self.S // 2, self.R * self.I
        self.HL, self.QL = self.H // self.C, self.Q // self.C
        self.HW = p.shape[1] // self.C
        self.F = self.R // self.C
        self.NT = -(-self.N // LANES)

    def place(self, row, col):
        turn = lax.rem(row // self.F - col + self.C, self.C)
        return pl.multiple_of((turn * self.F + lax.rem(row, self.F)) * self.I, self.I)


def shift(array, axis, k):
    count = lax.axis_size(axis)
    return lax.ppermute(array, axis, [(i, (i + k) % count) for i in range(count)])


def from_all(array, axis):
    return [array] + [shift(array, axis, k) for k in range(1, lax.axis_size(axis))]


def to_all(arrays, axis):
    return [arrays[0]] + [shift(a, axis, k) for k, a in enumerate(arrays) if k > 0]


def per_device(
    homolog_ensemble,
    duplex_embedding,
    homolog_present_flags,
    resolved_position_flags,
    payload_weights,
    sigmoid_weights,
    averager_final_weights,
    first_operand_weights,
    second_operand_weights,
    duplex_logit_weights,
    tensor_product_weights,
    averager_upstream_adjoint,
    duplex_upstream_adjoint,
):
    g = Sizes(
        homolog_ensemble, duplex_embedding, duplex_logit_weights, payload_weights, first_operand_weights
    )
    shape = jax.ShapeDtypeStruct

    def call(kernel, name, args, outs, scratch=(), smem=(), flops=0):
        size = sum(a.size * a.dtype.itemsize for a in args) + sum(
            math.prod(o.shape) * o.dtype.itemsize for o in outs
        )
        single = len(outs) == 1
        return pl.pallas_call(
            functools.partial(kernel, g),
            out_shape=outs[0] if single else tuple(outs),
            in_specs=[SMEM if k in smem else VMEM for k in range(len(args))],
            out_specs=VMEM if single else (VMEM,) * len(outs),
            scratch_shapes=[pltpu.VMEM(*s) for s in scratch],
            compiler_params=pltpu.CompilerParams(vmem_limit_bytes=40 * 1024 * 1024),
            cost_estimate=pl.CostEstimate(flops=flops, bytes_accessed=size, transcendentals=0),
            name=name,
        )(*args)

    cotangents = from_all(duplex_upstream_adjoint, "col")
    heads = g.HL * g.I
    entries = g.S * g.I
    packed = (g.SP, g.I, 2 * g.M)
    xn, *logits = call(
        normalise_kernel,
        "normalise",
        (homolog_ensemble, duplex_embedding, resolved_position_flags.reshape(1, g.JC), duplex_logit_weights),
        [shape(packed, BF16)] + [shape((heads, g.JC), F32)] * g.C,
        [((g.I * g.H, LANES), F32), ((g.H, g.I, g.JC), F32)],
    )
    everyone = from_all(xn, "row")
    logits = to_all(logits, "col")
    blended, gate_factor, left, weights, left_weights = call(
        local_kernel,
        "local",
        (xn, averager_upstream_adjoint, sigmoid_weights, averager_final_weights, first_operand_weights, tensor_product_weights, homolog_present_flags),
        [
            shape((g.SP * g.I, 2 * g.HW), BF16),
            shape((g.SP * g.I, 2 * g.HW), F32),
            shape((entries, g.Q), BF16),
            shape((g.QL, g.Q, g.Z), BF16),
            shape((g.I, g.QL * g.S, g.Z), BF16),
        ],
        [(tensor_product_weights.shape, F32), ((2, g.SP * g.I, LANES), F32)],
        smem=(6,),
    )
    share = g.QL // g.D * g.Q
    xall, *rest = call(
        outer_kernel,
        "outer",
        (*everyone, *cotangents, left, weights, left_weights, first_operand_weights, second_operand_weights, homolog_present_flags),
        [shape((g.SP, g.N, 2 * g.M), BF16)]
        + [shape((share, g.Z), F32)] * g.D
        + [shape((g.SP, g.N, 2 * g.M), F32), shape(packed, F32)],
        [
            ((g.I, g.N, g.Z), BF16),
            ((g.NT, g.SP * 2 * g.QL, LANES), F32),
            ((g.QL * g.S, g.N), BF16),
            ((g.QL, 2, g.I, g.SP, g.Z), BF16),
            ((g.QL, g.Q, g.Z), F32),
            ((g.SP * g.I, 2 * g.M), F32),
            ((g.NT, g.QL * g.S, LANES), F32),
        ],
        smem=(g.R + g.C + 5,),
    )
    matrix_parts, (second_term, first_term) = rest[: g.D], rest[g.D :]
    chunk = share // g.R
    matrix_parts = [a.reshape(g.R, chunk, g.Z) for a in to_all(matrix_parts, "depth")]
    matrix_parts = call(
        half_sum_kernel, "half_sum", matrix_parts, [shape((chunk, g.Z), F32)] * g.R,
        [((g.R, chunk, g.Z), F32)],
    )
    matrix_chunk = call(
        row_sum_kernel, "matrix_sum", to_all(matrix_parts, "row"), [shape((chunk, g.Z), BF16)]
    )
    soft, grad_soft, own, *sends = call(
        attend_kernel,
        "attend",
        (xall, *logits, blended, gate_factor, payload_weights, sigmoid_weights, second_term, first_term),
        [shape((heads, g.N), F32), shape((heads, g.N), F32), shape(packed, F32)]
        + [shape(packed, BF16)] * (g.R - 1),
        [((g.SP, g.N, 2 * g.M), F32), ((g.SP * g.I, 2 * g.HW), BF16)],
    )
    grad_softs = from_all(grad_soft, "depth")
    ensemble_part = call(
        row_sum_kernel, "row_sum", to_all([own] + sends, "row"), [shape(packed, BF16)]
    )
    grad_logits = call(
        logit_grad_kernel,
        "logit_grad",
        (soft, *grad_softs),
        [shape((heads, g.JC), F32)] * g.C,
        [((g.D, heads, g.N), F32)],
    )
    ensemble_derivative = call(
        ensemble_kernel,
        "ensemble",
        (homolog_ensemble, *from_all(ensemble_part, "col")),
        [shape(homolog_ensemble.shape, BF16)],
        [((g.C, *packed), BF16)],
    )
    pairwise_gradient = call(
        pair_kernel,
        "pair",
        (duplex_embedding, duplex_logit_weights, *to_all(grad_logits, "col")),
        [shape(duplex_embedding.shape, BF16)],
        [((g.H * g.I, LANES), F32)],
    )
    chunks = []
    for across in from_all(matrix_chunk, "col"):
        chunks += from_all(across, "row")
    gathered = call(
        gather_kernel, "gather", chunks, [shape((g.C, g.R, chunk, g.Z), BF16)]
    ).reshape(g.C, g.QL // g.D, g.Q, g.Z)
    outer_matrix_gradient = call(
        matrix_kernel,
        "matrix",
        from_all(gathered, "depth"),
        [shape(tensor_product_weights.shape, F32)],
        [((g.D, *gathered.shape), BF16)],
    )
    return (ensemble_derivative, pairwise_gradient, outer_matrix_gradient)


def solution(mesh):
    in_specs = (
        P(("parts", "depth"), "row", None),
        P(("parts", "row"), "col", None),
        P("parts"),
        P(("parts", "col")),
        P(),
        P(),
        P(),
        P(),
        P(),
        P(),
        P(),
        P(("parts", "depth"), "row", None),
        P(("parts", "row"), "col", None),
    )
    out_specs = (
        P(("parts", "depth"), "row", None),
        P(("parts", "row"), "col", None),
        P("parts", None),
    )
    return jax.shard_map(
        per_device, mesh=mesh, in_specs=in_specs, out_specs=out_specs, check_vma=False
    )
```

```python
import functools
import math

import jax
import jax.numpy as jnp
from jax import lax
from jax.experimental import pallas as pl
from jax.experimental.pallas import tpu as pltpu
from jax.sharding import PartitionSpec as P

EPS = 1e-05
PENALTY = 10000.0
F32 = jnp.float32
BF16 = jnp.bfloat16
LANES = 128
NN = (((1,), (0,)), ((), ()))
NT = (((1,), (1,)), ((), ()))
VMEM = pl.BlockSpec(memory_space=pltpu.VMEM)
FAR = pl.BlockSpec(memory_space=pl.ANY)


def mm(a, b, dims=NN):
    return lax.dot_general(a, b, dims, preferred_element_type=F32)


def split_high_low(value):
    high = value.astype(BF16)
    return high, (value - high.astype(F32)).astype(BF16)


def iota(shape, dim):
    return lax.broadcasted_iota(jnp.int32, shape, dim)


def lanes_of(pieces):
    return pieces[0] if len(pieces) == 1 else jnp.concatenate(pieces, axis=-1)


def rows_of(pieces):
    return pieces[0] if len(pieces) == 1 else jnp.concatenate(pieces, axis=0)


def standardize(values):
    centred = values - jnp.mean(values, -1, keepdims=True)
    inverse = lax.rsqrt(jnp.mean(centred * centred, -1, keepdims=True) + EPS)
    return centred * inverse, inverse


def standardize_backward(values, upstream):
    scaled, inverse = standardize(values)
    mean_grad = jnp.mean(upstream, -1, keepdims=True)
    mean_cross = jnp.mean(upstream * scaled, -1, keepdims=True)
    return (upstream - mean_grad - scaled * mean_cross) * inverse


def on_diagonal(block, width):
    rows, lanes = block.shape
    same = iota(block.shape, 0) // (rows // 2) == iota(block.shape, 1) // width
    return jnp.where(same, block, jnp.zeros_like(block))


def split_three(value):
    high = value.astype(BF16)
    rest = value - high.astype(F32)
    middle = rest.astype(BF16)
    return [high, middle, (rest - middle.astype(F32)).astype(BF16)]


def three_lanes(value):
    rows, width = value.shape
    fill = -(3 * width) % LANES
    return lanes_of(split_three(value) + [jnp.zeros((rows, fill), BF16)])


def join_three(parts, width):
    wide = parts.astype(F32)
    return (wide[:, :width] + wide[:, width : 2 * width]) + wide[:, 2 * width : 3 * width]


def normalise_kernel(g, x_ref, e_ref, dd_ref, flag_ref, live_ref, wl_ref, *refs):
    refs = list(refs)
    count = g.carried
    sources, refs = refs[:count], refs[count:]
    xn_ref, own_ref, refs = refs[0], refs[1], refs[2:]
    out_refs, refs = refs[: g.C - 1], refs[g.C - 1 :]
    mask_ref, refs = refs[0], refs[1:]
    targets, refs = refs[:count], refs[count:]
    x_in, e_in, flag_in, live_in, wl_in, rows_ref, heads_ref, first_sem, cot_sem, later_sem = refs
    firsts = [
        pltpu.make_async_copy(a, b, first_sem.at[k])
        for k, (a, b) in enumerate(
            [(e_ref, e_in), (wl_ref, wl_in), (flag_ref, flag_in), (x_ref, x_in), (live_ref, live_in)]
        )
    ]
    cots = [
        pltpu.make_async_copy(dd_ref, ref.at[pl.ds(0, g.I * g.JC)], cot_sem.at[k])
        for k, ref in enumerate(out_refs)
    ]
    laters = [
        pltpu.make_async_copy(a, b, later_sem.at[k])
        for k, (a, b) in enumerate(zip(sources, targets, strict=True))
    ]
    for copy in firsts + cots + laters:
        copy.start()
    for copy in firsts[:3]:
        copy.wait()
    pair = standardize(e_in[...].astype(F32).reshape(g.I * g.JC, g.Z))[0].astype(BF16)
    penalty = (flag_in[...].astype(F32) - 1.0) * PENALTY
    weights = wl_in[...]
    for i in range(g.I):
        rows_ref[i * g.H : (i + 1) * g.H, : g.JC] = (
            mm(weights, pair[i * g.JC : (i + 1) * g.JC], NT) + penalty
        )
    for h in range(g.H):
        heads_ref[h] = rows_ref[pl.ds(h, g.I, stride=g.H), :][:, : g.JC]
    col = lax.axis_index("col")
    for k in range(g.C):
        first = lax.rem(col + k, g.C) * g.HL
        logits = heads_ref[pl.ds(first, g.HL)].reshape(g.HL * g.I, g.JC)
        if k == 0:
            own_ref[...] = logits
        else:
            out_refs[k - 1][g.I * g.JC :, :] = three_lanes(logits)
    for copy in firsts[3:]:
        copy.wait()
    normed = standardize(x_in[...].astype(F32))[0].reshape(g.SP, 2, g.I, g.M)
    packed = jnp.concatenate([normed[:, 0], normed[:, 1]], axis=-1).astype(BF16)
    for r in range(g.R):
        xn_ref[r] = packed
    first = lax.axis_index("depth") * g.S
    lane = iota((1, 2 * g.M), 1)
    for k in range(g.SP):
        pair_flags = jnp.where(lane < g.M, live_in[first + 2 * k], live_in[first + 2 * k + 1])
        mask_ref[k : k + 1, :] = pair_flags.astype(F32)
    total = live_in[0]
    for s in range(1, live_in.shape[0]):
        total = total + live_in[s]
    mask_ref[g.SP : g.SP + 1, :] = 1.0 / (0.001 + jnp.full((1, 2 * g.M), total, jnp.int32).astype(F32))
    for copy in cots + laters:
        copy.wait()


def local_kernel(
    g, xn_ref, u_ref, sg_ref, wf_ref, w1_ref, t_ref, mask_ref,
    gm_ref, gate_ref, left_ref, ts_ref, lt_ref, wide_ref, half_ref,
):
    col = lax.axis_index("col")
    rows = g.SP * g.I
    xn = xn_ref[0]
    wide = g.HW * g.C
    pick = (iota((wide, 2 * g.HW), 0) == col * g.HW + iota((wide, 2 * g.HW), 1) % g.HW).astype(BF16)
    sg, wf = sg_ref[...], wf_ref[...]
    gate_weights = on_diagonal(mm(rows_of([sg, sg]), pick), g.HW).astype(BF16)
    gates = jax.nn.sigmoid(mm(xn.reshape(rows, 2 * g.M), gate_weights))
    u = u_ref[...].reshape(g.SP, 2, g.I, g.M)
    packed_u = jnp.concatenate([u[:, 0], u[:, 1]], axis=-1).reshape(rows, 2 * g.M)
    final_weights = on_diagonal(mm(rows_of([wf, wf]), pick), g.HW).astype(BF16)
    gated = mm(packed_u, final_weights)
    blended = gated * gates
    gm_ref[...] = blended.astype(BF16)
    gate_ref[...] = blended * (1.0 - gates)
    live_xn = rows_of(
        [(xn[k].astype(F32) * mask_ref[k : k + 1, :]).astype(BF16) for k in range(g.SP)]
    )
    w1 = rows_of([w1_ref[...], jnp.zeros((LANES - g.Q, g.M), BF16)])
    zero = jnp.zeros_like(w1)
    half_ref[0] = mm(live_xn, lanes_of([w1, zero]), NT)
    half_ref[1] = mm(live_xn, lanes_of([zero, w1]), NT)
    for half in range(2):
        for i in range(g.I):
            first = (half * g.I + i) * g.SP
            left_ref[first : first + g.SP, :] = half_ref[half, pl.ds(i, g.SP, stride=g.I), :][
                :, : g.Q
            ].astype(BF16)
    wide_ref[...] = t_ref[...].astype(F32)
    for q in range(g.QL):
        ts_ref[q] = wide_ref[pl.ds(col * g.QL + q, g.Q, stride=g.Q), :].astype(BF16)
    left = left_ref[...]
    for q in range(0, g.QL, 2):
        product = mm(left, lanes_of([ts_ref[q], ts_ref[q + 1]]))
        for k in range(2):
            for half in range(2):
                block = product[half * g.I * g.SP : (half + 1) * g.I * g.SP, k * g.Z : (k + 1) * g.Z]
                first = (q + k) * g.S + half * g.SP
                lt_ref[:, first : first + g.SP, :] = block.reshape(g.I, g.SP, g.Z).astype(BF16)


def outer_kernel(g, *refs):
    refs = list(refs)
    x_ref, refs = refs[0], refs[1:]
    d_refs, refs = refs[: g.C], refs[g.C :]
    left_ref, ts_ref, lt_ref, w1_ref, w2_ref, mask_ref = refs[:6]
    refs = refs[6:]
    xall_ref, w_refs, refs = refs[0], refs[1 : 1 + g.D], refs[1 + g.D :]
    go_ref, gl_ref, d_ref, spread_ref, rt_ref, ds_ref, all_ref, turn_ref, rg_ref = refs
    col, depth = lax.axis_index("col"), lax.axis_index("depth")
    masks = [mask_ref[k : k + 1, :] for k in range(g.SP)]
    scale = mask_ref[g.SP : g.SP + 1, :]
    for r in range(g.R):
        xall_ref[:, pl.ds(g.place(r, col), g.I), :] = x_ref[r]
    for k in range(g.C):
        spot = (g.C - k) % g.C
        block = d_refs[k][: g.I * g.JC, :].reshape(g.I, g.JC, g.Z)
        d_ref[:, spot * g.JC : (spot + 1) * g.JC, :] = block
    w2 = w2_ref[...]
    doubled = lanes_of([w2, w2])
    pick = (iota((2 * g.QL, g.Q), 1) == col * g.QL + iota((2 * g.QL, g.Q), 0) % g.QL).astype(BF16)
    second = on_diagonal(mm(pick, doubled), g.M).astype(BF16)
    for k in range(g.SP):
        live_x = (xall_ref[k].astype(F32) * masks[k]).astype(BF16)
        part = mm(second, live_x, NT)
        for t in range(g.NT):
            lanes = min(LANES, g.N - t * LANES)
            spread_ref[t, k * 2 * g.QL : (k + 1) * 2 * g.QL, :lanes] = part[
                :, t * LANES : t * LANES + lanes
            ]
    for q in range(g.QL):
        for half in range(2):
            first = q * g.S + half * g.SP
            for t in range(g.NT):
                lanes = min(LANES, g.N - t * LANES)
                piece = spread_ref[t, pl.ds(half * g.QL + q, g.SP, stride=2 * g.QL), :]
                rt_ref[first : first + g.SP, t * LANES : t * LANES + lanes] = piece[
                    :, :lanes
                ].astype(BF16)
    rt = rt_ref[...]
    for i in range(0, g.I, 2):
        product = mm(rt, lanes_of([d_ref[i], d_ref[i + 1]]))
        for k in range(2):
            block = product[:, k * g.Z : (k + 1) * g.Z]
            ds_ref[:, :, i + k] = block.reshape(g.QL, 2, g.SP, g.Z).astype(BF16)
    left = left_ref[...]
    eye = (iota((g.Q, g.Q), 0) == iota((g.Q, g.Q), 1)).astype(BF16)
    left_t = mm(eye, left, NT).astype(BF16)
    entries = g.S * g.I
    left_grad = jnp.zeros((entries, g.Q), F32)
    for q in range(0, g.QL, 2):
        both = lanes_of([ds_ref[q].reshape(entries, g.Z), ds_ref[q + 1].reshape(entries, g.Z)])
        part = mm(left_t, both)
        all_ref[q] = part[:, : g.Z] * scale
        all_ref[q + 1] = part[:, g.Z :] * scale
        left_grad = left_grad + mm(both, lanes_of([ts_ref[q], ts_ref[q + 1]]), NT)
    share = g.QL // g.D
    for k in range(g.D):
        first = lax.rem(depth + k, g.D) * share
        w_refs[k][...] = all_ref[pl.ds(first, share)].reshape(share * g.Q, g.Z)
    w1 = w1_ref[...]
    zero = jnp.zeros_like(w1)
    first_term = jnp.zeros((entries // 2, 2 * g.M), F32)
    for half in range(2):
        weights = lanes_of([w1, zero] if half == 0 else [zero, w1])
        block = left_grad[half * (entries // 2) : (half + 1) * (entries // 2)] * scale[:, : g.Q]
        for piece in split_high_low(block):
            first_term = first_term + mm(piece, weights)
    turn_ref[...] = first_term
    for k in range(g.SP):
        gl_ref[k] = turn_ref[pl.ds(k, g.I, stride=g.SP), :] * masks[k]
    right_grad = jnp.zeros((g.QL * g.S, g.N), F32)
    for i in range(0, g.I, 2):
        right_grad = right_grad + mm(
            lanes_of([lt_ref[i], lt_ref[i + 1]]), lanes_of([d_ref[i], d_ref[i + 1]]), NT
        )
    for t in range(g.NT):
        lanes = min(LANES, g.N - t * LANES)
        piece = right_grad[:, t * LANES : t * LANES + lanes]
        if lanes < LANES:
            piece = lanes_of([piece, jnp.zeros((g.QL * g.S, LANES - lanes), F32)])
        rg_ref[t] = piece
    deep = 2 * g.QL
    group = min(g.SP, LANES // deep)
    order = iota((group * deep, g.Q), 0) % deep // 2
    pick = (iota((group * deep, g.Q), 1) == col * g.QL + order).astype(BF16)
    base = mm(pick, doubled)
    which = iota(base.shape, 0)
    base = jnp.where(which % 2 == iota(base.shape, 1) // g.M, base, 0.0)
    weights = lanes_of([jnp.where(which // deep == k, base, 0.0) for k in range(group)]).astype(BF16)
    for k in range(0, g.SP, group):
        for t in range(g.NT):
            lanes = min(LANES, g.N - t * LANES)
            tall = rows_of(
                [rg_ref[t, pl.ds(k + m, deep, stride=g.SP), :] for m in range(group)]
            )
            tall = (tall * scale).T[:lanes]
            high, low = split_high_low(tall)
            part = mm(high, weights) + mm(low, weights)
            for m in range(group):
                go_ref[k + m, t * LANES : t * LANES + lanes, :] = (
                    part[:, m * 2 * g.M : (m + 1) * 2 * g.M] * masks[k + m]
                )


def attend_kernel(g, *refs):
    refs = list(refs)
    xall_ref, logit_ref, refs = refs[0], refs[1], refs[2:]
    d_refs, refs = refs[: g.C - 1], refs[g.C - 1 :]
    gm_ref, gate_ref, p_ref, sg_ref, go_ref, gl_ref = refs[:6]
    soft_ref, gs_ref, own_ref, send_ref, total_ref, gg_ref = refs[6:]
    row, col = lax.axis_index("row"), lax.axis_index("col")
    blocks = [logit_ref[...]]
    for k in range(1, g.C):
        blocks.append(join_three(d_refs[(g.C - k) - 1][g.I * g.JC :, :], g.JC))
    logits = lanes_of(blocks)
    shifted = jnp.exp(logits - jnp.max(logits, -1, keepdims=True))
    soft = shifted / jnp.sum(shifted, -1, keepdims=True)
    soft_ref[...] = soft
    low = soft.astype(BF16)
    eye = (iota((g.N, g.N), 0) == iota((g.N, g.N), 1)).astype(BF16)
    low_t = mm(eye, low, NT).astype(BF16)
    wide = g.HW * g.C
    pick = (iota((wide, 2 * g.HW), 0) == col * g.HW + iota((wide, 2 * g.HW), 1) % g.HW).astype(BF16)
    p, sg = p_ref[...], sg_ref[...]
    value_weights = on_diagonal(mm(rows_of([p, p]), pick), g.HW).astype(BF16)
    gate_weights = on_diagonal(mm(rows_of([sg, sg]), pick), g.HW).astype(BF16)
    values = mm(xall_ref[...].reshape(g.SP * g.N, 2 * g.M), value_weights).astype(BF16)
    head = iota((1, 2 * g.HW), 1) % g.HW // (g.HW // g.HL)
    grad_soft = jnp.zeros((g.HL * g.I, g.N), F32)
    for k in range(g.SP):
        v = values[k * g.N : (k + 1) * g.N]
        crossed = mm(low, v)
        mixed = jnp.zeros((g.I, 2 * g.HW), F32)
        for h in range(g.HL):
            mixed = mixed + jnp.where(head == h, crossed[h * g.I : (h + 1) * g.I], 0.0)
        rows = slice(k * g.I, (k + 1) * g.I)
        gg_ref[rows, :] = (gate_ref[rows, :] * mixed).astype(BF16)
        blended = gm_ref[rows, :]
        by_head = rows_of(
            [jnp.where(head == h, blended, jnp.zeros_like(blended)) for h in range(g.HL)]
        )
        grad_soft = grad_soft + mm(by_head, v, NT)
        part = go_ref[k]
        for piece in split_high_low(mm(low_t, by_head)):
            part = part + mm(piece, value_weights, NT)
        total_ref[k] = part
    gs_ref[...] = grad_soft
    own = total_ref[:, pl.ds(g.place(row, col), g.I), :]
    gate_term = mm(gg_ref[...], gate_weights, NT).reshape(g.SP, g.I, 2 * g.M)
    own_ref[...] = (own + gate_term + gl_ref[...]).reshape(g.SP * g.I, 2 * g.M)
    for r in range(g.R):
        block = total_ref[:, pl.ds(g.place(r, col), g.I), :]
        send_ref[r] = block.reshape(g.SP * g.I, 2 * g.M).astype(BF16)


def pack_kernel(g, send_ref, *refs):
    parts, out_ref = refs[: g.D], refs[g.D]
    total = parts[0][...]
    for ref in parts[1:]:
        total = total + ref[...]
    high, low = split_high_low(total)
    chunk = total.shape[0] // g.R
    rows = g.SP * g.I
    for r in range(g.R):
        out_ref[r, :rows, :] = send_ref[r]
        out_ref[r, rows : rows + chunk, :] = high[r * chunk : (r + 1) * chunk]
        out_ref[r, rows + chunk :, :] = low[r * chunk : (r + 1) * chunk]


def reduce_kernel(g, own_ref, got_ref, soft_ref, *refs):
    parts, refs = refs[: g.D], refs[g.D :]
    sum_ref, grad_ref, refs = refs[0], refs[1], refs[2:]
    out_refs, (matrix_ref, order_ref) = refs[: g.C - 1], refs[g.C - 1 :]
    row, depth = lax.axis_index("row"), lax.axis_index("depth")
    rows = g.SP * g.I
    total = own_ref[...]
    for k in range(1, g.R):
        total = total + got_ref[lax.rem(row + k, g.R), :rows, :].astype(F32)
    total = total.astype(BF16)
    sum_ref[...] = total
    chunk = (got_ref.shape[1] - rows) // 2
    matrix = jnp.zeros((chunk, g.Z), F32)
    for r in range(g.R):
        for first in (rows, rows + chunk):
            matrix = matrix + got_ref[r, first : first + chunk, :].astype(F32)
    matrix = matrix.astype(BF16)
    for k in range(g.R * g.C):
        matrix_ref[k] = matrix
    for k in range(g.D):
        order_ref[lax.rem(depth - k + g.D, g.D)] = parts[k][...]
    grad_soft = order_ref[0]
    for k in range(1, g.D):
        grad_soft = grad_soft + order_ref[k]
    soft = soft_ref[...]
    grad = soft * (grad_soft - jnp.sum(soft * grad_soft, -1, keepdims=True))
    grad_ref[...] = grad[:, : g.JC]
    for k in range(1, g.C):
        out_refs[k - 1][:rows, :] = total
        out_refs[k - 1][rows:, :] = three_lanes(grad[:, k * g.JC : (k + 1) * g.JC])


def finish_kernel(g, x_ref, e_ref, wl_ref, sum_ref, grad_ref, *refs):
    got, (msa_ref, pair_ref, sums_ref, grads_ref) = refs[: g.C - 1], refs[g.C - 1 :]
    col = lax.axis_index("col")
    rows, heads = g.SP * g.I, g.HL * g.I
    sums_ref[col] = sum_ref[...]
    grads_ref[col, :, : g.JC] = grad_ref[...]
    for k in range(1, g.C):
        place = lax.rem(col - k + g.C, g.C)
        sums_ref[place] = got[k - 1][:rows, :]
        grads_ref[place, :, : g.JC] = join_three(got[k - 1][rows:, :], g.JC)
    if g.JC < LANES:
        grads_ref[:, :, g.JC :] = jnp.zeros((g.C, heads, LANES - g.JC), F32)
    total = sums_ref[0].astype(F32)
    for k in range(1, g.C):
        total = total + sums_ref[k].astype(F32)
    total = total.reshape(g.SP, 1, g.I, 2 * g.M)
    upstream = jnp.concatenate([total[..., : g.M], total[..., g.M :]], axis=1)
    upstream = upstream.reshape(g.S, g.I, g.M)
    msa_ref[...] = standardize_backward(x_ref[...].astype(F32), upstream).astype(BF16)
    count = g.H * g.I
    high, low = split_high_low(grads_ref[...].reshape(count, LANES).T[: g.JC])
    grads = lanes_of([high, low])
    pick = (iota((count, g.H), 0) // g.I == iota((count, g.H), 1)).astype(BF16)
    base = mm(pick, wl_ref[...]).astype(BF16)
    token = iota((count, 1), 0) % g.I
    for i in range(0, g.I, 2):
        weights = lanes_of(
            [jnp.where(token == i + k, base, jnp.zeros_like(base)) for k in range(2)]
        )
        upstream = mm(grads, rows_of([weights, weights]))
        for k in range(2):
            pair_ref[i + k] = standardize_backward(
                e_ref[i + k].astype(F32), upstream[:, k * g.Z : (k + 1) * g.Z]
            ).astype(BF16)


def matrix_kernel(g, *refs):
    parts, (out_ref, order_ref) = refs[: g.D], refs[g.D :]
    depth = lax.axis_index("depth")
    for k in range(g.D):
        order_ref[lax.rem(depth - k + g.D, g.D)] = parts[k][...].astype(F32)
    share = g.QL // g.D * g.Q // g.R
    for d in range(g.D):
        for c in range(g.C):
            for r in range(g.R):
                first = r * share
                while first < (r + 1) * share:
                    q, p = divmod(first, g.Q)
                    size = min(g.Q - p, (r + 1) * share - first)
                    place = p * g.Q + c * g.QL + d * (g.QL // g.D) + q
                    block = order_ref[d, r * g.C + c, first - r * share : first - r * share + size]
                    out_ref[pl.ds(place, size, stride=g.Q), :] = block
                    first += size


class Sizes:
    def __init__(self, x, e, wl, p, w1):
        self.R, self.C, self.D = (lax.axis_size(a) for a in ("row", "col", "depth"))
        self.S, self.I, self.M = x.shape
        self.JC, self.Z = e.shape[1:]
        self.H, self.Q = wl.shape[1], w1.shape[1]
        self.SP, self.N = self.S // 2, self.R * self.I
        self.HL, self.QL = self.H // self.C, self.Q // self.C
        self.HW = p.shape[1] // self.C
        self.F = self.R // self.C
        self.NT = -(-self.N // LANES)
        self.carried = 0

    def place(self, row, col):
        turn = lax.rem(row // self.F - col + self.C, self.C)
        return pl.multiple_of((turn * self.F + lax.rem(row, self.F)) * self.I, self.I)


def shift(array, axis, k):
    count = lax.axis_size(axis)
    return lax.ppermute(array, axis, [(i, (i + k) % count) for i in range(count)])


def from_all(array, axis):
    return [array] + [shift(array, axis, k) for k in range(1, lax.axis_size(axis))]


def to_all(arrays, axis):
    return [arrays[0]] + [shift(a, axis, k) for k, a in enumerate(arrays) if k > 0]


def per_device(
    homolog_ensemble,
    duplex_embedding,
    homolog_present_flags,
    resolved_position_flags,
    payload_weights,
    sigmoid_weights,
    averager_final_weights,
    first_operand_weights,
    second_operand_weights,
    duplex_logit_weights,
    tensor_product_weights,
    averager_upstream_adjoint,
    duplex_upstream_adjoint,
):
    g = Sizes(
        homolog_ensemble, duplex_embedding, duplex_logit_weights, payload_weights, first_operand_weights
    )
    shape = jax.ShapeDtypeStruct

    def call(kernel, name, args, outs, scratch=(), far=False):
        size = sum(a.size * a.dtype.itemsize for a in args) + sum(
            math.prod(o.shape) * o.dtype.itemsize for o in outs
        )
        single = len(outs) == 1
        if far:
            args = [pltpu.with_memory_space_constraint(a, pltpu.HBM) for a in args]
        return pl.pallas_call(
            functools.partial(kernel, g),
            out_shape=outs[0] if single else tuple(outs),
            in_specs=[FAR if far else VMEM] * len(args),
            out_specs=VMEM if single else (VMEM,) * len(outs),
            scratch_shapes=list(scratch),
            compiler_params=pltpu.CompilerParams(vmem_limit_bytes=40 * 1024 * 1024),
            cost_estimate=pl.CostEstimate(flops=0, bytes_accessed=size, transcendentals=0),
            name=name,
        )(*args)

    heads = g.HL * g.I
    entries = g.S * g.I
    rows = g.SP * g.I
    pairs = g.I * g.JC
    later = (
        payload_weights,
        sigmoid_weights,
        averager_final_weights.T,
        first_operand_weights.T,
        second_operand_weights.T,
        duplex_logit_weights.T,
        tensor_product_weights,
        averager_upstream_adjoint,
        homolog_ensemble,
        duplex_embedding,
    )
    g.carried = len(later)
    xn, logits, *rest = call(
        normalise_kernel,
        "normalise",
        (
            homolog_ensemble,
            duplex_embedding,
            duplex_upstream_adjoint.reshape(pairs, g.Z),
            resolved_position_flags.reshape(1, g.JC),
            homolog_present_flags,
            duplex_logit_weights.T,
            *later,
        ),
        [shape((g.R, g.SP, g.I, 2 * g.M), BF16), shape((heads, g.JC), F32)]
        + [shape((pairs + heads, g.Z), BF16)] * (g.C - 1)
        + [shape((g.SP + 8, 2 * g.M), F32)]
        + [shape(a.shape, a.dtype) for a in later],
        [
            pltpu.VMEM(homolog_ensemble.shape, BF16),
            pltpu.VMEM(duplex_embedding.shape, BF16),
            pltpu.VMEM((1, g.JC), jnp.int32),
            pltpu.SMEM(homolog_present_flags.shape, jnp.int32),
            pltpu.VMEM((g.H, g.Z), BF16),
            pltpu.VMEM((g.I * g.H, LANES), F32),
            pltpu.VMEM((g.H, g.I, g.JC), F32),
            pltpu.SemaphoreType.DMA((5,)),
            pltpu.SemaphoreType.DMA((g.C,)),
            pltpu.SemaphoreType.DMA((len(later),)),
        ],
        far=True,
    )
    sends, (masks, *rest) = rest[: g.C - 1], rest[g.C - 1 :]
    p, sg, wf, w1, w2, wl, outer_weights, u, x, e = rest
    arrived = [shift(a, "col", k + 1) for k, a in enumerate(sends)]
    everyone = lax.all_to_all(xn, "row", 0, 0, tiled=True)
    blended, gate_factor, left, weights, left_weights = call(
        local_kernel,
        "local",
        (xn, u, sg, wf, w1, outer_weights, masks),
        [
            shape((rows, 2 * g.HW), BF16),
            shape((rows, 2 * g.HW), F32),
            shape((entries, g.Q), BF16),
            shape((g.QL, g.Q, g.Z), BF16),
            shape((g.I, g.QL * g.S, g.Z), BF16),
        ],
        [pltpu.VMEM(outer_weights.shape, F32), pltpu.VMEM((2, rows, LANES), F32)],
    )
    share = g.QL // g.D * g.Q
    xall, *rest = call(
        outer_kernel,
        "outer",
        (everyone, sends[0], *arrived, left, weights, left_weights, w1, w2, masks),
        [shape((g.SP, g.N, 2 * g.M), BF16)]
        + [shape((share, g.Z), F32)] * g.D
        + [shape((g.SP, g.N, 2 * g.M), F32), shape((g.SP, g.I, 2 * g.M), F32)],
        [
            pltpu.VMEM((g.I, g.N, g.Z), BF16),
            pltpu.VMEM((g.NT, g.SP * 2 * g.QL, LANES), F32),
            pltpu.VMEM((g.QL * g.S, g.N), BF16),
            pltpu.VMEM((g.QL, 2, g.I, g.SP, g.Z), BF16),
            pltpu.VMEM((g.QL, g.Q, g.Z), F32),
            pltpu.VMEM((rows, 2 * g.M), F32),
            pltpu.VMEM((g.NT, g.QL * g.S, LANES), F32),
        ],
    )
    matrix_parts, (second_term, first_term) = rest[: g.D], rest[g.D :]
    matrix_parts = to_all(matrix_parts, "depth")
    soft, grad_soft, own, sums = call(
        attend_kernel,
        "attend",
        (xall, logits, *arrived, blended, gate_factor, p, sg, second_term, first_term),
        [
            shape((heads, g.N), F32),
            shape((heads, g.N), F32),
            shape((rows, 2 * g.M), F32),
            shape((g.R, rows, 2 * g.M), BF16),
        ],
        [pltpu.VMEM((g.SP, g.N, 2 * g.M), F32), pltpu.VMEM((rows, 2 * g.HW), BF16)],
    )
    grad_softs = from_all(grad_soft, "depth")
    chunk = share // g.R
    sums = call(
        pack_kernel, "pack", (sums, *matrix_parts), [shape((g.R, rows + 2 * chunk, 2 * g.M), BF16)]
    )
    sums = lax.all_to_all(sums, "row", 0, 0, tiled=True)
    own, grad_logits, *rest = call(
        reduce_kernel,
        "reduce",
        (own, sums, soft, *grad_softs),
        [shape((rows, 2 * g.M), BF16), shape((heads, g.JC), F32)]
        + [shape((rows + heads, 2 * g.M), BF16)] * (g.C - 1)
        + [shape((g.R * g.C, chunk, g.Z), BF16)],
        [pltpu.VMEM((g.D, heads, g.N), F32)],
    )
    sends, matrix = rest[: g.C - 1], rest[g.C - 1]
    arrived = [shift(a, "col", k + 1) for k, a in enumerate(sends)]
    matrix = lax.all_to_all(matrix, ("row", "col"), 0, 0, tiled=True)
    matrix_parts = from_all(matrix, "depth")
    ensemble_derivative, pairwise_gradient = call(
        finish_kernel,
        "finish",
        (x, e, wl, own, grad_logits, *arrived),
        [shape(homolog_ensemble.shape, BF16), shape(duplex_embedding.shape, BF16)],
        [pltpu.VMEM((g.C, rows, 2 * g.M), BF16), pltpu.VMEM((g.C, heads, LANES), F32)],
    )
    outer_matrix_gradient = call(
        matrix_kernel,
        "matrix",
        matrix_parts,
        [shape(tensor_product_weights.shape, F32)],
        [pltpu.VMEM((g.D, *matrix.shape), F32)],
    )
    return (ensemble_derivative, pairwise_gradient, outer_matrix_gradient)


def solution(mesh):
    in_specs = (
        P(("parts", "depth"), "row", None),
        P(("parts", "row"), "col", None),
        P("parts"),
        P(("parts", "col")),
        P(),
        P(),
        P(),
        P(),
        P(),
        P(),
        P(),
        P(("parts", "depth"), "row", None),
        P(("parts", "row"), "col", None),
    )
    out_specs = (
        P(("parts", "depth"), "row", None),
        P(("parts", "row"), "col", None),
        P("parts", None),
    )
    return jax.shard_map(
        per_device, mesh=mesh, in_specs=in_specs, out_specs=out_specs, check_vma=False
    )
```

```python
import functools
import math

import jax
import jax.numpy as jnp
from jax import lax
from jax.experimental import pallas as pl
from jax.experimental.pallas import tpu as pltpu
from jax.sharding import PartitionSpec as P

EPS = 1e-05
PENALTY = 10000.0
F32 = jnp.float32
BF16 = jnp.bfloat16
LANES = 128
NN = (((1,), (0,)), ((), ()))
NT = (((1,), (1,)), ((), ()))
VMEM = pl.BlockSpec(memory_space=pltpu.VMEM)
FAR = pl.BlockSpec(memory_space=pl.ANY)


def mm(a, b, dims=NN):
    return lax.dot_general(a, b, dims, preferred_element_type=F32)


def split_high_low(value):
    high = value.astype(BF16)
    return high, (value - high.astype(F32)).astype(BF16)


def iota(shape, dim):
    return lax.broadcasted_iota(jnp.int32, shape, dim)


def lanes_of(pieces):
    return pieces[0] if len(pieces) == 1 else jnp.concatenate(pieces, axis=-1)


def rows_of(pieces):
    return pieces[0] if len(pieces) == 1 else jnp.concatenate(pieces, axis=0)


def standardize(values):
    centred = values - jnp.mean(values, -1, keepdims=True)
    inverse = lax.rsqrt(jnp.mean(centred * centred, -1, keepdims=True) + EPS)
    return centred * inverse, inverse


def standardize_backward(values, upstream):
    scaled, inverse = standardize(values)
    mean_grad = jnp.mean(upstream, -1, keepdims=True)
    mean_cross = jnp.mean(upstream * scaled, -1, keepdims=True)
    return (upstream - mean_grad - scaled * mean_cross) * inverse


def on_diagonal(block, width):
    rows, lanes = block.shape
    same = iota(block.shape, 0) // (rows // 2) == iota(block.shape, 1) // width
    return jnp.where(same, block, jnp.zeros_like(block))


def split_three(value):
    high = value.astype(BF16)
    rest = value - high.astype(F32)
    middle = rest.astype(BF16)
    return [high, middle, (rest - middle.astype(F32)).astype(BF16)]


def three_lanes(value):
    rows, width = value.shape
    fill = -(3 * width) % LANES
    return lanes_of(split_three(value) + [jnp.zeros((rows, fill), BF16)])


def join_three(parts, width):
    wide = parts.astype(F32)
    return (wide[:, :width] + wide[:, width : 2 * width]) + wide[:, 2 * width : 3 * width]


def normalise_kernel(g, dd_ref, flag_ref, live_ref, *refs):
    refs = list(refs)
    count = g.carried
    sources, refs = refs[:count], refs[count:]
    xn_ref, own_ref, refs = refs[0], refs[1], refs[2:]
    out_refs, refs = refs[: g.C - 1], refs[g.C - 1 :]
    mask_ref, refs = refs[0], refs[1:]
    targets, refs = refs[:count], refs[count:]
    flag_in, live_in, rows_ref, heads_ref, flag_sem, cot_sem, later_sem = refs
    flags = [
        pltpu.make_async_copy(flag_ref, flag_in, flag_sem.at[0]),
        pltpu.make_async_copy(live_ref, live_in, flag_sem.at[1]),
    ]
    cots = [
        pltpu.make_async_copy(dd_ref, ref.at[pl.ds(0, g.I * g.JC)], cot_sem.at[k])
        for k, ref in enumerate(out_refs)
    ]
    copies = [
        pltpu.make_async_copy(a, b, later_sem.at[k])
        for k, (a, b) in enumerate(zip(sources, targets, strict=True))
    ]
    for copy in copies[:3] + flags + cots + copies[3:]:
        copy.start()
    x_ref, e_ref, wl_ref = targets[:3]
    copies[0].wait()
    normed = standardize(x_ref[...].astype(F32))[0].reshape(g.SP, 2, g.I, g.M)
    xn_ref[...] = jnp.concatenate([normed[:, 0], normed[:, 1]], axis=-1).astype(BF16)
    for copy in copies[1:3] + flags:
        copy.wait()
    pair = standardize(e_ref[...].astype(F32).reshape(g.I * g.JC, g.Z))[0].astype(BF16)
    penalty = (flag_in[...].astype(F32) - 1.0) * PENALTY
    weights = wl_ref[...]
    for i in range(g.I):
        rows_ref[i * g.H : (i + 1) * g.H, : g.JC] = (
            mm(weights, pair[i * g.JC : (i + 1) * g.JC], NT) + penalty
        )
    for h in range(g.H):
        heads_ref[h] = rows_ref[pl.ds(h, g.I, stride=g.H), :][:, : g.JC]
    col = lax.axis_index("col")
    for k in range(g.C):
        first = lax.rem(col + k, g.C) * g.HL
        logits = heads_ref[pl.ds(first, g.HL)].reshape(g.HL * g.I, g.JC)
        if k == 0:
            own_ref[...] = logits
        else:
            out_refs[k - 1][g.I * g.JC :, :] = three_lanes(logits)
    first = lax.axis_index("depth") * g.S
    lane = iota((1, 2 * g.M), 1)
    for k in range(g.SP):
        pair_flags = jnp.where(lane < g.M, live_in[first + 2 * k], live_in[first + 2 * k + 1])
        mask_ref[k : k + 1, :] = pair_flags.astype(F32)
    total = live_in[0]
    for s in range(1, live_in.shape[0]):
        total = total + live_in[s]
    mask_ref[g.SP : g.SP + 1, :] = 1.0 / (0.001 + jnp.full((1, 2 * g.M), total, jnp.int32).astype(F32))
    for copy in cots + copies[3:]:
        copy.wait()


def local_kernel(
    g, xn_ref, u_ref, sg_ref, wf_ref, w1_ref, t_ref, mask_ref,
    gm_ref, gate_ref, left_ref, ts_ref, lt_ref, wide_ref, half_ref,
):
    col = lax.axis_index("col")
    rows = g.SP * g.I
    xn = xn_ref[...]
    wide = g.HW * g.C
    pick = (iota((wide, 2 * g.HW), 0) == col * g.HW + iota((wide, 2 * g.HW), 1) % g.HW).astype(BF16)
    sg, wf = sg_ref[...], wf_ref[...]
    gate_weights = on_diagonal(mm(rows_of([sg, sg]), pick), g.HW).astype(BF16)
    gates = jax.nn.sigmoid(mm(xn.reshape(rows, 2 * g.M), gate_weights))
    u = u_ref[...].reshape(g.SP, 2, g.I, g.M)
    packed_u = jnp.concatenate([u[:, 0], u[:, 1]], axis=-1).reshape(rows, 2 * g.M)
    final_weights = on_diagonal(mm(rows_of([wf, wf]), pick), g.HW).astype(BF16)
    gated = mm(packed_u, final_weights)
    blended = gated * gates
    gm_ref[...] = blended.astype(BF16)
    gate_ref[...] = blended * (1.0 - gates)
    live_xn = rows_of(
        [(xn[k].astype(F32) * mask_ref[k : k + 1, :]).astype(BF16) for k in range(g.SP)]
    )
    w1 = rows_of([w1_ref[...], jnp.zeros((LANES - g.Q, g.M), BF16)])
    zero = jnp.zeros_like(w1)
    half_ref[0] = mm(live_xn, lanes_of([w1, zero]), NT)
    half_ref[1] = mm(live_xn, lanes_of([zero, w1]), NT)
    for half in range(2):
        for i in range(g.I):
            first = (half * g.I + i) * g.SP
            left_ref[first : first + g.SP, :] = half_ref[half, pl.ds(i, g.SP, stride=g.I), :][
                :, : g.Q
            ].astype(BF16)
    wide_ref[...] = t_ref[...].astype(F32)
    for q in range(g.QL):
        ts_ref[q] = wide_ref[pl.ds(col * g.QL + q, g.Q, stride=g.Q), :].astype(BF16)
    left = left_ref[...]
    for q in range(0, g.QL, 2):
        product = mm(left, lanes_of([ts_ref[q], ts_ref[q + 1]]))
        for k in range(2):
            for half in range(2):
                block = product[half * g.I * g.SP : (half + 1) * g.I * g.SP, k * g.Z : (k + 1) * g.Z]
                first = (q + k) * g.S + half * g.SP
                lt_ref[:, first : first + g.SP, :] = block.reshape(g.I, g.SP, g.Z).astype(BF16)


def outer_kernel(g, *refs):
    refs = list(refs)
    x_refs, refs = refs[: g.R], refs[g.R :]
    d_refs, refs = refs[: g.C], refs[g.C :]
    left_ref, ts_ref, lt_ref, w1_ref, w2_ref, mask_ref = refs[:6]
    refs = refs[6:]
    xall_ref, w_refs, refs = refs[0], refs[1 : 1 + g.D], refs[1 + g.D :]
    go_ref, gl_ref, d_ref, spread_ref, rt_ref, ds_ref, all_ref, turn_ref, rg_ref = refs
    row, col, depth = (lax.axis_index(a) for a in ("row", "col", "depth"))
    masks = [mask_ref[k : k + 1, :] for k in range(g.SP)]
    scale = mask_ref[g.SP : g.SP + 1, :]
    for x in range(g.R):
        xall_ref[:, pl.ds(g.place(jnp.bitwise_xor(row, x), col), g.I), :] = x_refs[x][...]
    for k in range(g.C):
        spot = (g.C - k) % g.C
        block = d_refs[k][: g.I * g.JC, :].reshape(g.I, g.JC, g.Z)
        d_ref[:, spot * g.JC : (spot + 1) * g.JC, :] = block
    w2 = w2_ref[...]
    doubled = lanes_of([w2, w2])
    pick = (iota((2 * g.QL, g.Q), 1) == col * g.QL + iota((2 * g.QL, g.Q), 0) % g.QL).astype(BF16)
    second = on_diagonal(mm(pick, doubled), g.M).astype(BF16)
    for k in range(g.SP):
        live_x = (xall_ref[k].astype(F32) * masks[k]).astype(BF16)
        part = mm(second, live_x, NT)
        for t in range(g.NT):
            lanes = min(LANES, g.N - t * LANES)
            spread_ref[t, k * 2 * g.QL : (k + 1) * 2 * g.QL, :lanes] = part[
                :, t * LANES : t * LANES + lanes
            ]
    for q in range(g.QL):
        for half in range(2):
            first = q * g.S + half * g.SP
            for t in range(g.NT):
                lanes = min(LANES, g.N - t * LANES)
                piece = spread_ref[t, pl.ds(half * g.QL + q, g.SP, stride=2 * g.QL), :]
                rt_ref[first : first + g.SP, t * LANES : t * LANES + lanes] = piece[
                    :, :lanes
                ].astype(BF16)
    rt = rt_ref[...]
    for i in range(0, g.I, 2):
        product = mm(rt, lanes_of([d_ref[i], d_ref[i + 1]]))
        for k in range(2):
            block = product[:, k * g.Z : (k + 1) * g.Z]
            ds_ref[:, :, i + k] = block.reshape(g.QL, 2, g.SP, g.Z).astype(BF16)
    left = left_ref[...]
    eye = (iota((g.Q, g.Q), 0) == iota((g.Q, g.Q), 1)).astype(BF16)
    left_t = mm(eye, left, NT).astype(BF16)
    entries = g.S * g.I
    left_grad = jnp.zeros((entries, g.Q), F32)
    for q in range(0, g.QL, 2):
        both = lanes_of([ds_ref[q].reshape(entries, g.Z), ds_ref[q + 1].reshape(entries, g.Z)])
        part = mm(left_t, both)
        all_ref[q] = part[:, : g.Z] * scale
        all_ref[q + 1] = part[:, g.Z :] * scale
        left_grad = left_grad + mm(both, lanes_of([ts_ref[q], ts_ref[q + 1]]), NT)
    share = g.QL // g.D
    for k in range(g.D):
        first = lax.rem(depth + k, g.D) * share
        w_refs[k][...] = all_ref[pl.ds(first, share)].reshape(share * g.Q, g.Z)
    w1 = w1_ref[...]
    zero = jnp.zeros_like(w1)
    first_term = jnp.zeros((entries // 2, 2 * g.M), F32)
    for half in range(2):
        weights = lanes_of([w1, zero] if half == 0 else [zero, w1])
        block = left_grad[half * (entries // 2) : (half + 1) * (entries // 2)] * scale[:, : g.Q]
        for piece in split_high_low(block):
            first_term = first_term + mm(piece, weights)
    turn_ref[...] = first_term
    for k in range(g.SP):
        gl_ref[k] = turn_ref[pl.ds(k, g.I, stride=g.SP), :] * masks[k]
    right_grad = jnp.zeros((g.QL * g.S, g.N), F32)
    for i in range(0, g.I, 2):
        right_grad = right_grad + mm(
            lanes_of([lt_ref[i], lt_ref[i + 1]]), lanes_of([d_ref[i], d_ref[i + 1]]), NT
        )
    for t in range(g.NT):
        lanes = min(LANES, g.N - t * LANES)
        piece = right_grad[:, t * LANES : t * LANES + lanes]
        if lanes < LANES:
            piece = lanes_of([piece, jnp.zeros((g.QL * g.S, LANES - lanes), F32)])
        rg_ref[t] = piece
    deep = 2 * g.QL
    group = min(g.SP, LANES // deep)
    order = iota((group * deep, g.Q), 0) % deep // 2
    pick = (iota((group * deep, g.Q), 1) == col * g.QL + order).astype(BF16)
    base = mm(pick, doubled)
    which = iota(base.shape, 0)
    base = jnp.where(which % 2 == iota(base.shape, 1) // g.M, base, 0.0)
    weights = lanes_of([jnp.where(which // deep == k, base, 0.0) for k in range(group)]).astype(BF16)
    for k in range(0, g.SP, group):
        for t in range(g.NT):
            lanes = min(LANES, g.N - t * LANES)
            tall = rows_of(
                [rg_ref[t, pl.ds(k + m, deep, stride=g.SP), :] for m in range(group)]
            )
            tall = (tall * scale).T[:lanes]
            high, low = split_high_low(tall)
            part = mm(high, weights) + mm(low, weights)
            for m in range(group):
                go_ref[k + m, t * LANES : t * LANES + lanes, :] = (
                    part[:, m * 2 * g.M : (m + 1) * 2 * g.M] * masks[k + m]
                )


def attend_kernel(g, *refs):
    refs = list(refs)
    xall_ref, logit_ref, refs = refs[0], refs[1], refs[2:]
    d_refs, refs = refs[: g.C - 1], refs[g.C - 1 :]
    gm_ref, gate_ref, p_ref, sg_ref, go_ref, gl_ref = refs[:6]
    soft_ref, gs_ref, own_ref, refs = refs[6], refs[7], refs[8], refs[9:]
    send_refs, (total_ref, gg_ref) = refs[: g.R - 1], refs[g.R - 1 :]
    row, col = lax.axis_index("row"), lax.axis_index("col")
    blocks = [logit_ref[...]]
    for k in range(1, g.C):
        blocks.append(join_three(d_refs[(g.C - k) - 1][g.I * g.JC :, :], g.JC))
    logits = lanes_of(blocks)
    shifted = jnp.exp(logits - jnp.max(logits, -1, keepdims=True))
    soft = shifted / jnp.sum(shifted, -1, keepdims=True)
    soft_ref[...] = soft
    low = soft.astype(BF16)
    eye = (iota((g.N, g.N), 0) == iota((g.N, g.N), 1)).astype(BF16)
    low_t = mm(eye, low, NT).astype(BF16)
    wide = g.HW * g.C
    pick = (iota((wide, 2 * g.HW), 0) == col * g.HW + iota((wide, 2 * g.HW), 1) % g.HW).astype(BF16)
    p, sg = p_ref[...], sg_ref[...]
    value_weights = on_diagonal(mm(rows_of([p, p]), pick), g.HW).astype(BF16)
    gate_weights = on_diagonal(mm(rows_of([sg, sg]), pick), g.HW).astype(BF16)
    values = mm(xall_ref[...].reshape(g.SP * g.N, 2 * g.M), value_weights).astype(BF16)
    head = iota((1, 2 * g.HW), 1) % g.HW // (g.HW // g.HL)
    grad_soft = jnp.zeros((g.HL * g.I, g.N), F32)
    for k in range(g.SP):
        v = values[k * g.N : (k + 1) * g.N]
        crossed = mm(low, v)
        mixed = jnp.zeros((g.I, 2 * g.HW), F32)
        for h in range(g.HL):
            mixed = mixed + jnp.where(head == h, crossed[h * g.I : (h + 1) * g.I], 0.0)
        rows = slice(k * g.I, (k + 1) * g.I)
        gg_ref[rows, :] = (gate_ref[rows, :] * mixed).astype(BF16)
        blended = gm_ref[rows, :]
        by_head = rows_of(
            [jnp.where(head == h, blended, jnp.zeros_like(blended)) for h in range(g.HL)]
        )
        grad_soft = grad_soft + mm(by_head, v, NT)
        part = go_ref[k]
        for piece in split_high_low(mm(low_t, by_head)):
            part = part + mm(piece, value_weights, NT)
        total_ref[k] = part
    gs_ref[...] = grad_soft
    own = total_ref[:, pl.ds(g.place(row, col), g.I), :]
    gate_term = mm(gg_ref[...], gate_weights, NT).reshape(g.SP, g.I, 2 * g.M)
    own_ref[...] = (own + gate_term + gl_ref[...]).reshape(g.SP * g.I, 2 * g.M)
    for x in range(1, g.R):
        block = total_ref[:, pl.ds(g.place(jnp.bitwise_xor(row, x), col), g.I), :]
        send_refs[x - 1][...] = block.reshape(g.SP * g.I, 2 * g.M).astype(BF16)


def pack_kernel(g, *refs):
    refs = list(refs)
    sums, refs = refs[: g.R - 1], refs[g.R - 1 :]
    parts, refs = refs[: g.D], refs[g.D :]
    outs, (own_ref, total_ref) = refs[: g.R - 1], refs[g.R - 1 :]
    row = lax.axis_index("row")
    total = parts[0][...]
    for ref in parts[1:]:
        total = total + ref[...]
    chunk, rows = own_ref.shape[0], g.SP * g.I
    for r in range(g.R):
        total_ref[r] = total[r * chunk : (r + 1) * chunk]
    own_ref[...] = total_ref[row]
    for x in range(1, g.R):
        out = outs[x - 1]
        out[:rows, :] = sums[x - 1][...]
        high, low = split_high_low(total_ref[jnp.bitwise_xor(row, x)])
        out[rows : rows + chunk, :] = high
        out[rows + chunk :, :] = low


def reduce_kernel(g, own_ref, matrix_ref, soft_ref, *refs):
    refs = list(refs)
    got, refs = refs[: g.R - 1], refs[g.R - 1 :]
    parts, refs = refs[: g.D], refs[g.D :]
    sum_ref, grad_ref, chunk_ref, refs = refs[0], refs[1], refs[2], refs[3:]
    out_refs, (order_ref,) = refs[: g.C - 1], refs[g.C - 1 :]
    depth = lax.axis_index("depth")
    rows, heads, chunk = g.SP * g.I, g.HL * g.I, matrix_ref.shape[0]
    total, matrix = own_ref[...], matrix_ref[...]
    for ref in got:
        total = total + ref[:rows, :].astype(F32)
        matrix = matrix + ref[rows : rows + chunk, :].astype(F32)
        matrix = matrix + ref[rows + chunk :, :].astype(F32)
    total, matrix = total.astype(BF16), matrix.astype(BF16)
    sum_ref[...] = total
    chunk_ref[...] = matrix
    for k in range(g.D):
        order_ref[lax.rem(depth - k + g.D, g.D)] = parts[k][...]
    grad_soft = order_ref[0]
    for k in range(1, g.D):
        grad_soft = grad_soft + order_ref[k]
    soft = soft_ref[...]
    grad = soft * (grad_soft - jnp.sum(soft * grad_soft, -1, keepdims=True))
    grad_ref[...] = grad[:, : g.JC]
    for k in range(1, g.C):
        out_refs[k - 1][:rows, :] = total
        out_refs[k - 1][rows : rows + heads, :] = three_lanes(grad[:, k * g.JC : (k + 1) * g.JC])
        out_refs[k - 1][rows + heads :, :] = matrix


def across_kernel(g, *refs):
    out_ref = refs[-1]
    col = lax.axis_index("col")
    chunk = out_ref.shape[1]
    for k, ref in enumerate(refs[:-1]):
        out_ref[lax.rem(col - k + g.C, g.C)] = ref[ref.shape[0] - chunk :, :]


def along_kernel(g, *refs):
    out_ref = refs[-1]
    row = lax.axis_index("row")
    for x, ref in enumerate(refs[:-1]):
        out_ref[jnp.bitwise_xor(row, x)] = ref[...]


def finish_kernel(g, x_ref, e_ref, wl_ref, sum_ref, grad_ref, *refs):
    got, (msa_ref, pair_ref, sums_ref, grads_ref) = refs[: g.C - 1], refs[g.C - 1 :]
    col = lax.axis_index("col")
    rows, heads = g.SP * g.I, g.HL * g.I
    sums_ref[col] = sum_ref[...]
    grads_ref[col, :, : g.JC] = grad_ref[...]
    for k in range(1, g.C):
        place = lax.rem(col - k + g.C, g.C)
        sums_ref[place] = got[k - 1][:rows, :]
        grads_ref[place, :, : g.JC] = join_three(got[k - 1][rows : rows + heads, :], g.JC)
    if g.JC < LANES:
        grads_ref[:, :, g.JC :] = jnp.zeros((g.C, heads, LANES - g.JC), F32)
    total = sums_ref[0].astype(F32)
    for k in range(1, g.C):
        total = total + sums_ref[k].astype(F32)
    total = total.reshape(g.SP, 1, g.I, 2 * g.M)
    upstream = jnp.concatenate([total[..., : g.M], total[..., g.M :]], axis=1)
    upstream = upstream.reshape(g.S, g.I, g.M)
    msa_ref[...] = standardize_backward(x_ref[...].astype(F32), upstream).astype(BF16)
    count = g.H * g.I
    high, low = split_high_low(grads_ref[...].reshape(count, LANES).T[: g.JC])
    grads = lanes_of([high, low])
    pick = (iota((count, g.H), 0) // g.I == iota((count, g.H), 1)).astype(BF16)
    base = mm(pick, wl_ref[...]).astype(BF16)
    token = iota((count, 1), 0) % g.I
    for i in range(0, g.I, 2):
        weights = lanes_of(
            [jnp.where(token == i + k, base, jnp.zeros_like(base)) for k in range(2)]
        )
        upstream = mm(grads, rows_of([weights, weights]))
        for k in range(2):
            pair_ref[i + k] = standardize_backward(
                e_ref[i + k].astype(F32), upstream[:, k * g.Z : (k + 1) * g.Z]
            ).astype(BF16)


def matrix_kernel(g, *refs):
    parts, (out_ref, order_ref) = refs[: g.D], refs[g.D :]
    depth = lax.axis_index("depth")
    for k in range(g.D):
        order_ref[lax.rem(depth - k + g.D, g.D)] = parts[k][...].astype(F32)
    share = g.QL // g.D * g.Q // g.R
    for d in range(g.D):
        for c in range(g.C):
            for r in range(g.R):
                first = r * share
                while first < (r + 1) * share:
                    q, p = divmod(first, g.Q)
                    size = min(g.Q - p, (r + 1) * share - first)
                    place = p * g.Q + c * g.QL + d * (g.QL // g.D) + q
                    block = order_ref[d, r, c, first - r * share : first - r * share + size]
                    out_ref[pl.ds(place, size, stride=g.Q), :] = block
                    first += size


class Sizes:
    def __init__(self, x, e, wl, p, w1):
        self.R, self.C, self.D = (lax.axis_size(a) for a in ("row", "col", "depth"))
        self.S, self.I, self.M = x.shape
        self.JC, self.Z = e.shape[1:]
        self.H, self.Q = wl.shape[1], w1.shape[1]
        self.SP, self.N = self.S // 2, self.R * self.I
        self.HL, self.QL = self.H // self.C, self.Q // self.C
        self.HW = p.shape[1] // self.C
        self.F = self.R // self.C
        self.NT = -(-self.N // LANES)
        self.carried = 0

    def place(self, row, col):
        turn = lax.rem(row // self.F - col + self.C, self.C)
        return pl.multiple_of((turn * self.F + lax.rem(row, self.F)) * self.I, self.I)


def shift(array, axis, k):
    count = lax.axis_size(axis)
    return lax.ppermute(array, axis, [(i, (i + k) % count) for i in range(count)])


def swap(array, axis, x):
    return lax.ppermute(array, axis, [(i, i ^ x) for i in range(lax.axis_size(axis))])


def from_all(array, axis):
    return [array] + [swap(array, axis, x) for x in range(1, lax.axis_size(axis))]


def per_device(
    homolog_ensemble,
    duplex_embedding,
    homolog_present_flags,
    resolved_position_flags,
    payload_weights,
    sigmoid_weights,
    averager_final_weights,
    first_operand_weights,
    second_operand_weights,
    duplex_logit_weights,
    tensor_product_weights,
    averager_upstream_adjoint,
    duplex_upstream_adjoint,
):
    g = Sizes(
        homolog_ensemble, duplex_embedding, duplex_logit_weights, payload_weights, first_operand_weights
    )
    shape = jax.ShapeDtypeStruct

    def call(kernel, name, args, outs, scratch=(), far=False):
        size = sum(a.size * a.dtype.itemsize for a in args) + sum(
            math.prod(o.shape) * jnp.dtype(o.dtype).itemsize for o in outs
        )
        single = len(outs) == 1
        if far:
            args = [pltpu.with_memory_space_constraint(a, pltpu.HBM) for a in args]
        return pl.pallas_call(
            functools.partial(kernel, g),
            out_shape=outs[0] if single else tuple(outs),
            in_specs=[FAR if far else VMEM] * len(args),
            out_specs=VMEM if single else (VMEM,) * len(outs),
            scratch_shapes=list(scratch),
            compiler_params=pltpu.CompilerParams(vmem_limit_bytes=40 * 1024 * 1024),
            cost_estimate=pl.CostEstimate(flops=0, bytes_accessed=size, transcendentals=0),
            name=name,
        )(*args)

    heads = g.HL * g.I
    entries = g.S * g.I
    rows = g.SP * g.I
    pairs = g.I * g.JC
    later = (
        homolog_ensemble,
        duplex_embedding,
        duplex_logit_weights.T,
        averager_upstream_adjoint,
        payload_weights,
        sigmoid_weights,
        averager_final_weights.T,
        first_operand_weights.T,
        second_operand_weights.T,
        tensor_product_weights,
    )
    g.carried = len(later)
    xn, logits, *rest = call(
        normalise_kernel,
        "normalise",
        (
            duplex_upstream_adjoint.reshape(pairs, g.Z),
            resolved_position_flags.reshape(1, g.JC),
            homolog_present_flags,
            *later,
        ),
        [pltpu.VMEM((g.SP, g.I, 2 * g.M), BF16), pltpu.VMEM((heads, g.JC), F32)]
        + [pltpu.VMEM((pairs + heads, g.Z), BF16)] * (g.C - 1)
        + [pltpu.VMEM((g.SP + 8, 2 * g.M), F32)]
        + [pltpu.VMEM(a.shape, a.dtype) for a in later],
        [
            pltpu.VMEM((1, g.JC), jnp.int32),
            pltpu.SMEM(homolog_present_flags.shape, jnp.int32),
            pltpu.VMEM((g.I * g.H, LANES), F32),
            pltpu.VMEM((g.H, g.I, g.JC), F32),
            pltpu.SemaphoreType.DMA((2,)),
            pltpu.SemaphoreType.DMA((g.C,)),
            pltpu.SemaphoreType.DMA((len(later),)),
        ],
        far=True,
    )
    sends, (masks, *rest) = rest[: g.C - 1], rest[g.C - 1 :]
    x, e, wl, u, p, sg, wf, w1, w2, outer_weights = rest
    everyone = from_all(xn, "row")
    arrived = [shift(a, "col", k + 1) for k, a in enumerate(sends)]
    blended, gate_factor, left, weights, left_weights = call(
        local_kernel,
        "local",
        (xn, u, sg, wf, w1, outer_weights, masks),
        [
            pltpu.VMEM((rows, 2 * g.HW), BF16),
            pltpu.VMEM((rows, 2 * g.HW), F32),
            pltpu.VMEM((entries, g.Q), BF16),
            pltpu.VMEM((g.QL, g.Q, g.Z), BF16),
            pltpu.VMEM((g.I, g.QL * g.S, g.Z), BF16),
        ],
        [pltpu.VMEM(outer_weights.shape, F32), pltpu.VMEM((2, rows, LANES), F32)],
    )
    share = g.QL // g.D * g.Q
    xall, *rest = call(
        outer_kernel,
        "outer",
        (*everyone, sends[0], *arrived, left, weights, left_weights, w1, w2, masks),
        [pltpu.VMEM((g.SP, g.N, 2 * g.M), BF16)]
        + [pltpu.VMEM((share, g.Z), F32)] * g.D
        + [pltpu.VMEM((g.SP, g.N, 2 * g.M), F32), pltpu.VMEM((g.SP, g.I, 2 * g.M), F32)],
        [
            pltpu.VMEM((g.I, g.N, g.Z), BF16),
            pltpu.VMEM((g.NT, g.SP * 2 * g.QL, LANES), F32),
            pltpu.VMEM((g.QL * g.S, g.N), BF16),
            pltpu.VMEM((g.QL, 2, g.I, g.SP, g.Z), BF16),
            pltpu.VMEM((g.QL, g.Q, g.Z), F32),
            pltpu.VMEM((rows, 2 * g.M), F32),
            pltpu.VMEM((g.NT, g.QL * g.S, LANES), F32),
        ],
    )
    matrix_parts, (second_term, first_term) = rest[: g.D], rest[g.D :]
    matrix_parts = [matrix_parts[0]] + [
        shift(a, "depth", k + 1) for k, a in enumerate(matrix_parts[1:])
    ]
    soft, grad_soft, own, *sums = call(
        attend_kernel,
        "attend",
        (xall, logits, *arrived, blended, gate_factor, p, sg, second_term, first_term),
        [
            pltpu.VMEM((heads, g.N), F32),
            pltpu.VMEM((heads, g.N), F32),
            pltpu.VMEM((rows, 2 * g.M), F32),
        ]
        + [pltpu.VMEM((rows, 2 * g.M), BF16)] * (g.R - 1),
        [pltpu.VMEM((g.SP, g.N, 2 * g.M), F32), pltpu.VMEM((rows, 2 * g.HW), BF16)],
    )
    grad_softs = [grad_soft] + [shift(grad_soft, "depth", k) for k in range(1, g.D)]
    chunk = share // g.R
    *sums, own_chunk = call(
        pack_kernel,
        "pack",
        (*sums, *matrix_parts),
        [pltpu.VMEM((rows + 2 * chunk, 2 * g.M), BF16)] * (g.R - 1)
        + [pltpu.VMEM((chunk, g.Z), F32)],
        [pltpu.VMEM((g.R, chunk, g.Z), F32)],
    )
    sums = [swap(a, "row", k + 1) for k, a in enumerate(sums)]
    own, grad_logits, own_chunk, *sends = call(
        reduce_kernel,
        "reduce",
        (own, own_chunk, soft, *sums, *grad_softs),
        [
            pltpu.VMEM((rows, 2 * g.M), BF16),
            pltpu.VMEM((heads, g.JC), F32),
            pltpu.VMEM((chunk, g.Z), BF16),
        ]
        + [pltpu.VMEM((rows + heads + chunk, 2 * g.M), BF16)] * (g.C - 1),
        [pltpu.VMEM((g.D, heads, g.N), F32)],
    )
    arrived = [shift(a, "col", k + 1) for k, a in enumerate(sends)]
    matrix = call(
        across_kernel, "across", (own_chunk, *arrived), [pltpu.VMEM((g.C, chunk, g.Z), BF16)]
    )
    matrix = call(
        along_kernel,
        "along",
        from_all(matrix, "row"),
        [pltpu.VMEM((g.R, g.C, chunk, g.Z), BF16)],
    )
    matrix_parts = [matrix] + [shift(matrix, "depth", k) for k in range(1, g.D)]
    ensemble_derivative, pairwise_gradient = call(
        finish_kernel,
        "finish",
        (x, e, wl, own, grad_logits, *arrived),
        [shape(homolog_ensemble.shape, BF16), shape(duplex_embedding.shape, BF16)],
        [pltpu.VMEM((g.C, rows, 2 * g.M), BF16), pltpu.VMEM((g.C, heads, LANES), F32)],
    )
    outer_matrix_gradient = call(
        matrix_kernel,
        "matrix",
        matrix_parts,
        [shape(tensor_product_weights.shape, F32)],
        [pltpu.VMEM((g.D, *matrix.shape), F32)],
    )
    return (ensemble_derivative, pairwise_gradient, outer_matrix_gradient)


def solution(mesh):
    in_specs = (
        P(("parts", "depth"), "row", None),
        P(("parts", "row"), "col", None),
        P("parts"),
        P(("parts", "col")),
        P(),
        P(),
        P(),
        P(),
        P(),
        P(),
        P(),
        P(("parts", "depth"), "row", None),
        P(("parts", "row"), "col", None),
    )
    out_specs = (
        P(("parts", "depth"), "row", None),
        P(("parts", "row"), "col", None),
        P("parts", None),
    )
    return jax.shard_map(
        per_device, mesh=mesh, in_specs=in_specs, out_specs=out_specs, check_vma=False
    )
```

```python
import functools
import math

import jax
import jax.numpy as jnp
from jax import lax
from jax.experimental import pallas as pl
from jax.experimental.pallas import tpu as pltpu
from jax.sharding import PartitionSpec as P

EPS = 1e-05
PENALTY = 10000.0
F32 = jnp.float32
BF16 = jnp.bfloat16
LANES = 128
NN = (((1,), (0,)), ((), ()))
NT = (((1,), (1,)), ((), ()))
VMEM = pl.BlockSpec(memory_space=pltpu.VMEM)
FAR = pl.BlockSpec(memory_space=pl.ANY)


def mm(a, b, dims=NN):
    return lax.dot_general(a, b, dims, preferred_element_type=F32)


def split_high_low(value):
    high = value.astype(BF16)
    return high, (value - high.astype(F32)).astype(BF16)


def iota(shape, dim):
    return lax.broadcasted_iota(jnp.int32, shape, dim)


def lanes_of(pieces):
    return pieces[0] if len(pieces) == 1 else jnp.concatenate(pieces, axis=-1)


def rows_of(pieces):
    return pieces[0] if len(pieces) == 1 else jnp.concatenate(pieces, axis=0)


def standardize(values):
    centred = values - jnp.mean(values, -1, keepdims=True)
    inverse = lax.rsqrt(jnp.mean(centred * centred, -1, keepdims=True) + EPS)
    return centred * inverse, inverse


def standardize_backward(values, upstream):
    scaled, inverse = standardize(values)
    mean_grad = jnp.mean(upstream, -1, keepdims=True)
    mean_cross = jnp.mean(upstream * scaled, -1, keepdims=True)
    return (upstream - mean_grad - scaled * mean_cross) * inverse


def on_diagonal(block, width):
    rows, lanes = block.shape
    same = iota(block.shape, 0) // (rows // 2) == iota(block.shape, 1) // width
    return jnp.where(same, block, jnp.zeros_like(block))


def split_three(value):
    high = value.astype(BF16)
    rest = value - high.astype(F32)
    middle = rest.astype(BF16)
    return [high, middle, (rest - middle.astype(F32)).astype(BF16)]


def three_lanes(value):
    rows, width = value.shape
    fill = -(3 * width) % LANES
    return lanes_of(split_three(value) + [jnp.zeros((rows, fill), BF16)])


def join_three(parts, width):
    wide = parts.astype(F32)
    return (wide[:, :width] + wide[:, width : 2 * width]) + wide[:, 2 * width : 3 * width]


def ensemble_norm_kernel(g, x_hbm, xn_ref, x_ref, sem):
    copy = pltpu.make_async_copy(x_hbm, x_ref, sem)
    copy.start()
    copy.wait()
    normed = standardize(x_ref[...].astype(F32))[0].reshape(g.SP, 2, g.I, g.M)
    xn_ref[...] = jnp.concatenate([normed[:, 0], normed[:, 1]], axis=-1).astype(BF16)


def prepare_kernel(g, xn_ref, flag_ref, live_ref, *refs):
    refs = list(refs)
    count = g.carried
    sources, refs = refs[:count], refs[count:]
    own_ref, refs = refs[0], refs[1:]
    out_refs, refs = refs[: g.C - 1], refs[g.C - 1 :]
    mask_ref, gm_ref, gate_ref, left_ref, ts_ref, lt_ref = refs[:6]
    refs = refs[6:]
    targets, refs = refs[:count], refs[count:]
    flag_in, live_in, rows_ref, heads_ref, wide_ref, half_ref, flag_sem, later_sem = refs
    flags = [
        pltpu.make_async_copy(flag_ref, flag_in, flag_sem.at[0]),
        pltpu.make_async_copy(live_ref, live_in, flag_sem.at[1]),
    ]
    copies = [
        pltpu.make_async_copy(a, b, later_sem.at[k])
        for k, (a, b) in enumerate(zip(sources, targets, strict=True))
    ]
    for copy in copies[:2] + flags + copies[2:]:
        copy.start()
    e_ref, wl_ref, u_ref, sg_ref, wf_ref, w1_ref, t_ref = targets[:7]
    for copy in copies[:2] + flags:
        copy.wait()
    pair = standardize(e_ref[...].astype(F32).reshape(g.I * g.JC, g.Z))[0].astype(BF16)
    penalty = (flag_in[...].astype(F32) - 1.0) * PENALTY
    weights = wl_ref[...]
    for i in range(g.I):
        rows_ref[i * g.H : (i + 1) * g.H, : g.JC] = (
            mm(weights, pair[i * g.JC : (i + 1) * g.JC], NT) + penalty
        )
    for h in range(g.H):
        heads_ref[h] = rows_ref[pl.ds(h, g.I, stride=g.H), :][:, : g.JC]
    col = lax.axis_index("col")
    for k in range(g.C):
        first = lax.rem(col + k, g.C) * g.HL
        logits = heads_ref[pl.ds(first, g.HL)].reshape(g.HL * g.I, g.JC)
        (own_ref if k == 0 else out_refs[k - 1])[...] = logits
    first = lax.axis_index("depth") * g.S
    lane = iota((1, 2 * g.M), 1)
    for k in range(g.SP):
        pair_flags = jnp.where(lane < g.M, live_in[first + 2 * k], live_in[first + 2 * k + 1])
        mask_ref[k : k + 1, :] = pair_flags.astype(F32)
    total = live_in[0]
    for s in range(1, live_in.shape[0]):
        total = total + live_in[s]
    mask_ref[g.SP : g.SP + 1, :] = 1.0 / (0.001 + jnp.full((1, 2 * g.M), total, jnp.int32).astype(F32))
    for copy in copies[2:]:
        copy.wait()
    rows = g.SP * g.I
    xn = xn_ref[...]
    wide = g.HW * g.C
    pick = (iota((wide, 2 * g.HW), 0) == col * g.HW + iota((wide, 2 * g.HW), 1) % g.HW).astype(BF16)
    sg, wf = sg_ref[...], wf_ref[...]
    gate_weights = on_diagonal(mm(rows_of([sg, sg]), pick), g.HW).astype(BF16)
    gates = jax.nn.sigmoid(mm(xn.reshape(rows, 2 * g.M), gate_weights))
    u = u_ref[...].reshape(g.SP, 2, g.I, g.M)
    packed_u = jnp.concatenate([u[:, 0], u[:, 1]], axis=-1).reshape(rows, 2 * g.M)
    final_weights = on_diagonal(mm(rows_of([wf, wf]), pick), g.HW).astype(BF16)
    gated = mm(packed_u, final_weights)
    blended = gated * gates
    gm_ref[...] = blended.astype(BF16)
    gate_ref[...] = blended * (1.0 - gates)
    live_xn = rows_of(
        [(xn[k].astype(F32) * mask_ref[k : k + 1, :]).astype(BF16) for k in range(g.SP)]
    )
    w1 = rows_of([w1_ref[...], jnp.zeros((LANES - g.Q, g.M), BF16)])
    zero = jnp.zeros_like(w1)
    half_ref[0] = mm(live_xn, lanes_of([w1, zero]), NT)
    half_ref[1] = mm(live_xn, lanes_of([zero, w1]), NT)
    for half in range(2):
        for i in range(g.I):
            first = (half * g.I + i) * g.SP
            left_ref[first : first + g.SP, :] = half_ref[half, pl.ds(i, g.SP, stride=g.I), :][
                :, : g.Q
            ].astype(BF16)
    wide_ref[...] = t_ref[...].astype(F32)
    for q in range(g.QL):
        ts_ref[q] = wide_ref[pl.ds(col * g.QL + q, g.Q, stride=g.Q), :].astype(BF16)
    left = left_ref[...]
    for q in range(0, g.QL, 2):
        product = mm(left, lanes_of([ts_ref[q], ts_ref[q + 1]]))
        for k in range(2):
            for half in range(2):
                block = product[half * g.I * g.SP : (half + 1) * g.I * g.SP, k * g.Z : (k + 1) * g.Z]
                first = (q + k) * g.S + half * g.SP
                lt_ref[:, first : first + g.SP, :] = block.reshape(g.I, g.SP, g.Z).astype(BF16)


def right_kernel(g, *refs):
    d_refs, (lt_ref, w2_ref, mask_ref, d_ref, go_ref, rg_ref) = refs[: g.C], refs[g.C :]
    col = lax.axis_index("col")
    masks = [mask_ref[k : k + 1, :] for k in range(g.SP)]
    scale = mask_ref[g.SP : g.SP + 1, :]
    for k in range(g.C):
        spot = (g.C - k) % g.C
        d_ref[:, spot * g.JC : (spot + 1) * g.JC, :] = d_refs[k][...]
    right_grad = jnp.zeros((g.QL * g.S, g.N), F32)
    for i in range(0, g.I, 2):
        right_grad = right_grad + mm(
            lanes_of([lt_ref[i], lt_ref[i + 1]]), lanes_of([d_ref[i], d_ref[i + 1]]), NT
        )
    for t in range(g.NT):
        lanes = min(LANES, g.N - t * LANES)
        piece = right_grad[:, t * LANES : t * LANES + lanes]
        if lanes < LANES:
            piece = lanes_of([piece, jnp.zeros((g.QL * g.S, LANES - lanes), F32)])
        rg_ref[t] = piece
    deep = 2 * g.QL
    group = min(g.SP, LANES // deep)
    order = iota((group * deep, g.Q), 0) % deep // 2
    pick = (iota((group * deep, g.Q), 1) == col * g.QL + order).astype(BF16)
    w2 = w2_ref[...]
    base = mm(pick, lanes_of([w2, w2]))
    which = iota(base.shape, 0)
    base = jnp.where(which % 2 == iota(base.shape, 1) // g.M, base, 0.0)
    weights = lanes_of([jnp.where(which // deep == k, base, 0.0) for k in range(group)]).astype(BF16)
    for k in range(0, g.SP, group):
        for t in range(g.NT):
            lanes = min(LANES, g.N - t * LANES)
            tall = rows_of(
                [rg_ref[t, pl.ds(k + m, deep, stride=g.SP), :] for m in range(group)]
            )
            tall = (tall * scale).T[:lanes]
            high, low = split_high_low(tall)
            part = mm(high, weights) + mm(low, weights)
            for m in range(group):
                go_ref[k + m, t * LANES : t * LANES + lanes, :] = (
                    part[:, m * 2 * g.M : (m + 1) * 2 * g.M] * masks[k + m]
                )


def outer_kernel(g, *refs):
    refs = list(refs)
    x_refs, refs = refs[: g.R], refs[g.R :]
    d_ref, left_ref, ts_ref, w1_ref, w2_ref, mask_ref = refs[:6]
    refs = refs[6:]
    xall_ref, w_refs, refs = refs[0], refs[1 : 1 + g.D], refs[1 + g.D :]
    gl_ref, spread_ref, rt_ref, ds_ref, all_ref, turn_ref = refs
    row, col, depth = (lax.axis_index(a) for a in ("row", "col", "depth"))
    masks = [mask_ref[k : k + 1, :] for k in range(g.SP)]
    scale = mask_ref[g.SP : g.SP + 1, :]
    for x in range(g.R):
        xall_ref[:, pl.ds(g.place(jnp.bitwise_xor(row, x), col), g.I), :] = x_refs[x][...]
    w2 = w2_ref[...]
    pick = (iota((2 * g.QL, g.Q), 1) == col * g.QL + iota((2 * g.QL, g.Q), 0) % g.QL).astype(BF16)
    second = on_diagonal(mm(pick, lanes_of([w2, w2])), g.M).astype(BF16)
    for k in range(g.SP):
        live_x = (xall_ref[k].astype(F32) * masks[k]).astype(BF16)
        part = mm(second, live_x, NT)
        for t in range(g.NT):
            lanes = min(LANES, g.N - t * LANES)
            spread_ref[t, k * 2 * g.QL : (k + 1) * 2 * g.QL, :lanes] = part[
                :, t * LANES : t * LANES + lanes
            ]
    for q in range(g.QL):
        for half in range(2):
            first = q * g.S + half * g.SP
            for t in range(g.NT):
                lanes = min(LANES, g.N - t * LANES)
                piece = spread_ref[t, pl.ds(half * g.QL + q, g.SP, stride=2 * g.QL), :]
                rt_ref[first : first + g.SP, t * LANES : t * LANES + lanes] = piece[
                    :, :lanes
                ].astype(BF16)
    rt = rt_ref[...]
    for i in range(0, g.I, 2):
        product = mm(rt, lanes_of([d_ref[i], d_ref[i + 1]]))
        for k in range(2):
            block = product[:, k * g.Z : (k + 1) * g.Z]
            ds_ref[:, :, i + k] = block.reshape(g.QL, 2, g.SP, g.Z).astype(BF16)
    left = left_ref[...]
    eye = (iota((g.Q, g.Q), 0) == iota((g.Q, g.Q), 1)).astype(BF16)
    left_t = mm(eye, left, NT).astype(BF16)
    entries = g.S * g.I
    left_grad = jnp.zeros((entries, g.Q), F32)
    for q in range(0, g.QL, 2):
        both = lanes_of([ds_ref[q].reshape(entries, g.Z), ds_ref[q + 1].reshape(entries, g.Z)])
        part = mm(left_t, both)
        all_ref[pl.ds(q, g.Q, stride=g.QL), :] = part[:, : g.Z] * scale
        all_ref[pl.ds(q + 1, g.Q, stride=g.QL), :] = part[:, g.Z :] * scale
        left_grad = left_grad + mm(both, lanes_of([ts_ref[q], ts_ref[q + 1]]), NT)
    share = g.QL * g.Q // g.D
    for k in range(g.D):
        first = pl.multiple_of(lax.rem(depth + k, g.D) * share, share)
        w_refs[k][...] = all_ref[pl.ds(first, share), :]
    w1 = w1_ref[...]
    zero = jnp.zeros_like(w1)
    first_term = jnp.zeros((entries // 2, 2 * g.M), F32)
    for half in range(2):
        weights = lanes_of([w1, zero] if half == 0 else [zero, w1])
        block = left_grad[half * (entries // 2) : (half + 1) * (entries // 2)] * scale[:, : g.Q]
        for piece in split_high_low(block):
            first_term = first_term + mm(piece, weights)
    turn_ref[...] = first_term
    for k in range(g.SP):
        gl_ref[k] = turn_ref[pl.ds(k, g.I, stride=g.SP), :] * masks[k]


def attend_kernel(g, *refs):
    refs = list(refs)
    xall_ref, refs = refs[0], refs[1:]
    logit_refs, refs = refs[: g.C], refs[g.C :]
    gm_ref, gate_ref, p_ref, sg_ref, go_ref, gl_ref = refs[:6]
    soft_ref, gs_ref, own_ref, refs = refs[6], refs[7], refs[8], refs[9:]
    send_refs, (total_ref, gg_ref) = refs[: g.R - 1], refs[g.R - 1 :]
    row, col = lax.axis_index("row"), lax.axis_index("col")
    logits = lanes_of([logit_refs[(g.C - k) % g.C][...] for k in range(g.C)])
    shifted = jnp.exp(logits - jnp.max(logits, -1, keepdims=True))
    soft = shifted / jnp.sum(shifted, -1, keepdims=True)
    soft_ref[...] = soft
    low = soft.astype(BF16)
    eye = (iota((g.N, g.N), 0) == iota((g.N, g.N), 1)).astype(BF16)
    low_t = mm(eye, low, NT).astype(BF16)
    wide = g.HW * g.C
    pick = (iota((wide, 2 * g.HW), 0) == col * g.HW + iota((wide, 2 * g.HW), 1) % g.HW).astype(BF16)
    p, sg = p_ref[...], sg_ref[...]
    value_weights = on_diagonal(mm(rows_of([p, p]), pick), g.HW).astype(BF16)
    gate_weights = on_diagonal(mm(rows_of([sg, sg]), pick), g.HW).astype(BF16)
    values = mm(xall_ref[...].reshape(g.SP * g.N, 2 * g.M), value_weights).astype(BF16)
    head = iota((1, 2 * g.HW), 1) % g.HW // (g.HW // g.HL)
    grad_soft = jnp.zeros((g.HL * g.I, g.N), F32)
    for k in range(g.SP):
        v = values[k * g.N : (k + 1) * g.N]
        crossed = mm(low, v)
        mixed = jnp.zeros((g.I, 2 * g.HW), F32)
        for h in range(g.HL):
            mixed = mixed + jnp.where(head == h, crossed[h * g.I : (h + 1) * g.I], 0.0)
        rows = slice(k * g.I, (k + 1) * g.I)
        gg_ref[rows, :] = (gate_ref[rows, :] * mixed).astype(BF16)
        blended = gm_ref[rows, :]
        by_head = rows_of(
            [jnp.where(head == h, blended, jnp.zeros_like(blended)) for h in range(g.HL)]
        )
        grad_soft = grad_soft + mm(by_head, v, NT)
        part = go_ref[k]
        for piece in split_high_low(mm(low_t, by_head)):
            part = part + mm(piece, value_weights, NT)
        total_ref[k] = part
    gs_ref[...] = grad_soft
    own = total_ref[:, pl.ds(g.place(row, col), g.I), :]
    gate_term = mm(gg_ref[...], gate_weights, NT).reshape(g.SP, g.I, 2 * g.M)
    own_ref[...] = (own + gate_term + gl_ref[...]).reshape(g.SP * g.I, 2 * g.M)
    for x in range(1, g.R):
        block = total_ref[:, pl.ds(g.place(jnp.bitwise_xor(row, x), col), g.I), :]
        send_refs[x - 1][...] = block.reshape(g.SP * g.I, 2 * g.M).astype(BF16)


def pack_kernel(g, *refs):
    refs = list(refs)
    sums, refs = refs[: g.R - 1], refs[g.R - 1 :]
    parts, refs = refs[: g.D], refs[g.D :]
    outs, (own_ref, total_ref) = refs[: g.R - 1], refs[g.R - 1 :]
    row = lax.axis_index("row")
    total = parts[0][...]
    for ref in parts[1:]:
        total = total + ref[...]
    chunk, rows = own_ref.shape[0], g.SP * g.I
    for r in range(g.R):
        total_ref[r] = total[r * chunk : (r + 1) * chunk]
    own_ref[...] = total_ref[row]
    for x in range(1, g.R):
        out = outs[x - 1]
        out[:rows, :] = sums[x - 1][...]
        high, low = split_high_low(total_ref[jnp.bitwise_xor(row, x)])
        out[rows : rows + chunk, :] = high
        out[rows + chunk :, :] = low


def reduce_kernel(g, own_ref, matrix_ref, soft_ref, *refs):
    refs = list(refs)
    got, refs = refs[: g.R - 1], refs[g.R - 1 :]
    parts, refs = refs[: g.D], refs[g.D :]
    sum_ref, grad_ref, chunk_ref, refs = refs[0], refs[1], refs[2], refs[3:]
    out_refs, (order_ref,) = refs[: g.C - 1], refs[g.C - 1 :]
    depth = lax.axis_index("depth")
    rows, chunk = g.SP * g.I, matrix_ref.shape[0]
    total, matrix = own_ref[...], matrix_ref[...]
    for ref in got:
        total = total + ref[:rows, :].astype(F32)
        matrix = matrix + ref[rows : rows + chunk, :].astype(F32)
        matrix = matrix + ref[rows + chunk :, :].astype(F32)
    total, matrix = total.astype(BF16), matrix.astype(BF16)
    sum_ref[...] = total
    chunk_ref[...] = matrix
    for k in range(g.D):
        order_ref[lax.rem(depth - k + g.D, g.D)] = parts[k][...]
    grad_soft = order_ref[0]
    for k in range(1, g.D):
        grad_soft = grad_soft + order_ref[k]
    soft = soft_ref[...]
    grad = soft * (grad_soft - jnp.sum(soft * grad_soft, -1, keepdims=True))
    grad_ref[...] = grad[:, : g.JC]
    for k in range(1, g.C):
        out_refs[k - 1][:rows, :] = total
        out_refs[k - 1][rows:, :] = three_lanes(grad[:, k * g.JC : (k + 1) * g.JC])


def along_kernel(g, *refs):
    out_ref = refs[-1]
    row = lax.axis_index("row")
    for x, ref in enumerate(refs[:-1]):
        out_ref[jnp.bitwise_xor(row, x)] = ref[...]


def across_kernel(g, *refs):
    out_ref = refs[-1]
    col = lax.axis_index("col")
    for k, ref in enumerate(refs[:-1]):
        out_ref[lax.rem(col - k + g.C, g.C)] = ref[...]


def ensemble_kernel(g, x_ref, sum_ref, *refs):
    got, (msa_ref, sums_ref) = refs[: g.C - 1], refs[g.C - 1 :]
    col = lax.axis_index("col")
    rows = g.SP * g.I
    sums_ref[col] = sum_ref[...]
    for k in range(1, g.C):
        sums_ref[lax.rem(col - k + g.C, g.C)] = got[k - 1][:rows, :]
    total = sums_ref[0].astype(F32)
    for k in range(1, g.C):
        total = total + sums_ref[k].astype(F32)
    total = total.reshape(g.SP, 1, g.I, 2 * g.M)
    upstream = jnp.concatenate([total[..., : g.M], total[..., g.M :]], axis=1)
    upstream = upstream.reshape(g.S, g.I, g.M)
    msa_ref[...] = standardize_backward(x_ref[...].astype(F32), upstream).astype(BF16)


def pair_kernel(g, e_ref, wl_ref, grad_ref, *refs):
    got, (pair_ref, grads_ref) = refs[: g.C - 1], refs[g.C - 1 :]
    col = lax.axis_index("col")
    rows, heads = g.SP * g.I, g.HL * g.I
    grads_ref[col, :, : g.JC] = grad_ref[...]
    for k in range(1, g.C):
        place = lax.rem(col - k + g.C, g.C)
        grads_ref[place, :, : g.JC] = join_three(got[k - 1][rows:, :], g.JC)
    if g.JC < LANES:
        grads_ref[:, :, g.JC :] = jnp.zeros((g.C, heads, LANES - g.JC), F32)
    count = g.H * g.I
    high, low = split_high_low(grads_ref[...].reshape(count, LANES).T[: g.JC])
    grads = lanes_of([high, low])
    pick = (iota((count, g.H), 0) // g.I == iota((count, g.H), 1)).astype(BF16)
    base = mm(pick, wl_ref[...]).astype(BF16)
    token = iota((count, 1), 0) % g.I
    for i in range(0, g.I, 2):
        weights = lanes_of(
            [jnp.where(token == i + k, base, jnp.zeros_like(base)) for k in range(2)]
        )
        upstream = mm(grads, rows_of([weights, weights]))
        for k in range(2):
            pair_ref[i + k] = standardize_backward(
                e_ref[i + k].astype(F32), upstream[:, k * g.Z : (k + 1) * g.Z]
            ).astype(BF16)


def matrix_kernel(g, *refs):
    parts, out_ref = refs[: g.D], refs[g.D]
    depth = lax.axis_index("depth")
    share = g.Q // g.D
    for k in range(g.D):
        first = lax.rem(depth - k + g.D, g.D) * share
        for c in range(g.C):
            out_ref[pl.ds(first, share), c * g.QL : (c + 1) * g.QL, :] = parts[k][c].astype(F32)


class Sizes:
    def __init__(self, x, e, wl, p, w1):
        self.R, self.C, self.D = (lax.axis_size(a) for a in ("row", "col", "depth"))
        self.S, self.I, self.M = x.shape
        self.JC, self.Z = e.shape[1:]
        self.H, self.Q = wl.shape[1], w1.shape[1]
        self.SP, self.N = self.S // 2, self.R * self.I
        self.HL, self.QL = self.H // self.C, self.Q // self.C
        self.HW = p.shape[1] // self.C
        self.F = self.R // self.C
        self.NT = -(-self.N // LANES)
        self.carried = 0

    def place(self, row, col):
        turn = lax.rem(row // self.F - col + self.C, self.C)
        return pl.multiple_of((turn * self.F + lax.rem(row, self.F)) * self.I, self.I)


def shift(array, axis, k):
    count = lax.axis_size(axis)
    return lax.ppermute(array, axis, [(i, (i + k) % count) for i in range(count)])


def swap(array, axis, x):
    return lax.ppermute(array, axis, [(i, i ^ x) for i in range(lax.axis_size(axis))])


def from_all(array, axis):
    return [array] + [swap(array, axis, x) for x in range(1, lax.axis_size(axis))]


def per_device(
    homolog_ensemble,
    duplex_embedding,
    homolog_present_flags,
    resolved_position_flags,
    payload_weights,
    sigmoid_weights,
    averager_final_weights,
    first_operand_weights,
    second_operand_weights,
    duplex_logit_weights,
    tensor_product_weights,
    averager_upstream_adjoint,
    duplex_upstream_adjoint,
):
    g = Sizes(
        homolog_ensemble, duplex_embedding, duplex_logit_weights, payload_weights, first_operand_weights
    )
    shape = jax.ShapeDtypeStruct

    def call(kernel, name, args, outs, scratch=(), far=None, after=(), distant=False, us=1.0):
        size = sum(a.size * a.dtype.itemsize for a in args) + sum(
            math.prod(o.shape) * jnp.dtype(o.dtype).itemsize for o in outs
        )
        single = len(outs) == 1
        near = len(args) if far is None else far
        args = list(args[:near]) + [
            pltpu.with_memory_space_constraint(a, pltpu.HBM) for a in args[near:]
        ]

        if distant:
            after = [pltpu.with_memory_space_constraint(a, pltpu.HBM) for a in after]

        def body(*refs):
            kernel(g, *refs[: len(args)], *refs[len(args) + len(after) :])

        return pl.pallas_call(
            body,
            out_shape=outs[0] if single else tuple(outs),
            in_specs=[VMEM] * near + [FAR] * (len(args) - near) + [FAR if distant else VMEM] * len(after),
            out_specs=VMEM if single else (VMEM,) * len(outs),
            scratch_shapes=list(scratch),
            compiler_params=pltpu.CompilerParams(vmem_limit_bytes=40 * 1024 * 1024),
            cost_estimate=pl.CostEstimate(
                flops=int(us * 1.15e9), bytes_accessed=size, transcendentals=0
            ),
            name=name,
        )(*args, *after)

    heads = g.HL * g.I
    entries = g.S * g.I
    rows = g.SP * g.I
    xn, x = call(
        ensemble_norm_kernel,
        "ensemble_norm",
        (homolog_ensemble,),
        [pltpu.VMEM((g.SP, g.I, 2 * g.M), BF16), pltpu.VMEM(homolog_ensemble.shape, BF16)],
        [pltpu.SemaphoreType.DMA],
        far=0,
    )
    everyone = from_all(xn, "row")
    cotangents = [duplex_upstream_adjoint] + [
        shift(duplex_upstream_adjoint, "col", k) for k in range(1, g.C)
    ]
    later = (
        duplex_embedding,
        duplex_logit_weights.T,
        averager_upstream_adjoint,
        sigmoid_weights,
        averager_final_weights.T,
        first_operand_weights.T,
        tensor_product_weights,
        payload_weights,
        second_operand_weights.T,
        duplex_upstream_adjoint,
    )
    g.carried = len(later)
    prepared = call(
        prepare_kernel,
        "prepare",
        (xn, resolved_position_flags.reshape(1, g.JC), homolog_present_flags, *later),
        [pltpu.VMEM((heads, g.JC), F32)] * g.C
        + [
            pltpu.VMEM((g.SP + 8, 2 * g.M), F32),
            pltpu.VMEM((rows, 2 * g.HW), BF16),
            pltpu.VMEM((rows, 2 * g.HW), F32),
            pltpu.VMEM((entries, g.Q), BF16),
            pltpu.VMEM((g.QL, g.Q, g.Z), BF16),
            pltpu.VMEM((g.I, g.QL * g.S, g.Z), BF16),
        ]
        + [pltpu.VMEM(a.shape, a.dtype) for a in later],
        [
            pltpu.VMEM((1, g.JC), jnp.int32),
            pltpu.SMEM(homolog_present_flags.shape, jnp.int32),
            pltpu.VMEM((g.I * g.H, LANES), F32),
            pltpu.VMEM((g.H, g.I, g.JC), F32),
            pltpu.VMEM(tensor_product_weights.shape, F32),
            pltpu.VMEM((2, rows, LANES), F32),
            pltpu.SemaphoreType.DMA((2,)),
            pltpu.SemaphoreType.DMA((len(later),)),
        ],
        far=1,
        us=3.0,
    )
    logits, prepared = prepared[: g.C], prepared[g.C :]
    masks, blended, gate_factor, left, weights, left_weights = prepared[:6]
    e, wl, _, sg, _, w1, _, p, w2, cotangents[0] = prepared[6:]
    logits = [logits[0]] + [shift(a, "col", k + 1) for k, a in enumerate(logits[1:])]
    cotangents, second_term = call(
        right_kernel,
        "right",
        (*cotangents, left_weights, w2, masks),
        [pltpu.VMEM((g.I, g.N, g.Z), BF16), pltpu.VMEM((g.SP, g.N, 2 * g.M), F32)],
        [pltpu.VMEM((g.NT, g.QL * g.S, LANES), F32)],
    )
    share = g.QL * g.Q // g.D
    xall, *rest = call(
        outer_kernel,
        "outer",
        (*everyone, cotangents, left, weights, w1, w2, masks),
        [pltpu.VMEM((g.SP, g.N, 2 * g.M), BF16)]
        + [pltpu.VMEM((share, g.Z), F32)] * g.D
        + [pltpu.VMEM((g.SP, g.I, 2 * g.M), F32)],
        [
            pltpu.VMEM((g.NT, g.SP * 2 * g.QL, LANES), F32),
            pltpu.VMEM((g.QL * g.S, g.N), BF16),
            pltpu.VMEM((g.QL, 2, g.I, g.SP, g.Z), BF16),
            pltpu.VMEM((g.QL * g.Q, g.Z), F32),
            pltpu.VMEM((rows, 2 * g.M), F32),
        ],
        after=logits[1:],
        us=3.0,
    )
    matrix_parts, first_term = rest[: g.D], rest[g.D]
    matrix_parts = [matrix_parts[0]] + [
        shift(a, "depth", k + 1) for k, a in enumerate(matrix_parts[1:])
    ]
    soft, grad_soft, own, *sums = call(
        attend_kernel,
        "attend",
        (xall, *logits, blended, gate_factor, p, sg, second_term, first_term),
        [
            pltpu.VMEM((heads, g.N), F32),
            pltpu.VMEM((heads, g.N), F32),
            pltpu.VMEM((rows, 2 * g.M), F32),
        ]
        + [pltpu.VMEM((rows, 2 * g.M), BF16)] * (g.R - 1),
        [pltpu.VMEM((g.SP, g.N, 2 * g.M), F32), pltpu.VMEM((rows, 2 * g.HW), BF16)],
    )
    grad_softs = [grad_soft] + [shift(grad_soft, "depth", k) for k in range(1, g.D)]
    chunk = share // g.R
    *sums, own_chunk = call(
        pack_kernel,
        "pack",
        (*sums, *matrix_parts),
        [pltpu.VMEM((rows + 2 * chunk, 2 * g.M), BF16)] * (g.R - 1)
        + [pltpu.VMEM((chunk, g.Z), F32)],
        [pltpu.VMEM((g.R, chunk, g.Z), F32)],
    )
    sums = [swap(a, "row", k + 1) for k, a in enumerate(sums)]
    own, grad_logits, own_chunk, *sends = call(
        reduce_kernel,
        "reduce",
        (own, own_chunk, soft, *sums, *grad_softs),
        [
            pltpu.VMEM((rows, 2 * g.M), BF16),
            pltpu.VMEM((heads, g.JC), F32),
            pltpu.VMEM((chunk, g.Z), BF16),
        ]
        + [pltpu.VMEM((rows + heads, 2 * g.M), BF16)] * (g.C - 1),
        [pltpu.VMEM((g.D, heads, g.N), F32)],
    )
    arrived = [shift(a, "col", k + 1) for k, a in enumerate(sends)]
    matrix = call(
        along_kernel,
        "along",
        from_all(own_chunk, "row"),
        [pltpu.VMEM((g.R, chunk, g.Z), BF16)],
        after=arrived,
        us=0.1,
    )
    matrices = [matrix] + [shift(matrix, "col", k) for k in range(1, g.C)]
    ensemble_derivative = call(
        ensemble_kernel,
        "ensemble",
        (x, own, *arrived),
        [shape(homolog_ensemble.shape, BF16)],
        [pltpu.VMEM((g.C, rows, 2 * g.M), BF16)],
        after=(matrix,),
    )
    matrix = call(
        across_kernel,
        "across",
        matrices,
        [pltpu.VMEM((g.C, g.R, chunk, g.Z), BF16)],
        after=(ensemble_derivative,),
        distant=True,
        us=0.1,
    ).reshape(g.C, g.Q // g.D, g.QL, g.Z)
    matrix_parts = [matrix] + [shift(matrix, "depth", k) for k in range(1, g.D)]
    pairwise_gradient = call(
        pair_kernel,
        "pair",
        (e, wl, grad_logits, *arrived),
        [shape(duplex_embedding.shape, BF16)],
        [pltpu.VMEM((g.C, heads, LANES), F32)],
        after=(matrix,),
        us=1.5,
    )
    outer_matrix_gradient = call(
        matrix_kernel,
        "matrix",
        matrix_parts,
        [shape((g.Q, g.Q, g.Z), F32)],
        after=(pairwise_gradient,),
        distant=True,
    ).reshape(tensor_product_weights.shape)
    return (ensemble_derivative, pairwise_gradient, outer_matrix_gradient)


def solution(mesh):
    in_specs = (
        P(("parts", "depth"), "row", None),
        P(("parts", "row"), "col", None),
        P("parts"),
        P(("parts", "col")),
        P(),
        P(),
        P(),
        P(),
        P(),
        P(),
        P(),
        P(("parts", "depth"), "row", None),
        P(("parts", "row"), "col", None),
    )
    out_specs = (
        P(("parts", "depth"), "row", None),
        P(("parts", "row"), "col", None),
        P("parts", None),
    )
    return jax.shard_map(
        per_device, mesh=mesh, in_specs=in_specs, out_specs=out_specs, check_vma=False
    )
```

```python
import functools
import math

import jax
import jax.numpy as jnp
from jax import lax
from jax.experimental import pallas as pl
from jax.experimental.pallas import tpu as pltpu
from jax.sharding import PartitionSpec as P

EPS = 1e-05
PENALTY = 10000.0
F32 = jnp.float32
BF16 = jnp.bfloat16
LANES = 128
NN = (((1,), (0,)), ((), ()))
NT = (((1,), (1,)), ((), ()))
VMEM = pl.BlockSpec(memory_space=pltpu.VMEM)
FAR = pl.BlockSpec(memory_space=pl.ANY)


def mm(a, b, dims=NN):
    return lax.dot_general(a, b, dims, preferred_element_type=F32)


def split_high_low(value):
    high = value.astype(BF16)
    return high, (value - high.astype(F32)).astype(BF16)


def iota(shape, dim):
    return lax.broadcasted_iota(jnp.int32, shape, dim)


def lanes_of(pieces):
    return pieces[0] if len(pieces) == 1 else jnp.concatenate(pieces, axis=-1)


def rows_of(pieces):
    return pieces[0] if len(pieces) == 1 else jnp.concatenate(pieces, axis=0)


def standardize(values):
    centred = values - jnp.mean(values, -1, keepdims=True)
    inverse = lax.rsqrt(jnp.mean(centred * centred, -1, keepdims=True) + EPS)
    return centred * inverse, inverse


def standardize_backward(values, upstream):
    scaled, inverse = standardize(values)
    mean_grad = jnp.mean(upstream, -1, keepdims=True)
    mean_cross = jnp.mean(upstream * scaled, -1, keepdims=True)
    return (upstream - mean_grad - scaled * mean_cross) * inverse


def on_diagonal(block, width):
    rows, lanes = block.shape
    same = iota(block.shape, 0) // (rows // 2) == iota(block.shape, 1) // width
    return jnp.where(same, block, jnp.zeros_like(block))


def split_three(value):
    high = value.astype(BF16)
    rest = value - high.astype(F32)
    middle = rest.astype(BF16)
    return [high, middle, (rest - middle.astype(F32)).astype(BF16)]


def three_lanes(value):
    rows, width = value.shape
    fill = -(3 * width) % LANES
    return lanes_of(split_three(value) + [jnp.zeros((rows, fill), BF16)])


def join_three(parts, width):
    wide = parts.astype(F32)
    return (wide[:, :width] + wide[:, width : 2 * width]) + wide[:, 2 * width : 3 * width]


def ensemble_norm_kernel(g, x_hbm, xn_ref, x_ref, sem):
    copy = pltpu.make_async_copy(x_hbm, x_ref, sem)
    copy.start()
    copy.wait()
    normed = standardize(x_ref[...].astype(F32))[0].reshape(g.SP, 2, g.I, g.M)
    xn_ref[...] = jnp.concatenate([normed[:, 0], normed[:, 1]], axis=-1).astype(BF16)


def prepare_kernel(g, xn_ref, flag_ref, live_ref, *refs):
    refs = list(refs)
    count = g.carried
    sources, refs = refs[:count], refs[count:]
    own_ref, refs = refs[0], refs[1:]
    out_refs, refs = refs[: g.C - 1], refs[g.C - 1 :]
    mask_ref, gm_ref, gate_ref, left_ref, ts_ref, lt_ref = refs[:6]
    refs = refs[6:]
    targets, refs = refs[:count], refs[count:]
    flag_in, live_in, rows_ref, heads_ref, wide_ref, half_ref, flag_sem, later_sem = refs
    flags = [
        pltpu.make_async_copy(flag_ref, flag_in, flag_sem.at[0]),
        pltpu.make_async_copy(live_ref, live_in, flag_sem.at[1]),
    ]
    copies = [
        pltpu.make_async_copy(a, b, later_sem.at[k])
        for k, (a, b) in enumerate(zip(sources, targets, strict=True))
    ]
    for copy in copies[:2] + flags + copies[2:]:
        copy.start()
    e_ref, wl_ref, u_ref, sg_ref, wf_ref, w1_ref, t_ref = targets[:7]
    for copy in copies[:2] + flags:
        copy.wait()
    pair = standardize(e_ref[...].astype(F32).reshape(g.I * g.JC, g.Z))[0].astype(BF16)
    penalty = (flag_in[...].astype(F32) - 1.0) * PENALTY
    weights = wl_ref[...]
    for i in range(g.I):
        rows_ref[i * g.H : (i + 1) * g.H, : g.JC] = (
            mm(weights, pair[i * g.JC : (i + 1) * g.JC], NT) + penalty
        )
    for h in range(g.H):
        heads_ref[h] = rows_ref[pl.ds(h, g.I, stride=g.H), :][:, : g.JC]
    col = lax.axis_index("col")
    for k in range(g.C):
        first = lax.rem(col + k, g.C) * g.HL
        logits = heads_ref[pl.ds(first, g.HL)].reshape(g.HL * g.I, g.JC)
        (own_ref if k == 0 else out_refs[k - 1])[...] = logits
    first = lax.axis_index("depth") * g.S
    lane = iota((1, 2 * g.M), 1)
    for k in range(g.SP):
        pair_flags = jnp.where(lane < g.M, live_in[first + 2 * k], live_in[first + 2 * k + 1])
        mask_ref[k : k + 1, :] = pair_flags.astype(F32)
    total = live_in[0]
    for s in range(1, live_in.shape[0]):
        total = total + live_in[s]
    mask_ref[g.SP : g.SP + 1, :] = 1.0 / (0.001 + jnp.full((1, 2 * g.M), total, jnp.int32).astype(F32))
    for copy in copies[2:]:
        copy.wait()
    rows = g.SP * g.I
    xn = xn_ref[...]
    wide = g.HW * g.C
    pick = (iota((wide, 2 * g.HW), 0) == col * g.HW + iota((wide, 2 * g.HW), 1) % g.HW).astype(BF16)
    sg, wf = sg_ref[...], wf_ref[...]
    gate_weights = on_diagonal(mm(rows_of([sg, sg]), pick), g.HW).astype(BF16)
    gates = jax.nn.sigmoid(mm(xn.reshape(rows, 2 * g.M), gate_weights))
    u = u_ref[...].reshape(g.SP, 2, g.I, g.M)
    packed_u = jnp.concatenate([u[:, 0], u[:, 1]], axis=-1).reshape(rows, 2 * g.M)
    final_weights = on_diagonal(mm(rows_of([wf, wf]), pick), g.HW).astype(BF16)
    gated = mm(packed_u, final_weights)
    blended = gated * gates
    gm_ref[...] = blended.astype(BF16)
    gate_ref[...] = blended * (1.0 - gates)
    live_xn = rows_of(
        [(xn[k].astype(F32) * mask_ref[k : k + 1, :]).astype(BF16) for k in range(g.SP)]
    )
    w1 = rows_of([w1_ref[...], jnp.zeros((LANES - g.Q, g.M), BF16)])
    zero = jnp.zeros_like(w1)
    half_ref[0] = mm(live_xn, lanes_of([w1, zero]), NT)
    half_ref[1] = mm(live_xn, lanes_of([zero, w1]), NT)
    for half in range(2):
        for i in range(g.I):
            first = (half * g.I + i) * g.SP
            left_ref[first : first + g.SP, :] = half_ref[half, pl.ds(i, g.SP, stride=g.I), :][
                :, : g.Q
            ].astype(BF16)
    wide_ref[...] = t_ref[...].astype(F32)
    for q in range(g.QL):
        ts_ref[q] = wide_ref[pl.ds(col * g.QL + q, g.Q, stride=g.Q), :].astype(BF16)
    left = left_ref[...]
    for q in range(0, g.QL, 2):
        product = mm(left, lanes_of([ts_ref[q], ts_ref[q + 1]]))
        for k in range(2):
            for half in range(2):
                block = product[half * g.I * g.SP : (half + 1) * g.I * g.SP, k * g.Z : (k + 1) * g.Z]
                first = (q + k) * g.S + half * g.SP
                lt_ref[:, first : first + g.SP, :] = block.reshape(g.I, g.SP, g.Z).astype(BF16)


def right_kernel(g, *refs):
    d_refs, (lt_ref, w2_ref, mask_ref, d_ref, go_ref, rg_ref) = refs[: g.C], refs[g.C :]
    col = lax.axis_index("col")
    masks = [mask_ref[k : k + 1, :] for k in range(g.SP)]
    scale = mask_ref[g.SP : g.SP + 1, :]
    for k in range(g.C):
        spot = (g.C - k) % g.C
        d_ref[:, spot * g.JC : (spot + 1) * g.JC, :] = d_refs[k][...]
    right_grad = jnp.zeros((g.QL * g.S, g.N), F32)
    for i in range(0, g.I, 2):
        right_grad = right_grad + mm(
            lanes_of([lt_ref[i], lt_ref[i + 1]]), lanes_of([d_ref[i], d_ref[i + 1]]), NT
        )
    for t in range(g.NT):
        lanes = min(LANES, g.N - t * LANES)
        piece = right_grad[:, t * LANES : t * LANES + lanes]
        if lanes < LANES:
            piece = lanes_of([piece, jnp.zeros((g.QL * g.S, LANES - lanes), F32)])
        rg_ref[t] = piece
    deep = 2 * g.QL
    group = min(g.SP, LANES // deep)
    order = iota((group * deep, g.Q), 0) % deep // 2
    pick = (iota((group * deep, g.Q), 1) == col * g.QL + order).astype(BF16)
    w2 = w2_ref[...]
    base = mm(pick, lanes_of([w2, w2]))
    which = iota(base.shape, 0)
    base = jnp.where(which % 2 == iota(base.shape, 1) // g.M, base, 0.0)
    weights = lanes_of([jnp.where(which // deep == k, base, 0.0) for k in range(group)]).astype(BF16)
    for k in range(0, g.SP, group):
        for t in range(g.NT):
            lanes = min(LANES, g.N - t * LANES)
            tall = rows_of(
                [rg_ref[t, pl.ds(k + m, deep, stride=g.SP), :] for m in range(group)]
            )
            tall = (tall * scale).T[:lanes]
            high, low = split_high_low(tall)
            part = mm(high, weights) + mm(low, weights)
            for m in range(group):
                go_ref[k + m, t * LANES : t * LANES + lanes, :] = (
                    part[:, m * 2 * g.M : (m + 1) * 2 * g.M] * masks[k + m]
                )


def outer_kernel(g, *refs):
    refs = list(refs)
    x_refs, refs = refs[: g.R], refs[g.R :]
    d_ref, left_ref, ts_ref, w1_ref, w2_ref, mask_ref = refs[:6]
    refs = refs[6:]
    xall_ref, w_refs, refs = refs[0], refs[1 : 1 + g.D], refs[1 + g.D :]
    gl_ref, spread_ref, rt_ref, ds_ref, all_ref, turn_ref = refs
    row, col, depth = (lax.axis_index(a) for a in ("row", "col", "depth"))
    masks = [mask_ref[k : k + 1, :] for k in range(g.SP)]
    scale = mask_ref[g.SP : g.SP + 1, :]
    for x in range(g.R):
        xall_ref[:, pl.ds(g.place(jnp.bitwise_xor(row, x), col), g.I), :] = x_refs[x][...]
    w2 = w2_ref[...]
    pick = (iota((2 * g.QL, g.Q), 1) == col * g.QL + iota((2 * g.QL, g.Q), 0) % g.QL).astype(BF16)
    second = on_diagonal(mm(pick, lanes_of([w2, w2])), g.M).astype(BF16)
    for k in range(g.SP):
        live_x = (xall_ref[k].astype(F32) * masks[k]).astype(BF16)
        part = mm(second, live_x, NT)
        for t in range(g.NT):
            lanes = min(LANES, g.N - t * LANES)
            spread_ref[t, k * 2 * g.QL : (k + 1) * 2 * g.QL, :lanes] = part[
                :, t * LANES : t * LANES + lanes
            ]
    for q in range(g.QL):
        for half in range(2):
            first = q * g.S + half * g.SP
            for t in range(g.NT):
                lanes = min(LANES, g.N - t * LANES)
                piece = spread_ref[t, pl.ds(half * g.QL + q, g.SP, stride=2 * g.QL), :]
                rt_ref[first : first + g.SP, t * LANES : t * LANES + lanes] = piece[
                    :, :lanes
                ].astype(BF16)
    rt = rt_ref[...]
    for i in range(0, g.I, 2):
        product = mm(rt, lanes_of([d_ref[i], d_ref[i + 1]]))
        for k in range(2):
            block = product[:, k * g.Z : (k + 1) * g.Z]
            ds_ref[:, :, i + k] = block.reshape(g.QL, 2, g.SP, g.Z).astype(BF16)
    left = left_ref[...]
    eye = (iota((g.Q, g.Q), 0) == iota((g.Q, g.Q), 1)).astype(BF16)
    left_t = mm(eye, left, NT).astype(BF16)
    entries = g.S * g.I
    left_grad = jnp.zeros((entries, g.Q), F32)
    for q in range(0, g.QL, 2):
        both = lanes_of([ds_ref[q].reshape(entries, g.Z), ds_ref[q + 1].reshape(entries, g.Z)])
        part = mm(left_t, both)
        all_ref[pl.ds(q, g.Q, stride=g.QL), :] = part[:, : g.Z] * scale
        all_ref[pl.ds(q + 1, g.Q, stride=g.QL), :] = part[:, g.Z :] * scale
        left_grad = left_grad + mm(both, lanes_of([ts_ref[q], ts_ref[q + 1]]), NT)
    share = g.QL * g.Q // g.D
    for k in range(g.D):
        first = pl.multiple_of(lax.rem(depth + k, g.D) * share, share)
        w_refs[k][...] = all_ref[pl.ds(first, share), :]
    w1 = w1_ref[...]
    zero = jnp.zeros_like(w1)
    first_term = jnp.zeros((entries // 2, 2 * g.M), F32)
    for half in range(2):
        weights = lanes_of([w1, zero] if half == 0 else [zero, w1])
        block = left_grad[half * (entries // 2) : (half + 1) * (entries // 2)] * scale[:, : g.Q]
        for piece in split_high_low(block):
            first_term = first_term + mm(piece, weights)
    turn_ref[...] = first_term
    for k in range(g.SP):
        gl_ref[k] = turn_ref[pl.ds(k, g.I, stride=g.SP), :] * masks[k]


def attend_kernel(g, *refs):
    refs = list(refs)
    xall_ref, refs = refs[0], refs[1:]
    logit_refs, refs = refs[: g.C], refs[g.C :]
    gm_ref, gate_ref, p_ref, sg_ref, go_ref, gl_ref = refs[:6]
    soft_ref, gs_ref, own_ref, refs = refs[6], refs[7], refs[8], refs[9:]
    send_refs, (total_ref, gg_ref) = refs[: g.R - 1], refs[g.R - 1 :]
    row, col = lax.axis_index("row"), lax.axis_index("col")
    logits = lanes_of([logit_refs[(g.C - k) % g.C][...] for k in range(g.C)])
    shifted = jnp.exp(logits - jnp.max(logits, -1, keepdims=True))
    soft = shifted / jnp.sum(shifted, -1, keepdims=True)
    soft_ref[...] = soft
    low = soft.astype(BF16)
    eye = (iota((g.N, g.N), 0) == iota((g.N, g.N), 1)).astype(BF16)
    low_t = mm(eye, low, NT).astype(BF16)
    wide = g.HW * g.C
    pick = (iota((wide, 2 * g.HW), 0) == col * g.HW + iota((wide, 2 * g.HW), 1) % g.HW).astype(BF16)
    p, sg = p_ref[...], sg_ref[...]
    value_weights = on_diagonal(mm(rows_of([p, p]), pick), g.HW).astype(BF16)
    gate_weights = on_diagonal(mm(rows_of([sg, sg]), pick), g.HW).astype(BF16)
    values = mm(xall_ref[...].reshape(g.SP * g.N, 2 * g.M), value_weights).astype(BF16)
    head = iota((1, 2 * g.HW), 1) % g.HW // (g.HW // g.HL)
    grad_soft = jnp.zeros((g.HL * g.I, g.N), F32)
    for k in range(g.SP):
        v = values[k * g.N : (k + 1) * g.N]
        crossed = mm(low, v)
        mixed = jnp.zeros((g.I, 2 * g.HW), F32)
        for h in range(g.HL):
            mixed = mixed + jnp.where(head == h, crossed[h * g.I : (h + 1) * g.I], 0.0)
        rows = slice(k * g.I, (k + 1) * g.I)
        gg_ref[rows, :] = (gate_ref[rows, :] * mixed).astype(BF16)
        blended = gm_ref[rows, :]
        by_head = rows_of(
            [jnp.where(head == h, blended, jnp.zeros_like(blended)) for h in range(g.HL)]
        )
        grad_soft = grad_soft + mm(by_head, v, NT)
        part = go_ref[k]
        for piece in split_high_low(mm(low_t, by_head)):
            part = part + mm(piece, value_weights, NT)
        total_ref[k] = part
    gs_ref[...] = grad_soft
    own = total_ref[:, pl.ds(g.place(row, col), g.I), :]
    gate_term = mm(gg_ref[...], gate_weights, NT).reshape(g.SP, g.I, 2 * g.M)
    own_ref[...] = (own + gate_term + gl_ref[...]).reshape(g.SP * g.I, 2 * g.M)
    for x in range(1, g.R):
        block = total_ref[:, pl.ds(g.place(jnp.bitwise_xor(row, x), col), g.I), :]
        send_refs[x - 1][...] = block.reshape(g.SP * g.I, 2 * g.M).astype(BF16)


def pack_kernel(g, *refs):
    refs = list(refs)
    sums, refs = refs[: g.R - 1], refs[g.R - 1 :]
    parts, refs = refs[: g.D], refs[g.D :]
    outs, (own_ref, total_ref) = refs[: g.R - 1], refs[g.R - 1 :]
    row = lax.axis_index("row")
    total = parts[0][...]
    for ref in parts[1:]:
        total = total + ref[...]
    chunk, rows = own_ref.shape[0], g.SP * g.I
    for r in range(g.R):
        total_ref[r] = total[r * chunk : (r + 1) * chunk]
    own_ref[...] = total_ref[row]
    for x in range(1, g.R):
        out = outs[x - 1]
        out[:rows, :] = sums[x - 1][...]
        high, low = split_high_low(total_ref[jnp.bitwise_xor(row, x)])
        out[rows : rows + chunk, :] = high
        out[rows + chunk :, :] = low


def reduce_kernel(g, own_ref, matrix_ref, soft_ref, *refs):
    refs = list(refs)
    got, refs = refs[: g.R - 1], refs[g.R - 1 :]
    parts, refs = refs[: g.D], refs[g.D :]
    sum_ref, grad_ref, chunk_ref, refs = refs[0], refs[1], refs[2], refs[3:]
    out_refs, (order_ref,) = refs[: g.C - 1], refs[g.C - 1 :]
    depth = lax.axis_index("depth")
    rows, chunk = g.SP * g.I, matrix_ref.shape[0]
    total, matrix = own_ref[...], matrix_ref[...]
    for ref in got:
        total = total + ref[:rows, :].astype(F32)
        matrix = matrix + ref[rows : rows + chunk, :].astype(F32)
        matrix = matrix + ref[rows + chunk :, :].astype(F32)
    total, matrix = total.astype(BF16), matrix.astype(BF16)
    sum_ref[...] = total
    chunk_ref[...] = matrix
    for k in range(g.D):
        order_ref[lax.rem(depth - k + g.D, g.D)] = parts[k][...]
    grad_soft = order_ref[0]
    for k in range(1, g.D):
        grad_soft = grad_soft + order_ref[k]
    soft = soft_ref[...]
    grad = soft * (grad_soft - jnp.sum(soft * grad_soft, -1, keepdims=True))
    grad_ref[...] = grad[:, : g.JC]
    for k in range(1, g.C):
        out_refs[k - 1][:rows, :] = total
        out_refs[k - 1][rows:, :] = three_lanes(grad[:, k * g.JC : (k + 1) * g.JC])


def join_kernel(g, *refs):
    out_ref, first = refs[-1], 0
    for ref in refs[:-1]:
        out_ref[first : first + ref.shape[0]] = ref[...]
        first += ref.shape[0]


def across_kernel(g, *refs):
    out_ref = refs[-1]
    row, col = lax.axis_index("row"), lax.axis_index("col")
    for k, ref in enumerate(refs[:-1]):
        for r in range(g.R):
            out_ref[lax.rem(col - k + g.C, g.C), r] = ref[jnp.bitwise_xor(row, r)]


def ensemble_kernel(g, x_ref, sum_ref, *refs):
    got, (msa_ref, sums_ref) = refs[: g.C - 1], refs[g.C - 1 :]
    col = lax.axis_index("col")
    rows = g.SP * g.I
    sums_ref[col] = sum_ref[...]
    for k in range(1, g.C):
        sums_ref[lax.rem(col - k + g.C, g.C)] = got[k - 1][:rows, :]
    total = sums_ref[0].astype(F32)
    for k in range(1, g.C):
        total = total + sums_ref[k].astype(F32)
    total = total.reshape(g.SP, 1, g.I, 2 * g.M)
    upstream = jnp.concatenate([total[..., : g.M], total[..., g.M :]], axis=1)
    upstream = upstream.reshape(g.S, g.I, g.M)
    msa_ref[...] = standardize_backward(x_ref[...].astype(F32), upstream).astype(BF16)


def pair_kernel(g, e_ref, wl_ref, grad_ref, *refs):
    got, (pair_ref, grads_ref) = refs[: g.C - 1], refs[g.C - 1 :]
    col = lax.axis_index("col")
    rows, heads = g.SP * g.I, g.HL * g.I
    grads_ref[col, :, : g.JC] = grad_ref[...]
    for k in range(1, g.C):
        place = lax.rem(col - k + g.C, g.C)
        grads_ref[place, :, : g.JC] = join_three(got[k - 1][rows:, :], g.JC)
    if g.JC < LANES:
        grads_ref[:, :, g.JC :] = jnp.zeros((g.C, heads, LANES - g.JC), F32)
    count = g.H * g.I
    high, low = split_high_low(grads_ref[...].reshape(count, LANES).T[: g.JC])
    grads = lanes_of([high, low])
    pick = (iota((count, g.H), 0) // g.I == iota((count, g.H), 1)).astype(BF16)
    base = mm(pick, wl_ref[...]).astype(BF16)
    token = iota((count, 1), 0) % g.I
    for i in range(0, g.I, 2):
        weights = lanes_of(
            [jnp.where(token == i + k, base, jnp.zeros_like(base)) for k in range(2)]
        )
        upstream = mm(grads, rows_of([weights, weights]))
        for k in range(2):
            pair_ref[i + k] = standardize_backward(
                e_ref[i + k].astype(F32), upstream[:, k * g.Z : (k + 1) * g.Z]
            ).astype(BF16)


def matrix_kernel(g, *refs):
    parts, out_ref = refs[: g.D], refs[g.D]
    depth = lax.axis_index("depth")
    share = g.Q // g.D
    for k in range(g.D):
        first = lax.rem(depth - k + g.D, g.D) * share
        for c in range(g.C):
            out_ref[pl.ds(first, share), c * g.QL : (c + 1) * g.QL, :] = parts[k][c].astype(F32)


class Sizes:
    def __init__(self, x, e, wl, p, w1):
        self.R, self.C, self.D = (lax.axis_size(a) for a in ("row", "col", "depth"))
        self.S, self.I, self.M = x.shape
        self.JC, self.Z = e.shape[1:]
        self.H, self.Q = wl.shape[1], w1.shape[1]
        self.SP, self.N = self.S // 2, self.R * self.I
        self.HL, self.QL = self.H // self.C, self.Q // self.C
        self.HW = p.shape[1] // self.C
        self.F = self.R // self.C
        self.NT = -(-self.N // LANES)
        self.carried = 0

    def place(self, row, col):
        turn = lax.rem(row // self.F - col + self.C, self.C)
        return pl.multiple_of((turn * self.F + lax.rem(row, self.F)) * self.I, self.I)


def shift(array, axis, k):
    count = lax.axis_size(axis)
    return lax.ppermute(array, axis, [(i, (i + k) % count) for i in range(count)])


def swap(array, axis, x):
    return lax.ppermute(array, axis, [(i, i ^ x) for i in range(lax.axis_size(axis))])


def from_all(array, axis):
    return [array] + [swap(array, axis, x) for x in range(1, lax.axis_size(axis))]


def per_device(
    homolog_ensemble,
    duplex_embedding,
    homolog_present_flags,
    resolved_position_flags,
    payload_weights,
    sigmoid_weights,
    averager_final_weights,
    first_operand_weights,
    second_operand_weights,
    duplex_logit_weights,
    tensor_product_weights,
    averager_upstream_adjoint,
    duplex_upstream_adjoint,
):
    g = Sizes(
        homolog_ensemble, duplex_embedding, duplex_logit_weights, payload_weights, first_operand_weights
    )
    shape = jax.ShapeDtypeStruct

    def call(kernel, name, args, outs, scratch=(), far=None, after=(), distant=False, us=1.0):
        size = sum(a.size * a.dtype.itemsize for a in args) + sum(
            math.prod(o.shape) * jnp.dtype(o.dtype).itemsize for o in outs
        )
        single = len(outs) == 1
        near = len(args) if far is None else far
        args = list(args[:near]) + [
            pltpu.with_memory_space_constraint(a, pltpu.HBM) for a in args[near:]
        ]

        if distant:
            after = [pltpu.with_memory_space_constraint(a, pltpu.HBM) for a in after]

        def body(*refs):
            kernel(g, *refs[: len(args)], *refs[len(args) + len(after) :])

        return pl.pallas_call(
            body,
            out_shape=outs[0] if single else tuple(outs),
            in_specs=[VMEM] * near + [FAR] * (len(args) - near) + [FAR if distant else VMEM] * len(after),
            out_specs=VMEM if single else (VMEM,) * len(outs),
            scratch_shapes=list(scratch),
            compiler_params=pltpu.CompilerParams(vmem_limit_bytes=40 * 1024 * 1024),
            cost_estimate=pl.CostEstimate(
                flops=int(us * 1.15e9), bytes_accessed=size, transcendentals=0
            ),
            name=name,
        )(*args, *after)

    heads = g.HL * g.I
    entries = g.S * g.I
    rows = g.SP * g.I
    xn, x = call(
        ensemble_norm_kernel,
        "ensemble_norm",
        (homolog_ensemble,),
        [pltpu.VMEM((g.SP, g.I, 2 * g.M), BF16), pltpu.VMEM(homolog_ensemble.shape, BF16)],
        [pltpu.SemaphoreType.DMA],
        far=0,
    )
    everyone = from_all(xn, "row")
    cotangents = [duplex_upstream_adjoint] + [
        shift(duplex_upstream_adjoint, "col", k) for k in range(1, g.C)
    ]
    later = (
        duplex_embedding,
        duplex_logit_weights.T,
        averager_upstream_adjoint,
        sigmoid_weights,
        averager_final_weights.T,
        first_operand_weights.T,
        tensor_product_weights,
        payload_weights,
        second_operand_weights.T,
        duplex_upstream_adjoint,
    )
    g.carried = len(later)
    prepared = call(
        prepare_kernel,
        "prepare",
        (xn, resolved_position_flags.reshape(1, g.JC), homolog_present_flags, *later),
        [pltpu.VMEM((heads, g.JC), F32)] * g.C
        + [
            pltpu.VMEM((g.SP + 8, 2 * g.M), F32),
            pltpu.VMEM((rows, 2 * g.HW), BF16),
            pltpu.VMEM((rows, 2 * g.HW), F32),
            pltpu.VMEM((entries, g.Q), BF16),
            pltpu.VMEM((g.QL, g.Q, g.Z), BF16),
            pltpu.VMEM((g.I, g.QL * g.S, g.Z), BF16),
        ]
        + [pltpu.VMEM(a.shape, a.dtype) for a in later],
        [
            pltpu.VMEM((1, g.JC), jnp.int32),
            pltpu.SMEM(homolog_present_flags.shape, jnp.int32),
            pltpu.VMEM((g.I * g.H, LANES), F32),
            pltpu.VMEM((g.H, g.I, g.JC), F32),
            pltpu.VMEM(tensor_product_weights.shape, F32),
            pltpu.VMEM((2, rows, LANES), F32),
            pltpu.SemaphoreType.DMA((2,)),
            pltpu.SemaphoreType.DMA((len(later),)),
        ],
        far=1,
        after=cotangents[1:],
        us=3.0,
    )
    logits, prepared = prepared[: g.C], prepared[g.C :]
    masks, blended, gate_factor, left, weights, left_weights = prepared[:6]
    e, wl, _, sg, _, w1, _, p, w2, cotangents[0] = prepared[6:]
    logits = [logits[0]] + [shift(a, "col", k + 1) for k, a in enumerate(logits[1:])]
    cotangents, second_term = call(
        right_kernel,
        "right",
        (*cotangents, left_weights, w2, masks),
        [pltpu.VMEM((g.I, g.N, g.Z), BF16), pltpu.VMEM((g.SP, g.N, 2 * g.M), F32)],
        [pltpu.VMEM((g.NT, g.QL * g.S, LANES), F32)],
    )
    share = g.QL * g.Q // g.D
    xall, *rest = call(
        outer_kernel,
        "outer",
        (*everyone, cotangents, left, weights, w1, w2, masks),
        [pltpu.VMEM((g.SP, g.N, 2 * g.M), BF16)]
        + [pltpu.VMEM((share, g.Z), F32)] * g.D
        + [pltpu.VMEM((g.SP, g.I, 2 * g.M), F32)],
        [
            pltpu.VMEM((g.NT, g.SP * 2 * g.QL, LANES), F32),
            pltpu.VMEM((g.QL * g.S, g.N), BF16),
            pltpu.VMEM((g.QL, 2, g.I, g.SP, g.Z), BF16),
            pltpu.VMEM((g.QL * g.Q, g.Z), F32),
            pltpu.VMEM((rows, 2 * g.M), F32),
        ],
        after=logits[1:],
        us=3.0,
    )
    matrix_parts, first_term = rest[: g.D], rest[g.D]
    matrix_parts = [matrix_parts[0]] + [
        shift(a, "depth", k + 1) for k, a in enumerate(matrix_parts[1:])
    ]
    soft, grad_soft, own, *sums = call(
        attend_kernel,
        "attend",
        (xall, *logits, blended, gate_factor, p, sg, second_term, first_term),
        [
            pltpu.VMEM((heads, g.N), F32),
            pltpu.VMEM((heads, g.N), F32),
            pltpu.VMEM((rows, 2 * g.M), F32),
        ]
        + [pltpu.VMEM((rows, 2 * g.M), BF16)] * (g.R - 1),
        [pltpu.VMEM((g.SP, g.N, 2 * g.M), F32), pltpu.VMEM((rows, 2 * g.HW), BF16)],
    )
    grad_softs = [grad_soft] + [shift(grad_soft, "depth", k) for k in range(1, g.D)]
    chunk = share // g.R
    *sums, own_chunk = call(
        pack_kernel,
        "pack",
        (*sums, *matrix_parts),
        [pltpu.VMEM((rows + 2 * chunk, 2 * g.M), BF16)] * (g.R - 1)
        + [pltpu.VMEM((chunk, g.Z), F32)],
        [pltpu.VMEM((g.R, chunk, g.Z), F32)],
    )
    sums = [swap(a, "row", k + 1) for k, a in enumerate(sums)]
    own, grad_logits, own_chunk, *sends = call(
        reduce_kernel,
        "reduce",
        (own, own_chunk, soft, *sums, *grad_softs),
        [
            pltpu.VMEM((rows, 2 * g.M), BF16),
            pltpu.VMEM((heads, g.JC), F32),
            pltpu.VMEM((chunk, g.Z), BF16),
        ]
        + [pltpu.VMEM((rows + heads, 2 * g.M), BF16)] * (g.C - 1),
        [pltpu.VMEM((g.D, heads, g.N), F32)],
    )
    arrived = [shift(a, "col", k + 1) for k, a in enumerate(sends)]
    def finish_ensemble(matrix):
        return call(
            ensemble_kernel,
            "ensemble",
            (x, own, *arrived),
            [shape(homolog_ensemble.shape, BF16)],
            [pltpu.VMEM((g.C, rows, 2 * g.M), BF16)],
            after=(matrix,),
        )

    matrix, ensemble_derivative, step = own_chunk.reshape(1, chunk, g.Z), None, 1
    while step < g.R:
        last = 2 * step >= g.R and ensemble_derivative is not None
        matrix = call(
            join_kernel,
            "join",
            (matrix, swap(matrix, "row", step)),
            [pltpu.VMEM((2 * step, chunk, g.Z), BF16)],
            after=(ensemble_derivative,) if last else (),
            distant=last,
            us=0.1,
        )
        step *= 2
        if 2 * step >= g.R and ensemble_derivative is None:
            ensemble_derivative = finish_ensemble(matrix)
    if ensemble_derivative is None:
        ensemble_derivative = finish_ensemble(matrix)
    pairwise_gradient = call(
        pair_kernel,
        "pair",
        (e, wl, grad_logits, *arrived),
        [shape(duplex_embedding.shape, BF16)],
        [pltpu.VMEM((g.C, heads, LANES), F32)],
        after=(matrix,),
        us=1.5,
    )
    matrices = [matrix] + [shift(matrix, "col", k) for k in range(1, g.C)]
    matrix = call(
        across_kernel,
        "across",
        matrices,
        [pltpu.VMEM((g.C, g.R, chunk, g.Z), BF16)],
        after=(pairwise_gradient,),
        distant=True,
        us=0.1,
    ).reshape(g.C, g.Q // g.D, g.QL, g.Z)
    matrix_parts = [matrix] + [shift(matrix, "depth", k) for k in range(1, g.D)]
    outer_matrix_gradient = call(
        matrix_kernel,
        "matrix",
        matrix_parts,
        [shape((g.Q, g.Q, g.Z), F32)],
    ).reshape(tensor_product_weights.shape)
    return (ensemble_derivative, pairwise_gradient, outer_matrix_gradient)


def solution(mesh):
    in_specs = (
        P(("parts", "depth"), "row", None),
        P(("parts", "row"), "col", None),
        P("parts"),
        P(("parts", "col")),
        P(),
        P(),
        P(),
        P(),
        P(),
        P(),
        P(),
        P(("parts", "depth"), "row", None),
        P(("parts", "row"), "col", None),
    )
    out_specs = (
        P(("parts", "depth"), "row", None),
        P(("parts", "row"), "col", None),
        P("parts", None),
    )
    return jax.shard_map(
        per_device, mesh=mesh, in_specs=in_specs, out_specs=out_specs, check_vma=False
    )
```

```python
import functools
import math

import jax
import jax.numpy as jnp
from jax import lax
from jax.experimental import pallas as pl
from jax.experimental.pallas import tpu as pltpu
from jax.sharding import PartitionSpec as P

EPS = 1e-05
PENALTY = 10000.0
F32 = jnp.float32
BF16 = jnp.bfloat16
LANES = 128
NN = (((1,), (0,)), ((), ()))
NT = (((1,), (1,)), ((), ()))
VMEM = pl.BlockSpec(memory_space=pltpu.VMEM)
FAR = pl.BlockSpec(memory_space=pl.ANY)


def mm(a, b, dims=NN):
    return lax.dot_general(a, b, dims, preferred_element_type=F32)


def split_high_low(value):
    high = value.astype(BF16)
    return high, (value - high.astype(F32)).astype(BF16)


def iota(shape, dim):
    return lax.broadcasted_iota(jnp.int32, shape, dim)


def lanes_of(pieces):
    return pieces[0] if len(pieces) == 1 else jnp.concatenate(pieces, axis=-1)


def rows_of(pieces):
    return pieces[0] if len(pieces) == 1 else jnp.concatenate(pieces, axis=0)


def standardize(values):
    centred = values - jnp.mean(values, -1, keepdims=True)
    inverse = lax.rsqrt(jnp.mean(centred * centred, -1, keepdims=True) + EPS)
    return centred * inverse, inverse


def standardize_backward(values, upstream):
    scaled, inverse = standardize(values)
    mean_grad = jnp.mean(upstream, -1, keepdims=True)
    mean_cross = jnp.mean(upstream * scaled, -1, keepdims=True)
    return (upstream - mean_grad - scaled * mean_cross) * inverse


def on_diagonal(block, width):
    rows, lanes = block.shape
    same = iota(block.shape, 0) // (rows // 2) == iota(block.shape, 1) // width
    return jnp.where(same, block, jnp.zeros_like(block))


def split_three(value):
    high = value.astype(BF16)
    rest = value - high.astype(F32)
    middle = rest.astype(BF16)
    return [high, middle, (rest - middle.astype(F32)).astype(BF16)]


def three_blocks(value):
    rows, width = value.shape
    fill = -(3 * width) % LANES
    wide = lanes_of(split_three(value) + [jnp.zeros((rows, fill), BF16)] * (fill > 0))
    return [wide[:, k : k + LANES] for k in range(0, wide.shape[1], LANES)]


def join_three(parts, width):
    wide = parts.astype(F32)
    return (wide[:, :width] + wide[:, width : 2 * width]) + wide[:, 2 * width : 3 * width]


def twice(weights):
    zero = jnp.zeros_like(weights)
    return rows_of([lanes_of([weights, zero]), lanes_of([zero, weights])])


def ensemble_norm_kernel(g, x_hbm, xn_ref, x_ref, sem):
    first = lax.axis_index("col") * g.SQ
    copy = pltpu.make_async_copy(x_hbm.at[pl.ds(first, g.SQ)], x_ref, sem)
    copy.start()
    copy.wait()
    normed = g.fill(standardize(x_ref[...].astype(F32))[0]).reshape(g.SP, 2, g.I, g.M)
    xn_ref[...] = jnp.concatenate([normed[:, 0], normed[:, 1]], axis=-1).astype(BF16)


def prepare_kernel(g, xn_ref, flag_ref, live_ref, u_ref, *refs):
    refs = list(refs)
    count = g.carried
    sources, refs = refs[:count], refs[count:]
    logit_ref, mask_ref, gate_weight_ref, gm_ref, gate_ref, left_ref, ts_ref, lt_ref = refs[:8]
    refs = refs[8:]
    targets, refs = refs[:count], refs[count:]
    flag_in, live_in, u_in, rows_ref, wide_ref, half_ref, first_sem, later_sem = refs
    col, depth = lax.axis_index("col"), lax.axis_index("depth")
    firsts = [
        pltpu.make_async_copy(flag_ref, flag_in, first_sem.at[0]),
        pltpu.make_async_copy(live_ref, live_in, first_sem.at[1]),
        pltpu.make_async_copy(u_ref.at[pl.ds(col * g.SQ, g.SQ)], u_in, first_sem.at[2]),
    ]
    copies = [
        pltpu.make_async_copy(a, b, later_sem.at[k])
        for k, (a, b) in enumerate(zip(sources, targets, strict=True))
    ]
    for copy in copies[:2] + firsts + copies[2:]:
        copy.start()
    e_ref, wl_ref, sg_ref, wf_ref, w1_ref, t_ref = targets[:6]
    for copy in copies[:2] + firsts[:2]:
        copy.wait()
    pair = standardize(e_ref[...].astype(F32).reshape(g.I * g.JC, g.Z))[0].astype(BF16)
    penalty = (flag_in[...].astype(F32) - 1.0) * PENALTY
    weights = wl_ref[...]
    for i in range(g.I):
        rows_ref[i * g.H : (i + 1) * g.H, : g.JC] = (
            mm(weights, pair[i * g.JC : (i + 1) * g.JC], NT) + penalty
        )
    for h in range(g.H):
        logit_ref[h * g.I : (h + 1) * g.I, :] = rows_ref[pl.ds(h, g.I, stride=g.H), :][:, : g.JC]
    first = depth * g.C * g.SQ + col * g.SQ
    lane = iota((1, 2 * g.M), 1)
    masks = []
    for k in range(g.SP):
        if 2 * k + 1 < g.SQ:
            flags = jnp.where(lane < g.M, live_in[first + 2 * k], live_in[first + 2 * k + 1])
            masks.append(flags.astype(F32))
        else:
            masks.append(jnp.zeros((1, 2 * g.M), F32))
        mask_ref[k : k + 1, :] = masks[-1]
    total = live_in[0]
    for s in range(1, live_in.shape[0]):
        total = total + live_in[s]
    mask_ref[g.SP : g.SP + 1, :] = 1.0 / (0.001 + jnp.full((1, 2 * g.M), total, jnp.int32).astype(F32))
    for copy in firsts[2:] + copies[2:]:
        copy.wait()
    rows = g.SP * g.I
    xn = xn_ref[...]
    gate_weights = twice(sg_ref[...])
    gate_weight_ref[...] = gate_weights
    gates = jax.nn.sigmoid(mm(xn.reshape(rows, 2 * g.M), gate_weights))
    u = g.fill(u_in[...]).reshape(g.SP, 2, g.I, g.M)
    packed_u = jnp.concatenate([u[:, 0], u[:, 1]], axis=-1).reshape(rows, 2 * g.M)
    gated = mm(packed_u, twice(wf_ref[...]))
    blended = gated * gates
    gm_ref[...] = blended.astype(BF16)
    gate_ref[...] = blended * (1.0 - gates)
    live_xn = rows_of([(xn[k].astype(F32) * masks[k]).astype(BF16) for k in range(g.SP)])
    w1 = rows_of([w1_ref[...], jnp.zeros((LANES - g.Q, g.M), BF16)])
    zero = jnp.zeros_like(w1)
    half_ref[0] = mm(live_xn, lanes_of([w1, zero]), NT)
    half_ref[1] = mm(live_xn, lanes_of([zero, w1]), NT)
    for i in range(g.I):
        halves = [half_ref[half, pl.ds(i, g.SP, stride=g.I), :] for half in range(2)]
        left_ref[i * g.S : (i + 1) * g.S, :] = rows_of(halves)[:, : g.Q].astype(BF16)
    wide_ref[...] = t_ref[...].astype(F32)
    for q in range(g.Q):
        ts_ref[q] = wide_ref[pl.ds(q, g.Q, stride=g.Q), :].astype(BF16)
    left = left_ref[...]
    for q in range(0, g.Q, 2):
        product = mm(left, lanes_of([ts_ref[q], ts_ref[q + 1]]))
        for k in range(2):
            block = product[:, k * g.Z : (k + 1) * g.Z].reshape(g.I, g.S, g.Z)
            lt_ref[:, (q + k) * g.S : (q + k + 1) * g.S, :] = block.astype(BF16)


def outer_kernel(g, *refs):
    refs = list(refs)
    x_refs, refs = refs[: g.R], refs[g.R :]
    d_refs, refs = refs[: g.C], refs[g.C :]
    left_ref, ts_ref, w1_ref, w2_ref, mask_ref = refs[:5]
    refs = refs[5:]
    xall_ref, d_ref, refs = refs[0], refs[1], refs[2:]
    w_refs, (gl_ref, spread_ref, rt_ref, ds_ref, all_ref, turn_ref) = refs[: g.D], refs[g.D :]
    row, col, depth = (lax.axis_index(a) for a in ("row", "col", "depth"))
    masks = [mask_ref[k : k + 1, :] for k in range(g.SP)]
    scale = mask_ref[g.SP : g.SP + 1, :]
    for x in range(g.R):
        xall_ref[:, pl.ds(g.place(jnp.bitwise_xor(row, x), col), g.I), :] = x_refs[x][...]
    for k in range(g.C):
        spot = (g.C - k) % g.C
        d_ref[:, spot * g.JC : (spot + 1) * g.JC, :] = d_refs[k][...]
    w2 = w2_ref[...]
    doubled = lanes_of([w2, w2])
    second = on_diagonal(rows_of([doubled, doubled]), g.M)
    for k in range(g.SP):
        live_x = (xall_ref[k].astype(F32) * masks[k]).astype(BF16)
        part = mm(second, live_x, NT)
        for t in range(g.NT):
            lanes = min(LANES, g.N - t * LANES)
            spread_ref[t, k * 2 * g.Q : (k + 1) * 2 * g.Q, :lanes] = part[
                :, t * LANES : t * LANES + lanes
            ]
    for q in range(g.Q):
        for t in range(g.NT):
            lanes = min(LANES, g.N - t * LANES)
            halves = [
                spread_ref[t, pl.ds(half * g.Q + q, g.SP, stride=2 * g.Q), :] for half in range(2)
            ]
            rt_ref[q * g.S : (q + 1) * g.S, t * LANES : t * LANES + lanes] = rows_of(halves)[
                :, :lanes
            ].astype(BF16)
    rt = rt_ref[...]
    for i in range(0, g.I, 2):
        product = mm(rt, lanes_of([d_ref[i], d_ref[i + 1]]))
        for k in range(2):
            block = product[:, k * g.Z : (k + 1) * g.Z]
            ds_ref[:, i + k] = block.reshape(g.Q, g.S, g.Z).astype(BF16)
    left = left_ref[...]
    eye = (iota((g.Q, g.Q), 0) == iota((g.Q, g.Q), 1)).astype(BF16)
    left_t = mm(eye, left, NT).astype(BF16)
    entries = g.S * g.I
    left_grad = jnp.zeros((entries, g.Q), F32)
    for q in range(0, g.Q, 2):
        both = lanes_of([ds_ref[q].reshape(entries, g.Z), ds_ref[q + 1].reshape(entries, g.Z)])
        part = mm(left_t, both)
        all_ref[pl.ds(q, g.Q, stride=g.Q), :] = part[:, : g.Z] * scale
        all_ref[pl.ds(q + 1, g.Q, stride=g.Q), :] = part[:, g.Z :] * scale
        left_grad = left_grad + mm(both, lanes_of([ts_ref[q], ts_ref[q + 1]]), NT)
    share = g.Q * g.Q // g.D
    for k in range(g.D):
        first = pl.multiple_of(lax.rem(depth + k, g.D) * share, share)
        w_refs[k][...] = all_ref[pl.ds(first, share), :]
    w1 = w1_ref[...]
    first_term = jnp.zeros((entries, 2 * g.M), F32)
    for piece in split_high_low(left_grad * scale[:, : g.Q]):
        first_term = first_term + mm(piece, lanes_of([w1, w1]))
    turn_ref[...] = first_term
    lane = iota((1, 2 * g.M), 1)
    for k in range(g.SP):
        halves = [turn_ref[pl.ds(half * g.SP + k, g.I, stride=g.S), :] for half in range(2)]
        gl_ref[k] = jnp.where(lane < g.M, halves[0], halves[1]) * masks[k]


def right_kernel(g, d_ref, lt_ref, w2_ref, mask_ref, go_ref, rg_ref):
    masks = [mask_ref[k : k + 1, :] for k in range(g.SP)]
    scale = mask_ref[g.SP : g.SP + 1, :]
    right_grad = jnp.zeros((g.Q * g.S, g.N), F32)
    for i in range(0, g.I, 2):
        right_grad = right_grad + mm(
            lanes_of([lt_ref[i], lt_ref[i + 1]]), lanes_of([d_ref[i], d_ref[i + 1]]), NT
        )
    for t in range(g.NT):
        lanes = min(LANES, g.N - t * LANES)
        piece = right_grad[:, t * LANES : t * LANES + lanes]
        if lanes < LANES:
            piece = lanes_of([piece, jnp.zeros((g.Q * g.S, LANES - lanes), F32)])
        rg_ref[t] = piece
    deep = 2 * g.Q
    group = min(g.SP, LANES // deep)
    which = iota((group * deep, g.Q), 0)
    pick = (iota((group * deep, g.Q), 1) == which % deep // 2).astype(BF16)
    w2 = w2_ref[...]
    base = mm(pick, lanes_of([w2, w2]))
    which = iota(base.shape, 0)
    base = jnp.where(which % 2 == iota(base.shape, 1) // g.M, base, 0.0)
    weights = lanes_of([jnp.where(which // deep == k, base, 0.0) for k in range(group)]).astype(BF16)
    for k in range(0, g.SP, group):
        for t in range(g.NT):
            lanes = min(LANES, g.N - t * LANES)
            tall = rows_of(
                [rg_ref[t, pl.ds(k + m, deep, stride=g.SP), :] for m in range(group)]
            )
            tall = (tall * scale).T[:lanes]
            high, low = split_high_low(tall)
            part = mm(high, weights) + mm(low, weights)
            for m in range(group):
                go_ref[k + m, t * LANES : t * LANES + lanes, :] = (
                    part[:, m * 2 * g.M : (m + 1) * 2 * g.M] * masks[k + m]
                )


def half_sum_kernel(g, *refs):
    parts, outs, total_ref = refs[: g.D], refs[g.D : g.D + g.C], refs[-1]
    total = parts[0][...]
    for ref in parts[1:]:
        total = total + ref[...]
    total_ref[...] = total
    share = total.shape[0] // g.C
    col = lax.axis_index("col")
    for k in range(g.C):
        first = pl.multiple_of(lax.rem(col + k, g.C) * share, share)
        outs[k][...] = total_ref[pl.ds(first, share), :]


def attend_kernel(g, *refs):
    refs = list(refs)
    xall_ref, refs = refs[0], refs[1:]
    logit_refs, refs = refs[: g.C], refs[g.C :]
    gm_ref, gate_ref, p_ref, gate_weight_ref, go_ref, gl_ref = refs[:6]
    soft_ref, gs_ref, own_ref, refs = refs[6], refs[7], refs[8], refs[9:]
    send_refs, (total_ref, gg_ref) = refs[: g.R - 1], refs[g.R - 1 :]
    row, col = lax.axis_index("row"), lax.axis_index("col")
    logits = lanes_of([logit_refs[(g.C - k) % g.C][...] for k in range(g.C)])
    shifted = jnp.exp(logits - jnp.max(logits, -1, keepdims=True))
    soft = shifted / jnp.sum(shifted, -1, keepdims=True)
    soft_ref[...] = soft
    low = soft.astype(BF16)
    eye = (iota((g.N, g.N), 0) == iota((g.N, g.N), 1)).astype(BF16)
    low_t = mm(eye, low, NT).astype(BF16)
    value_weights = twice(p_ref[...])
    values = mm(xall_ref[...].reshape(g.SP * g.N, 2 * g.M), value_weights).astype(BF16)
    wide = value_weights.shape[1]
    head = iota((1, wide), 1) % (wide // 2) // (wide // 2 // g.H)
    grad_soft = jnp.zeros((g.H * g.I, g.N), F32)
    for k in range(g.SP):
        v = values[k * g.N : (k + 1) * g.N]
        crossed = mm(low, v)
        mixed = jnp.where(head == 0, crossed[: g.I], 0.0)
        for h in range(1, g.H):
            mixed = jnp.where(head == h, crossed[h * g.I : (h + 1) * g.I], mixed)
        rows = slice(k * g.I, (k + 1) * g.I)
        gg_ref[rows, :] = (gate_ref[rows, :] * mixed).astype(BF16)
        blended = gm_ref[rows, :]
        by_head = rows_of(
            [jnp.where(head == h, blended, jnp.zeros_like(blended)) for h in range(g.H)]
        )
        grad_soft = grad_soft + mm(by_head, v, NT)
        part = go_ref[k]
        for piece in split_high_low(mm(low_t, by_head)):
            part = part + mm(piece, value_weights, NT)
        total_ref[k] = part
    gs_ref[...] = grad_soft
    own = total_ref[:, pl.ds(g.place(row, col), g.I), :]
    gate_term = mm(gg_ref[...], gate_weight_ref[...], NT).reshape(g.SP, g.I, 2 * g.M)
    own_ref[...] = (own + gate_term + gl_ref[...]).reshape(g.SP * g.I, 2 * g.M)
    for x in range(1, g.R):
        block = total_ref[:, pl.ds(g.place(jnp.bitwise_xor(row, x), col), g.I), :]
        send_refs[x - 1][...] = block.reshape(g.SP * g.I, 2 * g.M).astype(BF16)


def pack_kernel(g, *refs):
    refs = list(refs)
    sums, refs = refs[: g.R - 1], refs[g.R - 1 :]
    parts, refs = refs[: g.C], refs[g.C :]
    outs, (own_ref, total_ref) = refs[: g.R - 1], refs[g.R - 1 :]
    row = lax.axis_index("row")
    total = parts[0][...]
    for ref in parts[1:]:
        total = total + ref[...]
    chunk, rows = own_ref.shape[0], g.SP * g.I
    for r in range(g.R):
        total_ref[r] = total[r * chunk : (r + 1) * chunk]
    own_ref[...] = total_ref[row]
    for x in range(1, g.R):
        out = outs[x - 1]
        out[:rows, :] = sums[x - 1][...]
        high, low = split_high_low(total_ref[jnp.bitwise_xor(row, x)])
        out[rows : rows + chunk, :] = high
        out[rows + chunk :, :] = low


def chunk_kernel(g, own_ref, *refs):
    matrix, (chunk, _) = own_ref[...], own_ref.shape
    for ref in refs[:-1]:
        first = g.SP * g.I
        matrix = matrix + ref[first : first + chunk, :].astype(F32)
        matrix = matrix + ref[first + chunk :, :].astype(F32)
    refs[-1][...] = matrix.astype(BF16)


def reduce_kernel(g, x_ref, own_ref, *refs):
    refs = list(refs)
    got, refs = refs[: g.R - 1], refs[g.R - 1 :]
    parts, (out_ref, sum_ref, order_ref) = refs[: g.D], refs[g.D :]
    rows = g.SP * g.I
    total = own_ref[...]
    for ref in got:
        total = total + ref[:rows, :].astype(F32)
    total = total.reshape(g.SP, 1, g.I, 2 * g.M)
    upstream = jnp.concatenate([total[..., : g.M], total[..., g.M :]], axis=1)
    upstream = upstream.reshape(g.S, g.I, g.M)[: g.SQ]
    msa = g.fill(standardize_backward(x_ref[...].astype(F32), upstream))
    msa = msa.reshape(g.SP, 2, g.I, g.M)
    msa = jnp.concatenate([msa[:, 0], msa[:, 1]], axis=-1).astype(BF16)
    out_ref[:rows, :] = msa.reshape(rows, 2 * g.M)
    depth = lax.axis_index("depth")
    for k in range(g.D):
        order_ref[lax.rem(depth - k + g.D, g.D)] = parts[k][...]
    grad_soft = order_ref[0]
    for k in range(1, g.D):
        grad_soft = grad_soft + order_ref[k]
    sum_ref[...] = grad_soft
    heads = g.H * g.I
    for k, block in enumerate(three_blocks(grad_soft)):
        out_ref[rows + k * heads : rows + (k + 1) * heads, :] = block


def ensemble_kernel(g, own_ref, *refs):
    got, msa_ref = refs[:-1], refs[-1]
    col = lax.axis_index("col")
    rows = g.SP * g.I
    for k, ref in enumerate((own_ref, *got)):
        msa = ref[:rows, :].astype(F32).reshape(g.SP, 1, g.I, 2 * g.M)
        msa = jnp.concatenate([msa[..., : g.M], msa[..., g.M :]], axis=1)
        msa = msa.reshape(g.S, g.I, g.M)[: g.SQ].astype(BF16)
        msa_ref[pl.ds(lax.rem(col - k + g.C, g.C) * g.SQ, g.SQ)] = msa


def pair_kernel(g, e_ref, wl_ref, soft_ref, own_ref, *refs):
    got, pair_ref = refs[: g.C - 1], refs[g.C - 1]
    rows, heads = g.SP * g.I, g.H * g.I
    grad_soft = own_ref[...]
    for k in range(1, g.C):
        blocks = [
            got[k - 1][rows + m * heads : rows + (m + 1) * heads, :]
            for m in range(-(-3 * g.N // LANES))
        ]
        turn = k * g.JC
        part = join_three(lanes_of(blocks), g.N)
        grad_soft = grad_soft + lanes_of([part[:, turn:], part[:, :turn]])
    soft = soft_ref[...]
    grad = soft * (grad_soft - jnp.sum(soft * grad_soft, -1, keepdims=True))
    grad = grad[:, : g.JC]
    if g.JC < LANES:
        grad = lanes_of([grad, jnp.zeros((heads, LANES - g.JC), F32)])
    high, low = split_high_low(grad.T[: g.JC])
    grads = lanes_of([high, low])
    pick = (iota((heads, g.H), 0) // g.I == iota((heads, g.H), 1)).astype(BF16)
    base = mm(pick, wl_ref[...]).astype(BF16)
    token = iota((heads, 1), 0) % g.I
    for i in range(0, g.I, 2):
        weights = lanes_of(
            [jnp.where(token == i + k, base, jnp.zeros_like(base)) for k in range(2)]
        )
        upstream = mm(grads, rows_of([weights, weights]))
        for k in range(2):
            pair_ref[i + k] = standardize_backward(
                e_ref[i + k].astype(F32), upstream[:, k * g.Z : (k + 1) * g.Z]
            ).astype(BF16)


def join_kernel(g, *refs):
    out_ref, first = refs[-1], 0
    for ref in refs[:-1]:
        out_ref[first : first + ref.shape[0]] = ref[...]
        first += ref.shape[0]


def across_kernel(g, *refs):
    out_ref = refs[-1]
    row, col = lax.axis_index("row"), lax.axis_index("col")
    for k, ref in enumerate(refs[:-1]):
        for r in range(g.R):
            out_ref[lax.rem(col - k + g.C, g.C), r] = ref[jnp.bitwise_xor(row, r)]


def matrix_kernel(g, *refs):
    parts, out_ref = refs[: g.D], refs[g.D]
    depth = lax.axis_index("depth")
    for k in range(g.D):
        out_ref[lax.rem(depth - k + g.D, g.D)] = parts[k][...].astype(F32)


class Sizes:
    def __init__(self, x, e, wl, w1):
        self.R, self.C, self.D = (lax.axis_size(a) for a in ("row", "col", "depth"))
        self.I, self.M = x.shape[1:]
        self.JC, self.Z = e.shape[1:]
        self.H, self.Q = wl.shape[1], w1.shape[1]
        self.SQ = x.shape[0] // self.C
        self.S = -(-self.SQ // 16) * 16
        self.SP, self.N = self.S // 2, self.R * self.I
        self.F = self.R // self.C
        self.NT = -(-self.N // LANES)
        self.carried = 0

    def fill(self, rows):
        if self.SQ == self.S:
            return rows
        return rows_of([rows, jnp.zeros((self.S - self.SQ, *rows.shape[1:]), rows.dtype)])

    def place(self, row, col):
        turn = lax.rem(row // self.F - col + self.C, self.C)
        return pl.multiple_of((turn * self.F + lax.rem(row, self.F)) * self.I, self.I)


def shift(array, axis, k):
    count = lax.axis_size(axis)
    return lax.ppermute(array, axis, [(i, (i + k) % count) for i in range(count)])


def swap(array, axis, x):
    return lax.ppermute(array, axis, [(i, i ^ x) for i in range(lax.axis_size(axis))])


def shifted_all(array, axis):
    return [array] + [shift(array, axis, k) for k in range(1, lax.axis_size(axis))]


def per_device(
    homolog_ensemble,
    duplex_embedding,
    homolog_present_flags,
    resolved_position_flags,
    payload_weights,
    sigmoid_weights,
    averager_final_weights,
    first_operand_weights,
    second_operand_weights,
    duplex_logit_weights,
    tensor_product_weights,
    averager_upstream_adjoint,
    duplex_upstream_adjoint,
):
    g = Sizes(homolog_ensemble, duplex_embedding, duplex_logit_weights, first_operand_weights)
    shape = jax.ShapeDtypeStruct

    def call(kernel, name, args, outs, scratch=(), far=None, after=(), distant=False, us=1.0):
        size = sum(a.size * a.dtype.itemsize for a in args) + sum(
            math.prod(o.shape) * jnp.dtype(o.dtype).itemsize for o in outs
        )
        single = len(outs) == 1
        near = len(args) if far is None else far
        args = list(args[:near]) + [
            pltpu.with_memory_space_constraint(a, pltpu.HBM) for a in args[near:]
        ]

        if distant:
            after = [pltpu.with_memory_space_constraint(a, pltpu.HBM) for a in after]

        def body(*refs):
            kernel(g, *refs[: len(args)], *refs[len(args) + len(after) :])

        return pl.pallas_call(
            body,
            out_shape=outs[0] if single else tuple(outs),
            in_specs=[VMEM] * near + [FAR] * (len(args) - near) + [FAR if distant else VMEM] * len(after),
            out_specs=VMEM if single else (VMEM,) * len(outs),
            scratch_shapes=list(scratch),
            compiler_params=pltpu.CompilerParams(vmem_limit_bytes=40 * 1024 * 1024),
            cost_estimate=pl.CostEstimate(
                flops=int(us * 1.15e9), bytes_accessed=size, transcendentals=0
            ),
            name=name,
        )(*args, *after)

    heads = g.H * g.I
    rows = g.SP * g.I
    values = 2 * payload_weights.shape[1]
    xn, x = call(
        ensemble_norm_kernel,
        "ensemble_norm",
        (homolog_ensemble,),
        [pltpu.VMEM((g.SP, g.I, 2 * g.M), BF16), pltpu.VMEM((g.SQ, g.I, g.M), BF16)],
        [pltpu.SemaphoreType.DMA],
        far=0,
    )
    everyone = [xn] + [swap(xn, "row", k) for k in range(1, g.R)]
    cotangents = shifted_all(duplex_upstream_adjoint, "col")
    later = (
        duplex_embedding,
        duplex_logit_weights.T,
        sigmoid_weights,
        averager_final_weights.T,
        first_operand_weights.T,
        tensor_product_weights,
        payload_weights,
        second_operand_weights.T,
        duplex_upstream_adjoint,
    )
    g.carried = len(later)
    prepared = call(
        prepare_kernel,
        "prepare",
        (
            xn,
            resolved_position_flags.reshape(1, g.JC),
            homolog_present_flags,
            averager_upstream_adjoint,
            *later,
        ),
        [
            pltpu.VMEM((heads, g.JC), F32),
            pltpu.VMEM((g.SP + 8, 2 * g.M), F32),
            pltpu.VMEM((2 * g.M, values), BF16),
            pltpu.VMEM((rows, values), BF16),
            pltpu.VMEM((rows, values), F32),
            pltpu.VMEM((g.I * g.S, g.Q), BF16),
            pltpu.VMEM((g.Q, g.Q, g.Z), BF16),
            pltpu.VMEM((g.I, g.Q * g.S, g.Z), BF16),
        ]
        + [pltpu.VMEM(a.shape, a.dtype) for a in later],
        [
            pltpu.VMEM((1, g.JC), jnp.int32),
            pltpu.SMEM(homolog_present_flags.shape, jnp.int32),
            pltpu.VMEM((g.SQ, g.I, g.M), BF16),
            pltpu.VMEM((g.I * g.H, LANES), F32),
            pltpu.VMEM(tensor_product_weights.shape, F32),
            pltpu.VMEM((2, rows, LANES), F32),
            pltpu.SemaphoreType.DMA((3,)),
            pltpu.SemaphoreType.DMA((len(later),)),
        ],
        far=1,
        us=3.0,
    )
    logits, masks, gate_weights, blended, gate_factor, left, weights, left_weights = prepared[:8]
    e, wl, _, _, w1, _, p, w2, cotangents[0] = prepared[8:]
    logits = shifted_all(logits, "col")
    share = g.Q * g.Q // g.D
    xall, cotangents, *matrix_parts, first_term = call(
        outer_kernel,
        "outer",
        (*everyone, *cotangents, left, weights, w1, w2, masks),
        [pltpu.VMEM((g.SP, g.N, 2 * g.M), BF16), pltpu.VMEM((g.I, g.N, g.Z), BF16)]
        + [pltpu.VMEM((share, g.Z), F32)] * g.D
        + [pltpu.VMEM((g.SP, g.I, 2 * g.M), F32)],
        [
            pltpu.VMEM((g.NT, g.SP * 2 * g.Q, LANES), F32),
            pltpu.VMEM((g.Q * g.S, g.N), BF16),
            pltpu.VMEM((g.Q, g.I, g.S, g.Z), BF16),
            pltpu.VMEM((g.Q * g.Q, g.Z), F32),
            pltpu.VMEM((g.I * g.S, 2 * g.M), F32),
        ],
        after=logits[1:],
        us=3.0,
    )
    matrix_parts = [matrix_parts[0]] + [
        shift(a, "depth", k + 1) for k, a in enumerate(matrix_parts[1:])
    ]
    second_term = call(
        right_kernel,
        "right",
        (cotangents, left_weights, w2, masks),
        [pltpu.VMEM((g.SP, g.N, 2 * g.M), F32)],
        [pltpu.VMEM((g.NT, g.Q * g.S, LANES), F32)],
    )
    share //= g.C
    matrix_parts = call(
        half_sum_kernel,
        "half_sum",
        matrix_parts,
        [pltpu.VMEM((share, g.Z), F32)] * g.C,
        [pltpu.VMEM((share * g.C, g.Z), F32)],
        after=(second_term,),
        us=0.2,
    )
    matrix_parts = [matrix_parts[0]] + [
        shift(a, "col", k + 1) for k, a in enumerate(matrix_parts[1:])
    ]
    soft, grad_soft, own, *sums = call(
        attend_kernel,
        "attend",
        (xall, *logits, blended, gate_factor, p, gate_weights, second_term, first_term),
        [
            pltpu.VMEM((heads, g.N), F32),
            pltpu.VMEM((heads, g.N), F32),
            pltpu.VMEM((rows, 2 * g.M), F32),
        ]
        + [pltpu.VMEM((rows, 2 * g.M), BF16)] * (g.R - 1),
        [pltpu.VMEM((g.SP, g.N, 2 * g.M), F32), pltpu.VMEM((rows, values), BF16)],
        us=3.0,
    )
    grad_softs = shifted_all(grad_soft, "depth")
    chunk = share // g.R
    *sums, own_chunk = call(
        pack_kernel,
        "pack",
        (*sums, *matrix_parts),
        [pltpu.VMEM((rows + 2 * chunk, 2 * g.M), BF16)] * (g.R - 1)
        + [pltpu.VMEM((chunk, g.Z), F32)],
        [pltpu.VMEM((g.R, chunk, g.Z), F32)],
        us=0.2,
    )
    sums = [swap(a, "row", k + 1) for k, a in enumerate(sums)]
    own_chunk = call(
        chunk_kernel, "chunk", (own_chunk, *sums), [pltpu.VMEM((chunk, g.Z), BF16)], us=0.1
    )
    blocks = -(-3 * g.N // LANES)
    own, grad_soft = call(
        reduce_kernel,
        "reduce",
        (x, own, *sums, *grad_softs),
        [
            pltpu.VMEM((rows + blocks * heads, 2 * g.M), BF16),
            pltpu.VMEM((heads, g.N), F32),
        ],
        [pltpu.VMEM((g.D, heads, g.N), F32)],
        after=(own_chunk,),
    )
    arrived = [shift(own, "col", k) for k in range(1, g.C)]

    def finish_ensemble(matrix):
        return call(
            ensemble_kernel,
            "ensemble",
            (own, *arrived),
            [shape(homolog_ensemble.shape, BF16)],
            after=(matrix,),
        )

    matrix, ensemble_derivative, step = own_chunk.reshape(1, chunk, g.Z), None, 1
    while step < g.R:
        last = 2 * step >= g.R and ensemble_derivative is not None
        matrix = call(
            join_kernel,
            "join",
            (matrix, swap(matrix, "row", step)),
            [pltpu.VMEM((2 * step, chunk, g.Z), BF16)],
            after=(ensemble_derivative,) if last else (),
            distant=last,
            us=0.1,
        )
        step *= 2
        if 2 * step >= g.R and ensemble_derivative is None:
            ensemble_derivative = finish_ensemble(matrix)
    if ensemble_derivative is None:
        ensemble_derivative = finish_ensemble(matrix)
    pairwise_gradient = call(
        pair_kernel,
        "pair",
        (e, wl, soft, grad_soft, *arrived),
        [shape(duplex_embedding.shape, BF16)],
        after=(matrix,),
        us=1.5,
    )
    matrices = shifted_all(matrix, "col")
    matrix = call(
        across_kernel,
        "across",
        matrices,
        [pltpu.VMEM((g.C, g.R, chunk, g.Z), BF16)],
        after=(pairwise_gradient,),
        distant=True,
        us=0.1,
    ).reshape(g.C * share, g.Z)
    outer_matrix_gradient = call(
        matrix_kernel,
        "matrix",
        shifted_all(matrix, "depth"),
        [shape((g.D, g.C * share, g.Z), F32)],
    ).reshape(tensor_product_weights.shape)
    return (ensemble_derivative, pairwise_gradient, outer_matrix_gradient)


def solution(mesh):
    in_specs = (
        P(("parts", "depth"), "row", None),
        P(("parts", "row"), "col", None),
        P("parts"),
        P(("parts", "col")),
        P(),
        P(),
        P(),
        P(),
        P(),
        P(),
        P(),
        P(("parts", "depth"), "row", None),
        P(("parts", "row"), "col", None),
    )
    out_specs = (
        P(("parts", "depth"), "row", None),
        P(("parts", "row"), "col", None),
        P("parts", None),
    )
    return jax.shard_map(
        per_device, mesh=mesh, in_specs=in_specs, out_specs=out_specs, check_vma=False
    )
```

```python
import functools
import math

import jax
import jax.numpy as jnp
from jax import lax
from jax.experimental import pallas as pl
from jax.experimental.pallas import tpu as pltpu
from jax.sharding import PartitionSpec as P

EPS = 1e-05
PENALTY = 10000.0
F32 = jnp.float32
BF16 = jnp.bfloat16
LANES = 128
NN = (((1,), (0,)), ((), ()))
NT = (((1,), (1,)), ((), ()))
VMEM = pl.BlockSpec(memory_space=pltpu.VMEM)
FAR = pl.BlockSpec(memory_space=pl.ANY)


def mm(a, b, dims=NN):
    return lax.dot_general(a, b, dims, preferred_element_type=F32)


def split_high_low(value):
    high = value.astype(BF16)
    return high, (value - high.astype(F32)).astype(BF16)


def iota(shape, dim):
    return lax.broadcasted_iota(jnp.int32, shape, dim)


def lanes_of(pieces):
    return pieces[0] if len(pieces) == 1 else jnp.concatenate(pieces, axis=-1)


def rows_of(pieces):
    return pieces[0] if len(pieces) == 1 else jnp.concatenate(pieces, axis=0)


def standardize(values):
    centred = values - jnp.mean(values, -1, keepdims=True)
    inverse = lax.rsqrt(jnp.mean(centred * centred, -1, keepdims=True) + EPS)
    return centred * inverse, inverse


def standardize_backward(values, upstream):
    scaled, inverse = standardize(values)
    mean_grad = jnp.mean(upstream, -1, keepdims=True)
    mean_cross = jnp.mean(upstream * scaled, -1, keepdims=True)
    return (upstream - mean_grad - scaled * mean_cross) * inverse


def on_diagonal(block, width):
    rows, lanes = block.shape
    same = iota(block.shape, 0) // (rows // 2) == iota(block.shape, 1) // width
    return jnp.where(same, block, jnp.zeros_like(block))


def split_three(value):
    high = value.astype(BF16)
    rest = value - high.astype(F32)
    middle = rest.astype(BF16)
    return [high, middle, (rest - middle.astype(F32)).astype(BF16)]


def three_lanes(value):
    rows, width = value.shape
    fill = -(3 * width) % LANES
    return lanes_of(split_three(value) + [jnp.zeros((rows, fill), BF16)] * (fill > 0))


def join_three(parts, width):
    wide = parts.astype(F32)
    return (wide[:, :width] + wide[:, width : 2 * width]) + wide[:, 2 * width : 3 * width]


def twice(weights):
    zero = jnp.zeros_like(weights)
    return rows_of([lanes_of([weights, zero]), lanes_of([zero, weights])])


def ensemble_norm_kernel(g, x_hbm, xn_ref, x_ref, sem):
    first = lax.axis_index("col") * g.SQ
    copy = pltpu.make_async_copy(x_hbm.at[pl.ds(first, g.SQ)], x_ref, sem)
    copy.start()
    copy.wait()
    normed = g.fill(standardize(x_ref[...].astype(F32))[0]).reshape(g.SP, 2, g.I, g.M)
    xn_ref[...] = jnp.concatenate([normed[:, 0], normed[:, 1]], axis=-1).astype(BF16)


def prepare_kernel(g, xn_ref, flag_ref, live_ref, u_ref, *refs):
    refs = list(refs)
    count = g.carried
    sources, refs = refs[:count], refs[count:]
    logit_ref, mask_ref, gate_weight_ref, gm_ref, gate_ref, left_ref, ts_ref, lt_ref = refs[:8]
    refs = refs[8:]
    targets, refs = refs[:count], refs[count:]
    flag_in, live_in, u_in, rows_ref, wide_ref, half_ref, first_sem, later_sem = refs
    col, depth = lax.axis_index("col"), lax.axis_index("depth")
    firsts = [
        pltpu.make_async_copy(flag_ref, flag_in, first_sem.at[0]),
        pltpu.make_async_copy(live_ref, live_in, first_sem.at[1]),
        pltpu.make_async_copy(u_ref.at[pl.ds(col * g.SQ, g.SQ)], u_in, first_sem.at[2]),
    ]
    copies = [
        pltpu.make_async_copy(a, b, later_sem.at[k])
        for k, (a, b) in enumerate(zip(sources, targets, strict=True))
    ]
    for copy in copies[:2] + firsts + copies[2:]:
        copy.start()
    e_ref, wl_ref, sg_ref, wf_ref, w1_ref, t_ref = targets[:6]
    for copy in copies[:2] + firsts[:2]:
        copy.wait()
    pair = standardize(e_ref[...].astype(F32).reshape(g.I * g.JC, g.Z))[0].astype(BF16)
    penalty = (flag_in[...].astype(F32) - 1.0) * PENALTY
    weights = wl_ref[...]
    for i in range(g.I):
        rows_ref[i * g.H : (i + 1) * g.H, : g.JC] = (
            mm(weights, pair[i * g.JC : (i + 1) * g.JC], NT) + penalty
        )
    logits = rows_of([rows_ref[pl.ds(h, g.I, stride=g.H), :][:, : g.JC] for h in range(g.H)])
    tall = g.H * g.I // g.G
    logit_ref[...] = lanes_of([logits[k * tall : (k + 1) * tall] for k in range(g.G)])
    first = depth * g.C * g.SQ + col * g.SQ
    lane = iota((1, 2 * g.M), 1)
    masks = []
    for k in range(g.SP):
        if 2 * k + 1 < g.SQ:
            flags = jnp.where(lane < g.M, live_in[first + 2 * k], live_in[first + 2 * k + 1])
            masks.append(flags.astype(F32))
        else:
            masks.append(jnp.zeros((1, 2 * g.M), F32))
        mask_ref[k : k + 1, :] = masks[-1]
    total = live_in[0]
    for s in range(1, live_in.shape[0]):
        total = total + live_in[s]
    mask_ref[g.SP : g.SP + 1, :] = 1.0 / (0.001 + jnp.full((1, 2 * g.M), total, jnp.int32).astype(F32))
    for copy in firsts[2:] + copies[2:]:
        copy.wait()
    rows = g.SP * g.I
    xn = xn_ref[...]
    gate_weights = twice(sg_ref[...])
    gate_weight_ref[...] = gate_weights
    gates = jax.nn.sigmoid(mm(xn.reshape(rows, 2 * g.M), gate_weights))
    u = g.fill(u_in[...]).reshape(g.SP, 2, g.I, g.M)
    packed_u = jnp.concatenate([u[:, 0], u[:, 1]], axis=-1).reshape(rows, 2 * g.M)
    gated = mm(packed_u, twice(wf_ref[...]))
    blended = gated * gates
    gm_ref[...] = blended.astype(BF16)
    gate_ref[...] = blended * (1.0 - gates)
    live_xn = rows_of([(xn[k].astype(F32) * masks[k]).astype(BF16) for k in range(g.SP)])
    w1 = rows_of([w1_ref[...], jnp.zeros((LANES - g.Q, g.M), BF16)])
    zero = jnp.zeros_like(w1)
    half_ref[0] = mm(live_xn, lanes_of([w1, zero]), NT)
    half_ref[1] = mm(live_xn, lanes_of([zero, w1]), NT)
    for i in range(g.I):
        halves = [half_ref[half, pl.ds(i, g.SP, stride=g.I), :] for half in range(2)]
        left_ref[i * g.S : (i + 1) * g.S, :] = rows_of(halves)[:, : g.Q].astype(BF16)
    wide_ref[...] = t_ref[...].astype(F32)
    for q in range(g.Q):
        ts_ref[q] = wide_ref[pl.ds(q, g.Q, stride=g.Q), :].astype(BF16)
    left = left_ref[...]
    for q in range(0, g.Q, 2):
        product = mm(left, lanes_of([ts_ref[q], ts_ref[q + 1]]))
        for k in range(2):
            block = product[:, k * g.Z : (k + 1) * g.Z].reshape(g.I, g.S, g.Z)
            lt_ref[:, (q + k) * g.S : (q + k + 1) * g.S, :] = block.astype(BF16)


def outer_kernel(g, *refs):
    refs = list(refs)
    x_refs, refs = refs[: g.R], refs[g.R :]
    d_refs, refs = refs[: g.C], refs[g.C :]
    left_ref, ts_ref, w1_ref, w2_ref, mask_ref = refs[:5]
    refs = refs[5:]
    xall_ref, d_ref, refs = refs[0], refs[1], refs[2:]
    w_refs, (gl_ref, spread_ref, rt_ref, ds_ref, all_ref, turn_ref) = refs[: g.D], refs[g.D :]
    row, col, depth = (lax.axis_index(a) for a in ("row", "col", "depth"))
    masks = [mask_ref[k : k + 1, :] for k in range(g.SP)]
    scale = mask_ref[g.SP : g.SP + 1, :]
    for x in range(g.R):
        xall_ref[:, pl.ds(g.place(jnp.bitwise_xor(row, x), col), g.I), :] = x_refs[x][...]
    for k in range(g.C):
        spot = (g.C - k) % g.C
        d_ref[:, spot * g.JC : (spot + 1) * g.JC, :] = d_refs[k][...]
    w2 = w2_ref[...]
    doubled = lanes_of([w2, w2])
    second = on_diagonal(rows_of([doubled, doubled]), g.M)
    for k in range(g.SP):
        live_x = (xall_ref[k].astype(F32) * masks[k]).astype(BF16)
        part = mm(second, live_x, NT)
        for t in range(g.NT):
            lanes = min(LANES, g.N - t * LANES)
            spread_ref[t, k * 2 * g.Q : (k + 1) * 2 * g.Q, :lanes] = part[
                :, t * LANES : t * LANES + lanes
            ]
    for q in range(g.Q):
        for t in range(g.NT):
            lanes = min(LANES, g.N - t * LANES)
            halves = [
                spread_ref[t, pl.ds(half * g.Q + q, g.SP, stride=2 * g.Q), :] for half in range(2)
            ]
            rt_ref[q * g.S : (q + 1) * g.S, t * LANES : t * LANES + lanes] = rows_of(halves)[
                :, :lanes
            ].astype(BF16)
    rt = rt_ref[...]
    for i in range(0, g.I, 2):
        product = mm(rt, lanes_of([d_ref[i], d_ref[i + 1]]))
        for k in range(2):
            block = product[:, k * g.Z : (k + 1) * g.Z]
            ds_ref[:, i + k] = block.reshape(g.Q, g.S, g.Z).astype(BF16)
    left = left_ref[...]
    eye = (iota((g.Q, g.Q), 0) == iota((g.Q, g.Q), 1)).astype(BF16)
    left_t = mm(eye, left, NT).astype(BF16)
    entries = g.S * g.I
    left_grad = jnp.zeros((entries, g.Q), F32)
    for q in range(0, g.Q, 2):
        both = lanes_of([ds_ref[q].reshape(entries, g.Z), ds_ref[q + 1].reshape(entries, g.Z)])
        part = mm(left_t, both)
        all_ref[pl.ds(q, g.Q, stride=g.Q), :] = part[:, : g.Z] * scale
        all_ref[pl.ds(q + 1, g.Q, stride=g.Q), :] = part[:, g.Z :] * scale
        left_grad = left_grad + mm(both, lanes_of([ts_ref[q], ts_ref[q + 1]]), NT)
    share = g.Q * g.Q // g.D
    for k in range(g.D):
        first = pl.multiple_of(lax.rem(depth + k, g.D) * share, share)
        w_refs[k][...] = all_ref[pl.ds(first, share), :]
    w1 = w1_ref[...]
    first_term = jnp.zeros((entries, 2 * g.M), F32)
    for piece in split_high_low(left_grad * scale[:, : g.Q]):
        first_term = first_term + mm(piece, lanes_of([w1, w1]))
    turn_ref[...] = first_term
    lane = iota((1, 2 * g.M), 1)
    for k in range(g.SP):
        halves = [turn_ref[pl.ds(half * g.SP + k, g.I, stride=g.S), :] for half in range(2)]
        gl_ref[k] = jnp.where(lane < g.M, halves[0], halves[1]) * masks[k]


def right_kernel(g, d_ref, lt_ref, w2_ref, mask_ref, go_ref, rg_ref):
    masks = [mask_ref[k : k + 1, :] for k in range(g.SP)]
    scale = mask_ref[g.SP : g.SP + 1, :]
    right_grad = jnp.zeros((g.Q * g.S, g.N), F32)
    for i in range(0, g.I, 2):
        right_grad = right_grad + mm(
            lanes_of([lt_ref[i], lt_ref[i + 1]]), lanes_of([d_ref[i], d_ref[i + 1]]), NT
        )
    for t in range(g.NT):
        lanes = min(LANES, g.N - t * LANES)
        piece = right_grad[:, t * LANES : t * LANES + lanes]
        if lanes < LANES:
            piece = lanes_of([piece, jnp.zeros((g.Q * g.S, LANES - lanes), F32)])
        rg_ref[t] = piece
    deep = 2 * g.Q
    group = min(g.SP, LANES // deep)
    which = iota((group * deep, g.Q), 0)
    pick = (iota((group * deep, g.Q), 1) == which % deep // 2).astype(BF16)
    w2 = w2_ref[...]
    base = mm(pick, lanes_of([w2, w2]))
    which = iota(base.shape, 0)
    base = jnp.where(which % 2 == iota(base.shape, 1) // g.M, base, 0.0)
    weights = lanes_of([jnp.where(which // deep == k, base, 0.0) for k in range(group)]).astype(BF16)
    for k in range(0, g.SP, group):
        for t in range(g.NT):
            lanes = min(LANES, g.N - t * LANES)
            tall = rows_of(
                [rg_ref[t, pl.ds(k + m, deep, stride=g.SP), :] for m in range(group)]
            )
            tall = (tall * scale).T[:lanes]
            high, low = split_high_low(tall)
            part = mm(high, weights) + mm(low, weights)
            for m in range(group):
                go_ref[k + m, t * LANES : t * LANES + lanes, :] = (
                    part[:, m * 2 * g.M : (m + 1) * 2 * g.M] * masks[k + m]
                )


def half_sum_kernel(g, *refs):
    parts, outs, total_ref = refs[: g.D], refs[g.D : g.D + g.C], refs[-1]
    total = parts[0][...]
    for ref in parts[1:]:
        total = total + ref[...]
    total_ref[...] = total
    share = total.shape[0] // g.C
    col = lax.axis_index("col")
    for k in range(g.C):
        first = pl.multiple_of(lax.rem(col + k, g.C) * share, share)
        outs[k][...] = total_ref[pl.ds(first, share), :].astype(outs[k].dtype)


def attend_kernel(g, *refs):
    refs = list(refs)
    xall_ref, refs = refs[0], refs[1:]
    logit_refs, refs = refs[: g.C], refs[g.C :]
    gm_ref, gate_ref, p_ref, gate_weight_ref, go_ref, gl_ref = refs[:6]
    soft_ref, gs_ref, own_ref, refs = refs[6], refs[7], refs[8], refs[9:]
    send_refs, (total_ref, gg_ref) = refs[: g.R - 1], refs[g.R - 1 :]
    row, col = lax.axis_index("row"), lax.axis_index("col")
    blocks = [logit_refs[(g.C - k) % g.C][...] for k in range(g.C)]
    logits = lanes_of(
        [rows_of([b[:, k * g.JC : (k + 1) * g.JC] for k in range(g.G)]) for b in blocks]
    )
    shifted = jnp.exp(logits - jnp.max(logits, -1, keepdims=True))
    soft = shifted / jnp.sum(shifted, -1, keepdims=True)
    soft_ref[...] = soft
    low = soft.astype(BF16)
    eye = (iota((g.N, g.N), 0) == iota((g.N, g.N), 1)).astype(BF16)
    low_t = mm(eye, low, NT).astype(BF16)
    value_weights = twice(p_ref[...])
    values = mm(xall_ref[...].reshape(g.SP * g.N, 2 * g.M), value_weights).astype(BF16)
    wide = value_weights.shape[1]
    head = iota((1, wide), 1) % (wide // 2) // (wide // 2 // g.H)
    grad_soft = jnp.zeros((g.H * g.I, g.N), F32)
    for k in range(g.SP):
        v = values[k * g.N : (k + 1) * g.N]
        crossed = mm(low, v)
        mixed = jnp.where(head == 0, crossed[: g.I], 0.0)
        for h in range(1, g.H):
            mixed = jnp.where(head == h, crossed[h * g.I : (h + 1) * g.I], mixed)
        rows = slice(k * g.I, (k + 1) * g.I)
        gg_ref[rows, :] = (gate_ref[rows, :] * mixed).astype(BF16)
        blended = gm_ref[rows, :]
        by_head = rows_of(
            [jnp.where(head == h, blended, jnp.zeros_like(blended)) for h in range(g.H)]
        )
        grad_soft = grad_soft + mm(by_head, v, NT)
        part = go_ref[k]
        for piece in split_high_low(mm(low_t, by_head)):
            part = part + mm(piece, value_weights, NT)
        total_ref[k] = part
    gs_ref[...] = grad_soft
    own = total_ref[:, pl.ds(g.place(row, col), g.I), :]
    gate_term = mm(gg_ref[...], gate_weight_ref[...], NT).reshape(g.SP, g.I, 2 * g.M)
    own_ref[...] = (own + gate_term + gl_ref[...]).reshape(g.SP * g.I, 2 * g.M)
    for x in range(1, g.R):
        block = total_ref[:, pl.ds(g.place(jnp.bitwise_xor(row, x), col), g.I), :]
        send_refs[x - 1][...] = block.reshape(g.SP * g.I, 2 * g.M).astype(BF16)


def pack_kernel(g, *refs):
    refs = list(refs)
    sums, refs = refs[: g.R - 1], refs[g.R - 1 :]
    parts, refs = refs[: g.C], refs[g.C :]
    outs, (own_ref, total_ref) = refs[: g.R - 1], refs[g.R - 1 :]
    row = lax.axis_index("row")
    total = parts[0][...]
    for ref in parts[1:]:
        total = total + ref[...].astype(F32)
    chunk, rows = own_ref.shape[0], g.SP * g.I
    for r in range(g.R):
        total_ref[r] = total[r * chunk : (r + 1) * chunk]
    own_ref[...] = total_ref[row]
    for x in range(1, g.R):
        out = outs[x - 1]
        out[:rows, :] = sums[x - 1][...]
        out[rows:, :] = total_ref[jnp.bitwise_xor(row, x)].astype(BF16)


def chunk_kernel(g, own_ref, *refs):
    matrix = own_ref[...]
    for ref in refs[:-1]:
        matrix = matrix + ref[g.SP * g.I :, :].astype(F32)
    refs[-1][...] = matrix.astype(BF16)


def score_kernel(g, soft_ref, *refs):
    parts, refs = refs[: g.D], refs[g.D :]
    own_ref, out_refs, order_ref = refs[0], refs[1 : g.C], refs[g.C]
    depth = lax.axis_index("depth")
    for k in range(g.D):
        order_ref[lax.rem(depth - k + g.D, g.D)] = parts[k][...]
    grad_soft = order_ref[0]
    for k in range(1, g.D):
        grad_soft = grad_soft + order_ref[k]
    inner = jnp.sum(soft_ref[...] * grad_soft, -1, keepdims=True)
    for k in range(g.C):
        block = lanes_of([grad_soft[:, k * g.JC : (k + 1) * g.JC], inner])
        if k == 0:
            own_ref[...] = block
        else:
            out_refs[k - 1][...] = three_lanes(block)


def pair_kernel(g, e_ref, wl_ref, soft_ref, own_ref, *refs):
    got, pair_ref = refs[: g.C - 1], refs[g.C - 1]
    heads = g.H * g.I
    total = own_ref[...]
    for ref in got:
        total = total + join_three(ref[...], g.JC + 1)
    grad = soft_ref[:, : g.JC] * (total[:, : g.JC] - total[:, g.JC :])
    if g.JC < LANES:
        grad = lanes_of([grad, jnp.zeros((heads, LANES - g.JC), F32)])
    high, low = split_high_low(grad.T[: g.JC])
    grads = lanes_of([high, low])
    pick = (iota((heads, g.H), 0) // g.I == iota((heads, g.H), 1)).astype(BF16)
    base = mm(pick, wl_ref[...]).astype(BF16)
    token = iota((heads, 1), 0) % g.I
    for i in range(0, g.I, 2):
        weights = lanes_of(
            [jnp.where(token == i + k, base, jnp.zeros_like(base)) for k in range(2)]
        )
        upstream = mm(grads, rows_of([weights, weights]))
        for k in range(2):
            pair_ref[i + k] = standardize_backward(
                e_ref[i + k].astype(F32), upstream[:, k * g.Z : (k + 1) * g.Z]
            ).astype(BF16)


def reduce_kernel(g, x_ref, own_ref, *refs):
    got, out_ref = refs[:-1], refs[-1]
    rows = g.SP * g.I
    total = own_ref[...]
    for ref in got:
        total = total + ref[:rows, :].astype(F32)
    total = total.reshape(g.SP, 1, g.I, 2 * g.M)
    upstream = jnp.concatenate([total[..., : g.M], total[..., g.M :]], axis=1)
    upstream = upstream.reshape(g.S, g.I, g.M)[: g.SQ]
    msa = g.fill(standardize_backward(x_ref[...].astype(F32), upstream))
    msa = msa.reshape(g.SP, 2, g.I, g.M)
    msa = jnp.concatenate([msa[:, 0], msa[:, 1]], axis=-1).astype(BF16)
    out_ref[...] = msa.reshape(rows, 2 * g.M)


def ensemble_kernel(g, own_ref, *refs):
    got, msa_ref = refs[:-1], refs[-1]
    col = lax.axis_index("col")
    for k, ref in enumerate((own_ref, *got)):
        msa = ref[...].astype(F32).reshape(g.SP, 1, g.I, 2 * g.M)
        msa = jnp.concatenate([msa[..., : g.M], msa[..., g.M :]], axis=1)
        msa = msa.reshape(g.S, g.I, g.M)[: g.SQ].astype(BF16)
        msa_ref[pl.ds(lax.rem(col - k + g.C, g.C) * g.SQ, g.SQ)] = msa


def join_kernel(g, *refs):
    out_ref, first = refs[-1], 0
    for ref in refs[:-1]:
        out_ref[first : first + ref.shape[0]] = ref[...]
        first += ref.shape[0]


def across_kernel(g, *refs):
    out_ref = refs[-1]
    row, col = lax.axis_index("row"), lax.axis_index("col")
    for k, ref in enumerate(refs[:-1]):
        for r in range(g.R):
            out_ref[lax.rem(col - k + g.C, g.C), r] = ref[jnp.bitwise_xor(row, r)]


def matrix_kernel(g, *refs):
    parts, out_ref = refs[: g.D], refs[g.D]
    depth = lax.axis_index("depth")
    for k in range(g.D):
        out_ref[lax.rem(depth - k + g.D, g.D)] = parts[k][...].astype(F32)


class Sizes:
    def __init__(self, x, e, wl, w1):
        self.R, self.C, self.D = (lax.axis_size(a) for a in ("row", "col", "depth"))
        self.I, self.M = x.shape[1:]
        self.JC, self.Z = e.shape[1:]
        self.H, self.Q = wl.shape[1], w1.shape[1]
        self.SQ = x.shape[0] // self.C
        self.S = -(-self.SQ // 16) * 16
        self.SP, self.N = self.S // 2, self.R * self.I
        self.F = self.R // self.C
        self.NT = -(-self.N // LANES)
        self.G = max(1, LANES // self.JC)
        self.carried = 0

    def fill(self, rows):
        if self.SQ == self.S:
            return rows
        return rows_of([rows, jnp.zeros((self.S - self.SQ, *rows.shape[1:]), rows.dtype)])

    def place(self, row, col):
        turn = lax.rem(row // self.F - col + self.C, self.C)
        return pl.multiple_of((turn * self.F + lax.rem(row, self.F)) * self.I, self.I)


def shift(array, axis, k):
    count = lax.axis_size(axis)
    return lax.ppermute(array, axis, [(i, (i + k) % count) for i in range(count)])


def swap(array, axis, x):
    return lax.ppermute(array, axis, [(i, i ^ x) for i in range(lax.axis_size(axis))])


def shifted_all(array, axis):
    return [array] + [shift(array, axis, k) for k in range(1, lax.axis_size(axis))]


def per_device(
    homolog_ensemble,
    duplex_embedding,
    homolog_present_flags,
    resolved_position_flags,
    payload_weights,
    sigmoid_weights,
    averager_final_weights,
    first_operand_weights,
    second_operand_weights,
    duplex_logit_weights,
    tensor_product_weights,
    averager_upstream_adjoint,
    duplex_upstream_adjoint,
):
    g = Sizes(homolog_ensemble, duplex_embedding, duplex_logit_weights, first_operand_weights)
    shape = jax.ShapeDtypeStruct

    def call(kernel, name, args, outs, scratch=(), far=None, after=(), distant=False, us=1.0):
        size = sum(a.size * a.dtype.itemsize for a in args) + sum(
            math.prod(o.shape) * jnp.dtype(o.dtype).itemsize for o in outs
        )
        single = len(outs) == 1
        near = len(args) if far is None else far
        args = list(args[:near]) + [
            pltpu.with_memory_space_constraint(a, pltpu.HBM) for a in args[near:]
        ]

        if distant:
            after = [pltpu.with_memory_space_constraint(a, pltpu.HBM) for a in after]

        def body(*refs):
            kernel(g, *refs[: len(args)], *refs[len(args) + len(after) :])

        return pl.pallas_call(
            body,
            out_shape=outs[0] if single else tuple(outs),
            in_specs=[VMEM] * near + [FAR] * (len(args) - near) + [FAR if distant else VMEM] * len(after),
            out_specs=VMEM if single else (VMEM,) * len(outs),
            scratch_shapes=list(scratch),
            compiler_params=pltpu.CompilerParams(vmem_limit_bytes=40 * 1024 * 1024),
            cost_estimate=pl.CostEstimate(
                flops=int(us * 1.15e9), bytes_accessed=size, transcendentals=0
            ),
            name=name,
        )(*args, *after)

    heads = g.H * g.I
    rows = g.SP * g.I
    values = 2 * payload_weights.shape[1]
    xn, x = call(
        ensemble_norm_kernel,
        "ensemble_norm",
        (homolog_ensemble,),
        [pltpu.VMEM((g.SP, g.I, 2 * g.M), BF16), pltpu.VMEM((g.SQ, g.I, g.M), BF16)],
        [pltpu.SemaphoreType.DMA],
        far=0,
    )
    everyone = [xn] + [swap(xn, "row", k) for k in range(1, g.R)]
    cotangents = shifted_all(duplex_upstream_adjoint, "col")
    later = (
        duplex_embedding,
        duplex_logit_weights.T,
        sigmoid_weights,
        averager_final_weights.T,
        first_operand_weights.T,
        tensor_product_weights,
        payload_weights,
        second_operand_weights.T,
        duplex_upstream_adjoint,
    )
    g.carried = len(later)
    prepared = call(
        prepare_kernel,
        "prepare",
        (
            xn,
            resolved_position_flags.reshape(1, g.JC),
            homolog_present_flags,
            averager_upstream_adjoint,
            *later,
        ),
        [
            pltpu.VMEM((heads // g.G, g.G * g.JC), F32),
            pltpu.VMEM((g.SP + 8, 2 * g.M), F32),
            pltpu.VMEM((2 * g.M, values), BF16),
            pltpu.VMEM((rows, values), BF16),
            pltpu.VMEM((rows, values), F32),
            pltpu.VMEM((g.I * g.S, g.Q), BF16),
            pltpu.VMEM((g.Q, g.Q, g.Z), BF16),
            pltpu.VMEM((g.I, g.Q * g.S, g.Z), BF16),
        ]
        + [pltpu.VMEM(a.shape, a.dtype) for a in later],
        [
            pltpu.VMEM((1, g.JC), jnp.int32),
            pltpu.SMEM(homolog_present_flags.shape, jnp.int32),
            pltpu.VMEM((g.SQ, g.I, g.M), BF16),
            pltpu.VMEM((g.I * g.H, LANES), F32),
            pltpu.VMEM(tensor_product_weights.shape, F32),
            pltpu.VMEM((2, rows, LANES), F32),
            pltpu.SemaphoreType.DMA((3,)),
            pltpu.SemaphoreType.DMA((len(later),)),
        ],
        far=1,
        after=cotangents[1:],
        us=3.0,
    )
    logits, masks, gate_weights, blended, gate_factor, left, weights, left_weights = prepared[:8]
    e, wl, _, _, w1, _, p, w2, cotangents[0] = prepared[8:]
    logits = shifted_all(logits, "col")
    share = g.Q * g.Q // g.D
    xall, cotangents, *matrix_parts, first_term = call(
        outer_kernel,
        "outer",
        (*everyone, *cotangents, left, weights, w1, w2, masks),
        [pltpu.VMEM((g.SP, g.N, 2 * g.M), BF16), pltpu.VMEM((g.I, g.N, g.Z), BF16)]
        + [pltpu.VMEM((share, g.Z), F32)] * g.D
        + [pltpu.VMEM((g.SP, g.I, 2 * g.M), F32)],
        [
            pltpu.VMEM((g.NT, g.SP * 2 * g.Q, LANES), F32),
            pltpu.VMEM((g.Q * g.S, g.N), BF16),
            pltpu.VMEM((g.Q, g.I, g.S, g.Z), BF16),
            pltpu.VMEM((g.Q * g.Q, g.Z), F32),
            pltpu.VMEM((g.I * g.S, 2 * g.M), F32),
        ],
        after=logits[1:],
        us=3.0,
    )
    matrix_parts = [matrix_parts[0]] + [
        shift(a, "depth", k + 1) for k, a in enumerate(matrix_parts[1:])
    ]
    second_term = call(
        right_kernel,
        "right",
        (cotangents, left_weights, w2, masks),
        [pltpu.VMEM((g.SP, g.N, 2 * g.M), F32)],
        [pltpu.VMEM((g.NT, g.Q * g.S, LANES), F32)],
    )
    share //= g.C
    matrix_parts = call(
        half_sum_kernel,
        "half_sum",
        matrix_parts,
        [pltpu.VMEM((share, g.Z), F32)] + [pltpu.VMEM((share, g.Z), BF16)] * (g.C - 1),
        [pltpu.VMEM((share * g.C, g.Z), F32)],
        after=(second_term,),
        us=0.2,
    )
    matrix_parts = [matrix_parts[0]] + [
        shift(a, "col", k + 1) for k, a in enumerate(matrix_parts[1:])
    ]
    soft, grad_soft, own, *sums = call(
        attend_kernel,
        "attend",
        (xall, *logits, blended, gate_factor, p, gate_weights, second_term, first_term),
        [
            pltpu.VMEM((heads, g.N), F32),
            pltpu.VMEM((heads, g.N), F32),
            pltpu.VMEM((rows, 2 * g.M), F32),
        ]
        + [pltpu.VMEM((rows, 2 * g.M), BF16)] * (g.R - 1),
        [pltpu.VMEM((g.SP, g.N, 2 * g.M), F32), pltpu.VMEM((rows, values), BF16)],
        us=3.0,
    )
    chunk = share // g.R
    *sums, own_chunk = call(
        pack_kernel,
        "pack",
        (*sums, *matrix_parts),
        [pltpu.VMEM((rows + chunk, 2 * g.M), BF16)] * (g.R - 1)
        + [pltpu.VMEM((chunk, g.Z), F32)],
        [pltpu.VMEM((g.R, chunk, g.Z), F32)],
        us=0.2,
    )
    sums = [swap(a, "row", k + 1) for k, a in enumerate(sums)]
    wide = -(-3 * (g.JC + 1) // LANES) * LANES
    scores, *sends = call(
        score_kernel,
        "score",
        (soft, *shifted_all(grad_soft, "depth")),
        [pltpu.VMEM((heads, g.JC + 1), F32)] + [pltpu.VMEM((heads, wide), BF16)] * (g.C - 1),
        [pltpu.VMEM((g.D, heads, g.N), F32)],
        after=(own_chunk,),
        us=0.2,
    )
    arrived = [shift(a, "col", k + 1) for k, a in enumerate(sends)]
    pairwise_gradient = call(
        pair_kernel,
        "pair",
        (e, wl, soft, scores, *arrived),
        [shape(duplex_embedding.shape, BF16)],
        us=1.8,
    )
    own_chunk = call(
        chunk_kernel,
        "chunk",
        (own_chunk, *sums),
        [pltpu.VMEM((chunk, g.Z), BF16)],
        after=(pairwise_gradient,),
        distant=True,
        us=0.1,
    )

    def finish_ensemble(matrix):
        part = call(
            reduce_kernel,
            "reduce",
            (x, own, *sums),
            [pltpu.VMEM((rows, 2 * g.M), BF16)],
            after=(matrix,),
        )
        return shifted_all(part, "col")

    matrix, parts, step = own_chunk.reshape(1, chunk, g.Z), None, 1
    while step < g.R:
        matrix = call(
            join_kernel,
            "join",
            (matrix, swap(matrix, "row", step)),
            [pltpu.VMEM((2 * step, chunk, g.Z), BF16)],
            after=parts[:1] if parts and 2 * step >= g.R else (),
            us=0.1,
        )
        step *= 2
        if 2 * step >= g.R and parts is None:
            parts = finish_ensemble(matrix)
    if parts is None:
        parts = finish_ensemble(matrix)
    ensemble_derivative = call(
        ensemble_kernel,
        "ensemble",
        parts,
        [shape(homolog_ensemble.shape, BF16)],
        after=(matrix,),
    )
    matrices = shifted_all(matrix, "col")
    matrix = call(
        across_kernel,
        "across",
        matrices,
        [pltpu.VMEM((g.C, g.R, chunk, g.Z), BF16)],
        after=(ensemble_derivative,),
        distant=True,
        us=0.1,
    ).reshape(g.C * share, g.Z)
    outer_matrix_gradient = call(
        matrix_kernel,
        "matrix",
        shifted_all(matrix, "depth"),
        [shape((g.D, g.C * share, g.Z), F32)],
    ).reshape(tensor_product_weights.shape)
    return (ensemble_derivative, pairwise_gradient, outer_matrix_gradient)


def solution(mesh):
    in_specs = (
        P(("parts", "depth"), "row", None),
        P(("parts", "row"), "col", None),
        P("parts"),
        P(("parts", "col")),
        P(),
        P(),
        P(),
        P(),
        P(),
        P(),
        P(),
        P(("parts", "depth"), "row", None),
        P(("parts", "row"), "col", None),
    )
    out_specs = (
        P(("parts", "depth"), "row", None),
        P(("parts", "row"), "col", None),
        P("parts", None),
    )
    return jax.shard_map(
        per_device, mesh=mesh, in_specs=in_specs, out_specs=out_specs, check_vma=False
    )
```

```python
import functools
import math

import jax
import jax.numpy as jnp
from jax import lax
from jax.experimental import pallas as pl
from jax.experimental.pallas import tpu as pltpu
from jax.sharding import PartitionSpec as P

EPS = 1e-05
PENALTY = 10000.0
F32 = jnp.float32
BF16 = jnp.bfloat16
LANES = 128
NN = (((1,), (0,)), ((), ()))
NT = (((1,), (1,)), ((), ()))
VMEM = pl.BlockSpec(memory_space=pltpu.VMEM)
FAR = pl.BlockSpec(memory_space=pl.ANY)


def mm(a, b, dims=NN):
    return lax.dot_general(a, b, dims, preferred_element_type=F32)


def split_high_low(value):
    high = value.astype(BF16)
    return high, (value - high.astype(F32)).astype(BF16)


def iota(shape, dim):
    return lax.broadcasted_iota(jnp.int32, shape, dim)


def lanes_of(pieces):
    return pieces[0] if len(pieces) == 1 else jnp.concatenate(pieces, axis=-1)


def rows_of(pieces):
    return pieces[0] if len(pieces) == 1 else jnp.concatenate(pieces, axis=0)


def standardize(values):
    centred = values - jnp.mean(values, -1, keepdims=True)
    inverse = lax.rsqrt(jnp.mean(centred * centred, -1, keepdims=True) + EPS)
    return centred * inverse, inverse


def standardize_backward(values, upstream):
    scaled, inverse = standardize(values)
    mean_grad = jnp.mean(upstream, -1, keepdims=True)
    mean_cross = jnp.mean(upstream * scaled, -1, keepdims=True)
    return (upstream - mean_grad - scaled * mean_cross) * inverse


def on_diagonal(block, width):
    rows, lanes = block.shape
    same = iota(block.shape, 0) // (rows // 2) == iota(block.shape, 1) // width
    return jnp.where(same, block, jnp.zeros_like(block))


def split_three(value):
    high = value.astype(BF16)
    rest = value - high.astype(F32)
    middle = rest.astype(BF16)
    return [high, middle, (rest - middle.astype(F32)).astype(BF16)]


def three_lanes(value):
    rows, width = value.shape
    fill = -(3 * width) % LANES
    return lanes_of(split_three(value) + [jnp.zeros((rows, fill), BF16)] * (fill > 0))


def join_three(parts, width):
    wide = parts.astype(F32)
    return (wide[:, :width] + wide[:, width : 2 * width]) + wide[:, 2 * width : 3 * width]


def twice(weights):
    zero = jnp.zeros_like(weights)
    return rows_of([lanes_of([weights, zero]), lanes_of([zero, weights])])


def ensemble_norm_kernel(g, x_hbm, xn_ref, x_ref, sem):
    first = lax.axis_index("col") * g.SQ
    copy = pltpu.make_async_copy(x_hbm.at[pl.ds(first, g.SQ)], x_ref, sem)
    copy.start()
    copy.wait()
    normed = g.fill(standardize(x_ref[...].astype(F32))[0]).reshape(g.SP, 2, g.I, g.M)
    xn_ref[...] = jnp.concatenate([normed[:, 0], normed[:, 1]], axis=-1).astype(BF16)


def prepare_kernel(g, xn_ref, flag_ref, live_ref, u_ref, *refs):
    refs = list(refs)
    count = g.carried
    sources, refs = refs[:count], refs[count:]
    logit_ref, mask_ref, gate_weight_ref, gm_ref, gate_ref, left_ref, ts_ref, lt_ref = refs[:8]
    refs = refs[8:]
    targets, refs = refs[:count], refs[count:]
    flag_in, live_in, u_in, rows_ref, wide_ref, half_ref, first_sem, later_sem = refs
    col, depth = lax.axis_index("col"), lax.axis_index("depth")
    firsts = [
        pltpu.make_async_copy(flag_ref, flag_in, first_sem.at[0]),
        pltpu.make_async_copy(live_ref, live_in, first_sem.at[1]),
        pltpu.make_async_copy(u_ref.at[pl.ds(col * g.SQ, g.SQ)], u_in, first_sem.at[2]),
    ]
    copies = [
        pltpu.make_async_copy(a, b, later_sem.at[k])
        for k, (a, b) in enumerate(zip(sources, targets, strict=True))
    ]
    for copy in copies[:2] + firsts + copies[2:]:
        copy.start()
    e_ref, wl_ref, sg_ref, wf_ref, w1_ref, t_ref = targets[:6]
    for copy in copies[:2] + firsts[:2]:
        copy.wait()
    pair = standardize(e_ref[...].astype(F32).reshape(g.I * g.JC, g.Z))[0].astype(BF16)
    penalty = (flag_in[...].astype(F32) - 1.0) * PENALTY
    weights = wl_ref[...]
    for i in range(g.I):
        rows_ref[i * g.H : (i + 1) * g.H, : g.JC] = (
            mm(weights, pair[i * g.JC : (i + 1) * g.JC], NT) + penalty
        )
    logits = rows_of([rows_ref[pl.ds(h, g.I, stride=g.H), :][:, : g.JC] for h in range(g.H)])
    tall = g.H * g.I // g.G
    logit_ref[...] = lanes_of([logits[k * tall : (k + 1) * tall] for k in range(g.G)])
    first = depth * g.C * g.SQ + col * g.SQ
    lane = iota((1, 2 * g.M), 1)
    masks = []
    for k in range(g.SP):
        if 2 * k + 1 < g.SQ:
            flags = jnp.where(lane < g.M, live_in[first + 2 * k], live_in[first + 2 * k + 1])
            masks.append(flags.astype(F32))
        else:
            masks.append(jnp.zeros((1, 2 * g.M), F32))
        mask_ref[k : k + 1, :] = masks[-1]
    total = live_in[0]
    for s in range(1, live_in.shape[0]):
        total = total + live_in[s]
    mask_ref[g.SP : g.SP + 1, :] = 1.0 / (0.001 + jnp.full((1, 2 * g.M), total, jnp.int32).astype(F32))
    for copy in firsts[2:] + copies[2:]:
        copy.wait()
    rows = g.SP * g.I
    xn = xn_ref[...]
    gate_weights = twice(sg_ref[...])
    gate_weight_ref[...] = gate_weights
    gates = jax.nn.sigmoid(mm(xn.reshape(rows, 2 * g.M), gate_weights))
    u = g.fill(u_in[...]).reshape(g.SP, 2, g.I, g.M)
    packed_u = jnp.concatenate([u[:, 0], u[:, 1]], axis=-1).reshape(rows, 2 * g.M)
    gated = mm(packed_u, twice(wf_ref[...]))
    blended = gated * gates
    gm_ref[...] = blended.astype(BF16)
    gate_ref[...] = blended * (1.0 - gates)
    live_xn = rows_of([(xn[k].astype(F32) * masks[k]).astype(BF16) for k in range(g.SP)])
    w1 = rows_of([w1_ref[...], jnp.zeros((LANES - g.Q, g.M), BF16)])
    zero = jnp.zeros_like(w1)
    half_ref[0] = mm(live_xn, lanes_of([w1, zero]), NT)
    half_ref[1] = mm(live_xn, lanes_of([zero, w1]), NT)
    for i in range(g.I):
        halves = [half_ref[half, pl.ds(i, g.SP, stride=g.I), :] for half in range(2)]
        left_ref[i * g.S : (i + 1) * g.S, :] = rows_of(halves)[:, : g.Q].astype(BF16)
    wide_ref[...] = t_ref[...].astype(F32)
    for q in range(g.Q):
        ts_ref[q] = wide_ref[pl.ds(q, g.Q, stride=g.Q), :].astype(BF16)
    left = left_ref[...]
    for q in range(0, g.Q, 2):
        product = mm(left, lanes_of([ts_ref[q], ts_ref[q + 1]]))
        for k in range(2):
            block = product[:, k * g.Z : (k + 1) * g.Z].reshape(g.I, g.S, g.Z)
            lt_ref[:, (q + k) * g.S : (q + k + 1) * g.S, :] = block.astype(BF16)


def outer_kernel(g, *refs):
    refs = list(refs)
    x_refs, refs = refs[: g.R], refs[g.R :]
    d_refs, refs = refs[: g.C], refs[g.C :]
    left_ref, ts_ref, w1_ref, w2_ref, mask_ref = refs[:5]
    refs = refs[5:]
    xall_ref, d_ref, refs = refs[0], refs[1], refs[2:]
    w_refs, (gl_ref, spread_ref, rt_ref, ds_ref, all_ref, turn_ref) = refs[: g.D], refs[g.D :]
    row, col, depth = (lax.axis_index(a) for a in ("row", "col", "depth"))
    masks = [mask_ref[k : k + 1, :] for k in range(g.SP)]
    scale = mask_ref[g.SP : g.SP + 1, :]
    for k in range(g.R):
        place = g.place(jnp.bitwise_xor(row, (g.R - k) % g.R), col)
        xall_ref[:, pl.ds(place, g.I), :] = x_refs[k][...]
    for k in range(g.C):
        spot = (g.C - k) % g.C
        d_ref[:, spot * g.JC : (spot + 1) * g.JC, :] = d_refs[k][...]
    w2 = w2_ref[...]
    doubled = lanes_of([w2, w2])
    second = on_diagonal(rows_of([doubled, doubled]), g.M)
    for k in range(g.SP):
        live_x = (xall_ref[k].astype(F32) * masks[k]).astype(BF16)
        part = mm(second, live_x, NT)
        for t in range(g.NT):
            lanes = min(LANES, g.N - t * LANES)
            spread_ref[t, k * 2 * g.Q : (k + 1) * 2 * g.Q, :lanes] = part[
                :, t * LANES : t * LANES + lanes
            ]
    for q in range(g.Q):
        for t in range(g.NT):
            lanes = min(LANES, g.N - t * LANES)
            halves = [
                spread_ref[t, pl.ds(half * g.Q + q, g.SP, stride=2 * g.Q), :] for half in range(2)
            ]
            rt_ref[q * g.S : (q + 1) * g.S, t * LANES : t * LANES + lanes] = rows_of(halves)[
                :, :lanes
            ].astype(BF16)
    rt = rt_ref[...]
    for i in range(0, g.I, 2):
        product = mm(rt, lanes_of([d_ref[i], d_ref[i + 1]]))
        for k in range(2):
            block = product[:, k * g.Z : (k + 1) * g.Z]
            ds_ref[:, i + k] = block.reshape(g.Q, g.S, g.Z).astype(BF16)
    left = left_ref[...]
    eye = (iota((g.Q, g.Q), 0) == iota((g.Q, g.Q), 1)).astype(BF16)
    left_t = mm(eye, left, NT).astype(BF16)
    entries = g.S * g.I
    left_grad = jnp.zeros((entries, g.Q), F32)
    for q in range(0, g.Q, 2):
        both = lanes_of([ds_ref[q].reshape(entries, g.Z), ds_ref[q + 1].reshape(entries, g.Z)])
        part = mm(left_t, both)
        all_ref[pl.ds(q, g.Q, stride=g.Q), :] = part[:, : g.Z] * scale
        all_ref[pl.ds(q + 1, g.Q, stride=g.Q), :] = part[:, g.Z :] * scale
        left_grad = left_grad + mm(both, lanes_of([ts_ref[q], ts_ref[q + 1]]), NT)
    share = g.Q * g.Q // g.D
    for k in range(g.D):
        first = pl.multiple_of(lax.rem(depth + k, g.D) * share, share)
        w_refs[k][...] = all_ref[pl.ds(first, share), :]
    w1 = w1_ref[...]
    first_term = jnp.zeros((entries, 2 * g.M), F32)
    for piece in split_high_low(left_grad * scale[:, : g.Q]):
        first_term = first_term + mm(piece, lanes_of([w1, w1]))
    turn_ref[...] = first_term
    lane = iota((1, 2 * g.M), 1)
    for k in range(g.SP):
        halves = [turn_ref[pl.ds(half * g.SP + k, g.I, stride=g.S), :] for half in range(2)]
        gl_ref[k] = jnp.where(lane < g.M, halves[0], halves[1]) * masks[k]


def right_kernel(g, d_ref, lt_ref, w2_ref, mask_ref, go_ref, rg_ref):
    masks = [mask_ref[k : k + 1, :] for k in range(g.SP)]
    scale = mask_ref[g.SP : g.SP + 1, :]
    right_grad = jnp.zeros((g.Q * g.S, g.N), F32)
    for i in range(0, g.I, 2):
        right_grad = right_grad + mm(
            lanes_of([lt_ref[i], lt_ref[i + 1]]), lanes_of([d_ref[i], d_ref[i + 1]]), NT
        )
    for t in range(g.NT):
        lanes = min(LANES, g.N - t * LANES)
        piece = right_grad[:, t * LANES : t * LANES + lanes]
        if lanes < LANES:
            piece = lanes_of([piece, jnp.zeros((g.Q * g.S, LANES - lanes), F32)])
        rg_ref[t] = piece
    deep = 2 * g.Q
    group = min(g.SP, LANES // deep)
    which = iota((group * deep, g.Q), 0)
    pick = (iota((group * deep, g.Q), 1) == which % deep // 2).astype(BF16)
    w2 = w2_ref[...]
    base = mm(pick, lanes_of([w2, w2]))
    which = iota(base.shape, 0)
    base = jnp.where(which % 2 == iota(base.shape, 1) // g.M, base, 0.0)
    weights = lanes_of([jnp.where(which // deep == k, base, 0.0) for k in range(group)]).astype(BF16)
    for k in range(0, g.SP, group):
        for t in range(g.NT):
            lanes = min(LANES, g.N - t * LANES)
            tall = rows_of(
                [rg_ref[t, pl.ds(k + m, deep, stride=g.SP), :] for m in range(group)]
            )
            tall = (tall * scale).T[:lanes]
            high, low = split_high_low(tall)
            part = mm(high, weights) + mm(low, weights)
            for m in range(group):
                go_ref[k + m, t * LANES : t * LANES + lanes, :] = (
                    part[:, m * 2 * g.M : (m + 1) * 2 * g.M] * masks[k + m]
                )


def half_sum_kernel(g, *refs):
    parts, outs, total_ref = refs[: g.D], refs[g.D : g.D + g.C], refs[-1]
    total = parts[0][...]
    for ref in parts[1:]:
        total = total + ref[...]
    total_ref[...] = total
    share = total.shape[0] // g.C
    col = lax.axis_index("col")
    for k in range(g.C):
        first = pl.multiple_of(lax.rem(col + k, g.C) * share, share)
        outs[k][...] = total_ref[pl.ds(first, share), :].astype(outs[k].dtype)


def attend_kernel(g, *refs):
    refs = list(refs)
    xall_ref, refs = refs[0], refs[1:]
    logit_refs, refs = refs[: g.C], refs[g.C :]
    gm_ref, gate_ref, p_ref, gate_weight_ref, go_ref, gl_ref = refs[:6]
    soft_ref, gs_ref, own_ref, refs = refs[6], refs[7], refs[8], refs[9:]
    send_refs, (total_ref, gg_ref) = refs[: g.R - 1], refs[g.R - 1 :]
    row, col = lax.axis_index("row"), lax.axis_index("col")
    blocks = [logit_refs[(g.C - k) % g.C][...] for k in range(g.C)]
    logits = lanes_of(
        [rows_of([b[:, k * g.JC : (k + 1) * g.JC] for k in range(g.G)]) for b in blocks]
    )
    shifted = jnp.exp(logits - jnp.max(logits, -1, keepdims=True))
    soft = shifted / jnp.sum(shifted, -1, keepdims=True)
    soft_ref[...] = soft
    low = soft.astype(BF16)
    eye = (iota((g.N, g.N), 0) == iota((g.N, g.N), 1)).astype(BF16)
    low_t = mm(eye, low, NT).astype(BF16)
    value_weights = twice(p_ref[...])
    values = mm(xall_ref[...].reshape(g.SP * g.N, 2 * g.M), value_weights).astype(BF16)
    wide = value_weights.shape[1]
    head = iota((1, wide), 1) % (wide // 2) // (wide // 2 // g.H)
    grad_soft = jnp.zeros((g.H * g.I, g.N), F32)
    for k in range(g.SP):
        v = values[k * g.N : (k + 1) * g.N]
        crossed = mm(low, v)
        mixed = jnp.where(head == 0, crossed[: g.I], 0.0)
        for h in range(1, g.H):
            mixed = jnp.where(head == h, crossed[h * g.I : (h + 1) * g.I], mixed)
        rows = slice(k * g.I, (k + 1) * g.I)
        gg_ref[rows, :] = (gate_ref[rows, :] * mixed).astype(BF16)
        blended = gm_ref[rows, :]
        by_head = rows_of(
            [jnp.where(head == h, blended, jnp.zeros_like(blended)) for h in range(g.H)]
        )
        grad_soft = grad_soft + mm(by_head, v, NT)
        part = go_ref[k]
        for piece in split_high_low(mm(low_t, by_head)):
            part = part + mm(piece, value_weights, NT)
        total_ref[k] = part
    gs_ref[...] = grad_soft
    own = total_ref[:, pl.ds(g.place(row, col), g.I), :]
    gate_term = mm(gg_ref[...], gate_weight_ref[...], NT).reshape(g.SP, g.I, 2 * g.M)
    own_ref[...] = (own + gate_term + gl_ref[...]).reshape(g.SP * g.I, 2 * g.M)
    for x in range(1, g.R):
        block = total_ref[:, pl.ds(g.place(jnp.bitwise_xor(row, x), col), g.I), :]
        send_refs[x - 1][...] = block.reshape(g.SP * g.I, 2 * g.M).astype(BF16)


def pack_kernel(g, *refs):
    refs = list(refs)
    sums, refs = refs[: g.R - 1], refs[g.R - 1 :]
    parts, refs = refs[: g.C], refs[g.C :]
    outs, own_ref = refs[: g.R - 1], refs[g.R - 1]
    total = parts[0][...]
    for ref in parts[1:]:
        total = total + ref[...].astype(F32)
    total, rows = total.astype(BF16), g.SP * g.I
    own_ref[...] = total
    for x in range(1, g.R):
        outs[x - 1][:rows, :] = sums[x - 1][...]
        outs[x - 1][rows:, :] = total


def piece_kernel(g, own_ref, *refs):
    out_ref, order_ref = refs[-2:]
    row, rows = lax.axis_index("row"), g.SP * g.I
    order_ref[row] = own_ref[...]
    for k in range(1, g.R):
        order_ref[jnp.bitwise_xor(row, g.R - k)] = refs[k - 1][rows:, :]
    total = order_ref[0].astype(F32)
    for r in range(1, g.R):
        total = total + order_ref[r].astype(F32)
    out_ref[...] = total.astype(BF16)


def score_kernel(g, soft_ref, *refs):
    parts, refs = refs[: g.D], refs[g.D :]
    own_ref, out_refs, order_ref = refs[0], refs[1 : g.C], refs[g.C]
    depth = lax.axis_index("depth")
    for k in range(g.D):
        order_ref[lax.rem(depth - k + g.D, g.D)] = parts[k][...]
    grad_soft = order_ref[0]
    for k in range(1, g.D):
        grad_soft = grad_soft + order_ref[k]
    inner = jnp.sum(soft_ref[...] * grad_soft, -1, keepdims=True)
    for k in range(g.C):
        block = lanes_of([grad_soft[:, k * g.JC : (k + 1) * g.JC], inner])
        if k == 0:
            own_ref[...] = block
        else:
            out_refs[k - 1][...] = three_lanes(block)


def pair_kernel(g, e_ref, wl_ref, soft_ref, own_ref, *refs):
    got, pair_ref = refs[: g.C - 1], refs[g.C - 1]
    heads = g.H * g.I
    total = own_ref[...]
    for ref in got:
        total = total + join_three(ref[...], g.JC + 1)
    grad = soft_ref[:, : g.JC] * (total[:, : g.JC] - total[:, g.JC :])
    if g.JC < LANES:
        grad = lanes_of([grad, jnp.zeros((heads, LANES - g.JC), F32)])
    high, low = split_high_low(grad.T[: g.JC])
    grads = lanes_of([high, low])
    pick = (iota((heads, g.H), 0) // g.I == iota((heads, g.H), 1)).astype(BF16)
    base = mm(pick, wl_ref[...]).astype(BF16)
    token = iota((heads, 1), 0) % g.I
    for i in range(0, g.I, 2):
        weights = lanes_of(
            [jnp.where(token == i + k, base, jnp.zeros_like(base)) for k in range(2)]
        )
        upstream = mm(grads, rows_of([weights, weights]))
        for k in range(2):
            pair_ref[i + k] = standardize_backward(
                e_ref[i + k].astype(F32), upstream[:, k * g.Z : (k + 1) * g.Z]
            ).astype(BF16)


def reduce_kernel(g, x_ref, own_ref, *refs):
    got, out_ref = refs[:-1], refs[-1]
    rows = g.SP * g.I
    total = own_ref[...]
    for ref in got:
        total = total + ref[:rows, :].astype(F32)
    total = total.reshape(g.SP, 1, g.I, 2 * g.M)
    upstream = jnp.concatenate([total[..., : g.M], total[..., g.M :]], axis=1)
    upstream = upstream.reshape(g.S, g.I, g.M)[: g.SQ]
    msa = g.fill(standardize_backward(x_ref[...].astype(F32), upstream))
    msa = msa.reshape(g.SP, 2, g.I, g.M)
    msa = jnp.concatenate([msa[:, 0], msa[:, 1]], axis=-1).astype(BF16)
    out_ref[...] = msa.reshape(rows, 2 * g.M)


def ensemble_kernel(g, own_ref, *refs):
    got, msa_ref = refs[:-1], refs[-1]
    col = lax.axis_index("col")
    for k, ref in enumerate((own_ref, *got)):
        msa = ref[...].astype(F32).reshape(g.SP, 1, g.I, 2 * g.M)
        msa = jnp.concatenate([msa[..., : g.M], msa[..., g.M :]], axis=1)
        msa = msa.reshape(g.S, g.I, g.M)[: g.SQ].astype(BF16)
        msa_ref[pl.ds(lax.rem(col - k + g.C, g.C) * g.SQ, g.SQ)] = msa


def across_kernel(g, *refs):
    out_ref = refs[-1]
    col = lax.axis_index("col")
    for k, ref in enumerate(refs[:-1]):
        out_ref[lax.rem(col - k + g.C, g.C)] = ref[...]


def matrix_kernel(g, *refs):
    parts, out_ref = refs[: g.D], refs[g.D]
    depth = lax.axis_index("depth")
    for k in range(g.D):
        out_ref[lax.rem(depth - k + g.D, g.D)] = parts[k][...].astype(F32)


class Sizes:
    def __init__(self, x, e, wl, w1):
        self.R, self.C, self.D = (lax.axis_size(a) for a in ("row", "col", "depth"))
        self.I, self.M = x.shape[1:]
        self.JC, self.Z = e.shape[1:]
        self.H, self.Q = wl.shape[1], w1.shape[1]
        self.SQ = x.shape[0] // self.C
        self.S = -(-self.SQ // 16) * 16
        self.SP, self.N = self.S // 2, self.R * self.I
        self.F = self.R // self.C
        self.NT = -(-self.N // LANES)
        self.G = max(1, LANES // self.JC)
        self.carried = 0

    def fill(self, rows):
        if self.SQ == self.S:
            return rows
        return rows_of([rows, jnp.zeros((self.S - self.SQ, *rows.shape[1:]), rows.dtype)])

    def place(self, row, col):
        turn = lax.rem(row // self.F - col + self.C, self.C)
        return pl.multiple_of((turn * self.F + lax.rem(row, self.F)) * self.I, self.I)


def shift(array, axis, k):
    count = lax.axis_size(axis)
    return lax.ppermute(array, axis, [(i, (i + k) % count) for i in range(count)])


def swap(array, axis, x):
    return lax.ppermute(array, axis, [(i, i ^ x) for i in range(lax.axis_size(axis))])


def swapped(arrays, axis):
    return [swap(a, axis, k + 1) for k, a in reversed([*enumerate(arrays)])]


def shifted_all(array, axis):
    return [array] + [shift(array, axis, k) for k in range(1, lax.axis_size(axis))]


def per_device(
    homolog_ensemble,
    duplex_embedding,
    homolog_present_flags,
    resolved_position_flags,
    payload_weights,
    sigmoid_weights,
    averager_final_weights,
    first_operand_weights,
    second_operand_weights,
    duplex_logit_weights,
    tensor_product_weights,
    averager_upstream_adjoint,
    duplex_upstream_adjoint,
):
    g = Sizes(homolog_ensemble, duplex_embedding, duplex_logit_weights, first_operand_weights)
    shape = jax.ShapeDtypeStruct

    def call(kernel, name, args, outs, scratch=(), far=None, after=(), distant=False, us=1.0):
        size = sum(a.size * a.dtype.itemsize for a in args) + sum(
            math.prod(o.shape) * jnp.dtype(o.dtype).itemsize for o in outs
        )
        single = len(outs) == 1
        near = len(args) if far is None else far
        args = list(args[:near]) + [
            pltpu.with_memory_space_constraint(a, pltpu.HBM) for a in args[near:]
        ]

        if distant:
            after = [pltpu.with_memory_space_constraint(a, pltpu.HBM) for a in after]

        def body(*refs):
            kernel(g, *refs[: len(args)], *refs[len(args) + len(after) :])

        return pl.pallas_call(
            body,
            out_shape=outs[0] if single else tuple(outs),
            in_specs=[VMEM] * near + [FAR] * (len(args) - near) + [FAR if distant else VMEM] * len(after),
            out_specs=VMEM if single else (VMEM,) * len(outs),
            scratch_shapes=list(scratch),
            compiler_params=pltpu.CompilerParams(vmem_limit_bytes=40 * 1024 * 1024),
            cost_estimate=pl.CostEstimate(
                flops=int(us * 1.15e9), bytes_accessed=size, transcendentals=0
            ),
            name=name,
        )(*args, *after)

    heads = g.H * g.I
    rows = g.SP * g.I
    values = 2 * payload_weights.shape[1]
    xn, x = call(
        ensemble_norm_kernel,
        "ensemble_norm",
        (homolog_ensemble,),
        [pltpu.VMEM((g.SP, g.I, 2 * g.M), BF16), pltpu.VMEM((g.SQ, g.I, g.M), BF16)],
        [pltpu.SemaphoreType.DMA],
        far=0,
    )
    everyone = [xn] + swapped([xn] * (g.R - 1), "row")
    cotangents = shifted_all(duplex_upstream_adjoint, "col")
    later = (
        duplex_embedding,
        duplex_logit_weights.T,
        sigmoid_weights,
        averager_final_weights.T,
        first_operand_weights.T,
        tensor_product_weights,
        payload_weights,
        second_operand_weights.T,
        duplex_upstream_adjoint,
    )
    g.carried = len(later)
    prepared = call(
        prepare_kernel,
        "prepare",
        (
            xn,
            resolved_position_flags.reshape(1, g.JC),
            homolog_present_flags,
            averager_upstream_adjoint,
            *later,
        ),
        [
            pltpu.VMEM((heads // g.G, g.G * g.JC), F32),
            pltpu.VMEM((g.SP + 8, 2 * g.M), F32),
            pltpu.VMEM((2 * g.M, values), BF16),
            pltpu.VMEM((rows, values), BF16),
            pltpu.VMEM((rows, values), F32),
            pltpu.VMEM((g.I * g.S, g.Q), BF16),
            pltpu.VMEM((g.Q, g.Q, g.Z), BF16),
            pltpu.VMEM((g.I, g.Q * g.S, g.Z), BF16),
        ]
        + [pltpu.VMEM(a.shape, a.dtype) for a in later],
        [
            pltpu.VMEM((1, g.JC), jnp.int32),
            pltpu.SMEM(homolog_present_flags.shape, jnp.int32),
            pltpu.VMEM((g.SQ, g.I, g.M), BF16),
            pltpu.VMEM((g.I * g.H, LANES), F32),
            pltpu.VMEM(tensor_product_weights.shape, F32),
            pltpu.VMEM((2, rows, LANES), F32),
            pltpu.SemaphoreType.DMA((3,)),
            pltpu.SemaphoreType.DMA((len(later),)),
        ],
        far=1,
        after=cotangents[1:],
        us=3.0,
    )
    logits, masks, gate_weights, blended, gate_factor, left, weights, left_weights = prepared[:8]
    e, wl, _, _, w1, _, p, w2, cotangents[0] = prepared[8:]
    logits = shifted_all(logits, "col")
    share = g.Q * g.Q // g.D
    xall, cotangents, *matrix_parts, first_term = call(
        outer_kernel,
        "outer",
        (*everyone, *cotangents, left, weights, w1, w2, masks),
        [pltpu.VMEM((g.SP, g.N, 2 * g.M), BF16), pltpu.VMEM((g.I, g.N, g.Z), BF16)]
        + [pltpu.VMEM((share, g.Z), F32)] * g.D
        + [pltpu.VMEM((g.SP, g.I, 2 * g.M), F32)],
        [
            pltpu.VMEM((g.NT, g.SP * 2 * g.Q, LANES), F32),
            pltpu.VMEM((g.Q * g.S, g.N), BF16),
            pltpu.VMEM((g.Q, g.I, g.S, g.Z), BF16),
            pltpu.VMEM((g.Q * g.Q, g.Z), F32),
            pltpu.VMEM((g.I * g.S, 2 * g.M), F32),
        ],
        us=0.05,
    )
    matrix_parts = [matrix_parts[0]] + [
        shift(a, "depth", k + 1) for k, a in enumerate(matrix_parts[1:])
    ]
    second_term = call(
        right_kernel,
        "right",
        (cotangents, left_weights, w2, masks),
        [pltpu.VMEM((g.SP, g.N, 2 * g.M), F32)],
        [pltpu.VMEM((g.NT, g.Q * g.S, LANES), F32)],
    )
    share //= g.C
    matrix_parts = call(
        half_sum_kernel,
        "half_sum",
        matrix_parts,
        [pltpu.VMEM((share, g.Z), F32)] + [pltpu.VMEM((share, g.Z), BF16)] * (g.C - 1),
        [pltpu.VMEM((share * g.C, g.Z), F32)],
        after=(second_term,),
        us=0.2,
    )
    matrix_parts = [matrix_parts[0]] + [
        shift(a, "col", k + 1) for k, a in enumerate(matrix_parts[1:])
    ]
    soft, grad_soft, own, *sums = call(
        attend_kernel,
        "attend",
        (xall, *logits, blended, gate_factor, p, gate_weights, second_term, first_term),
        [
            pltpu.VMEM((heads, g.N), F32),
            pltpu.VMEM((heads, g.N), F32),
            pltpu.VMEM((rows, 2 * g.M), F32),
        ]
        + [pltpu.VMEM((rows, 2 * g.M), BF16)] * (g.R - 1),
        [pltpu.VMEM((g.SP, g.N, 2 * g.M), F32), pltpu.VMEM((rows, values), BF16)],
        us=3.0,
    )
    *sums, piece = call(
        pack_kernel,
        "pack",
        (*sums, *matrix_parts),
        [pltpu.VMEM((rows + share, 2 * g.M), BF16)] * (g.R - 1) + [pltpu.VMEM((share, g.Z), BF16)],
        us=0.2,
    )
    sums = swapped(sums, "row")
    wide = -(-3 * (g.JC + 1) // LANES) * LANES
    scores, *sends = call(
        score_kernel,
        "score",
        (soft, *shifted_all(grad_soft, "depth")),
        [pltpu.VMEM((heads, g.JC + 1), F32)] + [pltpu.VMEM((heads, wide), BF16)] * (g.C - 1),
        [pltpu.VMEM((g.D, heads, g.N), F32)],
        after=(piece,),
        us=0.2,
    )
    arrived = [shift(a, "col", k + 1) for k, a in enumerate(sends)]
    pairwise_gradient = call(
        pair_kernel,
        "pair",
        (e, wl, soft, scores, *arrived),
        [shape(duplex_embedding.shape, BF16)],
        us=1.8,
    )
    piece = call(
        piece_kernel,
        "piece",
        (piece, *sums),
        [pltpu.VMEM((share, g.Z), BF16)],
        [pltpu.VMEM((g.R, share, g.Z), BF16)],
        after=(pairwise_gradient,),
        distant=True,
        us=0.1,
    )
    pieces = shifted_all(piece, "col")
    part = call(
        reduce_kernel,
        "reduce",
        (x, own, *sums),
        [pltpu.VMEM((rows, 2 * g.M), BF16)],
        after=(piece,),
    )
    matrix = call(
        across_kernel,
        "across",
        pieces,
        [pltpu.VMEM((g.C, share, g.Z), BF16)],
        after=(part,),
        us=0.1,
    ).reshape(g.C * share, g.Z)
    ensemble_derivative = call(
        ensemble_kernel,
        "ensemble",
        shifted_all(part, "col"),
        [shape(homolog_ensemble.shape, BF16)],
        after=(matrix,),
    )
    outer_matrix_gradient = call(
        matrix_kernel,
        "matrix",
        shifted_all(matrix, "depth"),
        [shape((g.D, g.C * share, g.Z), F32)],
        after=(ensemble_derivative,),
        distant=True,
    ).reshape(tensor_product_weights.shape)
    return (ensemble_derivative, pairwise_gradient, outer_matrix_gradient)


def solution(mesh):
    in_specs = (
        P(("parts", "depth"), "row", None),
        P(("parts", "row"), "col", None),
        P("parts"),
        P(("parts", "col")),
        P(),
        P(),
        P(),
        P(),
        P(),
        P(),
        P(),
        P(("parts", "depth"), "row", None),
        P(("parts", "row"), "col", None),
    )
    out_specs = (
        P(("parts", "depth"), "row", None),
        P(("parts", "row"), "col", None),
        P("parts", None),
    )
    return jax.shard_map(
        per_device, mesh=mesh, in_specs=in_specs, out_specs=out_specs, check_vma=False
    )
```

```python
import functools
import math

import jax
import jax.numpy as jnp
from jax import lax
from jax.experimental import pallas as pl
from jax.experimental.pallas import tpu as pltpu
from jax.sharding import PartitionSpec as P

EPS = 1e-05
PENALTY = 10000.0
F32 = jnp.float32
BF16 = jnp.bfloat16
LANES = 128
NN = (((1,), (0,)), ((), ()))
NT = (((1,), (1,)), ((), ()))
VMEM = pl.BlockSpec(memory_space=pltpu.VMEM)
FAR = pl.BlockSpec(memory_space=pl.ANY)


def mm(a, b, dims=NN):
    return lax.dot_general(a, b, dims, preferred_element_type=F32)


def split_high_low(value):
    high = value.astype(BF16)
    return high, (value - high.astype(F32)).astype(BF16)


def iota(shape, dim):
    return lax.broadcasted_iota(jnp.int32, shape, dim)


def lanes_of(pieces):
    return pieces[0] if len(pieces) == 1 else jnp.concatenate(pieces, axis=-1)


def rows_of(pieces):
    return pieces[0] if len(pieces) == 1 else jnp.concatenate(pieces, axis=0)


def standardize(values):
    centred = values - jnp.mean(values, -1, keepdims=True)
    inverse = lax.rsqrt(jnp.mean(centred * centred, -1, keepdims=True) + EPS)
    return centred * inverse, inverse


def standardize_backward(values, upstream):
    scaled, inverse = standardize(values)
    mean_grad = jnp.mean(upstream, -1, keepdims=True)
    mean_cross = jnp.mean(upstream * scaled, -1, keepdims=True)
    return (upstream - mean_grad - scaled * mean_cross) * inverse


def on_diagonal(block, width):
    rows, lanes = block.shape
    same = iota(block.shape, 0) // (rows // 2) == iota(block.shape, 1) // width
    return jnp.where(same, block, jnp.zeros_like(block))


def split_three(value):
    high = value.astype(BF16)
    rest = value - high.astype(F32)
    middle = rest.astype(BF16)
    return [high, middle, (rest - middle.astype(F32)).astype(BF16)]


def three_lanes(value):
    rows, width = value.shape
    fill = -(3 * width) % LANES
    return lanes_of(split_three(value) + [jnp.zeros((rows, fill), BF16)] * (fill > 0))


def join_three(parts, width):
    wide = parts.astype(F32)
    return (wide[:, :width] + wide[:, width : 2 * width]) + wide[:, 2 * width : 3 * width]


def twice(weights):
    zero = jnp.zeros_like(weights)
    return rows_of([lanes_of([weights, zero]), lanes_of([zero, weights])])


def normalise_kernel(g, x_hbm, e_hbm, dd_hbm, flag_hbm, wl_hbm, *refs):
    xn_ref, logit_ref, near_ref, x_ref, e_ref, wl_ref, flag_in, rows_ref, sem = refs
    first = lax.axis_index("col") * g.SQ
    pairs = g.I * g.JC
    copies = [
        pltpu.make_async_copy(a, b, sem.at[k])
        for k, (a, b) in enumerate(
            [
                (x_hbm.at[pl.ds(first, g.SQ)], x_ref),
                (e_hbm, e_ref),
                (wl_hbm, wl_ref),
                (flag_hbm, flag_in),
                (dd_hbm, near_ref.at[pl.ds(0, pairs)]),
            ]
        )
    ]
    for copy in copies:
        copy.start()
    copies[0].wait()
    normed = g.fill(standardize(x_ref[...].astype(F32))[0]).reshape(g.SP, 2, g.I, g.M)
    xn_ref[...] = jnp.concatenate([normed[:, 0], normed[:, 1]], axis=-1).astype(BF16)
    for copy in copies[1:4]:
        copy.wait()
    pair = standardize(e_ref[...].astype(F32).reshape(pairs, g.Z))[0].astype(BF16)
    penalty = (flag_in[...].astype(F32) - 1.0) * PENALTY
    weights = wl_ref[...]
    for i in range(g.I):
        rows_ref[i * g.H : (i + 1) * g.H, : g.JC] = (
            mm(weights, pair[i * g.JC : (i + 1) * g.JC], NT) + penalty
        )
    logits = rows_of([rows_ref[pl.ds(h, g.I, stride=g.H), :][:, : g.JC] for h in range(g.H)])
    tall = g.H * g.I // g.G
    packed = lanes_of([logits[k * tall : (k + 1) * tall] for k in range(g.G)])
    logit_ref[...] = packed
    near_ref[pairs:, :] = rows_of(split_three(packed))
    copies[4].wait()


def prepare_kernel(g, xn_ref, live_ref, u_ref, *refs):
    refs = list(refs)
    count = g.carried
    sources, refs = refs[:count], refs[count:]
    mask_ref, gate_weight_ref, gm_ref, gate_ref, left_ref, ts_ref, lt_ref = refs[:7]
    refs = refs[7:]
    targets, refs = refs[:count], refs[count:]
    live_in, u_in, wide_ref, half_ref, first_sem, later_sem = refs
    col, depth = lax.axis_index("col"), lax.axis_index("depth")
    firsts = [
        pltpu.make_async_copy(live_ref, live_in, first_sem.at[0]),
        pltpu.make_async_copy(u_ref.at[pl.ds(col * g.SQ, g.SQ)], u_in, first_sem.at[1]),
    ]
    copies = [
        pltpu.make_async_copy(a, b, later_sem.at[k])
        for k, (a, b) in enumerate(zip(sources, targets, strict=True))
    ]
    for copy in firsts + copies:
        copy.start()
    sg_ref, wf_ref, w1_ref, t_ref = targets[:4]
    for copy in firsts + copies:
        copy.wait()
    first = depth * g.C * g.SQ + col * g.SQ
    lane = iota((1, 2 * g.M), 1)
    masks = []
    for k in range(g.SP):
        if 2 * k + 1 < g.SQ:
            flags = jnp.where(lane < g.M, live_in[first + 2 * k], live_in[first + 2 * k + 1])
            masks.append(flags.astype(F32))
        else:
            masks.append(jnp.zeros((1, 2 * g.M), F32))
        mask_ref[k : k + 1, :] = masks[-1]
    total = live_in[0]
    for s in range(1, live_in.shape[0]):
        total = total + live_in[s]
    mask_ref[g.SP : g.SP + 1, :] = 1.0 / (0.001 + jnp.full((1, 2 * g.M), total, jnp.int32).astype(F32))
    rows = g.SP * g.I
    xn = xn_ref[...]
    gate_weights = twice(sg_ref[...])
    gate_weight_ref[...] = gate_weights
    gates = jax.nn.sigmoid(mm(xn.reshape(rows, 2 * g.M), gate_weights))
    u = g.fill(u_in[...]).reshape(g.SP, 2, g.I, g.M)
    packed_u = jnp.concatenate([u[:, 0], u[:, 1]], axis=-1).reshape(rows, 2 * g.M)
    gated = mm(packed_u, twice(wf_ref[...]))
    blended = gated * gates
    gm_ref[...] = blended.astype(BF16)
    gate_ref[...] = blended * (1.0 - gates)
    live_xn = rows_of([(xn[k].astype(F32) * masks[k]).astype(BF16) for k in range(g.SP)])
    w1 = rows_of([w1_ref[...], jnp.zeros((LANES - g.Q, g.M), BF16)])
    zero = jnp.zeros_like(w1)
    half_ref[0] = mm(live_xn, lanes_of([w1, zero]), NT)
    half_ref[1] = mm(live_xn, lanes_of([zero, w1]), NT)
    for i in range(g.I):
        halves = [half_ref[half, pl.ds(i, g.SP, stride=g.I), :] for half in range(2)]
        left_ref[i * g.S : (i + 1) * g.S, :] = rows_of(halves)[:, : g.Q].astype(BF16)
    wide_ref[...] = t_ref[...].astype(F32)
    for q in range(g.Q):
        ts_ref[q] = wide_ref[pl.ds(q, g.Q, stride=g.Q), :].astype(BF16)
    left = left_ref[...]
    for q in range(0, g.Q, 2):
        product = mm(left, lanes_of([ts_ref[q], ts_ref[q + 1]]))
        for k in range(2):
            block = product[:, k * g.Z : (k + 1) * g.Z].reshape(g.I, g.S, g.Z)
            lt_ref[:, (q + k) * g.S : (q + k + 1) * g.S, :] = block.astype(BF16)


def outer_kernel(g, *refs):
    refs = list(refs)
    x_refs, refs = refs[: g.R], refs[g.R :]
    d_refs, refs = refs[: g.C], refs[g.C :]
    left_ref, ts_ref, w1_ref, w2_ref, mask_ref = refs[:5]
    refs = refs[5:]
    xall_ref, d_ref, refs = refs[0], refs[1], refs[2:]
    w_refs, (gl_ref, spread_ref, rt_ref, ds_ref, all_ref, turn_ref) = refs[: g.D], refs[g.D :]
    row, col, depth = (lax.axis_index(a) for a in ("row", "col", "depth"))
    masks = [mask_ref[k : k + 1, :] for k in range(g.SP)]
    scale = mask_ref[g.SP : g.SP + 1, :]
    for k in range(g.R):
        place = g.place(jnp.bitwise_xor(row, k), col)
        xall_ref[:, pl.ds(place, g.I), :] = x_refs[k][...]
    for k in range(g.C):
        spot = (g.C - k) % g.C
        block = d_refs[k][: g.I * g.JC, :].reshape(g.I, g.JC, g.Z)
        d_ref[:, spot * g.JC : (spot + 1) * g.JC, :] = block
    w2 = w2_ref[...]
    doubled = lanes_of([w2, w2])
    second = on_diagonal(rows_of([doubled, doubled]), g.M)
    for k in range(g.SP):
        live_x = (xall_ref[k].astype(F32) * masks[k]).astype(BF16)
        part = mm(second, live_x, NT)
        for t in range(g.NT):
            lanes = min(LANES, g.N - t * LANES)
            spread_ref[t, k * 2 * g.Q : (k + 1) * 2 * g.Q, :lanes] = part[
                :, t * LANES : t * LANES + lanes
            ]
    for q in range(g.Q):
        for t in range(g.NT):
            lanes = min(LANES, g.N - t * LANES)
            halves = [
                spread_ref[t, pl.ds(half * g.Q + q, g.SP, stride=2 * g.Q), :] for half in range(2)
            ]
            rt_ref[q * g.S : (q + 1) * g.S, t * LANES : t * LANES + lanes] = rows_of(halves)[
                :, :lanes
            ].astype(BF16)
    rt = rt_ref[...]
    for i in range(0, g.I, 2):
        product = mm(rt, lanes_of([d_ref[i], d_ref[i + 1]]))
        for k in range(2):
            block = product[:, k * g.Z : (k + 1) * g.Z]
            ds_ref[:, i + k] = block.reshape(g.Q, g.S, g.Z).astype(BF16)
    left = left_ref[...]
    eye = (iota((g.Q, g.Q), 0) == iota((g.Q, g.Q), 1)).astype(BF16)
    left_t = mm(eye, left, NT).astype(BF16)
    entries = g.S * g.I
    left_grad = jnp.zeros((entries, g.Q), F32)
    for q in range(0, g.Q, 2):
        both = lanes_of([ds_ref[q].reshape(entries, g.Z), ds_ref[q + 1].reshape(entries, g.Z)])
        part = mm(left_t, both)
        all_ref[pl.ds(q, g.Q, stride=g.Q), :] = part[:, : g.Z] * scale
        all_ref[pl.ds(q + 1, g.Q, stride=g.Q), :] = part[:, g.Z :] * scale
        left_grad = left_grad + mm(both, lanes_of([ts_ref[q], ts_ref[q + 1]]), NT)
    share = g.Q * g.Q // g.D
    for k in range(g.D):
        first = pl.multiple_of(lax.rem(depth + k, g.D) * share, share)
        w_refs[k][...] = all_ref[pl.ds(first, share), :]
    w1 = w1_ref[...]
    first_term = jnp.zeros((entries, 2 * g.M), F32)
    for piece in split_high_low(left_grad * scale[:, : g.Q]):
        first_term = first_term + mm(piece, lanes_of([w1, w1]))
    turn_ref[...] = first_term
    lane = iota((1, 2 * g.M), 1)
    for k in range(g.SP):
        halves = [turn_ref[pl.ds(half * g.SP + k, g.I, stride=g.S), :] for half in range(2)]
        gl_ref[k] = jnp.where(lane < g.M, halves[0], halves[1]) * masks[k]


def right_kernel(g, d_ref, lt_ref, w2_ref, mask_ref, go_ref, rg_ref):
    masks = [mask_ref[k : k + 1, :] for k in range(g.SP)]
    scale = mask_ref[g.SP : g.SP + 1, :]
    right_grad = jnp.zeros((g.Q * g.S, g.N), F32)
    for i in range(0, g.I, 2):
        right_grad = right_grad + mm(
            lanes_of([lt_ref[i], lt_ref[i + 1]]), lanes_of([d_ref[i], d_ref[i + 1]]), NT
        )
    for t in range(g.NT):
        lanes = min(LANES, g.N - t * LANES)
        piece = right_grad[:, t * LANES : t * LANES + lanes]
        if lanes < LANES:
            piece = lanes_of([piece, jnp.zeros((g.Q * g.S, LANES - lanes), F32)])
        rg_ref[t] = piece
    deep = 2 * g.Q
    group = min(g.SP, LANES // deep)
    which = iota((group * deep, g.Q), 0)
    pick = (iota((group * deep, g.Q), 1) == which % deep // 2).astype(BF16)
    w2 = w2_ref[...]
    base = mm(pick, lanes_of([w2, w2]))
    which = iota(base.shape, 0)
    base = jnp.where(which % 2 == iota(base.shape, 1) // g.M, base, 0.0)
    weights = lanes_of([jnp.where(which // deep == k, base, 0.0) for k in range(group)]).astype(BF16)
    for k in range(0, g.SP, group):
        for t in range(g.NT):
            lanes = min(LANES, g.N - t * LANES)
            tall = rows_of(
                [rg_ref[t, pl.ds(k + m, deep, stride=g.SP), :] for m in range(group)]
            )
            tall = (tall * scale).T[:lanes]
            high, low = split_high_low(tall)
            part = mm(high, weights) + mm(low, weights)
            for m in range(group):
                go_ref[k + m, t * LANES : t * LANES + lanes, :] = (
                    part[:, m * 2 * g.M : (m + 1) * 2 * g.M] * masks[k + m]
                )


def half_sum_kernel(g, *refs):
    parts, outs, total_ref = refs[: g.D], refs[g.D : g.D + g.C], refs[-1]
    total = parts[0][...]
    for ref in parts[1:]:
        total = total + ref[...]
    total_ref[...] = total
    share = total.shape[0] // g.C
    col = lax.axis_index("col")
    for k in range(g.C):
        first = pl.multiple_of(lax.rem(col + k, g.C) * share, share)
        outs[k][...] = total_ref[pl.ds(first, share), :].astype(outs[k].dtype)


def attend_kernel(g, *refs):
    refs = list(refs)
    xall_ref, refs = refs[0], refs[1:]
    logit_ref, near_refs, refs = refs[0], refs[1 : g.C], refs[g.C :]
    gm_ref, gate_ref, p_ref, gate_weight_ref, go_ref, gl_ref = refs[:6]
    soft_ref, gs_ref, own_ref, refs = refs[6], refs[7], refs[8], refs[9:]
    send_refs, (total_ref, gg_ref) = refs[: g.R - 1], refs[g.R - 1 :]
    row, col = lax.axis_index("row"), lax.axis_index("col")
    tall, blocks = logit_ref.shape[0], [logit_ref[...]]
    for k in range(1, g.C):
        parts = near_refs[g.C - k - 1][g.I * g.JC :, :].astype(F32)
        blocks.append((parts[:tall] + parts[tall : 2 * tall]) + parts[2 * tall :])
    logits = lanes_of(
        [rows_of([b[:, k * g.JC : (k + 1) * g.JC] for k in range(g.G)]) for b in blocks]
    )
    shifted = jnp.exp(logits - jnp.max(logits, -1, keepdims=True))
    soft = shifted / jnp.sum(shifted, -1, keepdims=True)
    soft_ref[...] = soft
    low = soft.astype(BF16)
    eye = (iota((g.N, g.N), 0) == iota((g.N, g.N), 1)).astype(BF16)
    low_t = mm(eye, low, NT).astype(BF16)
    value_weights = twice(p_ref[...])
    values = mm(xall_ref[...].reshape(g.SP * g.N, 2 * g.M), value_weights).astype(BF16)
    wide = value_weights.shape[1]
    head = iota((1, wide), 1) % (wide // 2) // (wide // 2 // g.H)
    grad_soft = jnp.zeros((g.H * g.I, g.N), F32)
    for k in range(g.SP):
        v = values[k * g.N : (k + 1) * g.N]
        crossed = mm(low, v)
        mixed = jnp.where(head == 0, crossed[: g.I], 0.0)
        for h in range(1, g.H):
            mixed = jnp.where(head == h, crossed[h * g.I : (h + 1) * g.I], mixed)
        rows = slice(k * g.I, (k + 1) * g.I)
        gg_ref[rows, :] = (gate_ref[rows, :] * mixed).astype(BF16)
        blended = gm_ref[rows, :]
        by_head = rows_of(
            [jnp.where(head == h, blended, jnp.zeros_like(blended)) for h in range(g.H)]
        )
        grad_soft = grad_soft + mm(by_head, v, NT)
        part = go_ref[k]
        for piece in split_high_low(mm(low_t, by_head)):
            part = part + mm(piece, value_weights, NT)
        total_ref[k] = part
    gs_ref[...] = grad_soft
    own = total_ref[:, pl.ds(g.place(row, col), g.I), :]
    gate_term = mm(gg_ref[...], gate_weight_ref[...], NT).reshape(g.SP, g.I, 2 * g.M)
    own_ref[...] = (own + gate_term + gl_ref[...]).reshape(g.SP * g.I, 2 * g.M)
    for x in range(1, g.R):
        block = total_ref[:, pl.ds(g.place(jnp.bitwise_xor(row, x), col), g.I), :]
        send_refs[x - 1][...] = block.reshape(g.SP * g.I, 2 * g.M).astype(BF16)


def pack_kernel(g, *refs):
    refs = list(refs)
    sums, refs = refs[: g.R - 1], refs[g.R - 1 :]
    parts, refs = refs[: g.C], refs[g.C :]
    outs, own_ref = refs[: g.R - 1], refs[g.R - 1]
    total = parts[0][...]
    for ref in parts[1:]:
        total = total + ref[...].astype(F32)
    total, rows = total.astype(BF16), g.SP * g.I
    own_ref[...] = total
    for x in range(1, g.R):
        outs[x - 1][:rows, :] = sums[x - 1][...]
        outs[x - 1][rows:, :] = total


def piece_kernel(g, own_ref, *refs):
    out_ref, order_ref = refs[-2:]
    row, rows = lax.axis_index("row"), g.SP * g.I
    order_ref[row] = own_ref[...]
    for k in range(1, g.R):
        order_ref[jnp.bitwise_xor(row, g.R - k)] = refs[k - 1][rows:, :]
    total = order_ref[0].astype(F32)
    for r in range(1, g.R):
        total = total + order_ref[r].astype(F32)
    out_ref[...] = total.astype(BF16)


def score_kernel(g, soft_ref, *refs):
    parts, refs = refs[: g.D], refs[g.D :]
    own_ref, out_refs, order_ref = refs[0], refs[1 : g.C], refs[g.C]
    depth = lax.axis_index("depth")
    for k in range(g.D):
        order_ref[lax.rem(depth - k + g.D, g.D)] = parts[k][...]
    grad_soft = order_ref[0]
    for k in range(1, g.D):
        grad_soft = grad_soft + order_ref[k]
    inner = jnp.sum(soft_ref[...] * grad_soft, -1, keepdims=True)
    for k in range(g.C):
        block = lanes_of([grad_soft[:, k * g.JC : (k + 1) * g.JC], inner])
        if k == 0:
            own_ref[...] = block
        else:
            out_refs[k - 1][...] = three_lanes(block)


def pair_kernel(g, e_ref, wl_ref, soft_ref, own_ref, *refs):
    got, pair_ref = refs[: g.C - 1], refs[g.C - 1]
    heads = g.H * g.I
    total = own_ref[...]
    for ref in got:
        total = total + join_three(ref[...], g.JC + 1)
    grad = soft_ref[:, : g.JC] * (total[:, : g.JC] - total[:, g.JC :])
    if g.JC < LANES:
        grad = lanes_of([grad, jnp.zeros((heads, LANES - g.JC), F32)])
    high, low = split_high_low(grad.T[: g.JC])
    grads = lanes_of([high, low])
    pick = (iota((heads, g.H), 0) // g.I == iota((heads, g.H), 1)).astype(BF16)
    base = mm(pick, wl_ref[...]).astype(BF16)
    token = iota((heads, 1), 0) % g.I
    for i in range(0, g.I, 2):
        weights = lanes_of(
            [jnp.where(token == i + k, base, jnp.zeros_like(base)) for k in range(2)]
        )
        upstream = mm(grads, rows_of([weights, weights]))
        for k in range(2):
            pair_ref[i + k] = standardize_backward(
                e_ref[i + k].astype(F32), upstream[:, k * g.Z : (k + 1) * g.Z]
            ).astype(BF16)


def reduce_kernel(g, x_ref, own_ref, *refs):
    got, out_ref = refs[:-1], refs[-1]
    rows = g.SP * g.I
    total = own_ref[...]
    for ref in got:
        total = total + ref[:rows, :].astype(F32)
    total = total.reshape(g.SP, 1, g.I, 2 * g.M)
    upstream = jnp.concatenate([total[..., : g.M], total[..., g.M :]], axis=1)
    upstream = upstream.reshape(g.S, g.I, g.M)[: g.SQ]
    msa = g.fill(standardize_backward(x_ref[...].astype(F32), upstream))
    msa = msa.reshape(g.SP, 2, g.I, g.M)
    msa = jnp.concatenate([msa[:, 0], msa[:, 1]], axis=-1).astype(BF16)
    out_ref[...] = msa.reshape(rows, 2 * g.M)


def ensemble_kernel(g, own_ref, *refs):
    got, msa_ref = refs[:-1], refs[-1]
    col = lax.axis_index("col")
    for k, ref in enumerate((own_ref, *got)):
        msa = ref[...].astype(F32).reshape(g.SP, 1, g.I, 2 * g.M)
        msa = jnp.concatenate([msa[..., : g.M], msa[..., g.M :]], axis=1)
        msa = msa.reshape(g.S, g.I, g.M)[: g.SQ].astype(BF16)
        msa_ref[pl.ds(lax.rem(col - k + g.C, g.C) * g.SQ, g.SQ)] = msa


def across_kernel(g, *refs):
    out_ref = refs[-1]
    col = lax.axis_index("col")
    for k, ref in enumerate(refs[:-1]):
        out_ref[lax.rem(col - k + g.C, g.C)] = ref[...]


def matrix_kernel(g, *refs):
    parts, out_ref = refs[: g.D], refs[g.D]
    depth = lax.axis_index("depth")
    for k in range(g.D):
        out_ref[lax.rem(depth - k + g.D, g.D)] = parts[k][...].astype(F32)


class Sizes:
    def __init__(self, x, e, wl, w1):
        self.R, self.C, self.D = (lax.axis_size(a) for a in ("row", "col", "depth"))
        self.I, self.M = x.shape[1:]
        self.JC, self.Z = e.shape[1:]
        self.H, self.Q = wl.shape[1], w1.shape[1]
        self.SQ = x.shape[0] // self.C
        self.S = -(-self.SQ // 16) * 16
        self.SP, self.N = self.S // 2, self.R * self.I
        self.F = self.R // self.C
        self.NT = -(-self.N // LANES)
        self.G = max(1, LANES // self.JC)
        self.carried = 0

    def fill(self, rows):
        if self.SQ == self.S:
            return rows
        return rows_of([rows, jnp.zeros((self.S - self.SQ, *rows.shape[1:]), rows.dtype)])

    def place(self, row, col):
        turn = lax.rem(row // self.F - col + self.C, self.C)
        return pl.multiple_of((turn * self.F + lax.rem(row, self.F)) * self.I, self.I)


def shift(array, axis, k):
    count = lax.axis_size(axis)
    return lax.ppermute(array, axis, [(i, (i + k) % count) for i in range(count)])


def swap(array, axis, x):
    return lax.ppermute(array, axis, [(i, i ^ x) for i in range(lax.axis_size(axis))])


def swapped(arrays, axis):
    return [swap(a, axis, k + 1) for k, a in reversed([*enumerate(arrays)])]


def shifted_all(array, axis):
    return [array] + [shift(array, axis, k) for k in range(1, lax.axis_size(axis))]


def per_device(
    homolog_ensemble,
    duplex_embedding,
    homolog_present_flags,
    resolved_position_flags,
    payload_weights,
    sigmoid_weights,
    averager_final_weights,
    first_operand_weights,
    second_operand_weights,
    duplex_logit_weights,
    tensor_product_weights,
    averager_upstream_adjoint,
    duplex_upstream_adjoint,
):
    g = Sizes(homolog_ensemble, duplex_embedding, duplex_logit_weights, first_operand_weights)
    shape = jax.ShapeDtypeStruct

    def call(kernel, name, args, outs, scratch=(), far=None, after=(), distant=False, us=1.0):
        size = sum(a.size * a.dtype.itemsize for a in args) + sum(
            math.prod(o.shape) * jnp.dtype(o.dtype).itemsize for o in outs
        )
        single = len(outs) == 1
        near = len(args) if far is None else far
        args = list(args[:near]) + [
            pltpu.with_memory_space_constraint(a, pltpu.HBM) for a in args[near:]
        ]

        if distant:
            after = [pltpu.with_memory_space_constraint(a, pltpu.HBM) for a in after]

        def body(*refs):
            kernel(g, *refs[: len(args)], *refs[len(args) + len(after) :])

        return pl.pallas_call(
            body,
            out_shape=outs[0] if single else tuple(outs),
            in_specs=[VMEM] * near + [FAR] * (len(args) - near) + [FAR if distant else VMEM] * len(after),
            out_specs=VMEM if single else (VMEM,) * len(outs),
            scratch_shapes=list(scratch),
            compiler_params=pltpu.CompilerParams(vmem_limit_bytes=40 * 1024 * 1024),
            cost_estimate=pl.CostEstimate(
                flops=int(us * 1.15e9), bytes_accessed=size, transcendentals=0
            ),
            name=name,
        )(*args, *after)

    heads = g.H * g.I
    rows = g.SP * g.I
    values = 2 * payload_weights.shape[1]
    pairs, tall = g.I * g.JC, heads // g.G
    xn, logits, near, x, e, wl = call(
        normalise_kernel,
        "normalise",
        (
            homolog_ensemble,
            duplex_embedding,
            duplex_upstream_adjoint.reshape(pairs, g.Z),
            resolved_position_flags.reshape(1, g.JC),
            duplex_logit_weights.T,
        ),
        [
            pltpu.VMEM((g.SP, g.I, 2 * g.M), BF16),
            pltpu.VMEM((tall, g.G * g.JC), F32),
            pltpu.VMEM((pairs + 3 * tall, g.Z), BF16),
            pltpu.VMEM((g.SQ, g.I, g.M), BF16),
            pltpu.VMEM(duplex_embedding.shape, BF16),
            pltpu.VMEM((g.H, g.Z), BF16),
        ],
        [
            pltpu.VMEM((1, g.JC), jnp.int32),
            pltpu.VMEM((g.I * g.H, LANES), F32),
            pltpu.SemaphoreType.DMA((5,)),
        ],
        far=0,
        us=2.0,
    )
    everyone = [xn] + [swap(xn, "row", k) for k in range(1, g.R)]
    nears = shifted_all(near, "col")
    later = (
        sigmoid_weights,
        averager_final_weights.T,
        first_operand_weights.T,
        tensor_product_weights,
        payload_weights,
        second_operand_weights.T,
    )
    g.carried = len(later)
    prepared = call(
        prepare_kernel,
        "prepare",
        (xn, homolog_present_flags, averager_upstream_adjoint, *later),
        [
            pltpu.VMEM((g.SP + 8, 2 * g.M), F32),
            pltpu.VMEM((2 * g.M, values), BF16),
            pltpu.VMEM((rows, values), BF16),
            pltpu.VMEM((rows, values), F32),
            pltpu.VMEM((g.I * g.S, g.Q), BF16),
            pltpu.VMEM((g.Q, g.Q, g.Z), BF16),
            pltpu.VMEM((g.I, g.Q * g.S, g.Z), BF16),
        ]
        + [pltpu.VMEM(a.shape, a.dtype) for a in later],
        [
            pltpu.SMEM(homolog_present_flags.shape, jnp.int32),
            pltpu.VMEM((g.SQ, g.I, g.M), BF16),
            pltpu.VMEM(tensor_product_weights.shape, F32),
            pltpu.VMEM((2, rows, LANES), F32),
            pltpu.SemaphoreType.DMA((2,)),
            pltpu.SemaphoreType.DMA((len(later),)),
        ],
        far=1,
        after=nears[1:],
        us=3.0,
    )
    masks, gate_weights, blended, gate_factor, left, weights, left_weights = prepared[:7]
    _, _, w1, _, p, w2 = prepared[7:]
    share = g.Q * g.Q // g.D
    xall, cotangents, *matrix_parts, first_term = call(
        outer_kernel,
        "outer",
        (*everyone, *nears, left, weights, w1, w2, masks),
        [pltpu.VMEM((g.SP, g.N, 2 * g.M), BF16), pltpu.VMEM((g.I, g.N, g.Z), BF16)]
        + [pltpu.VMEM((share, g.Z), F32)] * g.D
        + [pltpu.VMEM((g.SP, g.I, 2 * g.M), F32)],
        [
            pltpu.VMEM((g.NT, g.SP * 2 * g.Q, LANES), F32),
            pltpu.VMEM((g.Q * g.S, g.N), BF16),
            pltpu.VMEM((g.Q, g.I, g.S, g.Z), BF16),
            pltpu.VMEM((g.Q * g.Q, g.Z), F32),
            pltpu.VMEM((g.I * g.S, 2 * g.M), F32),
        ],
        us=0.05,
    )
    matrix_parts = [matrix_parts[0]] + [
        shift(a, "depth", k + 1) for k, a in enumerate(matrix_parts[1:])
    ]
    second_term = call(
        right_kernel,
        "right",
        (cotangents, left_weights, w2, masks),
        [pltpu.VMEM((g.SP, g.N, 2 * g.M), F32)],
        [pltpu.VMEM((g.NT, g.Q * g.S, LANES), F32)],
    )
    share //= g.C
    matrix_parts = call(
        half_sum_kernel,
        "half_sum",
        matrix_parts,
        [pltpu.VMEM((share, g.Z), F32)] + [pltpu.VMEM((share, g.Z), BF16)] * (g.C - 1),
        [pltpu.VMEM((share * g.C, g.Z), F32)],
        after=(second_term,),
        us=0.2,
    )
    matrix_parts = [matrix_parts[0]] + [
        shift(a, "col", k + 1) for k, a in enumerate(matrix_parts[1:])
    ]
    soft, grad_soft, own, *sums = call(
        attend_kernel,
        "attend",
        (xall, logits, *nears[1:], blended, gate_factor, p, gate_weights, second_term, first_term),
        [
            pltpu.VMEM((heads, g.N), F32),
            pltpu.VMEM((heads, g.N), F32),
            pltpu.VMEM((rows, 2 * g.M), F32),
        ]
        + [pltpu.VMEM((rows, 2 * g.M), BF16)] * (g.R - 1),
        [pltpu.VMEM((g.SP, g.N, 2 * g.M), F32), pltpu.VMEM((rows, values), BF16)],
        us=3.0,
    )
    *sums, piece = call(
        pack_kernel,
        "pack",
        (*sums, *matrix_parts),
        [pltpu.VMEM((rows + share, 2 * g.M), BF16)] * (g.R - 1) + [pltpu.VMEM((share, g.Z), BF16)],
        us=0.2,
    )
    sums = swapped(sums, "row")
    wide = -(-3 * (g.JC + 1) // LANES) * LANES
    scores, *sends = call(
        score_kernel,
        "score",
        (soft, *shifted_all(grad_soft, "depth")),
        [pltpu.VMEM((heads, g.JC + 1), F32)] + [pltpu.VMEM((heads, wide), BF16)] * (g.C - 1),
        [pltpu.VMEM((g.D, heads, g.N), F32)],
        after=(piece,),
        us=0.2,
    )
    arrived = [shift(a, "col", k + 1) for k, a in enumerate(sends)]
    pairwise_gradient = call(
        pair_kernel,
        "pair",
        (e, wl, soft, scores, *arrived),
        [shape(duplex_embedding.shape, BF16)],
        us=0.01,
    )
    piece = call(
        piece_kernel,
        "piece",
        (piece, *sums),
        [pltpu.VMEM((share, g.Z), BF16)],
        [pltpu.VMEM((g.R, share, g.Z), BF16)],
        after=(pairwise_gradient,),
        distant=True,
        us=0.1,
    )
    pieces = shifted_all(piece, "col")
    part = call(
        reduce_kernel,
        "reduce",
        (x, own, *sums),
        [pltpu.VMEM((rows, 2 * g.M), BF16)],
        after=(piece,),
    )
    matrix = call(
        across_kernel,
        "across",
        pieces,
        [pltpu.VMEM((g.C, share, g.Z), BF16)],
        after=(part,),
        us=0.1,
    ).reshape(g.C * share, g.Z)
    ensemble_derivative = call(
        ensemble_kernel,
        "ensemble",
        shifted_all(part, "col"),
        [shape(homolog_ensemble.shape, BF16)],
        after=(matrix,),
    )
    outer_matrix_gradient = call(
        matrix_kernel,
        "matrix",
        shifted_all(matrix, "depth"),
        [shape((g.D, g.C * share, g.Z), F32)],
        after=(ensemble_derivative,),
        distant=True,
    ).reshape(tensor_product_weights.shape)
    return (ensemble_derivative, pairwise_gradient, outer_matrix_gradient)


def solution(mesh):
    in_specs = (
        P(("parts", "depth"), "row", None),
        P(("parts", "row"), "col", None),
        P("parts"),
        P(("parts", "col")),
        P(),
        P(),
        P(),
        P(),
        P(),
        P(),
        P(),
        P(("parts", "depth"), "row", None),
        P(("parts", "row"), "col", None),
    )
    out_specs = (
        P(("parts", "depth"), "row", None),
        P(("parts", "row"), "col", None),
        P("parts", None),
    )
    return jax.shard_map(
        per_device, mesh=mesh, in_specs=in_specs, out_specs=out_specs, check_vma=False
    )
```

```python
import functools
import math

import jax
import jax.numpy as jnp
from jax import lax
from jax.experimental import pallas as pl
from jax.experimental.pallas import tpu as pltpu
from jax.sharding import PartitionSpec as P

EPS = 1e-05
PENALTY = 10000.0
F32 = jnp.float32
BF16 = jnp.bfloat16
LANES = 128
NN = (((1,), (0,)), ((), ()))
NT = (((1,), (1,)), ((), ()))
VMEM = pl.BlockSpec(memory_space=pltpu.VMEM)
FAR = pl.BlockSpec(memory_space=pl.ANY)


def mm(a, b, dims=NN):
    return lax.dot_general(a, b, dims, preferred_element_type=F32)


def split_high_low(value):
    high = value.astype(BF16)
    return high, (value - high.astype(F32)).astype(BF16)


def iota(shape, dim):
    return lax.broadcasted_iota(jnp.int32, shape, dim)


def lanes_of(pieces):
    return pieces[0] if len(pieces) == 1 else jnp.concatenate(pieces, axis=-1)


def rows_of(pieces):
    return pieces[0] if len(pieces) == 1 else jnp.concatenate(pieces, axis=0)


def standardize(values):
    centred = values - jnp.mean(values, -1, keepdims=True)
    inverse = lax.rsqrt(jnp.mean(centred * centred, -1, keepdims=True) + EPS)
    return centred * inverse, inverse


def standardize_backward(values, upstream):
    scaled, inverse = standardize(values)
    mean_grad = jnp.mean(upstream, -1, keepdims=True)
    mean_cross = jnp.mean(upstream * scaled, -1, keepdims=True)
    return (upstream - mean_grad - scaled * mean_cross) * inverse


def on_diagonal(block, width):
    rows, lanes = block.shape
    same = iota(block.shape, 0) // (rows // 2) == iota(block.shape, 1) // width
    return jnp.where(same, block, jnp.zeros_like(block))


def split_three(value):
    high = value.astype(BF16)
    rest = value - high.astype(F32)
    middle = rest.astype(BF16)
    return [high, middle, (rest - middle.astype(F32)).astype(BF16)]


def three_lanes(value):
    rows, width = value.shape
    fill = -(3 * width) % LANES
    return lanes_of(split_three(value) + [jnp.zeros((rows, fill), BF16)] * (fill > 0))


def join_three(parts, width):
    wide = parts.astype(F32)
    return (wide[:, :width] + wide[:, width : 2 * width]) + wide[:, 2 * width : 3 * width]


def twice(weights):
    zero = jnp.zeros_like(weights)
    return rows_of([lanes_of([weights, zero]), lanes_of([zero, weights])])


def normalise_kernel(g, x_hbm, e_hbm, dd_hbm, flag_hbm, wl_hbm, *refs):
    xn_ref, logit_ref, near_ref, x_ref, e_ref, wl_ref, flag_in, rows_ref, sem = refs
    first = lax.axis_index("col") * g.SQ
    pairs = g.I * g.JC
    copies = [
        pltpu.make_async_copy(a, b, sem.at[k])
        for k, (a, b) in enumerate(
            [
                (x_hbm.at[pl.ds(first, g.SQ)], x_ref),
                (e_hbm, e_ref),
                (wl_hbm, wl_ref),
                (flag_hbm, flag_in),
                (dd_hbm, near_ref.at[pl.ds(0, pairs)]),
            ]
        )
    ]
    for copy in copies:
        copy.start()
    copies[0].wait()
    normed = g.fill(standardize(x_ref[...].astype(F32))[0]).reshape(g.SP, 2, g.I, g.M)
    xn_ref[...] = jnp.concatenate([normed[:, 0], normed[:, 1]], axis=-1).astype(BF16)
    for copy in copies[1:4]:
        copy.wait()
    pair = standardize(e_ref[...].astype(F32).reshape(pairs, g.Z))[0].astype(BF16)
    penalty = (flag_in[...].astype(F32) - 1.0) * PENALTY
    weights = wl_ref[...]
    for i in range(g.I):
        rows_ref[i * g.H : (i + 1) * g.H, : g.JC] = (
            mm(weights, pair[i * g.JC : (i + 1) * g.JC], NT) + penalty
        )
    logits = rows_of([rows_ref[pl.ds(h, g.I, stride=g.H), :][:, : g.JC] for h in range(g.H)])
    tall = g.H * g.I // g.G
    packed = lanes_of([logits[k * tall : (k + 1) * tall] for k in range(g.G)])
    logit_ref[...] = packed
    near_ref[pairs:, :] = rows_of(split_three(packed))
    copies[4].wait()


def prepare_kernel(g, xn_ref, live_ref, u_ref, *refs):
    refs = list(refs)
    count = g.carried
    sources, refs = refs[:count], refs[count:]
    mask_ref, gate_weight_ref, gm_ref, gate_ref, left_ref, ts_ref, lt_ref = refs[:7]
    refs = refs[7:]
    targets, refs = refs[:count], refs[count:]
    live_in, u_in, wide_ref, half_ref, first_sem, later_sem = refs
    col, depth = lax.axis_index("col"), lax.axis_index("depth")
    firsts = [
        pltpu.make_async_copy(live_ref, live_in, first_sem.at[0]),
        pltpu.make_async_copy(u_ref.at[pl.ds(col * g.SQ, g.SQ)], u_in, first_sem.at[1]),
    ]
    copies = [
        pltpu.make_async_copy(a, b, later_sem.at[k])
        for k, (a, b) in enumerate(zip(sources, targets, strict=True))
    ]
    for copy in firsts + copies:
        copy.start()
    sg_ref, wf_ref, w1_ref, t_ref = targets[:4]
    for copy in firsts + copies:
        copy.wait()
    first = depth * g.C * g.SQ + col * g.SQ
    lane = iota((1, 2 * g.M), 1)
    masks = []
    for k in range(g.SP):
        if 2 * k + 1 < g.SQ:
            flags = jnp.where(lane < g.M, live_in[first + 2 * k], live_in[first + 2 * k + 1])
            masks.append(flags.astype(F32))
        else:
            masks.append(jnp.zeros((1, 2 * g.M), F32))
        mask_ref[k : k + 1, :] = masks[-1]
    total = live_in[0]
    for s in range(1, live_in.shape[0]):
        total = total + live_in[s]
    mask_ref[g.SP : g.SP + 1, :] = 1.0 / (0.001 + jnp.full((1, 2 * g.M), total, jnp.int32).astype(F32))
    rows = g.SP * g.I
    xn = xn_ref[...]
    gate_weights = twice(sg_ref[...])
    gate_weight_ref[...] = gate_weights
    gates = jax.nn.sigmoid(mm(xn.reshape(rows, 2 * g.M), gate_weights))
    u = g.fill(u_in[...]).reshape(g.SP, 2, g.I, g.M)
    packed_u = jnp.concatenate([u[:, 0], u[:, 1]], axis=-1).reshape(rows, 2 * g.M)
    gated = mm(packed_u, twice(wf_ref[...]))
    blended = gated * gates
    gm_ref[...] = blended.astype(BF16)
    gate_ref[...] = blended * (1.0 - gates)
    live_xn = rows_of([(xn[k].astype(F32) * masks[k]).astype(BF16) for k in range(g.SP)])
    w1 = rows_of([w1_ref[...], jnp.zeros((LANES - g.Q, g.M), BF16)])
    zero = jnp.zeros_like(w1)
    half_ref[0] = mm(live_xn, lanes_of([w1, zero]), NT)
    half_ref[1] = mm(live_xn, lanes_of([zero, w1]), NT)
    for i in range(g.I):
        halves = [half_ref[half, pl.ds(i, g.SP, stride=g.I), :] for half in range(2)]
        left_ref[i * g.S : (i + 1) * g.S, :] = rows_of(halves)[:, : g.Q].astype(BF16)
    wide_ref[...] = t_ref[...].astype(F32)
    for q in range(g.Q):
        ts_ref[q] = wide_ref[pl.ds(q, g.Q, stride=g.Q), :].astype(BF16)
    left = left_ref[...]
    for q in range(0, g.Q, 2):
        product = mm(left, lanes_of([ts_ref[q], ts_ref[q + 1]]))
        for k in range(2):
            block = product[:, k * g.Z : (k + 1) * g.Z].reshape(g.I, g.S, g.Z)
            lt_ref[:, (q + k) * g.S : (q + k + 1) * g.S, :] = block.astype(BF16)


def outer_kernel(g, *refs):
    refs = list(refs)
    x_refs, refs = refs[: g.R], refs[g.R :]
    d_refs, refs = refs[: g.C], refs[g.C :]
    left_ref, w2_ref, mask_ref, xall_ref, d_ref, ds_ref, *refs = refs
    w_refs, (spread_ref, rt_ref, all_ref) = refs[: g.D], refs[g.D :]
    row, col, depth = (lax.axis_index(a) for a in ("row", "col", "depth"))
    masks = [mask_ref[k : k + 1, :] for k in range(g.SP)]
    scale = mask_ref[g.SP : g.SP + 1, :]
    for k, ref in zip((0, *g.order), x_refs, strict=True):
        place = g.place(jnp.bitwise_xor(row, k), col)
        xall_ref[:, pl.ds(place, g.I), :] = ref[...]
    for k in range(g.C):
        spot = (g.C - k) % g.C
        block = d_refs[k][: g.I * g.JC, :].reshape(g.I, g.JC, g.Z)
        d_ref[:, spot * g.JC : (spot + 1) * g.JC, :] = block
    w2 = w2_ref[...]
    doubled = lanes_of([w2, w2])
    second = on_diagonal(rows_of([doubled, doubled]), g.M)
    for k in range(g.SP):
        live_x = (xall_ref[k].astype(F32) * masks[k]).astype(BF16)
        part = mm(second, live_x, NT)
        for t in range(g.NT):
            lanes = min(LANES, g.N - t * LANES)
            spread_ref[t, k * 2 * g.Q : (k + 1) * 2 * g.Q, :lanes] = part[
                :, t * LANES : t * LANES + lanes
            ]
    for q in range(g.Q):
        for t in range(g.NT):
            lanes = min(LANES, g.N - t * LANES)
            halves = [
                spread_ref[t, pl.ds(half * g.Q + q, g.SP, stride=2 * g.Q), :] for half in range(2)
            ]
            rt_ref[q * g.S : (q + 1) * g.S, t * LANES : t * LANES + lanes] = rows_of(halves)[
                :, :lanes
            ].astype(BF16)
    rt = rt_ref[...]
    for i in range(0, g.I, 2):
        product = mm(rt, lanes_of([d_ref[i], d_ref[i + 1]]))
        for k in range(2):
            block = product[:, k * g.Z : (k + 1) * g.Z]
            ds_ref[:, i + k] = block.reshape(g.Q, g.S, g.Z).astype(BF16)
    left = left_ref[...]
    eye = (iota((g.Q, g.Q), 0) == iota((g.Q, g.Q), 1)).astype(BF16)
    left_t = mm(eye, left, NT).astype(BF16)
    entries = g.S * g.I
    for q in range(0, g.Q, 2):
        both = lanes_of([ds_ref[q].reshape(entries, g.Z), ds_ref[q + 1].reshape(entries, g.Z)])
        part = mm(left_t, both)
        all_ref[pl.ds(q, g.Q, stride=g.Q), :] = part[:, : g.Z] * scale
        all_ref[pl.ds(q + 1, g.Q, stride=g.Q), :] = part[:, g.Z :] * scale
    share = g.Q * g.Q // g.D
    for k in range(g.D):
        first = pl.multiple_of(lax.rem(depth + k, g.D) * share, share)
        w_refs[k][...] = all_ref[pl.ds(first, share), :]


def factors_kernel(
    g, d_ref, ds_ref, lt_ref, ts_ref, w1_ref, w2_ref, mask_ref, go_ref, gl_ref, rg_ref, turn_ref
):
    masks = [mask_ref[k : k + 1, :] for k in range(g.SP)]
    scale = mask_ref[g.SP : g.SP + 1, :]
    entries = g.S * g.I
    left_grad = jnp.zeros((entries, g.Q), F32)
    for q in range(0, g.Q, 2):
        both = lanes_of([ds_ref[q].reshape(entries, g.Z), ds_ref[q + 1].reshape(entries, g.Z)])
        left_grad = left_grad + mm(both, lanes_of([ts_ref[q], ts_ref[q + 1]]), NT)
    w1 = w1_ref[...]
    first_term = jnp.zeros((entries, 2 * g.M), F32)
    for piece in split_high_low(left_grad * scale[:, : g.Q]):
        first_term = first_term + mm(piece, lanes_of([w1, w1]))
    turn_ref[...] = first_term
    lane = iota((1, 2 * g.M), 1)
    for k in range(g.SP):
        halves = [turn_ref[pl.ds(half * g.SP + k, g.I, stride=g.S), :] for half in range(2)]
        gl_ref[k] = jnp.where(lane < g.M, halves[0], halves[1]) * masks[k]
    right_grad = jnp.zeros((g.Q * g.S, g.N), F32)
    for i in range(0, g.I, 2):
        right_grad = right_grad + mm(
            lanes_of([lt_ref[i], lt_ref[i + 1]]), lanes_of([d_ref[i], d_ref[i + 1]]), NT
        )
    for t in range(g.NT):
        lanes = min(LANES, g.N - t * LANES)
        piece = right_grad[:, t * LANES : t * LANES + lanes]
        if lanes < LANES:
            piece = lanes_of([piece, jnp.zeros((g.Q * g.S, LANES - lanes), F32)])
        rg_ref[t] = piece
    deep = 2 * g.Q
    group = min(g.SP, LANES // deep)
    which = iota((group * deep, g.Q), 0)
    pick = (iota((group * deep, g.Q), 1) == which % deep // 2).astype(BF16)
    w2 = w2_ref[...]
    base = mm(pick, lanes_of([w2, w2]))
    which = iota(base.shape, 0)
    base = jnp.where(which % 2 == iota(base.shape, 1) // g.M, base, 0.0)
    weights = lanes_of([jnp.where(which // deep == k, base, 0.0) for k in range(group)]).astype(BF16)
    for k in range(0, g.SP, group):
        for t in range(g.NT):
            lanes = min(LANES, g.N - t * LANES)
            tall = rows_of(
                [rg_ref[t, pl.ds(k + m, deep, stride=g.SP), :] for m in range(group)]
            )
            tall = (tall * scale).T[:lanes]
            high, low = split_high_low(tall)
            part = mm(high, weights) + mm(low, weights)
            for m in range(group):
                go_ref[k + m, t * LANES : t * LANES + lanes, :] = (
                    part[:, m * 2 * g.M : (m + 1) * 2 * g.M] * masks[k + m]
                )


def half_sum_kernel(g, *refs):
    parts, outs, total_ref = refs[: g.D], refs[g.D : g.D + g.C], refs[-1]
    total = parts[0][...]
    for ref in parts[1:]:
        total = total + ref[...]
    total_ref[...] = total
    share = total.shape[0] // g.C
    col = lax.axis_index("col")
    for k in range(g.C):
        first = pl.multiple_of(lax.rem(col + k, g.C) * share, share)
        outs[k][...] = total_ref[pl.ds(first, share), :].astype(outs[k].dtype)


def attend_kernel(g, *refs):
    refs = list(refs)
    xall_ref, refs = refs[0], refs[1:]
    logit_ref, near_refs, refs = refs[0], refs[1 : g.C], refs[g.C :]
    gm_ref, gate_ref, p_ref, gate_weight_ref, go_ref, gl_ref = refs[:6]
    soft_ref, gs_ref, own_ref, refs = refs[6], refs[7], refs[8], refs[9:]
    send_refs, (total_ref, gg_ref) = refs[: g.R - 1], refs[g.R - 1 :]
    row, col = lax.axis_index("row"), lax.axis_index("col")
    tall, blocks = logit_ref.shape[0], [logit_ref[...]]
    for k in range(1, g.C):
        parts = near_refs[g.C - k - 1][g.I * g.JC :, :].astype(F32)
        blocks.append((parts[:tall] + parts[tall : 2 * tall]) + parts[2 * tall :])
    logits = lanes_of(
        [rows_of([b[:, k * g.JC : (k + 1) * g.JC] for k in range(g.G)]) for b in blocks]
    )
    shifted = jnp.exp(logits - jnp.max(logits, -1, keepdims=True))
    soft = shifted / jnp.sum(shifted, -1, keepdims=True)
    soft_ref[...] = soft
    low = soft.astype(BF16)
    eye = (iota((g.N, g.N), 0) == iota((g.N, g.N), 1)).astype(BF16)
    low_t = mm(eye, low, NT).astype(BF16)
    value_weights = twice(p_ref[...])
    values = mm(xall_ref[...].reshape(g.SP * g.N, 2 * g.M), value_weights).astype(BF16)
    wide = value_weights.shape[1]
    head = iota((1, wide), 1) % (wide // 2) // (wide // 2 // g.H)
    grad_soft = jnp.zeros((g.H * g.I, g.N), F32)
    for k in range(g.SP):
        v = values[k * g.N : (k + 1) * g.N]
        crossed = mm(low, v)
        mixed = jnp.where(head == 0, crossed[: g.I], 0.0)
        for h in range(1, g.H):
            mixed = jnp.where(head == h, crossed[h * g.I : (h + 1) * g.I], mixed)
        rows = slice(k * g.I, (k + 1) * g.I)
        gg_ref[rows, :] = (gate_ref[rows, :] * mixed).astype(BF16)
        blended = gm_ref[rows, :]
        by_head = rows_of(
            [jnp.where(head == h, blended, jnp.zeros_like(blended)) for h in range(g.H)]
        )
        grad_soft = grad_soft + mm(by_head, v, NT)
        part = go_ref[k]
        for piece in split_high_low(mm(low_t, by_head)):
            part = part + mm(piece, value_weights, NT)
        total_ref[k] = part
    gs_ref[...] = grad_soft
    own = total_ref[:, pl.ds(g.place(row, col), g.I), :]
    gate_term = mm(gg_ref[...], gate_weight_ref[...], NT).reshape(g.SP, g.I, 2 * g.M)
    own_ref[...] = (own + gate_term + gl_ref[...]).reshape(g.SP * g.I, 2 * g.M)
    for x in range(1, g.R):
        block = total_ref[:, pl.ds(g.place(jnp.bitwise_xor(row, x), col), g.I), :]
        send_refs[x - 1][...] = block.reshape(g.SP * g.I, 2 * g.M).astype(BF16)


def pack_kernel(g, *refs):
    refs = list(refs)
    sums, refs = refs[: g.R - 1], refs[g.R - 1 :]
    parts, refs = refs[: g.C], refs[g.C :]
    outs, own_ref = refs[: g.R - 1], refs[g.R - 1]
    total = parts[0][...]
    for ref in parts[1:]:
        total = total + ref[...].astype(F32)
    total, rows = total.astype(BF16), g.SP * g.I
    own_ref[...] = total
    for x in range(1, g.R):
        outs[x - 1][:rows, :] = sums[x - 1][...]
        outs[x - 1][rows:, :] = total


def piece_kernel(g, own_ref, *refs):
    out_ref, order_ref = refs[-2:]
    row, rows = lax.axis_index("row"), g.SP * g.I
    order_ref[row] = own_ref[...]
    for k in range(1, g.R):
        order_ref[jnp.bitwise_xor(row, g.R - k)] = refs[k - 1][rows:, :]
    total = order_ref[0].astype(F32)
    for r in range(1, g.R):
        total = total + order_ref[r].astype(F32)
    out_ref[...] = total.astype(BF16)


def score_kernel(g, soft_ref, *refs):
    parts, refs = refs[: g.D], refs[g.D :]
    own_ref, out_refs, order_ref = refs[0], refs[1 : g.C], refs[g.C]
    depth = lax.axis_index("depth")
    for k in range(g.D):
        order_ref[lax.rem(depth - k + g.D, g.D)] = parts[k][...]
    grad_soft = order_ref[0]
    for k in range(1, g.D):
        grad_soft = grad_soft + order_ref[k]
    inner = jnp.sum(soft_ref[...] * grad_soft, -1, keepdims=True)
    for k in range(g.C):
        block = lanes_of([grad_soft[:, k * g.JC : (k + 1) * g.JC], inner])
        if k == 0:
            own_ref[...] = block
        else:
            out_refs[k - 1][...] = three_lanes(block)


def pair_kernel(g, e_ref, wl_ref, soft_ref, own_ref, *refs):
    got, pair_ref = refs[: g.C - 1], refs[g.C - 1]
    heads = g.H * g.I
    total = own_ref[...]
    for ref in got:
        total = total + join_three(ref[...], g.JC + 1)
    grad = soft_ref[:, : g.JC] * (total[:, : g.JC] - total[:, g.JC :])
    if g.JC < LANES:
        grad = lanes_of([grad, jnp.zeros((heads, LANES - g.JC), F32)])
    high, low = split_high_low(grad.T[: g.JC])
    grads = lanes_of([high, low])
    pick = (iota((heads, g.H), 0) // g.I == iota((heads, g.H), 1)).astype(BF16)
    base = mm(pick, wl_ref[...]).astype(BF16)
    token = iota((heads, 1), 0) % g.I
    for i in range(0, g.I, 2):
        weights = lanes_of(
            [jnp.where(token == i + k, base, jnp.zeros_like(base)) for k in range(2)]
        )
        upstream = mm(grads, rows_of([weights, weights]))
        for k in range(2):
            pair_ref[i + k] = standardize_backward(
                e_ref[i + k].astype(F32), upstream[:, k * g.Z : (k + 1) * g.Z]
            ).astype(BF16)


def reduce_kernel(g, x_ref, own_ref, *refs):
    got, out_ref = refs[:-1], refs[-1]
    rows = g.SP * g.I
    total = own_ref[...]
    for ref in got:
        total = total + ref[:rows, :].astype(F32)
    total = total.reshape(g.SP, 1, g.I, 2 * g.M)
    upstream = jnp.concatenate([total[..., : g.M], total[..., g.M :]], axis=1)
    upstream = upstream.reshape(g.S, g.I, g.M)[: g.SQ]
    msa = g.fill(standardize_backward(x_ref[...].astype(F32), upstream))
    msa = msa.reshape(g.SP, 2, g.I, g.M)
    msa = jnp.concatenate([msa[:, 0], msa[:, 1]], axis=-1).astype(BF16)
    out_ref[...] = msa.reshape(rows, 2 * g.M)


def ensemble_kernel(g, own_ref, *refs):
    got, msa_ref = refs[:-1], refs[-1]
    col = lax.axis_index("col")
    for k, ref in enumerate((own_ref, *got)):
        msa = ref[...].astype(F32).reshape(g.SP, 1, g.I, 2 * g.M)
        msa = jnp.concatenate([msa[..., : g.M], msa[..., g.M :]], axis=1)
        msa = msa.reshape(g.S, g.I, g.M)[: g.SQ].astype(BF16)
        msa_ref[pl.ds(lax.rem(col - k + g.C, g.C) * g.SQ, g.SQ)] = msa


def across_kernel(g, *refs):
    out_ref = refs[-1]
    col = lax.axis_index("col")
    for k, ref in enumerate(refs[:-1]):
        out_ref[lax.rem(col - k + g.C, g.C)] = ref[...]


def matrix_kernel(g, *refs):
    parts, out_ref = refs[: g.D], refs[g.D]
    depth = lax.axis_index("depth")
    for k in range(g.D):
        out_ref[lax.rem(depth - k + g.D, g.D)] = parts[k][...].astype(F32)


class Sizes:
    def __init__(self, x, e, wl, w1):
        self.R, self.C, self.D = (lax.axis_size(a) for a in ("row", "col", "depth"))
        self.I, self.M = x.shape[1:]
        self.JC, self.Z = e.shape[1:]
        self.H, self.Q = wl.shape[1], w1.shape[1]
        self.SQ = x.shape[0] // self.C
        self.S = -(-self.SQ // 16) * 16
        self.SP, self.N = self.S // 2, self.R * self.I
        self.F = self.R // self.C
        self.NT = -(-self.N // LANES)
        self.G = max(1, LANES // self.JC)
        self.carried = 0
        self.order = [*range(1, self.R // 2), *range(self.R // 2 + 1, self.R), self.R // 2]

    def fill(self, rows):
        if self.SQ == self.S:
            return rows
        return rows_of([rows, jnp.zeros((self.S - self.SQ, *rows.shape[1:]), rows.dtype)])

    def place(self, row, col):
        turn = lax.rem(row // self.F - col + self.C, self.C)
        return pl.multiple_of((turn * self.F + lax.rem(row, self.F)) * self.I, self.I)


def shift(array, axis, k):
    count = lax.axis_size(axis)
    return lax.ppermute(array, axis, [(i, (i + k) % count) for i in range(count)])


def swap(array, axis, x):
    return lax.ppermute(array, axis, [(i, i ^ x) for i in range(lax.axis_size(axis))])


def swapped(arrays, axis):
    return [swap(a, axis, k + 1) for k, a in reversed([*enumerate(arrays)])]


def shifted_all(array, axis):
    return [array] + [shift(array, axis, k) for k in range(1, lax.axis_size(axis))]


def per_device(
    homolog_ensemble,
    duplex_embedding,
    homolog_present_flags,
    resolved_position_flags,
    payload_weights,
    sigmoid_weights,
    averager_final_weights,
    first_operand_weights,
    second_operand_weights,
    duplex_logit_weights,
    tensor_product_weights,
    averager_upstream_adjoint,
    duplex_upstream_adjoint,
):
    g = Sizes(homolog_ensemble, duplex_embedding, duplex_logit_weights, first_operand_weights)
    shape = jax.ShapeDtypeStruct

    def call(kernel, name, args, outs, scratch=(), far=None, after=(), distant=False, us=1.0):
        size = sum(a.size * a.dtype.itemsize for a in args) + sum(
            math.prod(o.shape) * jnp.dtype(o.dtype).itemsize for o in outs
        )
        single = len(outs) == 1
        near = len(args) if far is None else far
        args = list(args[:near]) + [
            pltpu.with_memory_space_constraint(a, pltpu.HBM) for a in args[near:]
        ]

        if distant:
            after = [pltpu.with_memory_space_constraint(a, pltpu.HBM) for a in after]

        def body(*refs):
            kernel(g, *refs[: len(args)], *refs[len(args) + len(after) :])

        return pl.pallas_call(
            body,
            out_shape=outs[0] if single else tuple(outs),
            in_specs=[VMEM] * near + [FAR] * (len(args) - near) + [FAR if distant else VMEM] * len(after),
            out_specs=VMEM if single else (VMEM,) * len(outs),
            scratch_shapes=list(scratch),
            compiler_params=pltpu.CompilerParams(vmem_limit_bytes=40 * 1024 * 1024),
            cost_estimate=pl.CostEstimate(
                flops=int(us * 1.15e9), bytes_accessed=size, transcendentals=0
            ),
            name=name,
        )(*args, *after)

    heads = g.H * g.I
    rows = g.SP * g.I
    values = 2 * payload_weights.shape[1]
    pairs, tall = g.I * g.JC, heads // g.G
    xn, logits, near, x, e, wl = call(
        normalise_kernel,
        "normalise",
        (
            homolog_ensemble,
            duplex_embedding,
            duplex_upstream_adjoint.reshape(pairs, g.Z),
            resolved_position_flags.reshape(1, g.JC),
            duplex_logit_weights.T,
        ),
        [
            pltpu.VMEM((g.SP, g.I, 2 * g.M), BF16),
            pltpu.VMEM((tall, g.G * g.JC), F32),
            pltpu.VMEM((pairs + 3 * tall, g.Z), BF16),
            pltpu.VMEM((g.SQ, g.I, g.M), BF16),
            pltpu.VMEM(duplex_embedding.shape, BF16),
            pltpu.VMEM((g.H, g.Z), BF16),
        ],
        [
            pltpu.VMEM((1, g.JC), jnp.int32),
            pltpu.VMEM((g.I * g.H, LANES), F32),
            pltpu.SemaphoreType.DMA((5,)),
        ],
        far=0,
        us=2.0,
    )
    everyone = [xn] + [swap(xn, "row", k) for k in g.order]
    nears = shifted_all(near, "col")
    later = (
        sigmoid_weights,
        averager_final_weights.T,
        first_operand_weights.T,
        tensor_product_weights,
        payload_weights,
        second_operand_weights.T,
    )
    g.carried = len(later)
    prepared = call(
        prepare_kernel,
        "prepare",
        (xn, homolog_present_flags, averager_upstream_adjoint, *later),
        [
            pltpu.VMEM((g.SP + 8, 2 * g.M), F32),
            pltpu.VMEM((2 * g.M, values), BF16),
            pltpu.VMEM((rows, values), BF16),
            pltpu.VMEM((rows, values), F32),
            pltpu.VMEM((g.I * g.S, g.Q), BF16),
            pltpu.VMEM((g.Q, g.Q, g.Z), BF16),
            pltpu.VMEM((g.I, g.Q * g.S, g.Z), BF16),
        ]
        + [pltpu.VMEM(a.shape, a.dtype) for a in later],
        [
            pltpu.SMEM(homolog_present_flags.shape, jnp.int32),
            pltpu.VMEM((g.SQ, g.I, g.M), BF16),
            pltpu.VMEM(tensor_product_weights.shape, F32),
            pltpu.VMEM((2, rows, LANES), F32),
            pltpu.SemaphoreType.DMA((2,)),
            pltpu.SemaphoreType.DMA((len(later),)),
        ],
        far=1,
        after=nears[1:],
        us=3.0,
    )
    masks, gate_weights, blended, gate_factor, left, weights, left_weights = prepared[:7]
    _, _, w1, _, p, w2 = prepared[7:]
    share = g.Q * g.Q // g.D
    xall, cotangents, products, *matrix_parts = call(
        outer_kernel,
        "outer",
        (*everyone, *nears, left, w2, masks),
        [
            pltpu.VMEM((g.SP, g.N, 2 * g.M), BF16),
            pltpu.VMEM((g.I, g.N, g.Z), BF16),
            pltpu.VMEM((g.Q, g.I, g.S, g.Z), BF16),
        ]
        + [pltpu.VMEM((share, g.Z), F32)] * g.D,
        [
            pltpu.VMEM((g.NT, g.SP * 2 * g.Q, LANES), F32),
            pltpu.VMEM((g.Q * g.S, g.N), BF16),
            pltpu.VMEM((g.Q * g.Q, g.Z), F32),
        ],
        us=0.05,
    )
    matrix_parts = [matrix_parts[0]] + [
        shift(a, "depth", k + 1) for k, a in enumerate(matrix_parts[1:])
    ]
    second_term, first_term = call(
        factors_kernel,
        "factors",
        (cotangents, products, left_weights, weights, w1, w2, masks),
        [pltpu.VMEM((g.SP, g.N, 2 * g.M), F32), pltpu.VMEM((g.SP, g.I, 2 * g.M), F32)],
        [pltpu.VMEM((g.NT, g.Q * g.S, LANES), F32), pltpu.VMEM((g.I * g.S, 2 * g.M), F32)],
        us=1.8,
    )
    share //= g.C
    matrix_parts = call(
        half_sum_kernel,
        "half_sum",
        matrix_parts,
        [pltpu.VMEM((share, g.Z), F32)] + [pltpu.VMEM((share, g.Z), BF16)] * (g.C - 1),
        [pltpu.VMEM((share * g.C, g.Z), F32)],
        after=(second_term,),
        us=0.2,
    )
    matrix_parts = [matrix_parts[0]] + [
        shift(a, "col", k + 1) for k, a in enumerate(matrix_parts[1:])
    ]
    soft, grad_soft, own, *sums = call(
        attend_kernel,
        "attend",
        (xall, logits, *nears[1:], blended, gate_factor, p, gate_weights, second_term, first_term),
        [
            pltpu.VMEM((heads, g.N), F32),
            pltpu.VMEM((heads, g.N), F32),
            pltpu.VMEM((rows, 2 * g.M), F32),
        ]
        + [pltpu.VMEM((rows, 2 * g.M), BF16)] * (g.R - 1),
        [pltpu.VMEM((g.SP, g.N, 2 * g.M), F32), pltpu.VMEM((rows, values), BF16)],
        us=3.0,
    )
    *sums, piece = call(
        pack_kernel,
        "pack",
        (*sums, *matrix_parts),
        [pltpu.VMEM((rows + share, 2 * g.M), BF16)] * (g.R - 1) + [pltpu.VMEM((share, g.Z), BF16)],
        us=0.2,
    )
    sums = swapped(sums, "row")
    wide = -(-3 * (g.JC + 1) // LANES) * LANES
    scores, *sends = call(
        score_kernel,
        "score",
        (soft, *shifted_all(grad_soft, "depth")),
        [pltpu.VMEM((heads, g.JC + 1), F32)] + [pltpu.VMEM((heads, wide), BF16)] * (g.C - 1),
        [pltpu.VMEM((g.D, heads, g.N), F32)],
        after=(piece,),
        us=0.2,
    )
    arrived = [shift(a, "col", k + 1) for k, a in enumerate(sends)]
    piece = call(
        piece_kernel,
        "piece",
        (piece, *sums),
        [pltpu.VMEM((share, g.Z), BF16)],
        [pltpu.VMEM((g.R, share, g.Z), BF16)],
        after=(scores,),
        us=0.1,
    )
    pieces = shifted_all(piece, "col")
    part = call(
        reduce_kernel,
        "reduce",
        (x, own, *sums),
        [pltpu.VMEM((rows, 2 * g.M), BF16)],
        after=(piece,),
    )
    pairwise_gradient = call(
        pair_kernel,
        "pair",
        (e, wl, soft, scores, *arrived),
        [shape(duplex_embedding.shape, BF16)],
        after=(part,),
        us=1.8,
    )
    matrix = call(
        across_kernel,
        "across",
        pieces,
        [pltpu.VMEM((g.C, share, g.Z), BF16)],
        after=(pairwise_gradient,),
        distant=True,
        us=0.1,
    ).reshape(g.C * share, g.Z)
    ensemble_derivative = call(
        ensemble_kernel,
        "ensemble",
        shifted_all(part, "col"),
        [shape(homolog_ensemble.shape, BF16)],
        after=(matrix,),
    )
    outer_matrix_gradient = call(
        matrix_kernel,
        "matrix",
        shifted_all(matrix, "depth"),
        [shape((g.D, g.C * share, g.Z), F32)],
        after=(ensemble_derivative,),
        distant=True,
    ).reshape(tensor_product_weights.shape)
    return (ensemble_derivative, pairwise_gradient, outer_matrix_gradient)


def solution(mesh):
    in_specs = (
        P(("parts", "depth"), "row", None),
        P(("parts", "row"), "col", None),
        P("parts"),
        P(("parts", "col")),
        P(),
        P(),
        P(),
        P(),
        P(),
        P(),
        P(),
        P(("parts", "depth"), "row", None),
        P(("parts", "row"), "col", None),
    )
    out_specs = (
        P(("parts", "depth"), "row", None),
        P(("parts", "row"), "col", None),
        P("parts", None),
    )
    return jax.shard_map(
        per_device, mesh=mesh, in_specs=in_specs, out_specs=out_specs, check_vma=False
    )
```

```python
import functools
import math

import jax
import jax.numpy as jnp
from jax import lax
from jax.experimental import pallas as pl
from jax.experimental.pallas import tpu as pltpu
from jax.sharding import PartitionSpec as P

EPS = 1e-05
PENALTY = 10000.0
F32 = jnp.float32
BF16 = jnp.bfloat16
LANES = 128
NN = (((1,), (0,)), ((), ()))
NT = (((1,), (1,)), ((), ()))
VMEM = pl.BlockSpec(memory_space=pltpu.VMEM)
FAR = pl.BlockSpec(memory_space=pl.ANY)


def mm(a, b, dims=NN):
    return lax.dot_general(a, b, dims, preferred_element_type=F32)


def split_high_low(value):
    high = value.astype(BF16)
    return high, (value - high.astype(F32)).astype(BF16)


def iota(shape, dim):
    return lax.broadcasted_iota(jnp.int32, shape, dim)


def lanes_of(pieces):
    return pieces[0] if len(pieces) == 1 else jnp.concatenate(pieces, axis=-1)


def rows_of(pieces):
    return pieces[0] if len(pieces) == 1 else jnp.concatenate(pieces, axis=0)


def standardize(values):
    centred = values - jnp.mean(values, -1, keepdims=True)
    inverse = lax.rsqrt(jnp.mean(centred * centred, -1, keepdims=True) + EPS)
    return centred * inverse, inverse


def standardize_backward(values, upstream):
    scaled, inverse = standardize(values)
    mean_grad = jnp.mean(upstream, -1, keepdims=True)
    mean_cross = jnp.mean(upstream * scaled, -1, keepdims=True)
    return (upstream - mean_grad - scaled * mean_cross) * inverse


def on_diagonal(block, width):
    rows, lanes = block.shape
    same = iota(block.shape, 0) // (rows // 2) == iota(block.shape, 1) // width
    return jnp.where(same, block, jnp.zeros_like(block))


def split_three(value):
    high = value.astype(BF16)
    rest = value - high.astype(F32)
    middle = rest.astype(BF16)
    return [high, middle, (rest - middle.astype(F32)).astype(BF16)]


def three_lanes(value):
    rows, width = value.shape
    fill = -(3 * width) % LANES
    return lanes_of(split_three(value) + [jnp.zeros((rows, fill), BF16)] * (fill > 0))


def join_three(parts, width):
    wide = parts.astype(F32)
    return (wide[:, :width] + wide[:, width : 2 * width]) + wide[:, 2 * width : 3 * width]


def twice(weights):
    zero = jnp.zeros_like(weights)
    return rows_of([lanes_of([weights, zero]), lanes_of([zero, weights])])


def normalise_kernel(g, x_hbm, e_hbm, dd_hbm, flag_hbm, wl_hbm, *refs):
    xn_ref, logit_ref, near_ref, x_ref, e_ref, wl_ref, flag_in, rows_ref, sem = refs
    first = lax.axis_index("col") * g.SQ
    pairs = g.I * g.JC
    copies = [
        pltpu.make_async_copy(a, b, sem.at[k])
        for k, (a, b) in enumerate(
            [
                (x_hbm.at[pl.ds(first, g.SQ)], x_ref),
                (e_hbm, e_ref),
                (wl_hbm, wl_ref),
                (flag_hbm, flag_in),
                (dd_hbm, near_ref.at[pl.ds(0, pairs)]),
            ]
        )
    ]
    for copy in copies:
        copy.start()
    copies[0].wait()
    normed = g.fill(standardize(x_ref[...].astype(F32))[0]).reshape(g.SP, 2, g.I, g.M)
    xn_ref[...] = jnp.concatenate([normed[:, 0], normed[:, 1]], axis=-1).astype(BF16)
    for copy in copies[1:4]:
        copy.wait()
    pair = standardize(e_ref[...].astype(F32).reshape(pairs, g.Z))[0].astype(BF16)
    penalty = (flag_in[...].astype(F32) - 1.0) * PENALTY
    weights = wl_ref[...]
    for i in range(g.I):
        rows_ref[i * g.H : (i + 1) * g.H, : g.JC] = (
            mm(weights, pair[i * g.JC : (i + 1) * g.JC], NT) + penalty
        )
    logits = rows_of([rows_ref[pl.ds(h, g.I, stride=g.H), :][:, : g.JC] for h in range(g.H)])
    tall = g.H * g.I // g.G
    packed = lanes_of([logits[k * tall : (k + 1) * tall] for k in range(g.G)])
    logit_ref[...] = packed
    near_ref[pairs:, :] = rows_of(split_three(packed))
    copies[4].wait()


def prepare_kernel(g, xn_ref, live_ref, w1_hbm, t_hbm, *refs):
    mask_ref, left_ref, ts_ref, lt_ref, w1_ref, live_in, t_ref, wide_ref, half_ref, sem = refs
    col, depth = lax.axis_index("col"), lax.axis_index("depth")
    copies = [
        pltpu.make_async_copy(a, b, sem.at[k])
        for k, (a, b) in enumerate([(live_ref, live_in), (w1_hbm, w1_ref), (t_hbm, t_ref)])
    ]
    for copy in copies:
        copy.start()
    for copy in copies:
        copy.wait()
    first = depth * g.C * g.SQ + col * g.SQ
    lane = iota((1, 2 * g.M), 1)
    masks = []
    for k in range(g.SP):
        if 2 * k + 1 < g.SQ:
            flags = jnp.where(lane < g.M, live_in[first + 2 * k], live_in[first + 2 * k + 1])
            masks.append(flags.astype(F32))
        else:
            masks.append(jnp.zeros((1, 2 * g.M), F32))
        mask_ref[k : k + 1, :] = masks[-1]
    total = live_in[0]
    for s in range(1, live_in.shape[0]):
        total = total + live_in[s]
    mask_ref[g.SP : g.SP + 1, :] = 1.0 / (0.001 + jnp.full((1, 2 * g.M), total, jnp.int32).astype(F32))
    xn = xn_ref[...]
    live_xn = rows_of([(xn[k].astype(F32) * masks[k]).astype(BF16) for k in range(g.SP)])
    w1 = rows_of([w1_ref[...], jnp.zeros((LANES - g.Q, g.M), BF16)])
    zero = jnp.zeros_like(w1)
    half_ref[0] = mm(live_xn, lanes_of([w1, zero]), NT)
    half_ref[1] = mm(live_xn, lanes_of([zero, w1]), NT)
    for i in range(g.I):
        halves = [half_ref[half, pl.ds(i, g.SP, stride=g.I), :] for half in range(2)]
        left_ref[i * g.S : (i + 1) * g.S, :] = rows_of(halves)[:, : g.Q].astype(BF16)
    wide_ref[...] = t_ref[...].astype(F32)
    for q in range(g.Q):
        ts_ref[q] = wide_ref[pl.ds(q, g.Q, stride=g.Q), :].astype(BF16)
    left = left_ref[...]
    for q in range(0, g.Q, 2):
        product = mm(left, lanes_of([ts_ref[q], ts_ref[q + 1]]))
        for k in range(2):
            block = product[:, k * g.Z : (k + 1) * g.Z].reshape(g.I, g.S, g.Z)
            lt_ref[:, (q + k) * g.S : (q + k + 1) * g.S, :] = block.astype(BF16)


def gate_kernel(g, xn_ref, u_ref, *refs):
    refs = list(refs)
    count = g.carried
    sources, refs = refs[:count], refs[count:]
    gate_weight_ref, gm_ref, gate_ref, refs = refs[0], refs[1], refs[2], refs[3:]
    targets, (u_in, first_sem, later_sem) = refs[:count], refs[count:]
    first = lax.axis_index("col") * g.SQ
    copies = [pltpu.make_async_copy(u_ref.at[pl.ds(first, g.SQ)], u_in, first_sem)]
    copies += [
        pltpu.make_async_copy(a, b, later_sem.at[k])
        for k, (a, b) in enumerate(zip(sources, targets, strict=True))
    ]
    for copy in copies:
        copy.start()
    for copy in copies:
        copy.wait()
    sg_ref, wf_ref = targets[:2]
    rows = g.SP * g.I
    xn = xn_ref[...]
    gate_weights = twice(sg_ref[...])
    gate_weight_ref[...] = gate_weights
    gates = jax.nn.sigmoid(mm(xn.reshape(rows, 2 * g.M), gate_weights))
    u = g.fill(u_in[...]).reshape(g.SP, 2, g.I, g.M)
    packed_u = jnp.concatenate([u[:, 0], u[:, 1]], axis=-1).reshape(rows, 2 * g.M)
    gated = mm(packed_u, twice(wf_ref[...]))
    blended = gated * gates
    gm_ref[...] = blended.astype(BF16)
    gate_ref[...] = blended * (1.0 - gates)


def outer_kernel(g, *refs):
    refs = list(refs)
    x_refs, refs = refs[: g.R], refs[g.R :]
    d_refs, refs = refs[: g.C], refs[g.C :]
    left_ref, w2_ref, mask_ref, xall_ref, d_ref, ds_ref, *refs = refs
    w_refs, (spread_ref, rt_ref, all_ref) = refs[: g.D], refs[g.D :]
    row, col, depth = (lax.axis_index(a) for a in ("row", "col", "depth"))
    masks = [mask_ref[k : k + 1, :] for k in range(g.SP)]
    scale = mask_ref[g.SP : g.SP + 1, :]
    for k, ref in zip((0, *g.order), x_refs, strict=True):
        place = g.place(jnp.bitwise_xor(row, k), col)
        xall_ref[:, pl.ds(place, g.I), :] = ref[...]
    for k in range(g.C):
        spot = (g.C - k) % g.C
        block = d_refs[k][: g.I * g.JC, :].reshape(g.I, g.JC, g.Z)
        d_ref[:, spot * g.JC : (spot + 1) * g.JC, :] = block
    w2 = w2_ref[...]
    doubled = lanes_of([w2, w2])
    second = on_diagonal(rows_of([doubled, doubled]), g.M)
    for k in range(g.SP):
        live_x = (xall_ref[k].astype(F32) * masks[k]).astype(BF16)
        part = mm(second, live_x, NT)
        for t in range(g.NT):
            lanes = min(LANES, g.N - t * LANES)
            spread_ref[t, k * 2 * g.Q : (k + 1) * 2 * g.Q, :lanes] = part[
                :, t * LANES : t * LANES + lanes
            ]
    for q in range(g.Q):
        for t in range(g.NT):
            lanes = min(LANES, g.N - t * LANES)
            halves = [
                spread_ref[t, pl.ds(half * g.Q + q, g.SP, stride=2 * g.Q), :] for half in range(2)
            ]
            rt_ref[q * g.S : (q + 1) * g.S, t * LANES : t * LANES + lanes] = rows_of(halves)[
                :, :lanes
            ].astype(BF16)
    rt = rt_ref[...]
    for i in range(0, g.I, 2):
        product = mm(rt, lanes_of([d_ref[i], d_ref[i + 1]]))
        for k in range(2):
            block = product[:, k * g.Z : (k + 1) * g.Z]
            ds_ref[:, i + k] = block.reshape(g.Q, g.S, g.Z).astype(BF16)
    left = left_ref[...]
    eye = (iota((g.Q, g.Q), 0) == iota((g.Q, g.Q), 1)).astype(BF16)
    left_t = mm(eye, left, NT).astype(BF16)
    entries = g.S * g.I
    for q in range(0, g.Q, 2):
        both = lanes_of([ds_ref[q].reshape(entries, g.Z), ds_ref[q + 1].reshape(entries, g.Z)])
        part = mm(left_t, both)
        all_ref[pl.ds(q, g.Q, stride=g.Q), :] = part[:, : g.Z] * scale
        all_ref[pl.ds(q + 1, g.Q, stride=g.Q), :] = part[:, g.Z :] * scale
    share = g.Q * g.Q // g.D
    for k in range(g.D):
        first = pl.multiple_of(lax.rem(depth + k, g.D) * share, share)
        w_refs[k][...] = all_ref[pl.ds(first, share), :]


def right_kernel(g, d_ref, lt_ref, w2_ref, mask_ref, go_ref, rg_ref):
    masks = [mask_ref[k : k + 1, :] for k in range(g.SP)]
    scale = mask_ref[g.SP : g.SP + 1, :]
    right_grad = jnp.zeros((g.Q * g.S, g.N), F32)
    for i in range(0, g.I, 2):
        right_grad = right_grad + mm(
            lanes_of([lt_ref[i], lt_ref[i + 1]]), lanes_of([d_ref[i], d_ref[i + 1]]), NT
        )
    for t in range(g.NT):
        lanes = min(LANES, g.N - t * LANES)
        piece = right_grad[:, t * LANES : t * LANES + lanes]
        if lanes < LANES:
            piece = lanes_of([piece, jnp.zeros((g.Q * g.S, LANES - lanes), F32)])
        rg_ref[t] = piece
    deep = 2 * g.Q
    group = min(g.SP, LANES // deep)
    which = iota((group * deep, g.Q), 0)
    pick = (iota((group * deep, g.Q), 1) == which % deep // 2).astype(BF16)
    w2 = w2_ref[...]
    base = mm(pick, lanes_of([w2, w2]))
    which = iota(base.shape, 0)
    base = jnp.where(which % 2 == iota(base.shape, 1) // g.M, base, 0.0)
    weights = lanes_of([jnp.where(which // deep == k, base, 0.0) for k in range(group)]).astype(BF16)
    for k in range(0, g.SP, group):
        for t in range(g.NT):
            lanes = min(LANES, g.N - t * LANES)
            tall = rows_of(
                [rg_ref[t, pl.ds(k + m, deep, stride=g.SP), :] for m in range(group)]
            )
            tall = (tall * scale).T[:lanes]
            high, low = split_high_low(tall)
            part = mm(high, weights) + mm(low, weights)
            for m in range(group):
                go_ref[k + m, t * LANES : t * LANES + lanes, :] = (
                    part[:, m * 2 * g.M : (m + 1) * 2 * g.M] * masks[k + m]
                )


def own_kernel(
    g, ds_ref, ts_ref, w1_ref, mask_ref, part_ref, gg_ref, gate_weight_ref, own_ref, turn_ref
):
    scale = mask_ref[g.SP : g.SP + 1, :]
    entries = g.S * g.I
    left_grad = jnp.zeros((entries, g.Q), F32)
    for q in range(0, g.Q, 2):
        both = lanes_of([ds_ref[q].reshape(entries, g.Z), ds_ref[q + 1].reshape(entries, g.Z)])
        left_grad = left_grad + mm(both, lanes_of([ts_ref[q], ts_ref[q + 1]]), NT)
    w1 = w1_ref[...]
    first_term = jnp.zeros((entries, 2 * g.M), F32)
    for piece in split_high_low(left_grad * scale[:, : g.Q]):
        first_term = first_term + mm(piece, lanes_of([w1, w1]))
    turn_ref[...] = first_term
    gate_term = mm(gg_ref[...], gate_weight_ref[...], NT)
    lane = iota((1, 2 * g.M), 1)
    for k in range(g.SP):
        rows = slice(k * g.I, (k + 1) * g.I)
        halves = [turn_ref[pl.ds(half * g.SP + k, g.I, stride=g.S), :] for half in range(2)]
        term = jnp.where(lane < g.M, halves[0], halves[1]) * mask_ref[k : k + 1, :]
        own_ref[rows, :] = part_ref[rows, :] + gate_term[rows] + term


def half_sum_kernel(g, *refs):
    parts, outs, total_ref = refs[: g.D], refs[g.D : g.D + g.C], refs[-1]
    total = parts[0][...]
    for ref in parts[1:]:
        total = total + ref[...]
    total_ref[...] = total
    share = total.shape[0] // g.C
    col = lax.axis_index("col")
    for k in range(g.C):
        first = pl.multiple_of(lax.rem(col + k, g.C) * share, share)
        outs[k][...] = total_ref[pl.ds(first, share), :].astype(outs[k].dtype)


def attend_kernel(g, *refs):
    refs = list(refs)
    xall_ref, refs = refs[0], refs[1:]
    logit_ref, near_refs, refs = refs[0], refs[1 : g.C], refs[g.C :]
    gm_ref, gate_ref, p_ref, go_ref, soft_ref, gs_ref, own_ref, gg_ref, *refs = refs
    send_refs, (total_ref,) = refs[: g.R - 1], refs[g.R - 1 :]
    row, col = lax.axis_index("row"), lax.axis_index("col")
    tall, blocks = logit_ref.shape[0], [logit_ref[...]]
    for k in range(1, g.C):
        parts = near_refs[g.C - k - 1][g.I * g.JC :, :].astype(F32)
        blocks.append((parts[:tall] + parts[tall : 2 * tall]) + parts[2 * tall :])
    logits = lanes_of(
        [rows_of([b[:, k * g.JC : (k + 1) * g.JC] for k in range(g.G)]) for b in blocks]
    )
    shifted = jnp.exp(logits - jnp.max(logits, -1, keepdims=True))
    soft = shifted / jnp.sum(shifted, -1, keepdims=True)
    soft_ref[...] = soft
    low = soft.astype(BF16)
    eye = (iota((g.N, g.N), 0) == iota((g.N, g.N), 1)).astype(BF16)
    low_t = mm(eye, low, NT).astype(BF16)
    value_weights = twice(p_ref[...])
    values = mm(xall_ref[...].reshape(g.SP * g.N, 2 * g.M), value_weights).astype(BF16)
    wide = value_weights.shape[1]
    head = iota((1, wide), 1) % (wide // 2) // (wide // 2 // g.H)
    grad_soft = jnp.zeros((g.H * g.I, g.N), F32)
    for k in range(g.SP):
        v = values[k * g.N : (k + 1) * g.N]
        crossed = mm(low, v)
        mixed = jnp.where(head == 0, crossed[: g.I], 0.0)
        for h in range(1, g.H):
            mixed = jnp.where(head == h, crossed[h * g.I : (h + 1) * g.I], mixed)
        rows = slice(k * g.I, (k + 1) * g.I)
        gg_ref[rows, :] = (gate_ref[rows, :] * mixed).astype(BF16)
        blended = gm_ref[rows, :]
        by_head = rows_of(
            [jnp.where(head == h, blended, jnp.zeros_like(blended)) for h in range(g.H)]
        )
        grad_soft = grad_soft + mm(by_head, v, NT)
        part = go_ref[k]
        for piece in split_high_low(mm(low_t, by_head)):
            part = part + mm(piece, value_weights, NT)
        total_ref[k] = part
    gs_ref[...] = grad_soft
    own = total_ref[:, pl.ds(g.place(row, col), g.I), :]
    own_ref[...] = own.reshape(g.SP * g.I, 2 * g.M)
    for x in range(1, g.R):
        block = total_ref[:, pl.ds(g.place(jnp.bitwise_xor(row, x), col), g.I), :]
        send_refs[x - 1][...] = block.reshape(g.SP * g.I, 2 * g.M).astype(BF16)


def pack_kernel(g, *refs):
    refs = list(refs)
    sums, refs = refs[: g.R - 1], refs[g.R - 1 :]
    parts, refs = refs[: g.C], refs[g.C :]
    outs, own_ref = refs[: g.R - 1], refs[g.R - 1]
    total = parts[0][...]
    for ref in parts[1:]:
        total = total + ref[...].astype(F32)
    total, rows = total.astype(BF16), g.SP * g.I
    own_ref[...] = total
    for x in range(1, g.R):
        outs[x - 1][:rows, :] = sums[x - 1][...]
        outs[x - 1][rows:, :] = total


def piece_kernel(g, own_ref, *refs):
    out_ref, order_ref = refs[-2:]
    row, rows = lax.axis_index("row"), g.SP * g.I
    order_ref[row] = own_ref[...]
    for k in range(1, g.R):
        order_ref[jnp.bitwise_xor(row, g.R - k)] = refs[k - 1][rows:, :]
    total = order_ref[0].astype(F32)
    for r in range(1, g.R):
        total = total + order_ref[r].astype(F32)
    out_ref[...] = total.astype(BF16)


def score_kernel(g, soft_ref, *refs):
    parts, refs = refs[: g.D], refs[g.D :]
    own_ref, out_refs, order_ref = refs[0], refs[1 : g.C], refs[g.C]
    depth = lax.axis_index("depth")
    for k in range(g.D):
        order_ref[lax.rem(depth - k + g.D, g.D)] = parts[k][...]
    grad_soft = order_ref[0]
    for k in range(1, g.D):
        grad_soft = grad_soft + order_ref[k]
    inner = jnp.sum(soft_ref[...] * grad_soft, -1, keepdims=True)
    for k in range(g.C):
        block = lanes_of([grad_soft[:, k * g.JC : (k + 1) * g.JC], inner])
        if k == 0:
            own_ref[...] = block
        else:
            out_refs[k - 1][...] = three_lanes(block)


def pair_kernel(g, e_ref, wl_ref, soft_ref, own_ref, *refs):
    got, pair_ref = refs[: g.C - 1], refs[g.C - 1]
    heads = g.H * g.I
    total = own_ref[...]
    for ref in got:
        total = total + join_three(ref[...], g.JC + 1)
    grad = soft_ref[:, : g.JC] * (total[:, : g.JC] - total[:, g.JC :])
    if g.JC < LANES:
        grad = lanes_of([grad, jnp.zeros((heads, LANES - g.JC), F32)])
    high, low = split_high_low(grad.T[: g.JC])
    grads = lanes_of([high, low])
    pick = (iota((heads, g.H), 0) // g.I == iota((heads, g.H), 1)).astype(BF16)
    base = mm(pick, wl_ref[...]).astype(BF16)
    token = iota((heads, 1), 0) % g.I
    for i in range(0, g.I, 2):
        weights = lanes_of(
            [jnp.where(token == i + k, base, jnp.zeros_like(base)) for k in range(2)]
        )
        upstream = mm(grads, rows_of([weights, weights]))
        for k in range(2):
            pair_ref[i + k] = standardize_backward(
                e_ref[i + k].astype(F32), upstream[:, k * g.Z : (k + 1) * g.Z]
            ).astype(BF16)


def reduce_kernel(g, x_ref, own_ref, *refs):
    got, out_ref = refs[:-1], refs[-1]
    rows = g.SP * g.I
    total = own_ref[...]
    for ref in got:
        total = total + ref[:rows, :].astype(F32)
    total = total.reshape(g.SP, 1, g.I, 2 * g.M)
    upstream = jnp.concatenate([total[..., : g.M], total[..., g.M :]], axis=1)
    upstream = upstream.reshape(g.S, g.I, g.M)[: g.SQ]
    msa = g.fill(standardize_backward(x_ref[...].astype(F32), upstream))
    msa = msa.reshape(g.SP, 2, g.I, g.M)
    msa = jnp.concatenate([msa[:, 0], msa[:, 1]], axis=-1).astype(BF16)
    out_ref[...] = msa.reshape(rows, 2 * g.M)


def across_kernel(g, *refs):
    out_ref = refs[-1]
    col = lax.axis_index("col")
    for k, ref in enumerate(refs[:-1]):
        out_ref[lax.rem(col - k + g.C, g.C)] = ref[...]


def unpack_kernel(g, *refs):
    parts, msa_ref = refs[: g.C], refs[g.C]
    col = lax.axis_index("col")
    for k, ref in enumerate(parts):
        msa = ref[...].astype(F32).reshape(g.SP, 1, g.I, 2 * g.M)
        msa = jnp.concatenate([msa[..., : g.M], msa[..., g.M :]], axis=1)
        msa = msa.reshape(g.S, g.I, g.M)[: g.SQ].astype(BF16)
        msa_ref[pl.ds(lax.rem(col - k + g.C, g.C) * g.SQ, g.SQ)] = msa


def finish_kernel(g, msa_ref, *refs):
    parts, (out_ref, matrix_ref) = refs[: g.D], refs[g.D :]
    depth = lax.axis_index("depth")
    out_ref[...] = msa_ref[...]
    for k in range(g.D):
        matrix_ref[lax.rem(depth - k + g.D, g.D)] = parts[k][...].astype(F32)


class Sizes:
    def __init__(self, x, e, wl, w1):
        self.R, self.C, self.D = (lax.axis_size(a) for a in ("row", "col", "depth"))
        self.I, self.M = x.shape[1:]
        self.JC, self.Z = e.shape[1:]
        self.H, self.Q = wl.shape[1], w1.shape[1]
        self.SQ = x.shape[0] // self.C
        self.S = -(-self.SQ // 16) * 16
        self.SP, self.N = self.S // 2, self.R * self.I
        self.F = self.R // self.C
        self.NT = -(-self.N // LANES)
        self.G = max(1, LANES // self.JC)
        self.carried = 0
        self.order = [*range(1, self.R // 2), *range(self.R // 2 + 1, self.R), self.R // 2]

    def fill(self, rows):
        if self.SQ == self.S:
            return rows
        return rows_of([rows, jnp.zeros((self.S - self.SQ, *rows.shape[1:]), rows.dtype)])

    def place(self, row, col):
        turn = lax.rem(row // self.F - col + self.C, self.C)
        return pl.multiple_of((turn * self.F + lax.rem(row, self.F)) * self.I, self.I)


def shift(array, axis, k):
    count = lax.axis_size(axis)
    return lax.ppermute(array, axis, [(i, (i + k) % count) for i in range(count)])


def swap(array, axis, x):
    return lax.ppermute(array, axis, [(i, i ^ x) for i in range(lax.axis_size(axis))])


def swapped(arrays, axis):
    return [swap(a, axis, k + 1) for k, a in reversed([*enumerate(arrays)])]


def shifted_all(array, axis):
    return [array] + [shift(array, axis, k) for k in range(1, lax.axis_size(axis))]


def per_device(
    homolog_ensemble,
    duplex_embedding,
    homolog_present_flags,
    resolved_position_flags,
    payload_weights,
    sigmoid_weights,
    averager_final_weights,
    first_operand_weights,
    second_operand_weights,
    duplex_logit_weights,
    tensor_product_weights,
    averager_upstream_adjoint,
    duplex_upstream_adjoint,
):
    g = Sizes(homolog_ensemble, duplex_embedding, duplex_logit_weights, first_operand_weights)
    shape = jax.ShapeDtypeStruct

    def call(kernel, name, args, outs, scratch=(), far=None, after=(), distant=False, us=1.0):
        size = sum(a.size * a.dtype.itemsize for a in args) + sum(
            math.prod(o.shape) * jnp.dtype(o.dtype).itemsize for o in outs
        )
        single = len(outs) == 1
        near = len(args) if far is None else far
        args = list(args[:near]) + [
            pltpu.with_memory_space_constraint(a, pltpu.HBM) for a in args[near:]
        ]

        if distant:
            after = [pltpu.with_memory_space_constraint(a, pltpu.HBM) for a in after]

        def body(*refs):
            kernel(g, *refs[: len(args)], *refs[len(args) + len(after) :])

        return pl.pallas_call(
            body,
            out_shape=outs[0] if single else tuple(outs),
            in_specs=[VMEM] * near + [FAR] * (len(args) - near) + [FAR if distant else VMEM] * len(after),
            out_specs=VMEM if single else (VMEM,) * len(outs),
            scratch_shapes=list(scratch),
            compiler_params=pltpu.CompilerParams(vmem_limit_bytes=40 * 1024 * 1024),
            cost_estimate=pl.CostEstimate(
                flops=int(us * 1.15e9), bytes_accessed=size, transcendentals=0
            ),
            name=name,
        )(*args, *after)

    heads = g.H * g.I
    rows = g.SP * g.I
    values = 2 * payload_weights.shape[1]
    pairs, tall = g.I * g.JC, heads // g.G
    xn, logits, near, x, e, wl = call(
        normalise_kernel,
        "normalise",
        (
            homolog_ensemble,
            duplex_embedding,
            duplex_upstream_adjoint.reshape(pairs, g.Z),
            resolved_position_flags.reshape(1, g.JC),
            duplex_logit_weights.T,
        ),
        [
            pltpu.VMEM((g.SP, g.I, 2 * g.M), BF16),
            pltpu.VMEM((tall, g.G * g.JC), F32),
            pltpu.VMEM((pairs + 3 * tall, g.Z), BF16),
            pltpu.VMEM((g.SQ, g.I, g.M), BF16),
            pltpu.VMEM(duplex_embedding.shape, BF16),
            pltpu.VMEM((g.H, g.Z), BF16),
        ],
        [
            pltpu.VMEM((1, g.JC), jnp.int32),
            pltpu.VMEM((g.I * g.H, LANES), F32),
            pltpu.SemaphoreType.DMA((5,)),
        ],
        far=0,
        us=2.0,
    )
    everyone = [xn] + [swap(xn, "row", k) for k in g.order]
    nears = shifted_all(near, "col")
    masks, left, weights, left_weights, w1 = call(
        prepare_kernel,
        "prepare",
        (xn, homolog_present_flags, first_operand_weights.T, tensor_product_weights),
        [
            pltpu.VMEM((g.SP + 8, 2 * g.M), F32),
            pltpu.VMEM((g.I * g.S, g.Q), BF16),
            pltpu.VMEM((g.Q, g.Q, g.Z), BF16),
            pltpu.VMEM((g.I, g.Q * g.S, g.Z), BF16),
            pltpu.VMEM((g.Q, g.M), BF16),
        ],
        [
            pltpu.SMEM(homolog_present_flags.shape, jnp.int32),
            pltpu.VMEM(tensor_product_weights.shape, BF16),
            pltpu.VMEM(tensor_product_weights.shape, F32),
            pltpu.VMEM((2, rows, LANES), F32),
            pltpu.SemaphoreType.DMA((3,)),
        ],
        far=1,
        us=0.01,
    )
    later = (
        sigmoid_weights,
        averager_final_weights.T,
        payload_weights,
        second_operand_weights.T,
    )
    g.carried = len(later)
    gate_weights, blended, gate_factor, _, _, p, w2 = call(
        gate_kernel,
        "gate",
        (xn, averager_upstream_adjoint, *later),
        [
            pltpu.VMEM((2 * g.M, values), BF16),
            pltpu.VMEM((rows, values), BF16),
            pltpu.VMEM((rows, values), F32),
        ]
        + [pltpu.VMEM(a.shape, a.dtype) for a in later],
        [
            pltpu.VMEM((g.SQ, g.I, g.M), BF16),
            pltpu.SemaphoreType.DMA,
            pltpu.SemaphoreType.DMA((len(later),)),
        ],
        far=1,
        after=(*nears[1:], masks),
        us=0.01,
    )
    share = g.Q * g.Q // g.D
    xall, cotangents, products, *matrix_parts = call(
        outer_kernel,
        "outer",
        (*everyone, *nears, left, w2, masks),
        [
            pltpu.VMEM((g.SP, g.N, 2 * g.M), BF16),
            pltpu.VMEM((g.I, g.N, g.Z), BF16),
            pltpu.VMEM((g.Q, g.I, g.S, g.Z), BF16),
        ]
        + [pltpu.VMEM((share, g.Z), F32)] * g.D,
        [
            pltpu.VMEM((g.NT, g.SP * 2 * g.Q, LANES), F32),
            pltpu.VMEM((g.Q * g.S, g.N), BF16),
            pltpu.VMEM((g.Q * g.Q, g.Z), F32),
        ],
        us=0.05,
    )
    matrix_parts = [matrix_parts[0]] + [
        shift(a, "depth", k + 1) for k, a in enumerate(matrix_parts[1:])
    ]
    second_term = call(
        right_kernel,
        "right",
        (cotangents, left_weights, w2, masks),
        [pltpu.VMEM((g.SP, g.N, 2 * g.M), F32)],
        [pltpu.VMEM((g.NT, g.Q * g.S, LANES), F32)],
    )
    share //= g.C
    matrix_parts = call(
        half_sum_kernel,
        "half_sum",
        matrix_parts,
        [pltpu.VMEM((share, g.Z), F32)] + [pltpu.VMEM((share, g.Z), BF16)] * (g.C - 1),
        [pltpu.VMEM((share * g.C, g.Z), F32)],
        after=(second_term,),
        us=0.2,
    )
    matrix_parts = [matrix_parts[0]] + [
        shift(a, "col", k + 1) for k, a in enumerate(matrix_parts[1:])
    ]
    soft, grad_soft, own, gate_grads, *sums = call(
        attend_kernel,
        "attend",
        (xall, logits, *nears[1:], blended, gate_factor, p, second_term),
        [
            pltpu.VMEM((heads, g.N), F32),
            pltpu.VMEM((heads, g.N), F32),
            pltpu.VMEM((rows, 2 * g.M), F32),
            pltpu.VMEM((rows, values), BF16),
        ]
        + [pltpu.VMEM((rows, 2 * g.M), BF16)] * (g.R - 1),
        [pltpu.VMEM((g.SP, g.N, 2 * g.M), F32)],
        us=3.0,
    )
    *sums, piece = call(
        pack_kernel,
        "pack",
        (*sums, *matrix_parts),
        [pltpu.VMEM((rows + share, 2 * g.M), BF16)] * (g.R - 1) + [pltpu.VMEM((share, g.Z), BF16)],
        us=0.2,
    )
    sums = swapped(sums, "row")
    wide = -(-3 * (g.JC + 1) // LANES) * LANES
    scores, *sends = call(
        score_kernel,
        "score",
        (soft, *shifted_all(grad_soft, "depth")),
        [pltpu.VMEM((heads, g.JC + 1), F32)] + [pltpu.VMEM((heads, wide), BF16)] * (g.C - 1),
        [pltpu.VMEM((g.D, heads, g.N), F32)],
        after=(piece,),
        us=0.2,
    )
    arrived = [shift(a, "col", k + 1) for k, a in enumerate(sends)]
    own = call(
        own_kernel,
        "own",
        (products, weights, w1, masks, own, gate_grads, gate_weights),
        [pltpu.VMEM((rows, 2 * g.M), F32)],
        [pltpu.VMEM((g.I * g.S, 2 * g.M), F32)],
        after=(scores,),
        us=0.01,
    )
    piece = call(
        piece_kernel,
        "piece",
        (piece, *sums),
        [pltpu.VMEM((share, g.Z), BF16)],
        [pltpu.VMEM((g.R, share, g.Z), BF16)],
        after=(own,),
        us=0.1,
    )
    pieces = shifted_all(piece, "col")
    part = call(
        reduce_kernel,
        "reduce",
        (x, own, *sums),
        [pltpu.VMEM((rows, 2 * g.M), BF16)],
        after=(piece,),
    )
    pairwise_gradient = call(
        pair_kernel,
        "pair",
        (e, wl, soft, scores, *arrived),
        [shape(duplex_embedding.shape, BF16)],
        after=(part,),
        us=0.01,
    )
    matrix = call(
        across_kernel,
        "across",
        pieces,
        [pltpu.VMEM((g.C, share, g.Z), BF16)],
        after=(pairwise_gradient,),
        distant=True,
        us=0.1,
    ).reshape(g.C * share, g.Z)
    ensemble_derivative = call(
        unpack_kernel,
        "unpack",
        shifted_all(part, "col"),
        [pltpu.VMEM(homolog_ensemble.shape, BF16)],
        after=(matrix,),
    )
    ensemble_derivative, outer_matrix_gradient = call(
        finish_kernel,
        "finish",
        (ensemble_derivative, *shifted_all(matrix, "depth")),
        [shape(homolog_ensemble.shape, BF16), shape((g.D, g.C * share, g.Z), F32)],
    )
    outer_matrix_gradient = outer_matrix_gradient.reshape(tensor_product_weights.shape)
    return (ensemble_derivative, pairwise_gradient, outer_matrix_gradient)


def solution(mesh):
    in_specs = (
        P(("parts", "depth"), "row", None),
        P(("parts", "row"), "col", None),
        P("parts"),
        P(("parts", "col")),
        P(),
        P(),
        P(),
        P(),
        P(),
        P(),
        P(),
        P(("parts", "depth"), "row", None),
        P(("parts", "row"), "col", None),
    )
    out_specs = (
        P(("parts", "depth"), "row", None),
        P(("parts", "row"), "col", None),
        P("parts", None),
    )
    return jax.shard_map(
        per_device, mesh=mesh, in_specs=in_specs, out_specs=out_specs, check_vma=False
    )
```

```python
import functools
import math

import jax
import jax.numpy as jnp
from jax import lax
from jax.experimental import pallas as pl
from jax.experimental.pallas import tpu as pltpu
from jax.sharding import PartitionSpec as P

EPS = 1e-05
PENALTY = 10000.0
F32 = jnp.float32
BF16 = jnp.bfloat16
LANES = 128
NN = (((1,), (0,)), ((), ()))
NT = (((1,), (1,)), ((), ()))
VMEM = pl.BlockSpec(memory_space=pltpu.VMEM)
FAR = pl.BlockSpec(memory_space=pl.ANY)


def mm(a, b, dims=NN):
    return lax.dot_general(a, b, dims, preferred_element_type=F32)


def split_high_low(value):
    high = value.astype(BF16)
    return high, (value - high.astype(F32)).astype(BF16)


def iota(shape, dim):
    return lax.broadcasted_iota(jnp.int32, shape, dim)


def lanes_of(pieces):
    return pieces[0] if len(pieces) == 1 else jnp.concatenate(pieces, axis=-1)


def rows_of(pieces):
    return pieces[0] if len(pieces) == 1 else jnp.concatenate(pieces, axis=0)


def standardize(values):
    centred = values - jnp.mean(values, -1, keepdims=True)
    inverse = lax.rsqrt(jnp.mean(centred * centred, -1, keepdims=True) + EPS)
    return centred * inverse, inverse


def standardize_backward(values, upstream):
    scaled, inverse = standardize(values)
    mean_grad = jnp.mean(upstream, -1, keepdims=True)
    mean_cross = jnp.mean(upstream * scaled, -1, keepdims=True)
    return (upstream - mean_grad - scaled * mean_cross) * inverse


def on_diagonal(block, width):
    rows, lanes = block.shape
    same = iota(block.shape, 0) // (rows // 2) == iota(block.shape, 1) // width
    return jnp.where(same, block, jnp.zeros_like(block))


def split_three(value):
    high = value.astype(BF16)
    rest = value - high.astype(F32)
    middle = rest.astype(BF16)
    return [high, middle, (rest - middle.astype(F32)).astype(BF16)]


def three_lanes(value):
    rows, width = value.shape
    fill = -(3 * width) % LANES
    return lanes_of(split_three(value) + [jnp.zeros((rows, fill), BF16)] * (fill > 0))


def join_three(parts, width):
    wide = parts.astype(F32)
    return (wide[:, :width] + wide[:, width : 2 * width]) + wide[:, 2 * width : 3 * width]


def twice(weights):
    zero = jnp.zeros_like(weights)
    return rows_of([lanes_of([weights, zero]), lanes_of([zero, weights])])


def normalise_kernel(g, x_hbm, e_hbm, dd_hbm, flag_hbm, wl_hbm, live_hbm, w1_hbm, t_hbm, *refs):
    xn_ref, logit_ref, near_ref, x_ref, e_ref, wl_ref, mask_ref, w1_ref, t_ref = refs[:9]
    flag_in, live_in, rows_ref, sem = refs[9:]
    first = lax.axis_index("col") * g.SQ
    pairs = g.I * g.JC
    copies = [
        pltpu.make_async_copy(a, b, sem.at[k])
        for k, (a, b) in enumerate(
            [
                (x_hbm.at[pl.ds(first, g.SQ)], x_ref),
                (e_hbm, e_ref),
                (wl_hbm, wl_ref),
                (flag_hbm, flag_in),
                (dd_hbm, near_ref.at[pl.ds(0, pairs)]),
                (live_hbm, live_in),
                (w1_hbm, w1_ref),
                (t_hbm, t_ref),
            ]
        )
    ]
    for copy in copies:
        copy.start()
    copies[0].wait()
    normed = g.fill(standardize(x_ref[...].astype(F32))[0]).reshape(g.SP, 2, g.I, g.M)
    xn_ref[...] = jnp.concatenate([normed[:, 0], normed[:, 1]], axis=-1).astype(BF16)
    for copy in copies[1:4]:
        copy.wait()
    pair = standardize(e_ref[...].astype(F32).reshape(pairs, g.Z))[0].astype(BF16)
    penalty = (flag_in[...].astype(F32) - 1.0) * PENALTY
    weights = wl_ref[...]
    for i in range(g.I):
        rows_ref[i * g.H : (i + 1) * g.H, : g.JC] = (
            mm(weights, pair[i * g.JC : (i + 1) * g.JC], NT) + penalty
        )
    logits = rows_of([rows_ref[pl.ds(h, g.I, stride=g.H), :][:, : g.JC] for h in range(g.H)])
    tall = g.H * g.I // g.G
    packed = lanes_of([logits[k * tall : (k + 1) * tall] for k in range(g.G)])
    logit_ref[...] = packed
    near_ref[pairs:, :] = rows_of(split_three(packed))
    for copy in copies[4:]:
        copy.wait()
    first = lax.axis_index("depth") * g.C * g.SQ + first
    lane = iota((1, 2 * g.M), 1)
    for k in range(g.SP):
        if 2 * k + 1 < g.SQ:
            flags = jnp.where(lane < g.M, live_in[first + 2 * k], live_in[first + 2 * k + 1])
            mask_ref[k : k + 1, :] = flags.astype(F32)
        else:
            mask_ref[k : k + 1, :] = jnp.zeros((1, 2 * g.M), F32)
    total = live_in[0]
    for s in range(1, live_in.shape[0]):
        total = total + live_in[s]
    mask_ref[g.SP : g.SP + 1, :] = 1.0 / (0.001 + jnp.full((1, 2 * g.M), total, jnp.int32).astype(F32))


def prepare_kernel(g, xn_ref, w1_ref, t_ref, mask_ref, u_hbm, *refs):
    refs = list(refs)
    count = g.carried
    sources, refs = refs[:count], refs[count:]
    left_ref, ts_ref, lt_ref, u_ref, refs = refs[0], refs[1], refs[2], refs[3], refs[4:]
    targets, (wide_ref, half_ref, first_sem, later_sem) = refs[:count], refs[count:]
    first = lax.axis_index("col") * g.SQ
    copies = [pltpu.make_async_copy(u_hbm.at[pl.ds(first, g.SQ)], u_ref, first_sem)]
    copies += [
        pltpu.make_async_copy(a, b, later_sem.at[k])
        for k, (a, b) in enumerate(zip(sources, targets, strict=True))
    ]
    for copy in copies:
        copy.start()
    masks = [mask_ref[k : k + 1, :] for k in range(g.SP)]
    xn = xn_ref[...]
    live_xn = rows_of([(xn[k].astype(F32) * masks[k]).astype(BF16) for k in range(g.SP)])
    w1 = rows_of([w1_ref[...], jnp.zeros((LANES - g.Q, g.M), BF16)])
    zero = jnp.zeros_like(w1)
    half_ref[0] = mm(live_xn, lanes_of([w1, zero]), NT)
    half_ref[1] = mm(live_xn, lanes_of([zero, w1]), NT)
    for i in range(g.I):
        halves = [half_ref[half, pl.ds(i, g.SP, stride=g.I), :] for half in range(2)]
        left_ref[i * g.S : (i + 1) * g.S, :] = rows_of(halves)[:, : g.Q].astype(BF16)
    wide_ref[...] = t_ref[...].astype(F32)
    for q in range(g.Q):
        ts_ref[q] = wide_ref[pl.ds(q, g.Q, stride=g.Q), :].astype(BF16)
    left = left_ref[...]
    for q in range(0, g.Q, 2):
        product = mm(left, lanes_of([ts_ref[q], ts_ref[q + 1]]))
        for k in range(2):
            block = product[:, k * g.Z : (k + 1) * g.Z].reshape(g.I, g.S, g.Z)
            lt_ref[:, (q + k) * g.S : (q + k + 1) * g.S, :] = block.astype(BF16)
    for copy in copies:
        copy.wait()


def gate_kernel(g, xn_ref, u_ref, sg_ref, wf_ref, gate_weight_ref, gm_ref, gate_ref):
    rows = g.SP * g.I
    xn = xn_ref[...]
    gate_weights = twice(sg_ref[...])
    gate_weight_ref[...] = gate_weights
    gates = jax.nn.sigmoid(mm(xn.reshape(rows, 2 * g.M), gate_weights))
    u = g.fill(u_ref[...]).reshape(g.SP, 2, g.I, g.M)
    packed_u = jnp.concatenate([u[:, 0], u[:, 1]], axis=-1).reshape(rows, 2 * g.M)
    gated = mm(packed_u, twice(wf_ref[...]))
    blended = gated * gates
    gm_ref[...] = blended.astype(BF16)
    gate_ref[...] = blended * (1.0 - gates)


def outer_kernel(g, *refs):
    refs = list(refs)
    x_refs, refs = refs[: g.R], refs[g.R :]
    d_refs, refs = refs[: g.C], refs[g.C :]
    left_ref, w2_ref, mask_ref, xall_ref, d_ref, ds_ref, *refs = refs
    w_refs, (spread_ref, rt_ref, all_ref) = refs[: g.D], refs[g.D :]
    row, col, depth = (lax.axis_index(a) for a in ("row", "col", "depth"))
    masks = [mask_ref[k : k + 1, :] for k in range(g.SP)]
    scale = mask_ref[g.SP : g.SP + 1, :]
    for k, ref in zip((0, *g.order), x_refs, strict=True):
        place = g.place(jnp.bitwise_xor(row, k), col)
        xall_ref[:, pl.ds(place, g.I), :] = ref[...]
    for k in range(g.C):
        spot = (g.C - k) % g.C
        block = d_refs[k][: g.I * g.JC, :].reshape(g.I, g.JC, g.Z)
        d_ref[:, spot * g.JC : (spot + 1) * g.JC, :] = block
    w2 = w2_ref[...]
    doubled = lanes_of([w2, w2])
    second = on_diagonal(rows_of([doubled, doubled]), g.M)
    for k in range(g.SP):
        live_x = (xall_ref[k].astype(F32) * masks[k]).astype(BF16)
        part = mm(second, live_x, NT)
        for t in range(g.NT):
            lanes = min(LANES, g.N - t * LANES)
            spread_ref[t, k * 2 * g.Q : (k + 1) * 2 * g.Q, :lanes] = part[
                :, t * LANES : t * LANES + lanes
            ]
    for q in range(g.Q):
        for t in range(g.NT):
            lanes = min(LANES, g.N - t * LANES)
            halves = [
                spread_ref[t, pl.ds(half * g.Q + q, g.SP, stride=2 * g.Q), :] for half in range(2)
            ]
            rt_ref[q * g.S : (q + 1) * g.S, t * LANES : t * LANES + lanes] = rows_of(halves)[
                :, :lanes
            ].astype(BF16)
    rt = rt_ref[...]
    for i in range(0, g.I, 2):
        product = mm(rt, lanes_of([d_ref[i], d_ref[i + 1]]))
        for k in range(2):
            block = product[:, k * g.Z : (k + 1) * g.Z]
            ds_ref[:, i + k] = block.reshape(g.Q, g.S, g.Z).astype(BF16)
    left = left_ref[...]
    eye = (iota((g.Q, g.Q), 0) == iota((g.Q, g.Q), 1)).astype(BF16)
    left_t = mm(eye, left, NT).astype(BF16)
    entries = g.S * g.I
    for q in range(0, g.Q, 2):
        both = lanes_of([ds_ref[q].reshape(entries, g.Z), ds_ref[q + 1].reshape(entries, g.Z)])
        part = mm(left_t, both)
        all_ref[pl.ds(q, g.Q, stride=g.Q), :] = part[:, : g.Z] * scale
        all_ref[pl.ds(q + 1, g.Q, stride=g.Q), :] = part[:, g.Z :] * scale
    share = g.Q * g.Q // g.D
    for k in range(g.D):
        first = pl.multiple_of(lax.rem(depth + k, g.D) * share, share)
        w_refs[k][...] = all_ref[pl.ds(first, share), :]


def right_kernel(g, d_ref, lt_ref, w2_ref, mask_ref, go_ref, rg_ref):
    masks = [mask_ref[k : k + 1, :] for k in range(g.SP)]
    scale = mask_ref[g.SP : g.SP + 1, :]
    right_grad = jnp.zeros((g.Q * g.S, g.N), F32)
    for i in range(0, g.I, 2):
        right_grad = right_grad + mm(
            lanes_of([lt_ref[i], lt_ref[i + 1]]), lanes_of([d_ref[i], d_ref[i + 1]]), NT
        )
    for t in range(g.NT):
        lanes = min(LANES, g.N - t * LANES)
        piece = right_grad[:, t * LANES : t * LANES + lanes]
        if lanes < LANES:
            piece = lanes_of([piece, jnp.zeros((g.Q * g.S, LANES - lanes), F32)])
        rg_ref[t] = piece
    deep = 2 * g.Q
    group = min(g.SP, LANES // deep)
    which = iota((group * deep, g.Q), 0)
    pick = (iota((group * deep, g.Q), 1) == which % deep // 2).astype(BF16)
    w2 = w2_ref[...]
    base = mm(pick, lanes_of([w2, w2]))
    which = iota(base.shape, 0)
    base = jnp.where(which % 2 == iota(base.shape, 1) // g.M, base, 0.0)
    weights = lanes_of([jnp.where(which // deep == k, base, 0.0) for k in range(group)]).astype(BF16)
    for k in range(0, g.SP, group):
        for t in range(g.NT):
            lanes = min(LANES, g.N - t * LANES)
            tall = rows_of(
                [rg_ref[t, pl.ds(k + m, deep, stride=g.SP), :] for m in range(group)]
            )
            tall = (tall * scale).T[:lanes]
            high, low = split_high_low(tall)
            part = mm(high, weights) + mm(low, weights)
            for m in range(group):
                go_ref[k + m, t * LANES : t * LANES + lanes, :] = (
                    part[:, m * 2 * g.M : (m + 1) * 2 * g.M] * masks[k + m]
                )


def own_kernel(
    g, ds_ref, ts_ref, w1_ref, mask_ref, part_ref, gg_ref, gate_weight_ref, own_ref, turn_ref
):
    scale = mask_ref[g.SP : g.SP + 1, :]
    entries = g.S * g.I
    left_grad = jnp.zeros((entries, g.Q), F32)
    for q in range(0, g.Q, 2):
        both = lanes_of([ds_ref[q].reshape(entries, g.Z), ds_ref[q + 1].reshape(entries, g.Z)])
        left_grad = left_grad + mm(both, lanes_of([ts_ref[q], ts_ref[q + 1]]), NT)
    w1 = w1_ref[...]
    first_term = jnp.zeros((entries, 2 * g.M), F32)
    for piece in split_high_low(left_grad * scale[:, : g.Q]):
        first_term = first_term + mm(piece, lanes_of([w1, w1]))
    turn_ref[...] = first_term
    gate_term = mm(gg_ref[...], gate_weight_ref[...], NT)
    lane = iota((1, 2 * g.M), 1)
    for k in range(g.SP):
        rows = slice(k * g.I, (k + 1) * g.I)
        halves = [turn_ref[pl.ds(half * g.SP + k, g.I, stride=g.S), :] for half in range(2)]
        term = jnp.where(lane < g.M, halves[0], halves[1]) * mask_ref[k : k + 1, :]
        own_ref[rows, :] = part_ref[rows, :] + gate_term[rows] + term


def half_sum_kernel(g, *refs):
    parts, outs, total_ref = refs[: g.D], refs[g.D : g.D + g.C], refs[-1]
    total = parts[0][...]
    for ref in parts[1:]:
        total = total + ref[...]
    total_ref[...] = total
    share = total.shape[0] // g.C
    col = lax.axis_index("col")
    for k in range(g.C):
        first = pl.multiple_of(lax.rem(col + k, g.C) * share, share)
        outs[k][...] = total_ref[pl.ds(first, share), :].astype(outs[k].dtype)


def attend_kernel(g, *refs):
    refs = list(refs)
    xall_ref, refs = refs[0], refs[1:]
    logit_ref, near_refs, refs = refs[0], refs[1 : g.C], refs[g.C :]
    gm_ref, gate_ref, p_ref, go_ref, soft_ref, gs_ref, own_ref, gg_ref, *refs = refs
    send_refs, (total_ref,) = refs[: g.R - 1], refs[g.R - 1 :]
    row, col = lax.axis_index("row"), lax.axis_index("col")
    tall, blocks = logit_ref.shape[0], [logit_ref[...]]
    for k in range(1, g.C):
        parts = near_refs[g.C - k - 1][g.I * g.JC :, :].astype(F32)
        blocks.append((parts[:tall] + parts[tall : 2 * tall]) + parts[2 * tall :])
    logits = lanes_of(
        [rows_of([b[:, k * g.JC : (k + 1) * g.JC] for k in range(g.G)]) for b in blocks]
    )
    shifted = jnp.exp(logits - jnp.max(logits, -1, keepdims=True))
    soft = shifted / jnp.sum(shifted, -1, keepdims=True)
    soft_ref[...] = soft
    low = soft.astype(BF16)
    eye = (iota((g.N, g.N), 0) == iota((g.N, g.N), 1)).astype(BF16)
    low_t = mm(eye, low, NT).astype(BF16)
    value_weights = twice(p_ref[...])
    values = mm(xall_ref[...].reshape(g.SP * g.N, 2 * g.M), value_weights).astype(BF16)
    wide = value_weights.shape[1]
    head = iota((1, wide), 1) % (wide // 2) // (wide // 2 // g.H)
    grad_soft = jnp.zeros((g.H * g.I, g.N), F32)
    for k in range(g.SP):
        v = values[k * g.N : (k + 1) * g.N]
        crossed = mm(low, v)
        mixed = jnp.where(head == 0, crossed[: g.I], 0.0)
        for h in range(1, g.H):
            mixed = jnp.where(head == h, crossed[h * g.I : (h + 1) * g.I], mixed)
        rows = slice(k * g.I, (k + 1) * g.I)
        gg_ref[rows, :] = (gate_ref[rows, :] * mixed).astype(BF16)
        blended = gm_ref[rows, :]
        by_head = rows_of(
            [jnp.where(head == h, blended, jnp.zeros_like(blended)) for h in range(g.H)]
        )
        grad_soft = grad_soft + mm(by_head, v, NT)
        part = go_ref[k]
        for piece in split_high_low(mm(low_t, by_head)):
            part = part + mm(piece, value_weights, NT)
        total_ref[k] = part
    gs_ref[...] = grad_soft
    own = total_ref[:, pl.ds(g.place(row, col), g.I), :]
    own_ref[...] = own.reshape(g.SP * g.I, 2 * g.M)
    for x in range(1, g.R):
        block = total_ref[:, pl.ds(g.place(jnp.bitwise_xor(row, x), col), g.I), :]
        send_refs[x - 1][...] = block.reshape(g.SP * g.I, 2 * g.M).astype(BF16)


def pack_kernel(g, *refs):
    refs = list(refs)
    sums, refs = refs[: g.R - 1], refs[g.R - 1 :]
    parts, refs = refs[: g.C], refs[g.C :]
    outs, own_ref = refs[: g.R - 1], refs[g.R - 1]
    total = parts[0][...]
    for ref in parts[1:]:
        total = total + ref[...].astype(F32)
    total, rows = total.astype(BF16), g.SP * g.I
    own_ref[...] = total
    for x in range(1, g.R):
        outs[x - 1][:rows, :] = sums[x - 1][...]
        outs[x - 1][rows:, :] = total


def piece_kernel(g, own_ref, *refs):
    out_ref, order_ref = refs[-2:]
    row, rows = lax.axis_index("row"), g.SP * g.I
    order_ref[row] = own_ref[...]
    for k in range(1, g.R):
        order_ref[jnp.bitwise_xor(row, g.R - k)] = refs[k - 1][rows:, :]
    total = order_ref[0].astype(F32)
    for r in range(1, g.R):
        total = total + order_ref[r].astype(F32)
    out_ref[...] = total.astype(BF16)


def score_kernel(g, soft_ref, *refs):
    parts, refs = refs[: g.D], refs[g.D :]
    own_ref, out_refs, order_ref = refs[0], refs[1 : g.C], refs[g.C]
    depth = lax.axis_index("depth")
    for k in range(g.D):
        order_ref[lax.rem(depth - k + g.D, g.D)] = parts[k][...]
    grad_soft = order_ref[0]
    for k in range(1, g.D):
        grad_soft = grad_soft + order_ref[k]
    inner = jnp.sum(soft_ref[...] * grad_soft, -1, keepdims=True)
    for k in range(g.C):
        block = lanes_of([grad_soft[:, k * g.JC : (k + 1) * g.JC], inner])
        if k == 0:
            own_ref[...] = block
        else:
            out_refs[k - 1][...] = three_lanes(block)


def pair_kernel(g, e_ref, wl_ref, soft_ref, own_ref, *refs):
    got, pair_ref = refs[: g.C - 1], refs[g.C - 1]
    heads = g.H * g.I
    total = own_ref[...]
    for ref in got:
        total = total + join_three(ref[...], g.JC + 1)
    grad = soft_ref[:, : g.JC] * (total[:, : g.JC] - total[:, g.JC :])
    if g.JC < LANES:
        grad = lanes_of([grad, jnp.zeros((heads, LANES - g.JC), F32)])
    high, low = split_high_low(grad.T[: g.JC])
    grads = lanes_of([high, low])
    pick = (iota((heads, g.H), 0) // g.I == iota((heads, g.H), 1)).astype(BF16)
    base = mm(pick, wl_ref[...]).astype(BF16)
    token = iota((heads, 1), 0) % g.I
    for i in range(0, g.I, 2):
        weights = lanes_of(
            [jnp.where(token == i + k, base, jnp.zeros_like(base)) for k in range(2)]
        )
        upstream = mm(grads, rows_of([weights, weights]))
        for k in range(2):
            pair_ref[i + k] = standardize_backward(
                e_ref[i + k].astype(F32), upstream[:, k * g.Z : (k + 1) * g.Z]
            ).astype(BF16)


def reduce_kernel(g, x_ref, own_ref, *refs):
    got, out_ref = refs[:-1], refs[-1]
    rows = g.SP * g.I
    total = own_ref[...]
    for ref in got:
        total = total + ref[:rows, :].astype(F32)
    total = total.reshape(g.SP, 1, g.I, 2 * g.M)
    upstream = jnp.concatenate([total[..., : g.M], total[..., g.M :]], axis=1)
    upstream = upstream.reshape(g.S, g.I, g.M)[: g.SQ]
    msa = g.fill(standardize_backward(x_ref[...].astype(F32), upstream))
    msa = msa.reshape(g.SP, 2, g.I, g.M)
    msa = jnp.concatenate([msa[:, 0], msa[:, 1]], axis=-1).astype(BF16)
    out_ref[...] = msa.reshape(rows, 2 * g.M)


def across_kernel(g, *refs):
    out_ref = refs[-1]
    col = lax.axis_index("col")
    for k, ref in enumerate(refs[:-1]):
        out_ref[lax.rem(col - k + g.C, g.C)] = ref[...]


def unpack_kernel(g, *refs):
    parts, msa_ref = refs[: g.C], refs[g.C]
    col = lax.axis_index("col")
    for k, ref in enumerate(parts):
        msa = ref[...].astype(F32).reshape(g.SP, 1, g.I, 2 * g.M)
        msa = jnp.concatenate([msa[..., : g.M], msa[..., g.M :]], axis=1)
        msa = msa.reshape(g.S, g.I, g.M)[: g.SQ].astype(BF16)
        msa_ref[pl.ds(lax.rem(col - k + g.C, g.C) * g.SQ, g.SQ)] = msa


def first_half_kernel(g, part_ref, out_ref, wide_ref, sem):
    wide_ref[...] = part_ref[...].astype(F32)
    copy = pltpu.make_async_copy(wide_ref, out_ref.at[lax.axis_index("depth")], sem)
    copy.start()
    copy.wait()


def finish_kernel(g, msa_ref, *refs):
    parts, (_, out_ref, matrix_ref, wide_ref, sem) = refs[: g.D - 1], refs[g.D - 1 :]
    depth = lax.axis_index("depth")
    copies = []
    for k, ref in enumerate(parts):
        wide_ref[k] = ref[...].astype(F32)
        place = lax.rem(depth - k - 1 + g.D, g.D)
        copies.append(pltpu.make_async_copy(wide_ref.at[k], matrix_ref.at[place], sem.at[k]))
        copies[-1].start()
    out_ref[...] = msa_ref[...]
    for copy in copies:
        copy.wait()


class Sizes:
    def __init__(self, x, e, wl, w1):
        self.R, self.C, self.D = (lax.axis_size(a) for a in ("row", "col", "depth"))
        self.I, self.M = x.shape[1:]
        self.JC, self.Z = e.shape[1:]
        self.H, self.Q = wl.shape[1], w1.shape[1]
        self.SQ = x.shape[0] // self.C
        self.S = -(-self.SQ // 16) * 16
        self.SP, self.N = self.S // 2, self.R * self.I
        self.F = self.R // self.C
        self.NT = -(-self.N // LANES)
        self.G = max(1, LANES // self.JC)
        self.carried = 0
        self.order = [*range(1, self.R // 2), *range(self.R // 2 + 1, self.R), self.R // 2]

    def fill(self, rows):
        if self.SQ == self.S:
            return rows
        return rows_of([rows, jnp.zeros((self.S - self.SQ, *rows.shape[1:]), rows.dtype)])

    def place(self, row, col):
        turn = lax.rem(row // self.F - col + self.C, self.C)
        return pl.multiple_of((turn * self.F + lax.rem(row, self.F)) * self.I, self.I)


def shift(array, axis, k):
    count = lax.axis_size(axis)
    return lax.ppermute(array, axis, [(i, (i + k) % count) for i in range(count)])


def swap(array, axis, x):
    return lax.ppermute(array, axis, [(i, i ^ x) for i in range(lax.axis_size(axis))])


def swapped(arrays, axis):
    return [swap(a, axis, k + 1) for k, a in reversed([*enumerate(arrays)])]


def shifted_all(array, axis):
    return [array] + [shift(array, axis, k) for k in range(1, lax.axis_size(axis))]


def per_device(
    homolog_ensemble,
    duplex_embedding,
    homolog_present_flags,
    resolved_position_flags,
    payload_weights,
    sigmoid_weights,
    averager_final_weights,
    first_operand_weights,
    second_operand_weights,
    duplex_logit_weights,
    tensor_product_weights,
    averager_upstream_adjoint,
    duplex_upstream_adjoint,
):
    g = Sizes(homolog_ensemble, duplex_embedding, duplex_logit_weights, first_operand_weights)
    shape = jax.ShapeDtypeStruct

    def call(kernel, name, args, outs, scratch=(), far=None, after=(), distant=False, us=1.0):
        size = sum(a.size * a.dtype.itemsize for a in args) + sum(
            math.prod(o.shape) * jnp.dtype(o.dtype).itemsize for o in outs
        )
        single = len(outs) == 1
        near = len(args) if far is None else far
        args = list(args[:near]) + [
            pltpu.with_memory_space_constraint(a, pltpu.HBM) for a in args[near:]
        ]

        if distant:
            after = [pltpu.with_memory_space_constraint(a, pltpu.HBM) for a in after]

        def body(*refs):
            kernel(g, *refs[: len(args)], *refs[len(args) + len(after) :])

        return pl.pallas_call(
            body,
            out_shape=outs[0] if single else tuple(outs),
            in_specs=[VMEM] * near + [FAR] * (len(args) - near) + [FAR if distant else VMEM] * len(after),
            out_specs=VMEM if single else (VMEM,) * len(outs),
            scratch_shapes=list(scratch),
            compiler_params=pltpu.CompilerParams(vmem_limit_bytes=40 * 1024 * 1024),
            cost_estimate=pl.CostEstimate(
                flops=int(us * 1.15e9), bytes_accessed=size, transcendentals=0
            ),
            name=name,
        )(*args, *after)

    heads = g.H * g.I
    rows = g.SP * g.I
    values = 2 * payload_weights.shape[1]
    pairs, tall = g.I * g.JC, heads // g.G
    xn, logits, near, x, e, wl, masks, w1, outer_weights = call(
        normalise_kernel,
        "normalise",
        (
            homolog_ensemble,
            duplex_embedding,
            duplex_upstream_adjoint.reshape(pairs, g.Z),
            resolved_position_flags.reshape(1, g.JC),
            duplex_logit_weights.T,
            homolog_present_flags,
            first_operand_weights.T,
            tensor_product_weights,
        ),
        [
            pltpu.VMEM((g.SP, g.I, 2 * g.M), BF16),
            pltpu.VMEM((tall, g.G * g.JC), F32),
            pltpu.VMEM((pairs + 3 * tall, g.Z), BF16),
            pltpu.VMEM((g.SQ, g.I, g.M), BF16),
            pltpu.VMEM(duplex_embedding.shape, BF16),
            pltpu.VMEM((g.H, g.Z), BF16),
            pltpu.VMEM((g.SP + 8, 2 * g.M), F32),
            pltpu.VMEM((g.Q, g.M), BF16),
            pltpu.VMEM(tensor_product_weights.shape, BF16),
        ],
        [
            pltpu.VMEM((1, g.JC), jnp.int32),
            pltpu.SMEM(homolog_present_flags.shape, jnp.int32),
            pltpu.VMEM((g.I * g.H, LANES), F32),
            pltpu.SemaphoreType.DMA((8,)),
        ],
        far=0,
        us=2.0,
    )
    everyone = [xn] + [swap(xn, "row", k) for k in g.order]
    nears = shifted_all(near, "col")
    later = (
        sigmoid_weights,
        averager_final_weights.T,
        payload_weights,
        second_operand_weights.T,
    )
    g.carried = len(later)
    left, weights, left_weights, u, sg, wf, p, w2 = call(
        prepare_kernel,
        "prepare",
        (xn, w1, outer_weights, masks, averager_upstream_adjoint, *later),
        [
            pltpu.VMEM((g.I * g.S, g.Q), BF16),
            pltpu.VMEM((g.Q, g.Q, g.Z), BF16),
            pltpu.VMEM((g.I, g.Q * g.S, g.Z), BF16),
            pltpu.VMEM((g.SQ, g.I, g.M), BF16),
        ]
        + [pltpu.VMEM(a.shape, a.dtype) for a in later],
        [
            pltpu.VMEM(tensor_product_weights.shape, F32),
            pltpu.VMEM((2, rows, LANES), F32),
            pltpu.SemaphoreType.DMA,
            pltpu.SemaphoreType.DMA((len(later),)),
        ],
        far=4,
        us=0.01,
    )
    gate_weights, blended, gate_factor = call(
        gate_kernel,
        "gate",
        (xn, u, sg, wf),
        [
            pltpu.VMEM((2 * g.M, values), BF16),
            pltpu.VMEM((rows, values), BF16),
            pltpu.VMEM((rows, values), F32),
        ],
        after=nears[1:],
        us=0.01,
    )
    share = g.Q * g.Q // g.D
    xall, cotangents, products, *matrix_parts = call(
        outer_kernel,
        "outer",
        (*everyone, *nears, left, w2, masks),
        [
            pltpu.VMEM((g.SP, g.N, 2 * g.M), BF16),
            pltpu.VMEM((g.I, g.N, g.Z), BF16),
            pltpu.VMEM((g.Q, g.I, g.S, g.Z), BF16),
        ]
        + [pltpu.VMEM((share, g.Z), F32)] * g.D,
        [
            pltpu.VMEM((g.NT, g.SP * 2 * g.Q, LANES), F32),
            pltpu.VMEM((g.Q * g.S, g.N), BF16),
            pltpu.VMEM((g.Q * g.Q, g.Z), F32),
        ],
        after=(gate_weights,),
        us=0.05,
    )
    matrix_parts = [matrix_parts[0]] + [
        shift(a, "depth", k + 1) for k, a in enumerate(matrix_parts[1:])
    ]
    second_term = call(
        right_kernel,
        "right",
        (cotangents, left_weights, w2, masks),
        [pltpu.VMEM((g.SP, g.N, 2 * g.M), F32)],
        [pltpu.VMEM((g.NT, g.Q * g.S, LANES), F32)],
    )
    share //= g.C
    matrix_parts = call(
        half_sum_kernel,
        "half_sum",
        matrix_parts,
        [pltpu.VMEM((share, g.Z), F32)] + [pltpu.VMEM((share, g.Z), BF16)] * (g.C - 1),
        [pltpu.VMEM((share * g.C, g.Z), F32)],
        after=(second_term,),
        us=0.2,
    )
    matrix_parts = [matrix_parts[0]] + [
        shift(a, "col", k + 1) for k, a in enumerate(matrix_parts[1:])
    ]
    soft, grad_soft, own, gate_grads, *sums = call(
        attend_kernel,
        "attend",
        (xall, logits, *nears[1:], blended, gate_factor, p, second_term),
        [
            pltpu.VMEM((heads, g.N), F32),
            pltpu.VMEM((heads, g.N), F32),
            pltpu.VMEM((rows, 2 * g.M), F32),
            pltpu.VMEM((rows, values), BF16),
        ]
        + [pltpu.VMEM((rows, 2 * g.M), BF16)] * (g.R - 1),
        [pltpu.VMEM((g.SP, g.N, 2 * g.M), F32)],
        us=3.0,
    )
    *sums, piece = call(
        pack_kernel,
        "pack",
        (*sums, *matrix_parts),
        [pltpu.VMEM((rows + share, 2 * g.M), BF16)] * (g.R - 1) + [pltpu.VMEM((share, g.Z), BF16)],
        us=0.2,
    )
    sums = swapped(sums, "row")
    wide = -(-3 * (g.JC + 1) // LANES) * LANES
    scores, *sends = call(
        score_kernel,
        "score",
        (soft, *shifted_all(grad_soft, "depth")),
        [pltpu.VMEM((heads, g.JC + 1), F32)] + [pltpu.VMEM((heads, wide), BF16)] * (g.C - 1),
        [pltpu.VMEM((g.D, heads, g.N), F32)],
        after=(piece,),
        us=0.2,
    )
    arrived = [shift(a, "col", k + 1) for k, a in enumerate(sends)]
    own = call(
        own_kernel,
        "own",
        (products, weights, w1, masks, own, gate_grads, gate_weights),
        [pltpu.VMEM((rows, 2 * g.M), F32)],
        [pltpu.VMEM((g.I * g.S, 2 * g.M), F32)],
        after=(scores,),
        us=0.01,
    )
    piece = call(
        piece_kernel,
        "piece",
        (piece, *sums),
        [pltpu.VMEM((share, g.Z), BF16)],
        [pltpu.VMEM((g.R, share, g.Z), BF16)],
        after=(own,),
        us=0.1,
    )
    pieces = shifted_all(piece, "col")
    part = call(
        reduce_kernel,
        "reduce",
        (x, own, *sums),
        [pltpu.VMEM((rows, 2 * g.M), BF16)],
        after=(piece,),
    )
    pairwise_gradient = call(
        pair_kernel,
        "pair",
        (e, wl, soft, scores, *arrived),
        [shape(duplex_embedding.shape, BF16)],
        after=(part,),
        us=0.01,
    )
    matrix = call(
        across_kernel,
        "across",
        pieces,
        [pltpu.VMEM((g.C, share, g.Z), BF16)],
        after=(pairwise_gradient,),
        distant=True,
        us=0.1,
    ).reshape(g.C * share, g.Z)
    whole = shape((g.D, g.C * share, g.Z), F32)
    first_half = pl.pallas_call(
        functools.partial(first_half_kernel, g),
        out_shape=whole,
        in_specs=[VMEM],
        out_specs=FAR,
        scratch_shapes=[pltpu.VMEM((g.C * share, g.Z), F32), pltpu.SemaphoreType.DMA],
        cost_estimate=pl.CostEstimate(flops=10**9, bytes_accessed=10**6, transcendentals=0),
        name="first_half",
    )(matrix)
    ensemble_derivative = call(
        unpack_kernel,
        "unpack",
        shifted_all(part, "col"),
        [pltpu.VMEM(homolog_ensemble.shape, BF16)],
        after=(first_half,),
        distant=True,
    )
    others = shifted_all(matrix, "depth")[1:]
    ensemble_derivative, outer_matrix_gradient = pl.pallas_call(
        functools.partial(finish_kernel, g),
        out_shape=(shape(homolog_ensemble.shape, BF16), whole),
        in_specs=[VMEM] * g.D + [FAR],
        out_specs=(VMEM, FAR),
        scratch_shapes=[
            pltpu.VMEM((g.D - 1, g.C * share, g.Z), F32),
            pltpu.SemaphoreType.DMA((g.D - 1,)),
        ],
        input_output_aliases={g.D: 1},
        cost_estimate=pl.CostEstimate(flops=10**9, bytes_accessed=10**6, transcendentals=0),
        name="finish",
    )(ensemble_derivative, *others, pltpu.with_memory_space_constraint(first_half, pltpu.HBM))
    outer_matrix_gradient = outer_matrix_gradient.reshape(tensor_product_weights.shape)
    return (ensemble_derivative, pairwise_gradient, outer_matrix_gradient)


def solution(mesh):
    in_specs = (
        P(("parts", "depth"), "row", None),
        P(("parts", "row"), "col", None),
        P("parts"),
        P(("parts", "col")),
        P(),
        P(),
        P(),
        P(),
        P(),
        P(),
        P(),
        P(("parts", "depth"), "row", None),
        P(("parts", "row"), "col", None),
    )
    out_specs = (
        P(("parts", "depth"), "row", None),
        P(("parts", "row"), "col", None),
        P("parts", None),
    )
    return jax.shard_map(
        per_device, mesh=mesh, in_specs=in_specs, out_specs=out_specs, check_vma=False
    )
```

```python
import functools
import math

import jax
import jax.numpy as jnp
from jax import lax
from jax.experimental import pallas as pl
from jax.experimental.pallas import tpu as pltpu
from jax.sharding import PartitionSpec as P

EPS = 1e-05
PENALTY = 10000.0
F32 = jnp.float32
BF16 = jnp.bfloat16
LANES = 128
NN = (((1,), (0,)), ((), ()))
NT = (((1,), (1,)), ((), ()))
VMEM = pl.BlockSpec(memory_space=pltpu.VMEM)
FAR = pl.BlockSpec(memory_space=pl.ANY)


def mm(a, b, dims=NN):
    return lax.dot_general(a, b, dims, preferred_element_type=F32)


def split_high_low(value):
    high = value.astype(BF16)
    return high, (value - high.astype(F32)).astype(BF16)


def iota(shape, dim):
    return lax.broadcasted_iota(jnp.int32, shape, dim)


def lanes_of(pieces):
    return pieces[0] if len(pieces) == 1 else jnp.concatenate(pieces, axis=-1)


def rows_of(pieces):
    return pieces[0] if len(pieces) == 1 else jnp.concatenate(pieces, axis=0)


def standardize(values):
    centred = values - jnp.mean(values, -1, keepdims=True)
    inverse = lax.rsqrt(jnp.mean(centred * centred, -1, keepdims=True) + EPS)
    return centred * inverse, inverse


def standardize_backward(values, upstream):
    scaled, inverse = standardize(values)
    mean_grad = jnp.mean(upstream, -1, keepdims=True)
    mean_cross = jnp.mean(upstream * scaled, -1, keepdims=True)
    return (upstream - mean_grad - scaled * mean_cross) * inverse


def on_diagonal(block, width):
    rows, lanes = block.shape
    same = iota(block.shape, 0) // (rows // 2) == iota(block.shape, 1) // width
    return jnp.where(same, block, jnp.zeros_like(block))


def split_three(value):
    high = value.astype(BF16)
    rest = value - high.astype(F32)
    middle = rest.astype(BF16)
    return [high, middle, (rest - middle.astype(F32)).astype(BF16)]


def three_lanes(value):
    rows, width = value.shape
    fill = -(3 * width) % LANES
    return lanes_of(split_three(value) + [jnp.zeros((rows, fill), BF16)] * (fill > 0))


def join_three(parts, width):
    wide = parts.astype(F32)
    return (wide[:, :width] + wide[:, width : 2 * width]) + wide[:, 2 * width : 3 * width]


def twice(weights):
    zero = jnp.zeros_like(weights)
    return rows_of([lanes_of([weights, zero]), lanes_of([zero, weights])])


def column_weights(g, w2):
    rows = iota((2 * g.QL, g.Q), 0) % g.QL + lax.axis_index("col") * g.QL
    pick = (iota((2 * g.QL, g.Q), 1) == rows).astype(BF16)
    return on_diagonal(mm(pick, lanes_of([w2, w2])), g.M).astype(BF16)


def normalise_kernel(
    g, x_hbm, e_hbm, dd_hbm, flag_hbm, wl_hbm, live_hbm, w1_hbm, t_hbm, w2_hbm, *refs
):
    xn_ref, send_ref, logit_ref, near_ref, x_ref, e_ref, wl_ref, mask_ref, w1_ref, t_ref, w2_ref = refs[:11]
    flag_in, live_in, x_in, norm_ref, rows_ref, sem = refs[11:]
    col = lax.axis_index("col")
    pairs = g.I * g.JC
    copies = [
        pltpu.make_async_copy(a, b, sem.at[k])
        for k, (a, b) in enumerate(
            [
                (x_hbm, x_in),
                (e_hbm, e_ref),
                (wl_hbm, wl_ref),
                (flag_hbm, flag_in),
                (dd_hbm, near_ref.at[pl.ds(0, pairs)]),
                (live_hbm, live_in),
                (w1_hbm, w1_ref),
                (t_hbm, t_ref),
                (w2_hbm, w2_ref),
            ]
        )
    ]
    for copy in copies:
        copy.start()
    copies[5].wait()
    lane = iota((1, 2 * g.M), 1)
    groups = [lax.rem(col + m, g.C) for m in range(g.C)]
    for m, group in enumerate(groups):
        first = (lax.axis_index("depth") * g.C + group) * g.SQ
        for k in range(g.SP):
            if 2 * k + 1 < g.SQ:
                flags = jnp.where(lane < g.M, live_in[first + 2 * k], live_in[first + 2 * k + 1])
                flags = flags.astype(F32)
            else:
                flags = jnp.zeros((1, 2 * g.M), F32)
            mask_ref[m * g.SP + k : m * g.SP + k + 1, :] = flags
    total = live_in[0]
    for k in range(1, live_in.shape[0]):
        total = total + live_in[k]
    count = jnp.full((1, 2 * g.M), total, jnp.int32).astype(F32)
    mask_ref[g.C * g.SP : g.C * g.SP + 1, :] = 1.0 / (0.001 + count)
    copies[0].wait()
    copies[8].wait()
    norm_ref[...] = standardize(x_in[...].astype(F32))[0]
    x_ref[...] = x_in[pl.ds(col * g.SQ, g.SQ)]
    second = column_weights(g, w2_ref[...])
    rows, blocks = g.SP * g.I, []
    for m, group in enumerate(groups):
        normed = g.fill(norm_ref[pl.ds(group * g.SQ, g.SQ)]).reshape(g.SP, 2, g.I, g.M)
        packed = jnp.concatenate([normed[:, 0], normed[:, 1]], axis=-1).astype(BF16)
        xn_ref[m] = packed
        if m == 0:
            send_ref[:rows, :] = packed.reshape(rows, 2 * g.M)
        else:
            masks = [mask_ref[m * g.SP + k : m * g.SP + k + 1, :] for k in range(g.SP)]
            live = rows_of([(packed[k].astype(F32) * masks[k]).astype(BF16) for k in range(g.SP)])
            factors = mm(live, second, NT)
            blocks += [factors[k * g.I : (k + 1) * g.I] for k in range(g.SP)]
    if blocks:
        wide = lanes_of(blocks)
        fill = -wide.shape[1] % LANES
        if fill:
            wide = lanes_of([wide, jnp.zeros((g.I, fill), F32)])
        for k in range(g.EXTRA):
            block = wide[:, k * LANES : (k + 1) * LANES]
            send_ref[rows + k * g.I : rows + (k + 1) * g.I, :] = block.astype(BF16)
    for copy in copies[1:4]:
        copy.wait()
    pair = standardize(e_ref[...].astype(F32).reshape(pairs, g.Z))[0].astype(BF16)
    penalty = (flag_in[...].astype(F32) - 1.0) * PENALTY
    weights = wl_ref[...]
    for i in range(g.I):
        rows_ref[i * g.H : (i + 1) * g.H, : g.JC] = (
            mm(weights, pair[i * g.JC : (i + 1) * g.JC], NT) + penalty
        )
    logits = rows_of([rows_ref[pl.ds(h, g.I, stride=g.H), :][:, : g.JC] for h in range(g.H)])
    tall = g.H * g.I // g.G
    packed = lanes_of([logits[k * tall : (k + 1) * tall] for k in range(g.G)])
    logit_ref[...] = packed
    near_ref[pairs:, :] = rows_of(split_three(packed))
    for copy in (copies[4], *copies[6:8]):
        copy.wait()


def prepare_kernel(g, xn_ref, w1_ref, t_ref, mask_ref, u_hbm, *refs):
    refs = list(refs)
    count = g.carried
    sources, refs = refs[:count], refs[count:]
    left_ref, ts_ref, lt_ref, u_ref, refs = refs[0], refs[1], refs[2], refs[3], refs[4:]
    targets, (wide_ref, half_ref, first_sem, later_sem) = refs[:count], refs[count:]
    first = lax.axis_index("col") * g.SQ
    copies = [pltpu.make_async_copy(u_hbm.at[pl.ds(first, g.SQ)], u_ref, first_sem)]
    copies += [
        pltpu.make_async_copy(a, b, later_sem.at[k])
        for k, (a, b) in enumerate(zip(sources, targets, strict=True))
    ]
    for copy in copies:
        copy.start()
    w1 = rows_of([w1_ref[...], jnp.zeros((LANES - g.Q, g.M), BF16)])
    zero = jnp.zeros_like(w1)
    for m in range(g.C):
        masks = [mask_ref[m * g.SP + k : m * g.SP + k + 1, :] for k in range(g.SP)]
        live_xn = rows_of(
            [(xn_ref[m, k].astype(F32) * masks[k]).astype(BF16) for k in range(g.SP)]
        )
        half_ref[0] = mm(live_xn, lanes_of([w1, zero]), NT)
        half_ref[1] = mm(live_xn, lanes_of([zero, w1]), NT)
        for i in range(g.I):
            halves = [half_ref[half, pl.ds(i, g.SP, stride=g.I), :] for half in range(2)]
            first = (m * g.I + i) * g.S
            left_ref[first : first + g.S, :] = rows_of(halves)[:, : g.Q].astype(BF16)
    wide_ref[...] = t_ref[...].astype(F32)
    for q in range(g.Q):
        ts_ref[q] = wide_ref[pl.ds(q, g.Q, stride=g.Q), :].astype(BF16)
    left = left_ref[: g.I * g.S, :]
    for q in range(0, g.Q, 2):
        product = mm(left, lanes_of([ts_ref[q], ts_ref[q + 1]]))
        for k in range(2):
            block = product[:, k * g.Z : (k + 1) * g.Z].reshape(g.I, g.S, g.Z)
            lt_ref[:, (q + k) * g.S : (q + k + 1) * g.S, :] = block.astype(BF16)
    for copy in copies:
        copy.wait()


def gate_kernel(g, xn_ref, u_ref, sg_ref, wf_ref, gate_weight_ref, gm_ref, gate_ref):
    rows = g.SP * g.I
    xn = xn_ref[0]
    gate_weights = twice(sg_ref[...])
    gate_weight_ref[...] = gate_weights
    gates = jax.nn.sigmoid(mm(xn.reshape(rows, 2 * g.M), gate_weights))
    u = g.fill(u_ref[...]).reshape(g.SP, 2, g.I, g.M)
    packed_u = jnp.concatenate([u[:, 0], u[:, 1]], axis=-1).reshape(rows, 2 * g.M)
    gated = mm(packed_u, twice(wf_ref[...]))
    blended = gated * gates
    gm_ref[...] = blended.astype(BF16)
    gate_ref[...] = blended * (1.0 - gates)


def right_kernel(g, *refs):
    near_refs, (lt_ref, w2_ref, mask_ref, d_ref, go_ref, rg_ref) = refs[: g.C], refs[g.C :]
    for k in range(g.C):
        spot = (g.C - k) % g.C
        block = near_refs[k][: g.I * g.JC, :].reshape(g.I, g.JC, g.Z)
        d_ref[:, spot * g.JC : (spot + 1) * g.JC, :] = block
    masks = [mask_ref[k : k + 1, :] for k in range(g.SP)]
    scale = mask_ref[g.C * g.SP : g.C * g.SP + 1, :]
    right_grad = jnp.zeros((g.Q * g.S, g.N), F32)
    for i in range(0, g.I, 2):
        right_grad = right_grad + mm(
            lanes_of([lt_ref[i], lt_ref[i + 1]]), lanes_of([d_ref[i], d_ref[i + 1]]), NT
        )
    for t in range(g.NT):
        lanes = min(LANES, g.N - t * LANES)
        piece = right_grad[:, t * LANES : t * LANES + lanes]
        if lanes < LANES:
            piece = lanes_of([piece, jnp.zeros((g.Q * g.S, LANES - lanes), F32)])
        rg_ref[t] = piece
    deep = 2 * g.Q
    group = min(g.SP, LANES // deep)
    which = iota((group * deep, g.Q), 0)
    pick = (iota((group * deep, g.Q), 1) == which % deep // 2).astype(BF16)
    w2 = w2_ref[...]
    base = mm(pick, lanes_of([w2, w2]))
    which = iota(base.shape, 0)
    base = jnp.where(which % 2 == iota(base.shape, 1) // g.M, base, 0.0)
    weights = lanes_of([jnp.where(which // deep == k, base, 0.0) for k in range(group)]).astype(BF16)
    for k in range(0, g.SP, group):
        for t in range(g.NT):
            lanes = min(LANES, g.N - t * LANES)
            tall = rows_of(
                [rg_ref[t, pl.ds(k + m, deep, stride=g.SP), :] for m in range(group)]
            )
            tall = (tall * scale).T[:lanes]
            high, low = split_high_low(tall)
            part = mm(high, weights) + mm(low, weights)
            for m in range(group):
                go_ref[k + m, t * LANES : t * LANES + lanes, :] = (
                    part[:, m * 2 * g.M : (m + 1) * 2 * g.M] * masks[k + m]
                )


def outer_kernel(g, *refs):
    refs = list(refs)
    x_refs, refs = refs[: g.R], refs[g.R :]
    d_ref, left_ref, w2_ref, mask_ref, xall_ref, *refs = refs
    w_refs, (others_ref, spread_ref, rt_ref, ds_ref, all_ref) = refs[: g.D], refs[g.D :]
    row, col, depth = (lax.axis_index(a) for a in ("row", "col", "depth"))
    rows, deep = g.SP * g.I, 2 * g.QL
    for k, ref in zip((0, *g.order), x_refs, strict=True):
        place = g.place(jnp.bitwise_xor(row, k), col)
        xall_ref[:, pl.ds(place, g.I), :] = ref[:rows, :].reshape(g.SP, g.I, 2 * g.M)
        for m in range(g.EXTRA):
            block = ref[rows + m * g.I : rows + (m + 1) * g.I, :]
            others_ref[pl.ds(place, g.I), m * LANES : (m + 1) * LANES] = block
    second = column_weights(g, w2_ref[...])
    parts = [
        mm(second, (xall_ref[k].astype(F32) * mask_ref[k : k + 1, :]).astype(BF16), NT)
        for k in range(g.SP)
    ]
    if g.EXTRA:
        lanes = g.EXTRA * LANES
        eye = (iota((lanes, lanes), 0) == iota((lanes, lanes), 1)).astype(BF16)
        parts.append(mm(eye, others_ref[...], NT)[: (g.C - 1) * g.SP * deep])
    first = 0
    for part in parts:
        for t in range(g.NT):
            lanes = min(LANES, g.N - t * LANES)
            piece = part[:, t * LANES : t * LANES + lanes]
            spread_ref[t, first : first + part.shape[0], :lanes] = piece
        first += part.shape[0]
    for q in range(g.QL):
        for m in range(g.C):
            spot = (q * g.C + m) * g.S
            for t in range(g.NT):
                lanes = min(LANES, g.N - t * LANES)
                halves = [
                    spread_ref[t, pl.ds(m * g.SP * deep + half * g.QL + q, g.SP, stride=deep), :]
                    for half in range(2)
                ]
                rt_ref[spot : spot + g.S, t * LANES : t * LANES + lanes] = rows_of(halves)[
                    :, :lanes
                ].astype(BF16)
    rt = rt_ref[...]
    for i in range(0, g.I, 2):
        product = mm(rt, lanes_of([d_ref[i], d_ref[i + 1]]))
        for k in range(2):
            block = product[:, k * g.Z : (k + 1) * g.Z]
            ds_ref[:, :, i + k] = block.reshape(g.QL, g.C, g.S, g.Z).astype(BF16)
    eye = (iota((g.Q, g.Q), 0) == iota((g.Q, g.Q), 1)).astype(BF16)
    left_t = mm(eye, left_ref[...], NT).astype(BF16)
    scale = mask_ref[g.C * g.SP : g.C * g.SP + 1, :]
    entries = g.C * g.S * g.I
    for q in range(0, g.QL, 2):
        both = lanes_of([ds_ref[q].reshape(entries, g.Z), ds_ref[q + 1].reshape(entries, g.Z)])
        part = mm(left_t, both)
        all_ref[pl.ds(q, g.Q, stride=g.QL), :] = part[:, : g.Z] * scale
        all_ref[pl.ds(q + 1, g.Q, stride=g.QL), :] = part[:, g.Z :] * scale
    share = g.Q * g.QL // g.D
    for k in range(g.D):
        first = pl.multiple_of(lax.rem(depth + k, g.D) * share, share)
        w_refs[k][...] = all_ref[pl.ds(first, share), :]


def own_kernel(
    g, xall_ref, d_ref, ts_ref, w1_ref, w2_ref, mask_ref, part_ref, gg_ref, gate_weight_ref, own_ref,
    spread_ref, rt_ref, ds_ref, turn_ref,
):
    scale = mask_ref[g.C * g.SP : g.C * g.SP + 1, :]
    masks = [mask_ref[k : k + 1, :] for k in range(g.SP)]
    w2 = w2_ref[...]
    doubled = lanes_of([w2, w2])
    second = on_diagonal(rows_of([doubled, doubled]), g.M)
    for k in range(g.SP):
        live_x = (xall_ref[k].astype(F32) * masks[k]).astype(BF16)
        part = mm(second, live_x, NT)
        for t in range(g.NT):
            lanes = min(LANES, g.N - t * LANES)
            spread_ref[t, k * 2 * g.Q : (k + 1) * 2 * g.Q, :lanes] = part[
                :, t * LANES : t * LANES + lanes
            ]
    for q in range(g.Q):
        for t in range(g.NT):
            lanes = min(LANES, g.N - t * LANES)
            halves = [
                spread_ref[t, pl.ds(half * g.Q + q, g.SP, stride=2 * g.Q), :] for half in range(2)
            ]
            rt_ref[q * g.S : (q + 1) * g.S, t * LANES : t * LANES + lanes] = rows_of(halves)[
                :, :lanes
            ].astype(BF16)
    rt = rt_ref[...]
    for i in range(0, g.I, 2):
        product = mm(rt, lanes_of([d_ref[i], d_ref[i + 1]]))
        for k in range(2):
            block = product[:, k * g.Z : (k + 1) * g.Z]
            ds_ref[:, i + k] = block.reshape(g.Q, g.S, g.Z).astype(BF16)
    entries = g.S * g.I
    left_grad = jnp.zeros((entries, g.Q), F32)
    for q in range(0, g.Q, 2):
        both = lanes_of([ds_ref[q].reshape(entries, g.Z), ds_ref[q + 1].reshape(entries, g.Z)])
        left_grad = left_grad + mm(both, lanes_of([ts_ref[q], ts_ref[q + 1]]), NT)
    w1 = w1_ref[...]
    first_term = jnp.zeros((entries, 2 * g.M), F32)
    for piece in split_high_low(left_grad * scale[:, : g.Q]):
        first_term = first_term + mm(piece, lanes_of([w1, w1]))
    turn_ref[...] = first_term
    gate_term = mm(gg_ref[...], gate_weight_ref[...], NT)
    lane = iota((1, 2 * g.M), 1)
    for k in range(g.SP):
        rows = slice(k * g.I, (k + 1) * g.I)
        halves = [turn_ref[pl.ds(half * g.SP + k, g.I, stride=g.S), :] for half in range(2)]
        term = jnp.where(lane < g.M, halves[0], halves[1]) * mask_ref[k : k + 1, :]
        own_ref[rows, :] = part_ref[rows, :] + gate_term[rows] + term


def attend_kernel(g, *refs):
    refs = list(refs)
    xall_ref, refs = refs[0], refs[1:]
    logit_ref, near_refs, refs = refs[0], refs[1 : g.C], refs[g.C :]
    gm_ref, gate_ref, p_ref, go_ref, soft_ref, gs_ref, own_ref, gg_ref, *refs = refs
    send_refs, (total_ref,) = refs[: g.R - 1], refs[g.R - 1 :]
    row, col = lax.axis_index("row"), lax.axis_index("col")
    tall, blocks = logit_ref.shape[0], [logit_ref[...]]
    for k in range(1, g.C):
        parts = near_refs[g.C - k - 1][g.I * g.JC :, :].astype(F32)
        blocks.append((parts[:tall] + parts[tall : 2 * tall]) + parts[2 * tall :])
    logits = lanes_of(
        [rows_of([b[:, k * g.JC : (k + 1) * g.JC] for k in range(g.G)]) for b in blocks]
    )
    shifted = jnp.exp(logits - jnp.max(logits, -1, keepdims=True))
    soft = shifted / jnp.sum(shifted, -1, keepdims=True)
    soft_ref[...] = soft
    low = soft.astype(BF16)
    eye = (iota((g.N, g.N), 0) == iota((g.N, g.N), 1)).astype(BF16)
    low_t = mm(eye, low, NT).astype(BF16)
    value_weights = twice(p_ref[...])
    values = mm(xall_ref[...].reshape(g.SP * g.N, 2 * g.M), value_weights).astype(BF16)
    wide = value_weights.shape[1]
    head = iota((1, wide), 1) % (wide // 2) // (wide // 2 // g.H)
    grad_soft = jnp.zeros((g.H * g.I, g.N), F32)
    for k in range(g.SP):
        v = values[k * g.N : (k + 1) * g.N]
        crossed = mm(low, v)
        mixed = jnp.where(head == 0, crossed[: g.I], 0.0)
        for h in range(1, g.H):
            mixed = jnp.where(head == h, crossed[h * g.I : (h + 1) * g.I], mixed)
        rows = slice(k * g.I, (k + 1) * g.I)
        gg_ref[rows, :] = (gate_ref[rows, :] * mixed).astype(BF16)
        blended = gm_ref[rows, :]
        by_head = rows_of(
            [jnp.where(head == h, blended, jnp.zeros_like(blended)) for h in range(g.H)]
        )
        grad_soft = grad_soft + mm(by_head, v, NT)
        part = go_ref[k]
        for piece in split_high_low(mm(low_t, by_head)):
            part = part + mm(piece, value_weights, NT)
        total_ref[k] = part
    gs_ref[...] = grad_soft
    own = total_ref[:, pl.ds(g.place(row, col), g.I), :]
    own_ref[...] = own.reshape(g.SP * g.I, 2 * g.M)
    for x in range(1, g.R):
        block = total_ref[:, pl.ds(g.place(jnp.bitwise_xor(row, x), col), g.I), :]
        send_refs[x - 1][...] = block.reshape(g.SP * g.I, 2 * g.M).astype(BF16)


def pack_kernel(g, *refs):
    refs = list(refs)
    sums, refs = refs[: g.R - 1], refs[g.R - 1 :]
    parts, refs = refs[: g.D], refs[g.D :]
    outs, own_ref = refs[: g.R - 1], refs[g.R - 1]
    total = parts[0][...]
    for ref in parts[1:]:
        total = total + ref[...]
    total, rows = total.astype(BF16), g.SP * g.I
    own_ref[...] = total
    for x in range(1, g.R):
        outs[x - 1][:rows, :] = sums[x - 1][...]
        outs[x - 1][rows:, :] = total


def piece_kernel(g, own_ref, *refs):
    out_ref, order_ref = refs[-2:]
    row, rows = lax.axis_index("row"), g.SP * g.I
    order_ref[row] = own_ref[...]
    for k in range(1, g.R):
        order_ref[jnp.bitwise_xor(row, g.R - k)] = refs[k - 1][rows:, :]
    total = order_ref[0].astype(F32)
    for r in range(1, g.R):
        total = total + order_ref[r].astype(F32)
    out_ref[...] = total.astype(BF16)


def score_kernel(g, soft_ref, *refs):
    parts, refs = refs[: g.D], refs[g.D :]
    own_ref, out_refs, order_ref = refs[0], refs[1 : g.C], refs[g.C]
    depth = lax.axis_index("depth")
    for k in range(g.D):
        order_ref[lax.rem(depth - k + g.D, g.D)] = parts[k][...]
    grad_soft = order_ref[0]
    for k in range(1, g.D):
        grad_soft = grad_soft + order_ref[k]
    inner = jnp.sum(soft_ref[...] * grad_soft, -1, keepdims=True)
    for k in range(g.C):
        block = lanes_of([grad_soft[:, k * g.JC : (k + 1) * g.JC], inner])
        if k == 0:
            own_ref[...] = block
        else:
            out_refs[k - 1][...] = three_lanes(block)


def pair_kernel(g, e_ref, wl_ref, soft_ref, own_ref, *refs):
    got, pair_ref = refs[: g.C - 1], refs[g.C - 1]
    heads = g.H * g.I
    total = own_ref[...]
    for ref in got:
        total = total + join_three(ref[...], g.JC + 1)
    grad = soft_ref[:, : g.JC] * (total[:, : g.JC] - total[:, g.JC :])
    if g.JC < LANES:
        grad = lanes_of([grad, jnp.zeros((heads, LANES - g.JC), F32)])
    high, low = split_high_low(grad.T[: g.JC])
    grads = lanes_of([high, low])
    pick = (iota((heads, g.H), 0) // g.I == iota((heads, g.H), 1)).astype(BF16)
    base = mm(pick, wl_ref[...]).astype(BF16)
    token = iota((heads, 1), 0) % g.I
    for i in range(0, g.I, 2):
        weights = lanes_of(
            [jnp.where(token == i + k, base, jnp.zeros_like(base)) for k in range(2)]
        )
        upstream = mm(grads, rows_of([weights, weights]))
        for k in range(2):
            pair_ref[i + k] = standardize_backward(
                e_ref[i + k].astype(F32), upstream[:, k * g.Z : (k + 1) * g.Z]
            ).astype(BF16)


def reduce_kernel(g, x_ref, own_ref, *refs):
    got, out_ref = refs[:-1], refs[-1]
    rows = g.SP * g.I
    total = own_ref[...]
    for ref in got:
        total = total + ref[:rows, :].astype(F32)
    total = total.reshape(g.SP, 1, g.I, 2 * g.M)
    upstream = jnp.concatenate([total[..., : g.M], total[..., g.M :]], axis=1)
    upstream = upstream.reshape(g.S, g.I, g.M)[: g.SQ]
    msa = g.fill(standardize_backward(x_ref[...].astype(F32), upstream))
    msa = msa.reshape(g.SP, 2, g.I, g.M)
    msa = jnp.concatenate([msa[:, 0], msa[:, 1]], axis=-1).astype(BF16)
    out_ref[...] = msa.reshape(rows, 2 * g.M)


def across_kernel(g, *refs):
    out_ref = refs[-1]
    col = lax.axis_index("col")
    for k, ref in enumerate(refs[:-1]):
        out_ref[lax.rem(col - k + g.C, g.C)] = ref[...]


def unpack_kernel(g, *refs):
    parts, msa_ref = refs[: g.C], refs[g.C]
    col = lax.axis_index("col")
    for k, ref in enumerate(parts):
        msa = ref[...].astype(F32).reshape(g.SP, 1, g.I, 2 * g.M)
        msa = jnp.concatenate([msa[..., : g.M], msa[..., g.M :]], axis=1)
        msa = msa.reshape(g.S, g.I, g.M)[: g.SQ].astype(BF16)
        msa_ref[pl.ds(lax.rem(col - k + g.C, g.C) * g.SQ, g.SQ)] = msa


def finish_kernel(g, msa_ref, *refs):
    parts, (out_ref, matrix_ref) = refs[: g.D], refs[g.D :]
    depth = lax.axis_index("depth")
    out_ref[...] = msa_ref[...]
    share = g.Q // g.D
    for k in range(g.D):
        first = lax.rem(depth - k + g.D, g.D) * share
        for c in range(g.C):
            block = parts[k][c].astype(F32)
            matrix_ref[pl.ds(first, share), c * g.QL : (c + 1) * g.QL, :] = block


class Sizes:
    def __init__(self, x, e, wl, w1):
        self.R, self.C, self.D = (lax.axis_size(a) for a in ("row", "col", "depth"))
        self.I, self.M = x.shape[1:]
        self.JC, self.Z = e.shape[1:]
        self.H, self.Q = wl.shape[1], w1.shape[1]
        self.QL = self.Q // self.C
        self.SQ = x.shape[0] // self.C
        self.S = -(-self.SQ // 16) * 16
        self.SP, self.N = self.S // 2, self.R * self.I
        self.F = self.R // self.C
        self.NT = -(-self.N // LANES)
        self.G = max(1, LANES // self.JC)
        self.EXTRA = -(-(self.C - 1) * self.S * self.QL // LANES)
        self.carried = 0
        self.order = [*range(self.R // 2, self.R), *range(1, self.R // 2)]

    def fill(self, rows):
        if self.SQ == self.S:
            return rows
        return rows_of([rows, jnp.zeros((self.S - self.SQ, *rows.shape[1:]), rows.dtype)])

    def place(self, row, col):
        turn = lax.rem(row // self.F - col + self.C, self.C)
        return pl.multiple_of((turn * self.F + lax.rem(row, self.F)) * self.I, self.I)


def shift(array, axis, k):
    count = lax.axis_size(axis)
    return lax.ppermute(array, axis, [(i, (i + k) % count) for i in range(count)])


def swap(array, axis, x):
    return lax.ppermute(array, axis, [(i, i ^ x) for i in range(lax.axis_size(axis))])


def swapped(arrays, axis):
    return [swap(a, axis, k + 1) for k, a in reversed([*enumerate(arrays)])]


def shifted_all(array, axis):
    return [array] + [shift(array, axis, k) for k in range(1, lax.axis_size(axis))]


def per_device(
    homolog_ensemble,
    duplex_embedding,
    homolog_present_flags,
    resolved_position_flags,
    payload_weights,
    sigmoid_weights,
    averager_final_weights,
    first_operand_weights,
    second_operand_weights,
    duplex_logit_weights,
    tensor_product_weights,
    averager_upstream_adjoint,
    duplex_upstream_adjoint,
):
    g = Sizes(homolog_ensemble, duplex_embedding, duplex_logit_weights, first_operand_weights)
    shape = jax.ShapeDtypeStruct

    def call(kernel, name, args, outs, scratch=(), far=None, after=(), distant=False, us=1.0):
        size = sum(a.size * a.dtype.itemsize for a in args) + sum(
            math.prod(o.shape) * jnp.dtype(o.dtype).itemsize for o in outs
        )
        single = len(outs) == 1
        near = len(args) if far is None else far
        args = list(args[:near]) + [
            pltpu.with_memory_space_constraint(a, pltpu.HBM) for a in args[near:]
        ]

        if distant:
            after = [pltpu.with_memory_space_constraint(a, pltpu.HBM) for a in after]

        def body(*refs):
            kernel(g, *refs[: len(args)], *refs[len(args) + len(after) :])

        return pl.pallas_call(
            body,
            out_shape=outs[0] if single else tuple(outs),
            in_specs=[VMEM] * near + [FAR] * (len(args) - near) + [FAR if distant else VMEM] * len(after),
            out_specs=VMEM if single else (VMEM,) * len(outs),
            scratch_shapes=list(scratch),
            compiler_params=pltpu.CompilerParams(vmem_limit_bytes=40 * 1024 * 1024),
            cost_estimate=pl.CostEstimate(
                flops=int(us * 1.15e9), bytes_accessed=size, transcendentals=0
            ),
            name=name,
        )(*args, *after)

    heads = g.H * g.I
    rows = g.SP * g.I
    values = 2 * payload_weights.shape[1]
    pairs, tall = g.I * g.JC, heads // g.G
    xn, send, logits, near, x, e, wl, masks, w1, outer_weights, w2 = call(
        normalise_kernel,
        "normalise",
        (
            homolog_ensemble,
            duplex_embedding,
            duplex_upstream_adjoint.reshape(pairs, g.Z),
            resolved_position_flags.reshape(1, g.JC),
            duplex_logit_weights.T,
            homolog_present_flags,
            first_operand_weights.T,
            tensor_product_weights,
            second_operand_weights.T,
        ),
        [
            pltpu.VMEM((g.C, g.SP, g.I, 2 * g.M), BF16),
            pltpu.VMEM((rows + g.EXTRA * g.I, 2 * g.M), BF16),
            pltpu.VMEM((tall, g.G * g.JC), F32),
            pltpu.VMEM((pairs + 3 * tall, g.Z), BF16),
            pltpu.VMEM((g.SQ, g.I, g.M), BF16),
            pltpu.VMEM(duplex_embedding.shape, BF16),
            pltpu.VMEM((g.H, g.Z), BF16),
            pltpu.VMEM((g.C * g.SP + 8, 2 * g.M), F32),
            pltpu.VMEM((g.Q, g.M), BF16),
            pltpu.VMEM(tensor_product_weights.shape, BF16),
            pltpu.VMEM((g.Q, g.M), BF16),
        ],
        [
            pltpu.VMEM((1, g.JC), jnp.int32),
            pltpu.SMEM(homolog_present_flags.shape, jnp.int32),
            pltpu.VMEM(homolog_ensemble.shape, BF16),
            pltpu.VMEM(homolog_ensemble.shape, F32),
            pltpu.VMEM((g.I * g.H, LANES), F32),
            pltpu.SemaphoreType.DMA((9,)),
        ],
        far=0,
        us=2.0,
    )
    everyone = [send] + [swap(send, "row", k) for k in g.order]
    nears = shifted_all(near, "col")
    later = (
        sigmoid_weights,
        averager_final_weights.T,
        payload_weights,
    )
    g.carried = len(later)
    left, weights, left_weights, u, sg, wf, p = call(
        prepare_kernel,
        "prepare",
        (xn, w1, outer_weights, masks, averager_upstream_adjoint, *later),
        [
            pltpu.VMEM((g.C * g.I * g.S, g.Q), BF16),
            pltpu.VMEM((g.Q, g.Q, g.Z), BF16),
            pltpu.VMEM((g.I, g.Q * g.S, g.Z), BF16),
            pltpu.VMEM((g.SQ, g.I, g.M), BF16),
        ]
        + [pltpu.VMEM(a.shape, a.dtype) for a in later],
        [
            pltpu.VMEM(tensor_product_weights.shape, F32),
            pltpu.VMEM((2, rows, LANES), F32),
            pltpu.SemaphoreType.DMA,
            pltpu.SemaphoreType.DMA((len(later),)),
        ],
        far=4,
        us=0.01,
    )
    gate_weights, blended, gate_factor = call(
        gate_kernel,
        "gate",
        (xn, u, sg, wf),
        [
            pltpu.VMEM((2 * g.M, values), BF16),
            pltpu.VMEM((rows, values), BF16),
            pltpu.VMEM((rows, values), F32),
        ],
        after=nears[1:],
        us=0.01,
    )
    cotangents, second_term = call(
        right_kernel,
        "right",
        (*nears, left_weights, w2, masks),
        [pltpu.VMEM((g.I, g.N, g.Z), BF16), pltpu.VMEM((g.SP, g.N, 2 * g.M), F32)],
        [pltpu.VMEM((g.NT, g.Q * g.S, LANES), F32)],
        after=(gate_weights,),
        us=0.01,
    )
    share = g.Q * g.QL // g.D
    xall, *matrix_parts = call(
        outer_kernel,
        "outer",
        (*everyone, cotangents, left, w2, masks),
        [pltpu.VMEM((g.SP, g.N, 2 * g.M), BF16)] + [pltpu.VMEM((share, g.Z), F32)] * g.D,
        [
            pltpu.VMEM((g.N, max(1, g.EXTRA) * LANES), BF16),
            pltpu.VMEM((g.NT, g.C * g.SP * 2 * g.QL, LANES), F32),
            pltpu.VMEM((g.QL * g.C * g.S, g.N), BF16),
            pltpu.VMEM((g.QL, g.C, g.I, g.S, g.Z), BF16),
            pltpu.VMEM((g.Q * g.QL, g.Z), F32),
        ],
        after=(second_term,),
        us=0.05,
    )
    matrix_parts = [matrix_parts[0]] + [
        shift(a, "depth", k + 1) for k, a in enumerate(matrix_parts[1:])
    ]
    soft, grad_soft, own, gate_grads, *sums = call(
        attend_kernel,
        "attend",
        (xall, logits, *nears[1:], blended, gate_factor, p, second_term),
        [
            pltpu.VMEM((heads, g.N), F32),
            pltpu.VMEM((heads, g.N), F32),
            pltpu.VMEM((rows, 2 * g.M), F32),
            pltpu.VMEM((rows, values), BF16),
        ]
        + [pltpu.VMEM((rows, 2 * g.M), BF16)] * (g.R - 1),
        [pltpu.VMEM((g.SP, g.N, 2 * g.M), F32)],
        us=3.0,
    )
    *sums, piece = call(
        pack_kernel,
        "pack",
        (*sums, *matrix_parts),
        [pltpu.VMEM((rows + share, 2 * g.M), BF16)] * (g.R - 1) + [pltpu.VMEM((share, g.Z), BF16)],
        us=0.2,
    )
    sums = swapped(sums, "row")
    wide = -(-3 * (g.JC + 1) // LANES) * LANES
    scores, *sends = call(
        score_kernel,
        "score",
        (soft, *shifted_all(grad_soft, "depth")),
        [pltpu.VMEM((heads, g.JC + 1), F32)] + [pltpu.VMEM((heads, wide), BF16)] * (g.C - 1),
        [pltpu.VMEM((g.D, heads, g.N), F32)],
        after=(piece,),
        us=0.2,
    )
    arrived = [shift(a, "col", k + 1) for k, a in enumerate(sends)]
    own = call(
        own_kernel,
        "own",
        (xall, cotangents, weights, w1, w2, masks, own, gate_grads, gate_weights),
        [pltpu.VMEM((rows, 2 * g.M), F32)],
        [
            pltpu.VMEM((g.NT, g.SP * 2 * g.Q, LANES), F32),
            pltpu.VMEM((g.Q * g.S, g.N), BF16),
            pltpu.VMEM((g.Q, g.I, g.S, g.Z), BF16),
            pltpu.VMEM((g.I * g.S, 2 * g.M), F32),
        ],
        after=(scores,),
        us=0.01,
    )
    piece = call(
        piece_kernel,
        "piece",
        (piece, *sums),
        [pltpu.VMEM((share, g.Z), BF16)],
        [pltpu.VMEM((g.R, share, g.Z), BF16)],
        after=(own,),
        us=0.1,
    )
    pieces = shifted_all(piece, "col")
    part = call(
        reduce_kernel,
        "reduce",
        (x, own, *sums),
        [pltpu.VMEM((rows, 2 * g.M), BF16)],
        after=(piece,),
    )
    pairwise_gradient = call(
        pair_kernel,
        "pair",
        (e, wl, soft, scores, *arrived),
        [shape(duplex_embedding.shape, BF16)],
        after=(part,),
        us=0.01,
    )
    matrix = call(
        across_kernel,
        "across",
        pieces,
        [pltpu.VMEM((g.C, share, g.Z), BF16)],
        after=(pairwise_gradient,),
        distant=True,
        us=0.1,
    ).reshape(g.C, g.Q // g.D, g.QL, g.Z)
    ensemble_derivative = call(
        unpack_kernel,
        "unpack",
        shifted_all(part, "col"),
        [pltpu.VMEM(homolog_ensemble.shape, BF16)],
        after=(matrix,),
    )
    ensemble_derivative, outer_matrix_gradient = call(
        finish_kernel,
        "finish",
        (ensemble_derivative, *shifted_all(matrix, "depth")),
        [shape(homolog_ensemble.shape, BF16), shape((g.Q, g.Q, g.Z), F32)],
    )
    outer_matrix_gradient = outer_matrix_gradient.reshape(tensor_product_weights.shape)
    return (ensemble_derivative, pairwise_gradient, outer_matrix_gradient)


def solution(mesh):
    in_specs = (
        P(("parts", "depth"), "row", None),
        P(("parts", "row"), "col", None),
        P("parts"),
        P(("parts", "col")),
        P(),
        P(),
        P(),
        P(),
        P(),
        P(),
        P(),
        P(("parts", "depth"), "row", None),
        P(("parts", "row"), "col", None),
    )
    out_specs = (
        P(("parts", "depth"), "row", None),
        P(("parts", "row"), "col", None),
        P("parts", None),
    )
    return jax.shard_map(
        per_device, mesh=mesh, in_specs=in_specs, out_specs=out_specs, check_vma=False
    )
```

```python
import functools
import math

import jax
import jax.numpy as jnp
from jax import lax
from jax.experimental import pallas as pl
from jax.experimental.pallas import tpu as pltpu
from jax.sharding import PartitionSpec as P

EPS = 1e-05
PENALTY = 10000.0
F32 = jnp.float32
BF16 = jnp.bfloat16
LANES = 128
NN = (((1,), (0,)), ((), ()))
NT = (((1,), (1,)), ((), ()))
VMEM = pl.BlockSpec(memory_space=pltpu.VMEM)
FAR = pl.BlockSpec(memory_space=pl.ANY)


def mm(a, b, dims=NN):
    return lax.dot_general(a, b, dims, preferred_element_type=F32)


def split_high_low(value):
    high = value.astype(BF16)
    return high, (value - high.astype(F32)).astype(BF16)


def iota(shape, dim):
    return lax.broadcasted_iota(jnp.int32, shape, dim)


def lanes_of(pieces):
    return pieces[0] if len(pieces) == 1 else jnp.concatenate(pieces, axis=-1)


def rows_of(pieces):
    return pieces[0] if len(pieces) == 1 else jnp.concatenate(pieces, axis=0)


def standardize(values):
    centred = values - jnp.mean(values, -1, keepdims=True)
    inverse = lax.rsqrt(jnp.mean(centred * centred, -1, keepdims=True) + EPS)
    return centred * inverse, inverse


def standardize_backward(values, upstream):
    scaled, inverse = standardize(values)
    mean_grad = jnp.mean(upstream, -1, keepdims=True)
    mean_cross = jnp.mean(upstream * scaled, -1, keepdims=True)
    return (upstream - mean_grad - scaled * mean_cross) * inverse


def on_diagonal(block, width):
    rows, lanes = block.shape
    same = iota(block.shape, 0) // (rows // 2) == iota(block.shape, 1) // width
    return jnp.where(same, block, jnp.zeros_like(block))


def split_three(value):
    high = value.astype(BF16)
    rest = value - high.astype(F32)
    middle = rest.astype(BF16)
    return [high, middle, (rest - middle.astype(F32)).astype(BF16)]


def three_lanes(value):
    rows, width = value.shape
    fill = -(3 * width) % LANES
    return lanes_of(split_three(value) + [jnp.zeros((rows, fill), BF16)] * (fill > 0))


def join_three(parts, width):
    wide = parts.astype(F32)
    return (wide[:, :width] + wide[:, width : 2 * width]) + wide[:, 2 * width : 3 * width]


def twice(weights):
    zero = jnp.zeros_like(weights)
    return rows_of([lanes_of([weights, zero]), lanes_of([zero, weights])])


def column_weights(g, w2):
    rows = iota((2 * g.QL, g.Q), 0) % g.QL + lax.axis_index("col") * g.QL
    pick = (iota((2 * g.QL, g.Q), 1) == rows).astype(BF16)
    return on_diagonal(mm(pick, lanes_of([w2, w2])), g.M).astype(BF16)


def normalise_kernel(
    g, x_hbm, e_hbm, dd_hbm, flag_hbm, wl_hbm, live_hbm, w1_hbm, t_hbm, w2_hbm, every_hbm, *refs
):
    xn_ref, send_ref, logit_ref, near_ref, x_ref, e_ref, wl_ref, mask_ref, w1_ref, t_ref, w2_ref = refs[:11]
    flag_in, live_in, every_in, x_in, norm_ref, rows_ref, sem = refs[11:]
    col = lax.axis_index("col")
    pairs = g.I * g.JC
    copies = [
        pltpu.make_async_copy(a, b, sem.at[k])
        for k, (a, b) in enumerate(
            [
                (x_hbm, x_in),
                (e_hbm, e_ref),
                (wl_hbm, wl_ref),
                (flag_hbm, flag_in),
                (dd_hbm, near_ref.at[pl.ds(0, pairs)]),
                (live_hbm, live_in),
                (w1_hbm, w1_ref),
                (t_hbm, t_ref),
                (w2_hbm, w2_ref),
                (every_hbm, every_in),
            ]
        )
    ]
    for copy in copies:
        copy.start()
    copies[5].wait()
    lane = iota((1, 2 * g.M), 1)
    groups = [lax.rem(col + m, g.C) for m in range(g.C)]
    for m, group in enumerate(groups):
        first = (lax.axis_index("depth") * g.C + group) * g.SQ
        for k in range(g.SP):
            if 2 * k + 1 < g.SQ:
                flags = jnp.where(lane < g.M, live_in[first + 2 * k], live_in[first + 2 * k + 1])
                flags = flags.astype(F32)
            else:
                flags = jnp.zeros((1, 2 * g.M), F32)
            mask_ref[m * g.SP + k : m * g.SP + k + 1, :] = flags
    copies[9].wait()
    count = jnp.sum(every_in[...].astype(F32), -1, keepdims=True)
    mask_ref[g.C * g.SP : g.C * g.SP + 1, :] = jnp.broadcast_to(1.0 / (0.001 + count), (1, 2 * g.M))
    copies[0].wait()
    copies[8].wait()
    norm_ref[...] = standardize(x_in[...].astype(F32))[0]
    x_ref[...] = x_in[pl.ds(col * g.SQ, g.SQ)]
    second = column_weights(g, w2_ref[...])
    rows, blocks = g.SP * g.I, []
    for m, group in enumerate(groups):
        normed = g.fill(norm_ref[pl.ds(group * g.SQ, g.SQ)]).reshape(g.SP, 2, g.I, g.M)
        packed = jnp.concatenate([normed[:, 0], normed[:, 1]], axis=-1).astype(BF16)
        xn_ref[m] = packed
        if m == 0:
            send_ref[:rows, :] = packed.reshape(rows, 2 * g.M)
        else:
            masks = [mask_ref[m * g.SP + k : m * g.SP + k + 1, :] for k in range(g.SP)]
            live = rows_of([(packed[k].astype(F32) * masks[k]).astype(BF16) for k in range(g.SP)])
            factors = mm(live, second, NT)
            blocks += [factors[k * g.I : (k + 1) * g.I] for k in range(g.SP)]
    if blocks:
        wide = lanes_of(blocks)
        fill = -wide.shape[1] % LANES
        if fill:
            wide = lanes_of([wide, jnp.zeros((g.I, fill), F32)])
        for k in range(g.EXTRA):
            block = wide[:, k * LANES : (k + 1) * LANES]
            send_ref[rows + k * g.I : rows + (k + 1) * g.I, :] = block.astype(BF16)
    for copy in copies[1:4]:
        copy.wait()
    pair = standardize(e_ref[...].astype(F32).reshape(pairs, g.Z))[0].astype(BF16)
    penalty = (flag_in[...].astype(F32) - 1.0) * PENALTY
    weights = wl_ref[...]
    for i in range(g.I):
        rows_ref[i * g.H : (i + 1) * g.H, : g.JC] = (
            mm(weights, pair[i * g.JC : (i + 1) * g.JC], NT) + penalty
        )
    logits = rows_of([rows_ref[pl.ds(h, g.I, stride=g.H), :][:, : g.JC] for h in range(g.H)])
    tall = g.H * g.I // g.G
    packed = lanes_of([logits[k * tall : (k + 1) * tall] for k in range(g.G)])
    logit_ref[...] = packed
    near_ref[pairs:, :] = rows_of(split_three(packed))
    for copy in (copies[4], *copies[6:8]):
        copy.wait()


def prepare_kernel(g, xn_ref, w1_ref, t_ref, mask_ref, u_hbm, *refs):
    refs = list(refs)
    count = g.carried
    sources, refs = refs[:count], refs[count:]
    left_ref, ts_ref, lt_ref, u_ref, refs = refs[0], refs[1], refs[2], refs[3], refs[4:]
    targets, (wide_ref, half_ref, first_sem, later_sem) = refs[:count], refs[count:]
    first = lax.axis_index("col") * g.SQ
    copies = [pltpu.make_async_copy(u_hbm.at[pl.ds(first, g.SQ)], u_ref, first_sem)]
    copies += [
        pltpu.make_async_copy(a, b, later_sem.at[k])
        for k, (a, b) in enumerate(zip(sources, targets, strict=True))
    ]
    for copy in copies:
        copy.start()
    w1 = rows_of([w1_ref[...], jnp.zeros((LANES - g.Q, g.M), BF16)])
    zero = jnp.zeros_like(w1)
    for m in range(g.C):
        masks = [mask_ref[m * g.SP + k : m * g.SP + k + 1, :] for k in range(g.SP)]
        live_xn = rows_of(
            [(xn_ref[m, k].astype(F32) * masks[k]).astype(BF16) for k in range(g.SP)]
        )
        half_ref[0] = mm(live_xn, lanes_of([w1, zero]), NT)
        half_ref[1] = mm(live_xn, lanes_of([zero, w1]), NT)
        for i in range(g.I):
            halves = [half_ref[half, pl.ds(i, g.SP, stride=g.I), :] for half in range(2)]
            first = (m * g.I + i) * g.S
            left_ref[first : first + g.S, :] = rows_of(halves)[:, : g.Q].astype(BF16)
    wide_ref[...] = t_ref[...].astype(F32)
    for q in range(g.Q):
        ts_ref[q] = wide_ref[pl.ds(q, g.Q, stride=g.Q), :].astype(BF16)
    left = left_ref[: g.I * g.S, :]
    for q in range(0, g.Q, 2):
        product = mm(left, lanes_of([ts_ref[q], ts_ref[q + 1]]))
        for k in range(2):
            block = product[:, k * g.Z : (k + 1) * g.Z].reshape(g.I, g.S, g.Z)
            lt_ref[:, (q + k) * g.S : (q + k + 1) * g.S, :] = block.astype(BF16)
    for copy in copies:
        copy.wait()


def gate_kernel(g, xn_ref, u_ref, sg_ref, wf_ref, gate_weight_ref, gm_ref, gate_ref):
    rows = g.SP * g.I
    xn = xn_ref[0]
    gate_weights = twice(sg_ref[...])
    gate_weight_ref[...] = gate_weights
    gates = jax.nn.sigmoid(mm(xn.reshape(rows, 2 * g.M), gate_weights))
    u = g.fill(u_ref[...]).reshape(g.SP, 2, g.I, g.M)
    packed_u = jnp.concatenate([u[:, 0], u[:, 1]], axis=-1).reshape(rows, 2 * g.M)
    gated = mm(packed_u, twice(wf_ref[...]))
    blended = gated * gates
    gm_ref[...] = blended.astype(BF16)
    gate_ref[...] = blended * (1.0 - gates)


def right_kernel(g, *refs):
    near_refs, (lt_ref, w2_ref, mask_ref, d_ref, go_ref, rg_ref) = refs[: g.C], refs[g.C :]
    for k in range(g.C):
        spot = (g.C - k) % g.C
        block = near_refs[k][: g.I * g.JC, :].reshape(g.I, g.JC, g.Z)
        d_ref[:, spot * g.JC : (spot + 1) * g.JC, :] = block
    masks = [mask_ref[k : k + 1, :] for k in range(g.SP)]
    scale = mask_ref[g.C * g.SP : g.C * g.SP + 1, :]
    right_grad = jnp.zeros((g.Q * g.S, g.N), F32)
    for i in range(0, g.I, 2):
        right_grad = right_grad + mm(
            lanes_of([lt_ref[i], lt_ref[i + 1]]), lanes_of([d_ref[i], d_ref[i + 1]]), NT
        )
    for t in range(g.NT):
        lanes = min(LANES, g.N - t * LANES)
        piece = right_grad[:, t * LANES : t * LANES + lanes]
        if lanes < LANES:
            piece = lanes_of([piece, jnp.zeros((g.Q * g.S, LANES - lanes), F32)])
        rg_ref[t] = piece
    deep = 2 * g.Q
    group = min(g.SP, LANES // deep)
    which = iota((group * deep, g.Q), 0)
    pick = (iota((group * deep, g.Q), 1) == which % deep // 2).astype(BF16)
    w2 = w2_ref[...]
    base = mm(pick, lanes_of([w2, w2]))
    which = iota(base.shape, 0)
    base = jnp.where(which % 2 == iota(base.shape, 1) // g.M, base, 0.0)
    weights = lanes_of([jnp.where(which // deep == k, base, 0.0) for k in range(group)]).astype(BF16)
    for k in range(0, g.SP, group):
        for t in range(g.NT):
            lanes = min(LANES, g.N - t * LANES)
            tall = rows_of(
                [rg_ref[t, pl.ds(k + m, deep, stride=g.SP), :] for m in range(group)]
            )
            tall = (tall * scale).T[:lanes]
            high, low = split_high_low(tall)
            part = mm(high, weights) + mm(low, weights)
            for m in range(group):
                go_ref[k + m, t * LANES : t * LANES + lanes, :] = (
                    part[:, m * 2 * g.M : (m + 1) * 2 * g.M] * masks[k + m]
                )


def outer_kernel(g, *refs):
    refs = list(refs)
    x_refs, refs = refs[: g.R], refs[g.R :]
    d_ref, left_ref, w2_ref, mask_ref, xall_ref, *refs = refs
    w_refs, (others_ref, spread_ref, rt_ref, ds_ref, all_ref) = refs[: g.D], refs[g.D :]
    row, col, depth = (lax.axis_index(a) for a in ("row", "col", "depth"))
    rows, deep = g.SP * g.I, 2 * g.QL
    for k, ref in zip((0, *g.order), x_refs, strict=True):
        place = g.place(jnp.bitwise_xor(row, k), col)
        xall_ref[:, pl.ds(place, g.I), :] = ref[:rows, :].reshape(g.SP, g.I, 2 * g.M)
        for m in range(g.EXTRA):
            block = ref[rows + m * g.I : rows + (m + 1) * g.I, :]
            others_ref[pl.ds(place, g.I), m * LANES : (m + 1) * LANES] = block
    second = column_weights(g, w2_ref[...])
    parts = [
        mm(second, (xall_ref[k].astype(F32) * mask_ref[k : k + 1, :]).astype(BF16), NT)
        for k in range(g.SP)
    ]
    if g.EXTRA:
        lanes = g.EXTRA * LANES
        eye = (iota((lanes, lanes), 0) == iota((lanes, lanes), 1)).astype(BF16)
        parts.append(mm(eye, others_ref[...], NT)[: (g.C - 1) * g.SP * deep])
    first = 0
    for part in parts:
        for t in range(g.NT):
            lanes = min(LANES, g.N - t * LANES)
            piece = part[:, t * LANES : t * LANES + lanes]
            spread_ref[t, first : first + part.shape[0], :lanes] = piece
        first += part.shape[0]
    for q in range(g.QL):
        for m in range(g.C):
            spot = (q * g.C + m) * g.S
            for t in range(g.NT):
                lanes = min(LANES, g.N - t * LANES)
                halves = [
                    spread_ref[t, pl.ds(m * g.SP * deep + half * g.QL + q, g.SP, stride=deep), :]
                    for half in range(2)
                ]
                rt_ref[spot : spot + g.S, t * LANES : t * LANES + lanes] = rows_of(halves)[
                    :, :lanes
                ].astype(BF16)
    rt = rt_ref[...]
    for i in range(0, g.I, 2):
        product = mm(rt, lanes_of([d_ref[i], d_ref[i + 1]]))
        for k in range(2):
            block = product[:, k * g.Z : (k + 1) * g.Z]
            ds_ref[:, :, i + k] = block.reshape(g.QL, g.C, g.S, g.Z).astype(BF16)
    eye = (iota((g.Q, g.Q), 0) == iota((g.Q, g.Q), 1)).astype(BF16)
    left_t = mm(eye, left_ref[...], NT).astype(BF16)
    scale = mask_ref[g.C * g.SP : g.C * g.SP + 1, :]
    entries = g.C * g.S * g.I
    for q in range(0, g.QL, 2):
        both = lanes_of([ds_ref[q].reshape(entries, g.Z), ds_ref[q + 1].reshape(entries, g.Z)])
        part = mm(left_t, both)
        all_ref[pl.ds(q, g.Q, stride=g.QL), :] = part[:, : g.Z] * scale
        all_ref[pl.ds(q + 1, g.Q, stride=g.QL), :] = part[:, g.Z :] * scale
    share = g.Q * g.QL // g.D
    for k in range(g.D):
        first = pl.multiple_of(lax.rem(depth + k, g.D) * share, share)
        w_refs[k][...] = all_ref[pl.ds(first, share), :]


def own_kernel(
    g, xall_ref, d_ref, ts_ref, w1_ref, w2_ref, mask_ref, part_ref, gg_ref, gate_weight_ref, own_ref,
    spread_ref, rt_ref, ds_ref, turn_ref,
):
    scale = mask_ref[g.C * g.SP : g.C * g.SP + 1, :]
    masks = [mask_ref[k : k + 1, :] for k in range(g.SP)]
    w2 = w2_ref[...]
    doubled = lanes_of([w2, w2])
    second = on_diagonal(rows_of([doubled, doubled]), g.M)
    for k in range(g.SP):
        live_x = (xall_ref[k].astype(F32) * masks[k]).astype(BF16)
        part = mm(second, live_x, NT)
        for t in range(g.NT):
            lanes = min(LANES, g.N - t * LANES)
            spread_ref[t, k * 2 * g.Q : (k + 1) * 2 * g.Q, :lanes] = part[
                :, t * LANES : t * LANES + lanes
            ]
    for q in range(g.Q):
        for t in range(g.NT):
            lanes = min(LANES, g.N - t * LANES)
            halves = [
                spread_ref[t, pl.ds(half * g.Q + q, g.SP, stride=2 * g.Q), :] for half in range(2)
            ]
            rt_ref[q * g.S : (q + 1) * g.S, t * LANES : t * LANES + lanes] = rows_of(halves)[
                :, :lanes
            ].astype(BF16)
    rt = rt_ref[...]
    for i in range(0, g.I, 2):
        product = mm(rt, lanes_of([d_ref[i], d_ref[i + 1]]))
        for k in range(2):
            block = product[:, k * g.Z : (k + 1) * g.Z]
            ds_ref[:, i + k] = block.reshape(g.Q, g.S, g.Z).astype(BF16)
    entries = g.S * g.I
    left_grad = jnp.zeros((entries, g.Q), F32)
    for q in range(0, g.Q, 2):
        both = lanes_of([ds_ref[q].reshape(entries, g.Z), ds_ref[q + 1].reshape(entries, g.Z)])
        left_grad = left_grad + mm(both, lanes_of([ts_ref[q], ts_ref[q + 1]]), NT)
    w1 = w1_ref[...]
    first_term = jnp.zeros((entries, 2 * g.M), F32)
    for piece in split_high_low(left_grad * scale[:, : g.Q]):
        first_term = first_term + mm(piece, lanes_of([w1, w1]))
    turn_ref[...] = first_term
    gate_term = mm(gg_ref[...], gate_weight_ref[...], NT)
    lane = iota((1, 2 * g.M), 1)
    for k in range(g.SP):
        rows = slice(k * g.I, (k + 1) * g.I)
        halves = [turn_ref[pl.ds(half * g.SP + k, g.I, stride=g.S), :] for half in range(2)]
        term = jnp.where(lane < g.M, halves[0], halves[1]) * mask_ref[k : k + 1, :]
        own_ref[rows, :] = part_ref[rows, :] + gate_term[rows] + term


def attend_kernel(g, *refs):
    refs = list(refs)
    xall_ref, refs = refs[0], refs[1:]
    logit_ref, near_refs, refs = refs[0], refs[1 : g.C], refs[g.C :]
    gm_ref, gate_ref, p_ref, go_ref, soft_ref, gs_ref, own_ref, gg_ref, *refs = refs
    send_refs, (total_ref,) = refs[: g.R - 1], refs[g.R - 1 :]
    row, col = lax.axis_index("row"), lax.axis_index("col")
    tall, blocks = logit_ref.shape[0], [logit_ref[...]]
    for k in range(1, g.C):
        parts = near_refs[g.C - k - 1][g.I * g.JC :, :].astype(F32)
        blocks.append((parts[:tall] + parts[tall : 2 * tall]) + parts[2 * tall :])
    logits = lanes_of(
        [rows_of([b[:, k * g.JC : (k + 1) * g.JC] for k in range(g.G)]) for b in blocks]
    )
    shifted = jnp.exp(logits - jnp.max(logits, -1, keepdims=True))
    soft = shifted / jnp.sum(shifted, -1, keepdims=True)
    soft_ref[...] = soft
    low = soft.astype(BF16)
    eye = (iota((g.N, g.N), 0) == iota((g.N, g.N), 1)).astype(BF16)
    low_t = mm(eye, low, NT).astype(BF16)
    value_weights = twice(p_ref[...])
    values = mm(xall_ref[...].reshape(g.SP * g.N, 2 * g.M), value_weights).astype(BF16)
    half = value_weights.shape[1] // 2
    width = half // g.H
    group = LANES // width
    count = g.H // group
    tall = group * g.I
    head = iota((1, 2 * LANES), 1) % LANES // width

    def lanes(array, k):
        return lanes_of([array[:, s * half + k * LANES : s * half + (k + 1) * LANES] for s in range(2)])

    group_weights = [lanes(value_weights, k) for k in range(count)]
    low_t = lanes_of([low_t, low_t])
    grad_soft = [jnp.zeros((tall, g.N), F32) for _ in range(count)]
    for k in range(g.SP):
        v = values[k * g.N : (k + 1) * g.N]
        rows = slice(k * g.I, (k + 1) * g.I)
        blended, factor = gm_ref[rows, :], gate_ref[rows, :]
        projected = []
        for m in range(count):
            vm = lanes(v, m)
            crossed = mm(low[m * tall : (m + 1) * tall], vm)
            mixed = crossed[: g.I]
            for h in range(1, group):
                mixed = jnp.where(head == h, crossed[h * g.I : (h + 1) * g.I], mixed)
            gate_grad = (lanes(factor, m) * mixed).astype(BF16)
            for s in range(2):
                first = s * half + m * LANES
                gg_ref[rows, first : first + LANES] = gate_grad[:, s * LANES : (s + 1) * LANES]
            bm = lanes(blended, m)
            by_head = rows_of([jnp.where(head == h, bm, jnp.zeros_like(bm)) for h in range(group)])
            grad_soft[m] = grad_soft[m] + mm(by_head, vm, NT)
            projected.append(mm(by_head, group_weights[m], NT))
        total_ref[k] = go_ref[k] + mm(low_t, rows_of([*split_high_low(rows_of(projected))]))
    gs_ref[...] = rows_of(grad_soft)
    own = total_ref[:, pl.ds(g.place(row, col), g.I), :]
    own_ref[...] = own.reshape(g.SP * g.I, 2 * g.M)
    for x in range(1, g.R):
        block = total_ref[:, pl.ds(g.place(jnp.bitwise_xor(row, x), col), g.I), :]
        send_refs[x - 1][...] = block.reshape(g.SP * g.I, 2 * g.M).astype(BF16)


def pack_kernel(g, *refs):
    refs = list(refs)
    sums, refs = refs[: g.R - 1], refs[g.R - 1 :]
    parts, refs = refs[: g.D], refs[g.D :]
    outs, own_ref = refs[: g.R - 1], refs[g.R - 1]
    total = parts[0][...]
    for ref in parts[1:]:
        total = total + ref[...]
    total, rows = total.astype(BF16), g.SP * g.I
    own_ref[...] = total
    for x in range(1, g.R):
        outs[x - 1][:rows, :] = sums[x - 1][...]
        outs[x - 1][rows:, :] = total


def piece_kernel(g, own_ref, *refs):
    out_ref, order_ref = refs[-2:]
    row, rows = lax.axis_index("row"), g.SP * g.I
    order_ref[row] = own_ref[...]
    for k in range(1, g.R):
        order_ref[jnp.bitwise_xor(row, g.R - k)] = refs[k - 1][rows:, :]
    total = order_ref[0].astype(F32)
    for r in range(1, g.R):
        total = total + order_ref[r].astype(F32)
    out_ref[...] = total.astype(BF16)


def score_kernel(g, soft_ref, *refs):
    parts, refs = refs[: g.D], refs[g.D :]
    own_ref, out_refs, order_ref = refs[0], refs[1 : g.C], refs[g.C]
    depth = lax.axis_index("depth")
    for k in range(g.D):
        order_ref[lax.rem(depth - k + g.D, g.D)] = parts[k][...]
    grad_soft = order_ref[0]
    for k in range(1, g.D):
        grad_soft = grad_soft + order_ref[k]
    inner = jnp.sum(soft_ref[...] * grad_soft, -1, keepdims=True)
    for k in range(g.C):
        block = lanes_of([grad_soft[:, k * g.JC : (k + 1) * g.JC], inner])
        if k == 0:
            own_ref[...] = block
        else:
            out_refs[k - 1][...] = three_lanes(block)


def pair_kernel(g, e_ref, wl_ref, soft_ref, own_ref, *refs):
    got, pair_ref = refs[: g.C - 1], refs[g.C - 1]
    heads = g.H * g.I
    total = own_ref[...]
    for ref in got:
        total = total + join_three(ref[...], g.JC + 1)
    grad = soft_ref[:, : g.JC] * (total[:, : g.JC] - total[:, g.JC :])
    if g.JC < LANES:
        grad = lanes_of([grad, jnp.zeros((heads, LANES - g.JC), F32)])
    high, low = split_high_low(grad.T[: g.JC])
    grads = lanes_of([high, low])
    pick = (iota((heads, g.H), 0) // g.I == iota((heads, g.H), 1)).astype(BF16)
    base = mm(pick, wl_ref[...]).astype(BF16)
    token = iota((heads, 1), 0) % g.I
    for i in range(0, g.I, 2):
        weights = lanes_of(
            [jnp.where(token == i + k, base, jnp.zeros_like(base)) for k in range(2)]
        )
        upstream = mm(grads, rows_of([weights, weights]))
        for k in range(2):
            pair_ref[i + k] = standardize_backward(
                e_ref[i + k].astype(F32), upstream[:, k * g.Z : (k + 1) * g.Z]
            ).astype(BF16)


def reduce_kernel(g, x_ref, own_ref, *refs):
    got, out_ref = refs[:-1], refs[-1]
    rows = g.SP * g.I
    total = own_ref[...]
    for ref in got:
        total = total + ref[:rows, :].astype(F32)
    total = total.reshape(g.SP, 1, g.I, 2 * g.M)
    upstream = jnp.concatenate([total[..., : g.M], total[..., g.M :]], axis=1)
    upstream = upstream.reshape(g.S, g.I, g.M)[: g.SQ]
    msa = g.fill(standardize_backward(x_ref[...].astype(F32), upstream))
    msa = msa.reshape(g.SP, 2, g.I, g.M)
    msa = jnp.concatenate([msa[:, 0], msa[:, 1]], axis=-1).astype(BF16)
    out_ref[...] = msa.reshape(rows, 2 * g.M)


def across_kernel(g, *refs):
    out_ref = refs[-1]
    col = lax.axis_index("col")
    for k, ref in enumerate(refs[:-1]):
        out_ref[lax.rem(col - k + g.C, g.C)] = ref[...]


def unpack_kernel(g, *refs):
    parts, msa_ref = refs[: g.C], refs[g.C]
    col = lax.axis_index("col")
    for k, ref in enumerate(parts):
        msa = ref[...].astype(F32).reshape(g.SP, 1, g.I, 2 * g.M)
        msa = jnp.concatenate([msa[..., : g.M], msa[..., g.M :]], axis=1)
        msa = msa.reshape(g.S, g.I, g.M)[: g.SQ].astype(BF16)
        msa_ref[pl.ds(lax.rem(col - k + g.C, g.C) * g.SQ, g.SQ)] = msa


def finish_kernel(g, msa_ref, *refs):
    parts, (out_ref, matrix_ref) = refs[: g.D], refs[g.D :]
    depth = lax.axis_index("depth")
    out_ref[...] = msa_ref[...]
    share = g.Q // g.D
    for k in range(g.D):
        first = lax.rem(depth - k + g.D, g.D) * share
        for c in range(g.C):
            block = parts[k][c].astype(F32)
            matrix_ref[pl.ds(first, share), c * g.QL : (c + 1) * g.QL, :] = block


class Sizes:
    def __init__(self, x, e, wl, w1):
        self.R, self.C, self.D = (lax.axis_size(a) for a in ("row", "col", "depth"))
        self.I, self.M = x.shape[1:]
        self.JC, self.Z = e.shape[1:]
        self.H, self.Q = wl.shape[1], w1.shape[1]
        self.QL = self.Q // self.C
        self.SQ = x.shape[0] // self.C
        self.S = -(-self.SQ // 16) * 16
        self.SP, self.N = self.S // 2, self.R * self.I
        self.F = self.R // self.C
        self.NT = -(-self.N // LANES)
        self.G = max(1, LANES // self.JC)
        self.EXTRA = -(-(self.C - 1) * self.S * self.QL // LANES)
        self.carried = 0
        self.order = [*range(self.R // 2, self.R), *range(1, self.R // 2)]

    def fill(self, rows):
        if self.SQ == self.S:
            return rows
        return rows_of([rows, jnp.zeros((self.S - self.SQ, *rows.shape[1:]), rows.dtype)])

    def place(self, row, col):
        turn = lax.rem(row // self.F - col + self.C, self.C)
        return pl.multiple_of((turn * self.F + lax.rem(row, self.F)) * self.I, self.I)


def shift(array, axis, k):
    count = lax.axis_size(axis)
    return lax.ppermute(array, axis, [(i, (i + k) % count) for i in range(count)])


def swap(array, axis, x):
    return lax.ppermute(array, axis, [(i, i ^ x) for i in range(lax.axis_size(axis))])


def swapped(arrays, axis):
    return [swap(a, axis, k + 1) for k, a in reversed([*enumerate(arrays)])]


def shifted_all(array, axis):
    return [array] + [shift(array, axis, k) for k in range(1, lax.axis_size(axis))]


def per_device(
    homolog_ensemble,
    duplex_embedding,
    homolog_present_flags,
    resolved_position_flags,
    payload_weights,
    sigmoid_weights,
    averager_final_weights,
    first_operand_weights,
    second_operand_weights,
    duplex_logit_weights,
    tensor_product_weights,
    averager_upstream_adjoint,
    duplex_upstream_adjoint,
):
    g = Sizes(homolog_ensemble, duplex_embedding, duplex_logit_weights, first_operand_weights)
    shape = jax.ShapeDtypeStruct

    def call(kernel, name, args, outs, scratch=(), far=None, after=(), distant=False, us=1.0):
        size = sum(a.size * a.dtype.itemsize for a in args) + sum(
            math.prod(o.shape) * jnp.dtype(o.dtype).itemsize for o in outs
        )
        single = len(outs) == 1
        near = len(args) if far is None else far
        args = list(args[:near]) + [
            pltpu.with_memory_space_constraint(a, pltpu.HBM) for a in args[near:]
        ]

        if distant:
            after = [pltpu.with_memory_space_constraint(a, pltpu.HBM) for a in after]

        def body(*refs):
            kernel(g, *refs[: len(args)], *refs[len(args) + len(after) :])

        return pl.pallas_call(
            body,
            out_shape=outs[0] if single else tuple(outs),
            in_specs=[VMEM] * near + [FAR] * (len(args) - near) + [FAR if distant else VMEM] * len(after),
            out_specs=VMEM if single else (VMEM,) * len(outs),
            scratch_shapes=list(scratch),
            compiler_params=pltpu.CompilerParams(vmem_limit_bytes=40 * 1024 * 1024),
            cost_estimate=pl.CostEstimate(
                flops=int(us * 1.15e9), bytes_accessed=size, transcendentals=0
            ),
            name=name,
        )(*args, *after)

    heads = g.H * g.I
    rows = g.SP * g.I
    values = 2 * payload_weights.shape[1]
    pairs, tall = g.I * g.JC, heads // g.G
    xn, send, logits, near, x, e, wl, masks, w1, outer_weights, w2 = call(
        normalise_kernel,
        "normalise",
        (
            homolog_ensemble,
            duplex_embedding,
            duplex_upstream_adjoint.reshape(pairs, g.Z),
            resolved_position_flags.reshape(1, g.JC),
            duplex_logit_weights.T,
            homolog_present_flags,
            first_operand_weights.T,
            tensor_product_weights,
            second_operand_weights.T,
            homolog_present_flags.reshape(1, -1),
        ),
        [
            pltpu.VMEM((g.C, g.SP, g.I, 2 * g.M), BF16),
            pltpu.VMEM((rows + g.EXTRA * g.I, 2 * g.M), BF16),
            pltpu.VMEM((tall, g.G * g.JC), F32),
            pltpu.VMEM((pairs + 3 * tall, g.Z), BF16),
            pltpu.VMEM((g.SQ, g.I, g.M), BF16),
            pltpu.VMEM(duplex_embedding.shape, BF16),
            pltpu.VMEM((g.H, g.Z), BF16),
            pltpu.VMEM((g.C * g.SP + 8, 2 * g.M), F32),
            pltpu.VMEM((g.Q, g.M), BF16),
            pltpu.VMEM(tensor_product_weights.shape, BF16),
            pltpu.VMEM((g.Q, g.M), BF16),
        ],
        [
            pltpu.VMEM((1, g.JC), jnp.int32),
            pltpu.SMEM(homolog_present_flags.shape, jnp.int32),
            pltpu.VMEM((1, homolog_present_flags.shape[0]), jnp.int32),
            pltpu.VMEM(homolog_ensemble.shape, BF16),
            pltpu.VMEM(homolog_ensemble.shape, F32),
            pltpu.VMEM((g.I * g.H, LANES), F32),
            pltpu.SemaphoreType.DMA((10,)),
        ],
        far=0,
        us=2.0,
    )
    everyone = [send] + [swap(send, "row", k) for k in g.order]
    nears = shifted_all(near, "col")
    later = (
        sigmoid_weights,
        averager_final_weights.T,
        payload_weights,
    )
    g.carried = len(later)
    left, weights, left_weights, u, sg, wf, p = call(
        prepare_kernel,
        "prepare",
        (xn, w1, outer_weights, masks, averager_upstream_adjoint, *later),
        [
            pltpu.VMEM((g.C * g.I * g.S, g.Q), BF16),
            pltpu.VMEM((g.Q, g.Q, g.Z), BF16),
            pltpu.VMEM((g.I, g.Q * g.S, g.Z), BF16),
            pltpu.VMEM((g.SQ, g.I, g.M), BF16),
        ]
        + [pltpu.VMEM(a.shape, a.dtype) for a in later],
        [
            pltpu.VMEM(tensor_product_weights.shape, F32),
            pltpu.VMEM((2, rows, LANES), F32),
            pltpu.SemaphoreType.DMA,
            pltpu.SemaphoreType.DMA((len(later),)),
        ],
        far=4,
        us=0.01,
    )
    gate_weights, blended, gate_factor = call(
        gate_kernel,
        "gate",
        (xn, u, sg, wf),
        [
            pltpu.VMEM((2 * g.M, values), BF16),
            pltpu.VMEM((rows, values), BF16),
            pltpu.VMEM((rows, values), F32),
        ],
        after=nears[1:],
        us=0.01,
    )
    cotangents, second_term = call(
        right_kernel,
        "right",
        (*nears, left_weights, w2, masks),
        [pltpu.VMEM((g.I, g.N, g.Z), BF16), pltpu.VMEM((g.SP, g.N, 2 * g.M), F32)],
        [pltpu.VMEM((g.NT, g.Q * g.S, LANES), F32)],
        after=(gate_weights,),
        us=0.01,
    )
    share = g.Q * g.QL // g.D
    xall, *matrix_parts = call(
        outer_kernel,
        "outer",
        (*everyone, cotangents, left, w2, masks),
        [pltpu.VMEM((g.SP, g.N, 2 * g.M), BF16)] + [pltpu.VMEM((share, g.Z), F32)] * g.D,
        [
            pltpu.VMEM((g.N, max(1, g.EXTRA) * LANES), BF16),
            pltpu.VMEM((g.NT, g.C * g.SP * 2 * g.QL, LANES), F32),
            pltpu.VMEM((g.QL * g.C * g.S, g.N), BF16),
            pltpu.VMEM((g.QL, g.C, g.I, g.S, g.Z), BF16),
            pltpu.VMEM((g.Q * g.QL, g.Z), F32),
        ],
        after=(second_term,),
        us=0.05,
    )
    matrix_parts = [matrix_parts[0]] + [
        shift(a, "depth", k + 1) for k, a in enumerate(matrix_parts[1:])
    ]
    soft, grad_soft, own, gate_grads, *sums = call(
        attend_kernel,
        "attend",
        (xall, logits, *nears[1:], blended, gate_factor, p, second_term),
        [
            pltpu.VMEM((heads, g.N), F32),
            pltpu.VMEM((heads, g.N), F32),
            pltpu.VMEM((rows, 2 * g.M), F32),
            pltpu.VMEM((rows, values), BF16),
        ]
        + [pltpu.VMEM((rows, 2 * g.M), BF16)] * (g.R - 1),
        [pltpu.VMEM((g.SP, g.N, 2 * g.M), F32)],
        us=3.0,
    )
    *sums, piece = call(
        pack_kernel,
        "pack",
        (*sums, *matrix_parts),
        [pltpu.VMEM((rows + share, 2 * g.M), BF16)] * (g.R - 1) + [pltpu.VMEM((share, g.Z), BF16)],
        us=0.2,
    )
    sums = swapped(sums, "row")
    wide = -(-3 * (g.JC + 1) // LANES) * LANES
    scores, *sends = call(
        score_kernel,
        "score",
        (soft, *shifted_all(grad_soft, "depth")),
        [pltpu.VMEM((heads, g.JC + 1), F32)] + [pltpu.VMEM((heads, wide), BF16)] * (g.C - 1),
        [pltpu.VMEM((g.D, heads, g.N), F32)],
        after=(piece,),
        us=0.2,
    )
    arrived = [shift(a, "col", k + 1) for k, a in enumerate(sends)]
    own = call(
        own_kernel,
        "own",
        (xall, cotangents, weights, w1, w2, masks, own, gate_grads, gate_weights),
        [pltpu.VMEM((rows, 2 * g.M), F32)],
        [
            pltpu.VMEM((g.NT, g.SP * 2 * g.Q, LANES), F32),
            pltpu.VMEM((g.Q * g.S, g.N), BF16),
            pltpu.VMEM((g.Q, g.I, g.S, g.Z), BF16),
            pltpu.VMEM((g.I * g.S, 2 * g.M), F32),
        ],
        after=(scores,),
        us=0.01,
    )
    piece = call(
        piece_kernel,
        "piece",
        (piece, *sums),
        [pltpu.VMEM((share, g.Z), BF16)],
        [pltpu.VMEM((g.R, share, g.Z), BF16)],
        after=(own,),
        us=0.1,
    )
    pieces = shifted_all(piece, "col")
    part = call(
        reduce_kernel,
        "reduce",
        (x, own, *sums),
        [pltpu.VMEM((rows, 2 * g.M), BF16)],
        after=(piece,),
    )
    pairwise_gradient = call(
        pair_kernel,
        "pair",
        (e, wl, soft, scores, *arrived),
        [shape(duplex_embedding.shape, BF16)],
        after=(part,),
        us=0.01,
    )
    matrix = call(
        across_kernel,
        "across",
        pieces,
        [pltpu.VMEM((g.C, share, g.Z), BF16)],
        after=(pairwise_gradient,),
        distant=True,
        us=0.1,
    ).reshape(g.C, g.Q // g.D, g.QL, g.Z)
    ensemble_derivative = call(
        unpack_kernel,
        "unpack",
        shifted_all(part, "col"),
        [pltpu.VMEM(homolog_ensemble.shape, BF16)],
        after=(matrix,),
    )
    ensemble_derivative, outer_matrix_gradient = call(
        finish_kernel,
        "finish",
        (ensemble_derivative, *shifted_all(matrix, "depth")),
        [shape(homolog_ensemble.shape, BF16), shape((g.Q, g.Q, g.Z), F32)],
    )
    outer_matrix_gradient = outer_matrix_gradient.reshape(tensor_product_weights.shape)
    return (ensemble_derivative, pairwise_gradient, outer_matrix_gradient)


def solution(mesh):
    in_specs = (
        P(("parts", "depth"), "row", None),
        P(("parts", "row"), "col", None),
        P("parts"),
        P(("parts", "col")),
        P(),
        P(),
        P(),
        P(),
        P(),
        P(),
        P(),
        P(("parts", "depth"), "row", None),
        P(("parts", "row"), "col", None),
    )
    out_specs = (
        P(("parts", "depth"), "row", None),
        P(("parts", "row"), "col", None),
        P("parts", None),
    )
    return jax.shard_map(
        per_device, mesh=mesh, in_specs=in_specs, out_specs=out_specs, check_vma=False
    )
```

```python
import functools
import math

import jax
import jax.numpy as jnp
from jax import lax
from jax.experimental import pallas as pl
from jax.experimental.pallas import tpu as pltpu
from jax.sharding import PartitionSpec as P

EPS = 1e-05
PENALTY = 10000.0
F32 = jnp.float32
BF16 = jnp.bfloat16
LANES = 128
NN = (((1,), (0,)), ((), ()))
NT = (((1,), (1,)), ((), ()))
VMEM = pl.BlockSpec(memory_space=pltpu.VMEM)
FAR = pl.BlockSpec(memory_space=pl.ANY)


def mm(a, b, dims=NN):
    return lax.dot_general(a, b, dims, preferred_element_type=F32)


def split_high_low(value):
    high = value.astype(BF16)
    return high, (value - high.astype(F32)).astype(BF16)


def iota(shape, dim):
    return lax.broadcasted_iota(jnp.int32, shape, dim)


def lanes_of(pieces):
    return pieces[0] if len(pieces) == 1 else jnp.concatenate(pieces, axis=-1)


def rows_of(pieces):
    return pieces[0] if len(pieces) == 1 else jnp.concatenate(pieces, axis=0)


def standardize(values):
    centred = values - jnp.mean(values, -1, keepdims=True)
    inverse = lax.rsqrt(jnp.mean(centred * centred, -1, keepdims=True) + EPS)
    return centred * inverse, inverse


def standardize_backward(values, upstream):
    scaled, inverse = standardize(values)
    mean_grad = jnp.mean(upstream, -1, keepdims=True)
    mean_cross = jnp.mean(upstream * scaled, -1, keepdims=True)
    return (upstream - mean_grad - scaled * mean_cross) * inverse


def on_diagonal(block, width):
    rows, lanes = block.shape
    same = iota(block.shape, 0) // (rows // 2) == iota(block.shape, 1) // width
    return jnp.where(same, block, jnp.zeros_like(block))


def split_three(value):
    high = value.astype(BF16)
    rest = value - high.astype(F32)
    middle = rest.astype(BF16)
    return [high, middle, (rest - middle.astype(F32)).astype(BF16)]


def three_lanes(value):
    rows, width = value.shape
    fill = -(3 * width) % LANES
    return lanes_of(split_three(value) + [jnp.zeros((rows, fill), BF16)] * (fill > 0))


def join_three(parts, width):
    wide = parts.astype(F32)
    return (wide[:, :width] + wide[:, width : 2 * width]) + wide[:, 2 * width : 3 * width]


def twice(weights):
    zero = jnp.zeros_like(weights)
    return rows_of([lanes_of([weights, zero]), lanes_of([zero, weights])])


def column_weights(g, w2):
    rows = iota((2 * g.QL, g.Q), 0) % g.QL + lax.axis_index("col") * g.QL
    pick = (iota((2 * g.QL, g.Q), 1) == rows).astype(BF16)
    return on_diagonal(mm(pick, lanes_of([w2, w2])), g.M).astype(BF16)


def normalise_kernel(
    g, x_hbm, e_hbm, dd_hbm, flag_hbm, wl_hbm, live_hbm, w1_hbm, t_hbm, w2_hbm, every_hbm, *refs
):
    xn_ref, send_ref, logit_ref, near_ref, x_ref, e_ref, wl_ref, mask_ref, w1_ref, t_ref, w2_ref = refs[:11]
    flag_in, live_in, every_in, x_in, norm_ref, rows_ref, sem = refs[11:]
    col = lax.axis_index("col")
    pairs = g.I * g.JC
    copies = [
        pltpu.make_async_copy(a, b, sem.at[k])
        for k, (a, b) in enumerate(
            [
                (x_hbm, x_in),
                (e_hbm, e_ref),
                (wl_hbm, wl_ref),
                (flag_hbm, flag_in),
                (dd_hbm, near_ref.at[pl.ds(0, pairs)]),
                (live_hbm, live_in),
                (w1_hbm, w1_ref),
                (t_hbm, t_ref),
                (w2_hbm, w2_ref),
                (every_hbm, every_in),
            ]
        )
    ]
    for copy in copies:
        copy.start()
    for copy in (*copies[:4], copies[5], *copies[8:]):
        copy.wait()
    lane = iota((1, 2 * g.M), 1)
    groups = [lax.rem(col + m, g.C) for m in range(g.C)]
    for m, group in enumerate(groups):
        first = (lax.axis_index("depth") * g.C + group) * g.SQ
        for k in range(g.SP):
            if 2 * k + 1 < g.SQ:
                flags = jnp.where(lane < g.M, live_in[first + 2 * k], live_in[first + 2 * k + 1])
                flags = flags.astype(F32)
            else:
                flags = jnp.zeros((1, 2 * g.M), F32)
            mask_ref[m * g.SP + k : m * g.SP + k + 1, :] = flags
    count = jnp.sum(every_in[...].astype(F32), -1, keepdims=True)
    mask_ref[g.C * g.SP : g.C * g.SP + 1, :] = jnp.broadcast_to(1.0 / (0.001 + count), (1, 2 * g.M))
    norm_ref[...] = standardize(x_in[...].astype(F32))[0]
    x_ref[...] = x_in[pl.ds(col * g.SQ, g.SQ)]
    second = column_weights(g, w2_ref[...])
    rows, blocks = g.SP * g.I, []
    for m, group in enumerate(groups):
        normed = g.fill(norm_ref[pl.ds(group * g.SQ, g.SQ)]).reshape(g.SP, 2, g.I, g.M)
        packed = jnp.concatenate([normed[:, 0], normed[:, 1]], axis=-1).astype(BF16)
        xn_ref[m] = packed
        if m == 0:
            send_ref[:rows, :] = packed.reshape(rows, 2 * g.M)
        else:
            masks = [mask_ref[m * g.SP + k : m * g.SP + k + 1, :] for k in range(g.SP)]
            live = rows_of([(packed[k].astype(F32) * masks[k]).astype(BF16) for k in range(g.SP)])
            factors = mm(live, second, NT)
            blocks += [factors[k * g.I : (k + 1) * g.I] for k in range(g.SP)]
    if blocks:
        wide = lanes_of(blocks)
        fill = -wide.shape[1] % LANES
        if fill:
            wide = lanes_of([wide, jnp.zeros((g.I, fill), F32)])
        for k in range(g.EXTRA):
            block = wide[:, k * LANES : (k + 1) * LANES]
            send_ref[rows + k * g.I : rows + (k + 1) * g.I, :] = block.astype(BF16)
    pair = standardize(e_ref[...].astype(F32).reshape(pairs, g.Z))[0].astype(BF16)
    penalty = (flag_in[...].astype(F32) - 1.0) * PENALTY
    weights = wl_ref[...]
    for i in range(g.I):
        rows_ref[i * g.H : (i + 1) * g.H, : g.JC] = (
            mm(weights, pair[i * g.JC : (i + 1) * g.JC], NT) + penalty
        )
    logits = rows_of([rows_ref[pl.ds(h, g.I, stride=g.H), :][:, : g.JC] for h in range(g.H)])
    tall = g.H * g.I // g.G
    packed = lanes_of([logits[k * tall : (k + 1) * tall] for k in range(g.G)])
    logit_ref[...] = packed
    near_ref[pairs:, :] = rows_of(split_three(packed))
    for copy in (copies[4], *copies[6:8]):
        copy.wait()


def prepare_kernel(g, xn_ref, w1_ref, t_ref, mask_ref, u_hbm, *refs):
    refs = list(refs)
    count = g.carried
    sources, refs = refs[:count], refs[count:]
    left_ref, ts_ref, lt_ref, u_ref, refs = refs[0], refs[1], refs[2], refs[3], refs[4:]
    targets, (wide_ref, half_ref, first_sem, later_sem) = refs[:count], refs[count:]
    first = lax.axis_index("col") * g.SQ
    copies = [pltpu.make_async_copy(u_hbm.at[pl.ds(first, g.SQ)], u_ref, first_sem)]
    copies += [
        pltpu.make_async_copy(a, b, later_sem.at[k])
        for k, (a, b) in enumerate(zip(sources, targets, strict=True))
    ]
    for copy in copies:
        copy.start()
    w1 = rows_of([w1_ref[...], jnp.zeros((LANES - g.Q, g.M), BF16)])
    zero = jnp.zeros_like(w1)
    for m in range(g.C):
        masks = [mask_ref[m * g.SP + k : m * g.SP + k + 1, :] for k in range(g.SP)]
        live_xn = rows_of(
            [(xn_ref[m, k].astype(F32) * masks[k]).astype(BF16) for k in range(g.SP)]
        )
        half_ref[0] = mm(live_xn, lanes_of([w1, zero]), NT)
        half_ref[1] = mm(live_xn, lanes_of([zero, w1]), NT)
        for i in range(g.I):
            halves = [half_ref[half, pl.ds(i, g.SP, stride=g.I), :] for half in range(2)]
            first = (m * g.I + i) * g.S
            left_ref[first : first + g.S, :] = rows_of(halves)[:, : g.Q].astype(BF16)
    wide_ref[...] = t_ref[...].astype(F32)
    for q in range(g.Q):
        ts_ref[q] = wide_ref[pl.ds(q, g.Q, stride=g.Q), :].astype(BF16)
    left = left_ref[: g.I * g.S, :]
    for q in range(0, g.Q, 2):
        product = mm(left, lanes_of([ts_ref[q], ts_ref[q + 1]]))
        for k in range(2):
            block = product[:, k * g.Z : (k + 1) * g.Z].reshape(g.I, g.S, g.Z)
            lt_ref[:, (q + k) * g.S : (q + k + 1) * g.S, :] = block.astype(BF16)
    for copy in copies:
        copy.wait()


def gate_kernel(g, xn_ref, u_ref, sg_ref, wf_ref, gate_weight_ref, gm_ref, gate_ref):
    rows = g.SP * g.I
    xn = xn_ref[0]
    gate_weights = twice(sg_ref[...])
    gate_weight_ref[...] = gate_weights
    gates = jax.nn.sigmoid(mm(xn.reshape(rows, 2 * g.M), gate_weights))
    u = g.fill(u_ref[...]).reshape(g.SP, 2, g.I, g.M)
    packed_u = jnp.concatenate([u[:, 0], u[:, 1]], axis=-1).reshape(rows, 2 * g.M)
    gated = mm(packed_u, twice(wf_ref[...]))
    blended = gated * gates
    gm_ref[...] = blended.astype(BF16)
    gate_ref[...] = blended * (1.0 - gates)


def right_kernel(g, *refs):
    near_refs, (lt_ref, w2_ref, mask_ref, d_ref, go_ref, rg_ref) = refs[: g.C], refs[g.C :]
    for k in range(g.C):
        spot = (g.C - k) % g.C
        block = near_refs[k][: g.I * g.JC, :].reshape(g.I, g.JC, g.Z)
        d_ref[:, spot * g.JC : (spot + 1) * g.JC, :] = block
    masks = [mask_ref[k : k + 1, :] for k in range(g.SP)]
    scale = mask_ref[g.C * g.SP : g.C * g.SP + 1, :]
    right_grad = jnp.zeros((g.Q * g.S, g.N), F32)
    for i in range(0, g.I, 2):
        right_grad = right_grad + mm(
            lanes_of([lt_ref[i], lt_ref[i + 1]]), lanes_of([d_ref[i], d_ref[i + 1]]), NT
        )
    for t in range(g.NT):
        lanes = min(LANES, g.N - t * LANES)
        piece = right_grad[:, t * LANES : t * LANES + lanes]
        if lanes < LANES:
            piece = lanes_of([piece, jnp.zeros((g.Q * g.S, LANES - lanes), F32)])
        rg_ref[t] = piece
    deep = 2 * g.Q
    group = min(g.SP, LANES // deep)
    which = iota((group * deep, g.Q), 0)
    pick = (iota((group * deep, g.Q), 1) == which % deep // 2).astype(BF16)
    w2 = w2_ref[...]
    base = mm(pick, lanes_of([w2, w2]))
    which = iota(base.shape, 0)
    base = jnp.where(which % 2 == iota(base.shape, 1) // g.M, base, 0.0)
    weights = lanes_of([jnp.where(which // deep == k, base, 0.0) for k in range(group)]).astype(BF16)
    for k in range(0, g.SP, group):
        for t in range(g.NT):
            lanes = min(LANES, g.N - t * LANES)
            tall = rows_of(
                [rg_ref[t, pl.ds(k + m, deep, stride=g.SP), :] for m in range(group)]
            )
            tall = (tall * scale).T[:lanes]
            high, low = split_high_low(tall)
            part = mm(high, weights) + mm(low, weights)
            for m in range(group):
                go_ref[k + m, t * LANES : t * LANES + lanes, :] = (
                    part[:, m * 2 * g.M : (m + 1) * 2 * g.M] * masks[k + m]
                )


def outer_kernel(g, *refs):
    refs = list(refs)
    x_refs, refs = refs[: g.R], refs[g.R :]
    d_ref, left_ref, w2_ref, mask_ref, xall_ref, *refs = refs
    w_refs, (others_ref, spread_ref, rt_ref, ds_ref, all_ref) = refs[: g.D], refs[g.D :]
    row, col, depth = (lax.axis_index(a) for a in ("row", "col", "depth"))
    rows, deep = g.SP * g.I, 2 * g.QL
    for k, ref in zip((0, *g.order), x_refs, strict=True):
        place = g.place(jnp.bitwise_xor(row, k), col)
        xall_ref[:, pl.ds(place, g.I), :] = ref[:rows, :].reshape(g.SP, g.I, 2 * g.M)
        for m in range(g.EXTRA):
            block = ref[rows + m * g.I : rows + (m + 1) * g.I, :]
            others_ref[pl.ds(place, g.I), m * LANES : (m + 1) * LANES] = block
    second = column_weights(g, w2_ref[...])
    parts = [
        mm(second, (xall_ref[k].astype(F32) * mask_ref[k : k + 1, :]).astype(BF16), NT)
        for k in range(g.SP)
    ]
    if g.EXTRA:
        lanes = g.EXTRA * LANES
        eye = (iota((lanes, lanes), 0) == iota((lanes, lanes), 1)).astype(BF16)
        parts.append(mm(eye, others_ref[...], NT)[: (g.C - 1) * g.SP * deep])
    first = 0
    for part in parts:
        for t in range(g.NT):
            lanes = min(LANES, g.N - t * LANES)
            piece = part[:, t * LANES : t * LANES + lanes]
            spread_ref[t, first : first + part.shape[0], :lanes] = piece
        first += part.shape[0]
    for q in range(g.QL):
        for m in range(g.C):
            spot = (q * g.C + m) * g.S
            for t in range(g.NT):
                lanes = min(LANES, g.N - t * LANES)
                halves = [
                    spread_ref[t, pl.ds(m * g.SP * deep + half * g.QL + q, g.SP, stride=deep), :]
                    for half in range(2)
                ]
                rt_ref[spot : spot + g.S, t * LANES : t * LANES + lanes] = rows_of(halves)[
                    :, :lanes
                ].astype(BF16)
    rt = rt_ref[...]
    for i in range(0, g.I, 2):
        product = mm(rt, lanes_of([d_ref[i], d_ref[i + 1]]))
        for k in range(2):
            block = product[:, k * g.Z : (k + 1) * g.Z]
            ds_ref[:, :, i + k] = block.reshape(g.QL, g.C, g.S, g.Z).astype(BF16)
    eye = (iota((g.Q, g.Q), 0) == iota((g.Q, g.Q), 1)).astype(BF16)
    left_t = mm(eye, left_ref[...], NT).astype(BF16)
    scale = mask_ref[g.C * g.SP : g.C * g.SP + 1, :]
    entries = g.C * g.S * g.I
    for q in range(0, g.QL, 2):
        both = lanes_of([ds_ref[q].reshape(entries, g.Z), ds_ref[q + 1].reshape(entries, g.Z)])
        part = mm(left_t, both)
        all_ref[pl.ds(q, g.Q, stride=g.QL), :] = part[:, : g.Z] * scale
        all_ref[pl.ds(q + 1, g.Q, stride=g.QL), :] = part[:, g.Z :] * scale
    share = g.Q * g.QL // g.D
    for k in range(g.D):
        first = pl.multiple_of(lax.rem(depth + k, g.D) * share, share)
        w_refs[k][...] = all_ref[pl.ds(first, share), :]


def own_kernel(
    g, xall_ref, d_ref, ts_ref, w1_ref, w2_ref, mask_ref, part_ref, gg_ref, gate_weight_ref, own_ref,
    spread_ref, rt_ref, ds_ref, turn_ref,
):
    scale = mask_ref[g.C * g.SP : g.C * g.SP + 1, :]
    masks = [mask_ref[k : k + 1, :] for k in range(g.SP)]
    w2 = w2_ref[...]
    doubled = lanes_of([w2, w2])
    second = on_diagonal(rows_of([doubled, doubled]), g.M)
    for k in range(g.SP):
        live_x = (xall_ref[k].astype(F32) * masks[k]).astype(BF16)
        part = mm(second, live_x, NT)
        for t in range(g.NT):
            lanes = min(LANES, g.N - t * LANES)
            spread_ref[t, k * 2 * g.Q : (k + 1) * 2 * g.Q, :lanes] = part[
                :, t * LANES : t * LANES + lanes
            ]
    for q in range(g.Q):
        for t in range(g.NT):
            lanes = min(LANES, g.N - t * LANES)
            halves = [
                spread_ref[t, pl.ds(half * g.Q + q, g.SP, stride=2 * g.Q), :] for half in range(2)
            ]
            rt_ref[q * g.S : (q + 1) * g.S, t * LANES : t * LANES + lanes] = rows_of(halves)[
                :, :lanes
            ].astype(BF16)
    rt = rt_ref[...]
    for i in range(0, g.I, 2):
        product = mm(rt, lanes_of([d_ref[i], d_ref[i + 1]]))
        for k in range(2):
            block = product[:, k * g.Z : (k + 1) * g.Z]
            ds_ref[:, i + k] = block.reshape(g.Q, g.S, g.Z).astype(BF16)
    entries = g.S * g.I
    left_grad = jnp.zeros((entries, g.Q), F32)
    for q in range(0, g.Q, 2):
        both = lanes_of([ds_ref[q].reshape(entries, g.Z), ds_ref[q + 1].reshape(entries, g.Z)])
        left_grad = left_grad + mm(both, lanes_of([ts_ref[q], ts_ref[q + 1]]), NT)
    w1 = w1_ref[...]
    first_term = jnp.zeros((entries, 2 * g.M), F32)
    for piece in split_high_low(left_grad * scale[:, : g.Q]):
        first_term = first_term + mm(piece, lanes_of([w1, w1]))
    turn_ref[...] = first_term
    gate_term = mm(gg_ref[...], gate_weight_ref[...], NT)
    lane = iota((1, 2 * g.M), 1)
    for k in range(g.SP):
        rows = slice(k * g.I, (k + 1) * g.I)
        halves = [turn_ref[pl.ds(half * g.SP + k, g.I, stride=g.S), :] for half in range(2)]
        term = jnp.where(lane < g.M, halves[0], halves[1]) * mask_ref[k : k + 1, :]
        own_ref[rows, :] = part_ref[rows, :] + gate_term[rows] + term


def attend_kernel(g, *refs):
    refs = list(refs)
    xall_ref, refs = refs[0], refs[1:]
    logit_ref, near_refs, refs = refs[0], refs[1 : g.C], refs[g.C :]
    gm_ref, gate_ref, p_ref, go_ref, soft_ref, gs_ref, own_ref, gg_ref, *refs = refs
    send_refs, (total_ref,) = refs[: g.R - 1], refs[g.R - 1 :]
    row, col = lax.axis_index("row"), lax.axis_index("col")
    tall, blocks = logit_ref.shape[0], [logit_ref[...]]
    for k in range(1, g.C):
        parts = near_refs[g.C - k - 1][g.I * g.JC :, :].astype(F32)
        blocks.append((parts[:tall] + parts[tall : 2 * tall]) + parts[2 * tall :])
    logits = lanes_of(
        [rows_of([b[:, k * g.JC : (k + 1) * g.JC] for k in range(g.G)]) for b in blocks]
    )
    shifted = jnp.exp(logits - jnp.max(logits, -1, keepdims=True))
    soft = shifted / jnp.sum(shifted, -1, keepdims=True)
    soft_ref[...] = soft
    low = soft.astype(BF16)
    eye = (iota((g.N, g.N), 0) == iota((g.N, g.N), 1)).astype(BF16)
    low_t = mm(eye, low, NT).astype(BF16)
    value_weights = twice(p_ref[...])
    values = mm(xall_ref[...].reshape(g.SP * g.N, 2 * g.M), value_weights).astype(BF16)
    half = value_weights.shape[1] // 2
    width = half // g.H
    group = LANES // width
    count = g.H // group
    tall = group * g.I
    head = iota((1, 2 * LANES), 1) % LANES // width

    def lanes(array, k):
        return lanes_of([array[:, s * half + k * LANES : s * half + (k + 1) * LANES] for s in range(2)])

    group_weights = [lanes(value_weights, k) for k in range(count)]
    low_t = lanes_of([low_t, low_t])
    grad_soft = [jnp.zeros((tall, g.N), F32) for _ in range(count)]
    for k in range(g.SP):
        v = values[k * g.N : (k + 1) * g.N]
        rows = slice(k * g.I, (k + 1) * g.I)
        blended, factor = gm_ref[rows, :], gate_ref[rows, :]
        projected = []
        for m in range(count):
            vm = lanes(v, m)
            crossed = mm(low[m * tall : (m + 1) * tall], vm)
            mixed = crossed[: g.I]
            for h in range(1, group):
                mixed = jnp.where(head == h, crossed[h * g.I : (h + 1) * g.I], mixed)
            gate_grad = (lanes(factor, m) * mixed).astype(BF16)
            for s in range(2):
                first = s * half + m * LANES
                gg_ref[rows, first : first + LANES] = gate_grad[:, s * LANES : (s + 1) * LANES]
            bm = lanes(blended, m)
            by_head = rows_of([jnp.where(head == h, bm, jnp.zeros_like(bm)) for h in range(group)])
            grad_soft[m] = grad_soft[m] + mm(by_head, vm, NT)
            projected.append(mm(by_head, group_weights[m], NT))
        total_ref[k] = go_ref[k] + mm(low_t, rows_of([*split_high_low(rows_of(projected))]))
    gs_ref[...] = rows_of(grad_soft)
    own = total_ref[:, pl.ds(g.place(row, col), g.I), :]
    own_ref[...] = own.reshape(g.SP * g.I, 2 * g.M)
    for x in range(1, g.R):
        block = total_ref[:, pl.ds(g.place(jnp.bitwise_xor(row, x), col), g.I), :]
        send_refs[x - 1][...] = block.reshape(g.SP * g.I, 2 * g.M).astype(BF16)


def pack_kernel(g, *refs):
    refs = list(refs)
    sums, refs = refs[: g.R - 1], refs[g.R - 1 :]
    parts, refs = refs[: g.D], refs[g.D :]
    outs, own_ref = refs[: g.R - 1], refs[g.R - 1]
    total = parts[0][...]
    for ref in parts[1:]:
        total = total + ref[...]
    total, rows = total.astype(BF16), g.SP * g.I
    own_ref[...] = total
    for x in range(1, g.R):
        outs[x - 1][:rows, :] = sums[x - 1][...]
        outs[x - 1][rows:, :] = total


def piece_kernel(g, own_ref, *refs):
    out_ref, order_ref = refs[-2:]
    row, rows = lax.axis_index("row"), g.SP * g.I
    order_ref[row] = own_ref[...]
    for k in range(1, g.R):
        order_ref[jnp.bitwise_xor(row, g.R - k)] = refs[k - 1][rows:, :]
    total = order_ref[0].astype(F32)
    for r in range(1, g.R):
        total = total + order_ref[r].astype(F32)
    out_ref[...] = total.astype(BF16)


def score_kernel(g, soft_ref, *refs):
    parts, refs = refs[: g.D], refs[g.D :]
    own_ref, out_refs, order_ref = refs[0], refs[1 : g.C], refs[g.C]
    depth = lax.axis_index("depth")
    for k in range(g.D):
        order_ref[lax.rem(depth - k + g.D, g.D)] = parts[k][...]
    grad_soft = order_ref[0]
    for k in range(1, g.D):
        grad_soft = grad_soft + order_ref[k]
    inner = jnp.sum(soft_ref[...] * grad_soft, -1, keepdims=True)
    for k in range(g.C):
        block = lanes_of([grad_soft[:, k * g.JC : (k + 1) * g.JC], inner])
        if k == 0:
            own_ref[...] = block
        else:
            out_refs[k - 1][...] = three_lanes(block)


def pair_kernel(g, e_ref, wl_ref, soft_ref, own_ref, *refs):
    got, pair_ref = refs[: g.C - 1], refs[g.C - 1]
    heads = g.H * g.I
    total = own_ref[...]
    for ref in got:
        total = total + join_three(ref[...], g.JC + 1)
    grad = soft_ref[:, : g.JC] * (total[:, : g.JC] - total[:, g.JC :])
    if g.JC < LANES:
        grad = lanes_of([grad, jnp.zeros((heads, LANES - g.JC), F32)])
    high, low = split_high_low(grad.T[: g.JC])
    grads = lanes_of([high, low])
    pick = (iota((heads, g.H), 0) // g.I == iota((heads, g.H), 1)).astype(BF16)
    base = mm(pick, wl_ref[...]).astype(BF16)
    token = iota((heads, 1), 0) % g.I
    for i in range(0, g.I, 2):
        weights = lanes_of(
            [jnp.where(token == i + k, base, jnp.zeros_like(base)) for k in range(2)]
        )
        upstream = mm(grads, rows_of([weights, weights]))
        for k in range(2):
            pair_ref[i + k] = standardize_backward(
                e_ref[i + k].astype(F32), upstream[:, k * g.Z : (k + 1) * g.Z]
            ).astype(BF16)


def reduce_kernel(g, x_ref, own_ref, *refs):
    got, out_ref = refs[:-1], refs[-1]
    rows = g.SP * g.I
    total = own_ref[...]
    for ref in got:
        total = total + ref[:rows, :].astype(F32)
    total = total.reshape(g.SP, 1, g.I, 2 * g.M)
    upstream = jnp.concatenate([total[..., : g.M], total[..., g.M :]], axis=1)
    upstream = upstream.reshape(g.S, g.I, g.M)[: g.SQ]
    msa = g.fill(standardize_backward(x_ref[...].astype(F32), upstream))
    msa = msa.reshape(g.SP, 2, g.I, g.M)
    msa = jnp.concatenate([msa[:, 0], msa[:, 1]], axis=-1).astype(BF16)
    out_ref[...] = msa.reshape(rows, 2 * g.M)


def across_kernel(g, *refs):
    out_ref = refs[-1]
    col = lax.axis_index("col")
    for k, ref in enumerate(refs[:-1]):
        out_ref[lax.rem(col - k + g.C, g.C)] = ref[...]


def unpack_kernel(g, *refs):
    parts, msa_ref = refs[: g.C], refs[g.C]
    col = lax.axis_index("col")
    for k, ref in enumerate(parts):
        msa = ref[...].astype(F32).reshape(g.SP, 1, g.I, 2 * g.M)
        msa = jnp.concatenate([msa[..., : g.M], msa[..., g.M :]], axis=1)
        msa = msa.reshape(g.S, g.I, g.M)[: g.SQ].astype(BF16)
        msa_ref[pl.ds(lax.rem(col - k + g.C, g.C) * g.SQ, g.SQ)] = msa


def finish_kernel(g, msa_ref, *refs):
    parts, (out_ref, matrix_ref) = refs[: g.D], refs[g.D :]
    depth = lax.axis_index("depth")
    out_ref[...] = msa_ref[...]
    share = g.Q // g.D
    for k in range(g.D):
        first = lax.rem(depth - k + g.D, g.D) * share
        for c in range(g.C):
            block = parts[k][c].astype(F32)
            matrix_ref[pl.ds(first, share), c * g.QL : (c + 1) * g.QL, :] = block


class Sizes:
    def __init__(self, x, e, wl, w1):
        self.R, self.C, self.D = (lax.axis_size(a) for a in ("row", "col", "depth"))
        self.I, self.M = x.shape[1:]
        self.JC, self.Z = e.shape[1:]
        self.H, self.Q = wl.shape[1], w1.shape[1]
        self.QL = self.Q // self.C
        self.SQ = x.shape[0] // self.C
        self.S = -(-self.SQ // 16) * 16
        self.SP, self.N = self.S // 2, self.R * self.I
        self.F = self.R // self.C
        self.NT = -(-self.N // LANES)
        self.G = max(1, LANES // self.JC)
        self.EXTRA = -(-(self.C - 1) * self.S * self.QL // LANES)
        self.carried = 0
        self.order = [*range(self.R // 2, self.R), *range(1, self.R // 2)]

    def fill(self, rows):
        if self.SQ == self.S:
            return rows
        return rows_of([rows, jnp.zeros((self.S - self.SQ, *rows.shape[1:]), rows.dtype)])

    def place(self, row, col):
        turn = lax.rem(row // self.F - col + self.C, self.C)
        return pl.multiple_of((turn * self.F + lax.rem(row, self.F)) * self.I, self.I)


def shift(array, axis, k):
    count = lax.axis_size(axis)
    return lax.ppermute(array, axis, [(i, (i + k) % count) for i in range(count)])


def swap(array, axis, x):
    return lax.ppermute(array, axis, [(i, i ^ x) for i in range(lax.axis_size(axis))])


def swapped(arrays, axis):
    return [swap(a, axis, k + 1) for k, a in reversed([*enumerate(arrays)])]


def shifted_all(array, axis):
    return [array] + [shift(array, axis, k) for k in range(1, lax.axis_size(axis))]


def per_device(
    homolog_ensemble,
    duplex_embedding,
    homolog_present_flags,
    resolved_position_flags,
    payload_weights,
    sigmoid_weights,
    averager_final_weights,
    first_operand_weights,
    second_operand_weights,
    duplex_logit_weights,
    tensor_product_weights,
    averager_upstream_adjoint,
    duplex_upstream_adjoint,
):
    g = Sizes(homolog_ensemble, duplex_embedding, duplex_logit_weights, first_operand_weights)
    shape = jax.ShapeDtypeStruct

    def call(kernel, name, args, outs, scratch=(), far=None, after=(), distant=False, us=1.0):
        size = sum(a.size * a.dtype.itemsize for a in args) + sum(
            math.prod(o.shape) * jnp.dtype(o.dtype).itemsize for o in outs
        )
        single = len(outs) == 1
        near = len(args) if far is None else far
        args = list(args[:near]) + [
            pltpu.with_memory_space_constraint(a, pltpu.HBM) for a in args[near:]
        ]

        if distant:
            after = [pltpu.with_memory_space_constraint(a, pltpu.HBM) for a in after]

        def body(*refs):
            kernel(g, *refs[: len(args)], *refs[len(args) + len(after) :])

        return pl.pallas_call(
            body,
            out_shape=outs[0] if single else tuple(outs),
            in_specs=[VMEM] * near + [FAR] * (len(args) - near) + [FAR if distant else VMEM] * len(after),
            out_specs=VMEM if single else (VMEM,) * len(outs),
            scratch_shapes=list(scratch),
            compiler_params=pltpu.CompilerParams(vmem_limit_bytes=40 * 1024 * 1024),
            cost_estimate=pl.CostEstimate(
                flops=int(us * 1.15e9), bytes_accessed=size, transcendentals=0
            ),
            name=name,
        )(*args, *after)

    heads = g.H * g.I
    rows = g.SP * g.I
    values = 2 * payload_weights.shape[1]
    pairs, tall = g.I * g.JC, heads // g.G
    xn, send, logits, near, x, e, wl, masks, w1, outer_weights, w2 = call(
        normalise_kernel,
        "normalise",
        (
            homolog_ensemble,
            duplex_embedding,
            duplex_upstream_adjoint.reshape(pairs, g.Z),
            resolved_position_flags.reshape(1, g.JC),
            duplex_logit_weights.T,
            homolog_present_flags,
            first_operand_weights.T,
            tensor_product_weights,
            second_operand_weights.T,
            homolog_present_flags.reshape(1, -1),
        ),
        [
            pltpu.VMEM((g.C, g.SP, g.I, 2 * g.M), BF16),
            pltpu.VMEM((rows + g.EXTRA * g.I, 2 * g.M), BF16),
            pltpu.VMEM((tall, g.G * g.JC), F32),
            pltpu.VMEM((pairs + 3 * tall, g.Z), BF16),
            pltpu.VMEM((g.SQ, g.I, g.M), BF16),
            pltpu.VMEM(duplex_embedding.shape, BF16),
            pltpu.VMEM((g.H, g.Z), BF16),
            pltpu.VMEM((g.C * g.SP + 8, 2 * g.M), F32),
            pltpu.VMEM((g.Q, g.M), BF16),
            pltpu.VMEM(tensor_product_weights.shape, BF16),
            pltpu.VMEM((g.Q, g.M), BF16),
        ],
        [
            pltpu.VMEM((1, g.JC), jnp.int32),
            pltpu.SMEM(homolog_present_flags.shape, jnp.int32),
            pltpu.VMEM((1, homolog_present_flags.shape[0]), jnp.int32),
            pltpu.VMEM(homolog_ensemble.shape, BF16),
            pltpu.VMEM(homolog_ensemble.shape, F32),
            pltpu.VMEM((g.I * g.H, LANES), F32),
            pltpu.SemaphoreType.DMA((10,)),
        ],
        far=0,
        us=2.0,
    )
    everyone = [send] + [swap(send, "row", k) for k in g.order]
    nears = shifted_all(near, "col")
    later = (
        sigmoid_weights,
        averager_final_weights.T,
        payload_weights,
    )
    g.carried = len(later)
    left, weights, left_weights, u, sg, wf, p = call(
        prepare_kernel,
        "prepare",
        (xn, w1, outer_weights, masks, averager_upstream_adjoint, *later),
        [
            pltpu.VMEM((g.C * g.I * g.S, g.Q), BF16),
            pltpu.VMEM((g.Q, g.Q, g.Z), BF16),
            pltpu.VMEM((g.I, g.Q * g.S, g.Z), BF16),
            pltpu.VMEM((g.SQ, g.I, g.M), BF16),
        ]
        + [pltpu.VMEM(a.shape, a.dtype) for a in later],
        [
            pltpu.VMEM(tensor_product_weights.shape, F32),
            pltpu.VMEM((2, rows, LANES), F32),
            pltpu.SemaphoreType.DMA,
            pltpu.SemaphoreType.DMA((len(later),)),
        ],
        far=4,
        us=0.01,
    )
    gate_weights, blended, gate_factor = call(
        gate_kernel,
        "gate",
        (xn, u, sg, wf),
        [
            pltpu.VMEM((2 * g.M, values), BF16),
            pltpu.VMEM((rows, values), BF16),
            pltpu.VMEM((rows, values), F32),
        ],
        after=nears[1:],
        us=0.01,
    )
    cotangents, second_term = call(
        right_kernel,
        "right",
        (*nears, left_weights, w2, masks),
        [pltpu.VMEM((g.I, g.N, g.Z), BF16), pltpu.VMEM((g.SP, g.N, 2 * g.M), F32)],
        [pltpu.VMEM((g.NT, g.Q * g.S, LANES), F32)],
        after=(gate_weights,),
        us=0.01,
    )
    share = g.Q * g.QL // g.D
    xall, *matrix_parts = call(
        outer_kernel,
        "outer",
        (*everyone, cotangents, left, w2, masks),
        [pltpu.VMEM((g.SP, g.N, 2 * g.M), BF16)] + [pltpu.VMEM((share, g.Z), F32)] * g.D,
        [
            pltpu.VMEM((g.N, max(1, g.EXTRA) * LANES), BF16),
            pltpu.VMEM((g.NT, g.C * g.SP * 2 * g.QL, LANES), F32),
            pltpu.VMEM((g.QL * g.C * g.S, g.N), BF16),
            pltpu.VMEM((g.QL, g.C, g.I, g.S, g.Z), BF16),
            pltpu.VMEM((g.Q * g.QL, g.Z), F32),
        ],
        after=(second_term,),
        us=0.05,
    )
    matrix_parts = [matrix_parts[0]] + [
        shift(a, "depth", k + 1) for k, a in enumerate(matrix_parts[1:])
    ]
    soft, grad_soft, own, gate_grads, *sums = call(
        attend_kernel,
        "attend",
        (xall, logits, *nears[1:], blended, gate_factor, p, second_term),
        [
            pltpu.VMEM((heads, g.N), F32),
            pltpu.VMEM((heads, g.N), F32),
            pltpu.VMEM((rows, 2 * g.M), F32),
            pltpu.VMEM((rows, values), BF16),
        ]
        + [pltpu.VMEM((rows, 2 * g.M), BF16)] * (g.R - 1),
        [pltpu.VMEM((g.SP, g.N, 2 * g.M), F32)],
        us=3.0,
    )
    *sums, piece = call(
        pack_kernel,
        "pack",
        (*sums, *matrix_parts),
        [pltpu.VMEM((rows + share, 2 * g.M), BF16)] * (g.R - 1) + [pltpu.VMEM((share, g.Z), BF16)],
        us=0.2,
    )
    sums = swapped(sums, "row")
    wide = -(-3 * (g.JC + 1) // LANES) * LANES
    scores, *sends = call(
        score_kernel,
        "score",
        (soft, *shifted_all(grad_soft, "depth")),
        [pltpu.VMEM((heads, g.JC + 1), F32)] + [pltpu.VMEM((heads, wide), BF16)] * (g.C - 1),
        [pltpu.VMEM((g.D, heads, g.N), F32)],
        after=(piece,),
        us=0.2,
    )
    arrived = [shift(a, "col", k + 1) for k, a in enumerate(sends)]
    own = call(
        own_kernel,
        "own",
        (xall, cotangents, weights, w1, w2, masks, own, gate_grads, gate_weights),
        [pltpu.VMEM((rows, 2 * g.M), F32)],
        [
            pltpu.VMEM((g.NT, g.SP * 2 * g.Q, LANES), F32),
            pltpu.VMEM((g.Q * g.S, g.N), BF16),
            pltpu.VMEM((g.Q, g.I, g.S, g.Z), BF16),
            pltpu.VMEM((g.I * g.S, 2 * g.M), F32),
        ],
        after=(scores,),
        us=0.01,
    )
    piece = call(
        piece_kernel,
        "piece",
        (piece, *sums),
        [pltpu.VMEM((share, g.Z), BF16)],
        [pltpu.VMEM((g.R, share, g.Z), BF16)],
        after=(own,),
        us=0.1,
    )
    pieces = shifted_all(piece, "col")
    part = call(
        reduce_kernel,
        "reduce",
        (x, own, *sums),
        [pltpu.VMEM((rows, 2 * g.M), BF16)],
        after=(piece,),
    )
    pairwise_gradient = call(
        pair_kernel,
        "pair",
        (e, wl, soft, scores, *arrived),
        [shape(duplex_embedding.shape, BF16)],
        after=(part,),
        us=0.01,
    )
    matrix = call(
        across_kernel,
        "across",
        pieces,
        [pltpu.VMEM((g.C, share, g.Z), BF16)],
        after=(pairwise_gradient,),
        distant=True,
        us=0.1,
    ).reshape(g.C, g.Q // g.D, g.QL, g.Z)
    ensemble_derivative = call(
        unpack_kernel,
        "unpack",
        shifted_all(part, "col"),
        [pltpu.VMEM(homolog_ensemble.shape, BF16)],
        after=(matrix,),
    )
    ensemble_derivative, outer_matrix_gradient = call(
        finish_kernel,
        "finish",
        (ensemble_derivative, *shifted_all(matrix, "depth")),
        [shape(homolog_ensemble.shape, BF16), shape((g.Q, g.Q, g.Z), F32)],
    )
    outer_matrix_gradient = outer_matrix_gradient.reshape(tensor_product_weights.shape)
    return (ensemble_derivative, pairwise_gradient, outer_matrix_gradient)


def solution(mesh):
    in_specs = (
        P(("parts", "depth"), "row", None),
        P(("parts", "row"), "col", None),
        P("parts"),
        P(("parts", "col")),
        P(),
        P(),
        P(),
        P(),
        P(),
        P(),
        P(),
        P(("parts", "depth"), "row", None),
        P(("parts", "row"), "col", None),
    )
    out_specs = (
        P(("parts", "depth"), "row", None),
        P(("parts", "row"), "col", None),
        P("parts", None),
    )
    return jax.shard_map(
        per_device, mesh=mesh, in_specs=in_specs, out_specs=out_specs, check_vma=False
    )
```

```python
import functools
import math

import jax
import jax.numpy as jnp
from jax import lax
from jax.experimental import pallas as pl
from jax.experimental.pallas import tpu as pltpu
from jax.sharding import PartitionSpec as P

EPS = 1e-05
PENALTY = 10000.0
F32 = jnp.float32
BF16 = jnp.bfloat16
LANES = 128
NN = (((1,), (0,)), ((), ()))
NT = (((1,), (1,)), ((), ()))
VMEM = pl.BlockSpec(memory_space=pltpu.VMEM)
FAR = pl.BlockSpec(memory_space=pl.ANY)


def mm(a, b, dims=NN):
    return lax.dot_general(a, b, dims, preferred_element_type=F32)


def split_high_low(value):
    high = value.astype(BF16)
    return high, (value - high.astype(F32)).astype(BF16)


def iota(shape, dim):
    return lax.broadcasted_iota(jnp.int32, shape, dim)


def lanes_of(pieces):
    return pieces[0] if len(pieces) == 1 else jnp.concatenate(pieces, axis=-1)


def rows_of(pieces):
    return pieces[0] if len(pieces) == 1 else jnp.concatenate(pieces, axis=0)


def standardize(values):
    centred = values - jnp.mean(values, -1, keepdims=True)
    inverse = lax.rsqrt(jnp.mean(centred * centred, -1, keepdims=True) + EPS)
    return centred * inverse, inverse


def standardize_backward(values, upstream):
    scaled, inverse = standardize(values)
    mean_grad = jnp.mean(upstream, -1, keepdims=True)
    mean_cross = jnp.mean(upstream * scaled, -1, keepdims=True)
    return (upstream - mean_grad - scaled * mean_cross) * inverse


def on_diagonal(block, width):
    rows, lanes = block.shape
    same = iota(block.shape, 0) // (rows // 2) == iota(block.shape, 1) // width
    return jnp.where(same, block, jnp.zeros_like(block))


def split_three(value):
    high = value.astype(BF16)
    rest = value - high.astype(F32)
    middle = rest.astype(BF16)
    return [high, middle, (rest - middle.astype(F32)).astype(BF16)]


def three_lanes(value):
    rows, width = value.shape
    fill = -(3 * width) % LANES
    return lanes_of(split_three(value) + [jnp.zeros((rows, fill), BF16)] * (fill > 0))


def join_three(parts, width):
    wide = parts.astype(F32)
    return (wide[:, :width] + wide[:, width : 2 * width]) + wide[:, 2 * width : 3 * width]


def twice(weights):
    zero = jnp.zeros_like(weights)
    return rows_of([lanes_of([weights, zero]), lanes_of([zero, weights])])


def column_weights(g, w2):
    rows = iota((2 * g.QL, g.Q), 0) % g.QL + lax.axis_index("col") * g.QL
    pick = (iota((2 * g.QL, g.Q), 1) == rows).astype(BF16)
    return on_diagonal(mm(pick, lanes_of([w2, w2])), g.M).astype(BF16)


def normalise_kernel(
    g, x_hbm, e_hbm, dd_hbm, flag_hbm, wl_hbm, live_hbm, w1_hbm, t_hbm, w2_hbm, every_hbm, *refs
):
    xn_ref, send_ref, logit_ref, near_ref, x_ref, e_ref, wl_ref, mask_ref, w1_ref, t_ref, w2_ref = refs[:11]
    flag_in, live_in, every_in, x_in, norm_ref, rows_ref, sem = refs[11:]
    col = lax.axis_index("col")
    pairs = g.I * g.JC
    copies = [
        pltpu.make_async_copy(a, b, sem.at[k])
        for k, (a, b) in enumerate(
            [
                (x_hbm, x_in),
                (e_hbm, e_ref),
                (wl_hbm, wl_ref),
                (flag_hbm, flag_in),
                (dd_hbm, near_ref.at[pl.ds(0, pairs)]),
                (live_hbm, live_in),
                (w1_hbm, w1_ref),
                (t_hbm, t_ref),
                (w2_hbm, w2_ref),
                (every_hbm, every_in),
            ]
        )
    ]
    for copy in copies:
        copy.start()
    for copy in (*copies[:4], copies[5], *copies[8:]):
        copy.wait()
    lane = iota((1, 2 * g.M), 1)
    groups = [lax.rem(col + m, g.C) for m in range(g.C)]
    for m, group in enumerate(groups):
        first = (lax.axis_index("depth") * g.C + group) * g.SQ
        for k in range(g.SP):
            if 2 * k + 1 < g.SQ:
                flags = jnp.where(lane < g.M, live_in[first + 2 * k], live_in[first + 2 * k + 1])
                flags = flags.astype(F32)
            else:
                flags = jnp.zeros((1, 2 * g.M), F32)
            mask_ref[m * g.SP + k : m * g.SP + k + 1, :] = flags
    count = jnp.sum(every_in[...].astype(F32), -1, keepdims=True)
    mask_ref[g.C * g.SP : g.C * g.SP + 1, :] = jnp.broadcast_to(1.0 / (0.001 + count), (1, 2 * g.M))
    norm_ref[...] = standardize(x_in[...].astype(F32))[0]
    x_ref[...] = x_in[pl.ds(col * g.SQ, g.SQ)]
    second = column_weights(g, w2_ref[...])
    rows, blocks = g.SP * g.I, []
    for m, group in enumerate(groups):
        normed = g.fill(norm_ref[pl.ds(group * g.SQ, g.SQ)]).reshape(g.SP, 2, g.I, g.M)
        packed = jnp.concatenate([normed[:, 0], normed[:, 1]], axis=-1).astype(BF16)
        xn_ref[m] = packed
        if m == 0:
            send_ref[:rows, :] = packed.reshape(rows, 2 * g.M)
        else:
            masks = [mask_ref[m * g.SP + k : m * g.SP + k + 1, :] for k in range(g.SP)]
            live = rows_of([(packed[k].astype(F32) * masks[k]).astype(BF16) for k in range(g.SP)])
            factors = mm(live, second, NT)
            blocks += [factors[k * g.I : (k + 1) * g.I] for k in range(g.SP)]
    if blocks:
        wide = lanes_of(blocks)
        fill = -wide.shape[1] % LANES
        if fill:
            wide = lanes_of([wide, jnp.zeros((g.I, fill), F32)])
        for k in range(g.EXTRA):
            block = wide[:, k * LANES : (k + 1) * LANES]
            send_ref[rows + k * g.I : rows + (k + 1) * g.I, :] = block.astype(BF16)
    pair = standardize(e_ref[...].astype(F32).reshape(pairs, g.Z))[0].astype(BF16)
    penalty = (flag_in[...].astype(F32) - 1.0) * PENALTY
    weights = wl_ref[...]
    for i in range(g.I):
        rows_ref[i * g.H : (i + 1) * g.H, : g.JC] = (
            mm(weights, pair[i * g.JC : (i + 1) * g.JC], NT) + penalty
        )
    logits = rows_of([rows_ref[pl.ds(h, g.I, stride=g.H), :][:, : g.JC] for h in range(g.H)])
    tall = g.H * g.I // g.G
    packed = lanes_of([logits[k * tall : (k + 1) * tall] for k in range(g.G)])
    logit_ref[...] = packed
    near_ref[pairs:, :] = rows_of(split_three(packed))
    for copy in (copies[4], *copies[6:8]):
        copy.wait()


def prepare_kernel(g, xn_ref, w1_ref, t_ref, mask_ref, u_hbm, *refs):
    refs = list(refs)
    count = g.carried
    sources, refs = refs[:count], refs[count:]
    left_ref, ts_ref, lt_ref, u_ref, refs = refs[0], refs[1], refs[2], refs[3], refs[4:]
    targets, (wide_ref, half_ref, first_sem, later_sem) = refs[:count], refs[count:]
    first = lax.axis_index("col") * g.SQ
    copies = [pltpu.make_async_copy(u_hbm.at[pl.ds(first, g.SQ)], u_ref, first_sem)]
    copies += [
        pltpu.make_async_copy(a, b, later_sem.at[k])
        for k, (a, b) in enumerate(zip(sources, targets, strict=True))
    ]
    for copy in copies:
        copy.start()
    w1 = rows_of([w1_ref[...], jnp.zeros((LANES - g.Q, g.M), BF16)])
    zero = jnp.zeros_like(w1)
    for m in range(g.C):
        masks = [mask_ref[m * g.SP + k : m * g.SP + k + 1, :] for k in range(g.SP)]
        live_xn = rows_of(
            [(xn_ref[m, k].astype(F32) * masks[k]).astype(BF16) for k in range(g.SP)]
        )
        half_ref[0] = mm(live_xn, lanes_of([w1, zero]), NT)
        half_ref[1] = mm(live_xn, lanes_of([zero, w1]), NT)
        for i in range(g.I):
            halves = [half_ref[half, pl.ds(i, g.SP, stride=g.I), :] for half in range(2)]
            first = (m * g.I + i) * g.S
            left_ref[first : first + g.S, :] = rows_of(halves)[:, : g.Q].astype(BF16)
    wide_ref[...] = t_ref[...].astype(F32)
    for q in range(g.Q):
        ts_ref[q] = wide_ref[pl.ds(q, g.Q, stride=g.Q), :].astype(BF16)
    left = left_ref[: g.I * g.S, :]
    for q in range(0, g.Q, 2):
        product = mm(left, lanes_of([ts_ref[q], ts_ref[q + 1]]))
        for k in range(2):
            block = product[:, k * g.Z : (k + 1) * g.Z].reshape(g.I, g.S, g.Z)
            lt_ref[:, (q + k) * g.S : (q + k + 1) * g.S, :] = block.astype(BF16)
    for copy in copies:
        copy.wait()


def gate_kernel(g, xn_ref, u_ref, sg_ref, wf_ref, gate_weight_ref, gm_ref, gate_ref):
    rows = g.SP * g.I
    xn = xn_ref[0]
    gate_weights = twice(sg_ref[...])
    gate_weight_ref[...] = gate_weights
    gates = jax.nn.sigmoid(mm(xn.reshape(rows, 2 * g.M), gate_weights))
    u = g.fill(u_ref[...]).reshape(g.SP, 2, g.I, g.M)
    packed_u = jnp.concatenate([u[:, 0], u[:, 1]], axis=-1).reshape(rows, 2 * g.M)
    gated = mm(packed_u, twice(wf_ref[...]))
    blended = gated * gates
    gm_ref[...] = blended.astype(BF16)
    gate_ref[...] = blended * (1.0 - gates)


def right_kernel(g, *refs):
    near_refs, (lt_ref, w2_ref, mask_ref, d_ref, go_ref, rg_ref) = refs[: g.C], refs[g.C :]
    for k in range(g.C):
        spot = (g.C - k) % g.C
        block = near_refs[k][: g.I * g.JC, :].reshape(g.I, g.JC, g.Z)
        d_ref[:, spot * g.JC : (spot + 1) * g.JC, :] = block
    masks = [mask_ref[k : k + 1, :] for k in range(g.SP)]
    scale = mask_ref[g.C * g.SP : g.C * g.SP + 1, :]
    right_grad = jnp.zeros((g.Q * g.S, g.N), F32)
    for i in range(0, g.I, 2):
        right_grad = right_grad + mm(
            lanes_of([lt_ref[i], lt_ref[i + 1]]), lanes_of([d_ref[i], d_ref[i + 1]]), NT
        )
    for t in range(g.NT):
        lanes = min(LANES, g.N - t * LANES)
        piece = right_grad[:, t * LANES : t * LANES + lanes]
        if lanes < LANES:
            piece = lanes_of([piece, jnp.zeros((g.Q * g.S, LANES - lanes), F32)])
        rg_ref[t] = piece
    deep = 2 * g.Q
    group = min(g.SP, LANES // deep)
    which = iota((group * deep, g.Q), 0)
    pick = (iota((group * deep, g.Q), 1) == which % deep // 2).astype(BF16)
    w2 = w2_ref[...]
    base = mm(pick, lanes_of([w2, w2]))
    which = iota(base.shape, 0)
    base = jnp.where(which % 2 == iota(base.shape, 1) // g.M, base, 0.0)
    weights = lanes_of([jnp.where(which // deep == k, base, 0.0) for k in range(group)]).astype(BF16)
    for k in range(0, g.SP, group):
        for t in range(g.NT):
            lanes = min(LANES, g.N - t * LANES)
            tall = rows_of(
                [rg_ref[t, pl.ds(k + m, deep, stride=g.SP), :] for m in range(group)]
            )
            tall = (tall * scale).T[:lanes]
            high, low = split_high_low(tall)
            part = mm(high, weights) + mm(low, weights)
            for m in range(group):
                go_ref[k + m, t * LANES : t * LANES + lanes, :] = (
                    part[:, m * 2 * g.M : (m + 1) * 2 * g.M] * masks[k + m]
                )


def outer_kernel(g, *refs):
    refs = list(refs)
    x_refs, refs = refs[: g.R], refs[g.R :]
    d_ref, left_ref, w2_ref, mask_ref, xall_ref, ds_ref, *refs = refs
    w_refs, (others_ref, spread_ref, rt_ref, all_ref) = refs[: g.D], refs[g.D :]
    row, col, depth = (lax.axis_index(a) for a in ("row", "col", "depth"))
    rows, deep = g.SP * g.I, 2 * g.QL
    for k, ref in zip((0, *g.order), x_refs, strict=True):
        place = g.place(jnp.bitwise_xor(row, k), col)
        xall_ref[:, pl.ds(place, g.I), :] = ref[:rows, :].reshape(g.SP, g.I, 2 * g.M)
        for m in range(g.EXTRA):
            block = ref[rows + m * g.I : rows + (m + 1) * g.I, :]
            others_ref[pl.ds(place, g.I), m * LANES : (m + 1) * LANES] = block
    second = column_weights(g, w2_ref[...])
    parts = [
        mm(second, (xall_ref[k].astype(F32) * mask_ref[k : k + 1, :]).astype(BF16), NT)
        for k in range(g.SP)
    ]
    if g.EXTRA:
        lanes = g.EXTRA * LANES
        eye = (iota((lanes, lanes), 0) == iota((lanes, lanes), 1)).astype(BF16)
        parts.append(mm(eye, others_ref[...], NT)[: (g.C - 1) * g.SP * deep])
    first = 0
    for part in parts:
        for t in range(g.NT):
            lanes = min(LANES, g.N - t * LANES)
            piece = part[:, t * LANES : t * LANES + lanes]
            spread_ref[t, first : first + part.shape[0], :lanes] = piece
        first += part.shape[0]
    for q in range(g.QL):
        for m in range(g.C):
            spot = (q * g.C + m) * g.S
            for t in range(g.NT):
                lanes = min(LANES, g.N - t * LANES)
                halves = [
                    spread_ref[t, pl.ds(m * g.SP * deep + half * g.QL + q, g.SP, stride=deep), :]
                    for half in range(2)
                ]
                rt_ref[spot : spot + g.S, t * LANES : t * LANES + lanes] = rows_of(halves)[
                    :, :lanes
                ].astype(BF16)
    rt = rt_ref[...]
    for i in range(0, g.I, 2):
        product = mm(rt, lanes_of([d_ref[i], d_ref[i + 1]]))
        for k in range(2):
            block = product[:, k * g.Z : (k + 1) * g.Z]
            ds_ref[:, :, i + k] = block.reshape(g.QL, g.C, g.S, g.Z).astype(BF16)
    eye = (iota((g.Q, g.Q), 0) == iota((g.Q, g.Q), 1)).astype(BF16)
    left_t = mm(eye, left_ref[...], NT).astype(BF16)
    scale = mask_ref[g.C * g.SP : g.C * g.SP + 1, :]
    entries = g.C * g.S * g.I
    for q in range(0, g.QL, 2):
        both = lanes_of([ds_ref[q].reshape(entries, g.Z), ds_ref[q + 1].reshape(entries, g.Z)])
        part = mm(left_t, both)
        all_ref[pl.ds(q, g.Q, stride=g.QL), :] = part[:, : g.Z] * scale
        all_ref[pl.ds(q + 1, g.Q, stride=g.QL), :] = part[:, g.Z :] * scale
    share = g.Q * g.QL // g.D
    for k in range(g.D):
        first = pl.multiple_of(lax.rem(depth + k, g.D) * share, share)
        w_refs[k][...] = all_ref[pl.ds(first, share), :]


def own_kernel(
    g, xall_ref, near_ref, d_ref, ts_ref, w1_ref, w2_ref, mask_ref, part_ref, gg_ref, gate_weight_ref, own_ref,
    spread_ref, rt_ref, ds_ref, turn_ref,
):
    scale = mask_ref[g.C * g.SP : g.C * g.SP + 1, :]
    masks = [mask_ref[k : k + 1, :] for k in range(g.SP)]
    w2 = w2_ref[...]
    doubled = lanes_of([w2, w2])
    second = on_diagonal(rows_of([doubled, doubled]), g.M)
    for k in range(g.SP):
        live_x = (xall_ref[k].astype(F32) * masks[k]).astype(BF16)
        part = mm(second, live_x, NT)
        for t in range(g.NT):
            lanes = min(LANES, g.N - t * LANES)
            spread_ref[t, k * 2 * g.Q : (k + 1) * 2 * g.Q, :lanes] = part[
                :, t * LANES : t * LANES + lanes
            ]
    for q in range(g.Q):
        for t in range(g.NT):
            lanes = min(LANES, g.N - t * LANES)
            halves = [
                spread_ref[t, pl.ds(half * g.Q + q, g.SP, stride=2 * g.Q), :] for half in range(2)
            ]
            rt_ref[q * g.S : (q + 1) * g.S, t * LANES : t * LANES + lanes] = rows_of(halves)[
                :, :lanes
            ].astype(BF16)
    col = lax.axis_index("col")
    entries = g.S * g.I
    left_grad = jnp.zeros((entries, g.Q), F32)
    for m in range(g.C):
        first = lax.rem(col + m, g.C) * g.QL
        if m > 0:
            rt = rt_ref[pl.ds(pl.multiple_of(first * g.S, g.QL * g.S), g.QL * g.S), :]
            for i in range(0, g.I, 2):
                product = mm(rt, lanes_of([d_ref[i], d_ref[i + 1]]))
                for k in range(2):
                    block = product[:, k * g.Z : (k + 1) * g.Z]
                    ds_ref[m - 1, :, i + k] = block.reshape(g.QL, g.S, g.Z).astype(BF16)
        for q in range(0, g.QL, 2):
            pair = [near_ref[q + k, 0] if m == 0 else ds_ref[m - 1, q + k] for k in range(2)]
            both = lanes_of([part.reshape(entries, g.Z) for part in pair])
            left_grad = left_grad + mm(both, lanes_of([ts_ref[first + q], ts_ref[first + q + 1]]), NT)
    w1 = w1_ref[...]
    first_term = jnp.zeros((entries, 2 * g.M), F32)
    for piece in split_high_low(left_grad * scale[:, : g.Q]):
        first_term = first_term + mm(piece, lanes_of([w1, w1]))
    turn_ref[...] = first_term
    gate_term = mm(gg_ref[...], gate_weight_ref[...], NT)
    lane = iota((1, 2 * g.M), 1)
    for k in range(g.SP):
        rows = slice(k * g.I, (k + 1) * g.I)
        halves = [turn_ref[pl.ds(half * g.SP + k, g.I, stride=g.S), :] for half in range(2)]
        term = jnp.where(lane < g.M, halves[0], halves[1]) * mask_ref[k : k + 1, :]
        own_ref[rows, :] = part_ref[rows, :] + gate_term[rows] + term


def attend_kernel(g, *refs):
    refs = list(refs)
    xall_ref, refs = refs[0], refs[1:]
    logit_ref, near_refs, refs = refs[0], refs[1 : g.C], refs[g.C :]
    gm_ref, gate_ref, p_ref, go_ref, soft_ref, gs_ref, own_ref, gg_ref, *refs = refs
    send_refs, (total_ref,) = refs[: g.R - 1], refs[g.R - 1 :]
    row, col = lax.axis_index("row"), lax.axis_index("col")
    tall, blocks = logit_ref.shape[0], [logit_ref[...]]
    for k in range(1, g.C):
        parts = near_refs[g.C - k - 1][g.I * g.JC :, :].astype(F32)
        blocks.append((parts[:tall] + parts[tall : 2 * tall]) + parts[2 * tall :])
    logits = lanes_of(
        [rows_of([b[:, k * g.JC : (k + 1) * g.JC] for k in range(g.G)]) for b in blocks]
    )
    shifted = jnp.exp(logits - jnp.max(logits, -1, keepdims=True))
    soft = shifted / jnp.sum(shifted, -1, keepdims=True)
    soft_ref[...] = soft
    low = soft.astype(BF16)
    eye = (iota((g.N, g.N), 0) == iota((g.N, g.N), 1)).astype(BF16)
    low_t = mm(eye, low, NT).astype(BF16)
    value_weights = twice(p_ref[...])
    values = mm(xall_ref[...].reshape(g.SP * g.N, 2 * g.M), value_weights).astype(BF16)
    half = value_weights.shape[1] // 2
    width = half // g.H
    group = LANES // width
    count = g.H // group
    tall = group * g.I
    head = iota((1, 2 * LANES), 1) % LANES // width

    def lanes(array, k):
        return lanes_of([array[:, s * half + k * LANES : s * half + (k + 1) * LANES] for s in range(2)])

    group_weights = [lanes(value_weights, k) for k in range(count)]
    low_t = lanes_of([low_t, low_t])
    grad_soft = [jnp.zeros((tall, g.N), F32) for _ in range(count)]
    for k in range(g.SP):
        v = values[k * g.N : (k + 1) * g.N]
        rows = slice(k * g.I, (k + 1) * g.I)
        blended, factor = gm_ref[rows, :], gate_ref[rows, :]
        projected = []
        for m in range(count):
            vm = lanes(v, m)
            crossed = mm(low[m * tall : (m + 1) * tall], vm)
            mixed = crossed[: g.I]
            for h in range(1, group):
                mixed = jnp.where(head == h, crossed[h * g.I : (h + 1) * g.I], mixed)
            gate_grad = (lanes(factor, m) * mixed).astype(BF16)
            for s in range(2):
                first = s * half + m * LANES
                gg_ref[rows, first : first + LANES] = gate_grad[:, s * LANES : (s + 1) * LANES]
            bm = lanes(blended, m)
            by_head = rows_of([jnp.where(head == h, bm, jnp.zeros_like(bm)) for h in range(group)])
            grad_soft[m] = grad_soft[m] + mm(by_head, vm, NT)
            projected.append(mm(by_head, group_weights[m], NT))
        total_ref[k] = go_ref[k] + mm(low_t, rows_of([*split_high_low(rows_of(projected))]))
    gs_ref[...] = rows_of(grad_soft)
    own = total_ref[:, pl.ds(g.place(row, col), g.I), :]
    own_ref[...] = own.reshape(g.SP * g.I, 2 * g.M)
    for x in range(1, g.R):
        block = total_ref[:, pl.ds(g.place(jnp.bitwise_xor(row, x), col), g.I), :]
        send_refs[x - 1][...] = block.reshape(g.SP * g.I, 2 * g.M).astype(BF16)


def pack_kernel(g, *refs):
    refs = list(refs)
    sums, refs = refs[: g.R - 1], refs[g.R - 1 :]
    parts, refs = refs[: g.D], refs[g.D :]
    outs, (own_ref, halves_ref) = refs[: g.R - 1], refs[g.R - 1 :]
    row = lax.axis_index("row")
    total = parts[0][...]
    for ref in parts[1:]:
        total = total + ref[...]
    half, rows = own_ref.shape[0], g.SP * g.I
    for k in range(2):
        halves_ref[k] = total[k * half : (k + 1) * half].astype(BF16)
    own_ref[...] = halves_ref[lax.rem(row, 2)]
    for x in range(1, g.R):
        outs[x - 1][:rows, :] = sums[x - 1][...]
        outs[x - 1][rows:, :] = halves_ref[lax.rem(jnp.bitwise_xor(row, x), 2)]


def piece_kernel(g, own_ref, *refs):
    out_ref, order_ref = refs[-2:]
    row, rows = lax.axis_index("row"), g.SP * g.I
    order_ref[row] = own_ref[...]
    for k in range(1, g.R):
        order_ref[jnp.bitwise_xor(row, g.R - k)] = refs[k - 1][rows:, :]
    total = order_ref[0].astype(F32)
    for r in range(1, g.R):
        total = total + order_ref[r].astype(F32)
    out_ref[...] = total.astype(BF16)


def score_kernel(g, soft_ref, *refs):
    parts, refs = refs[: g.D], refs[g.D :]
    own_ref, out_refs, order_ref = refs[0], refs[1 : g.C], refs[g.C]
    depth = lax.axis_index("depth")
    for k in range(g.D):
        order_ref[lax.rem(depth - k + g.D, g.D)] = parts[k][...]
    grad_soft = order_ref[0]
    for k in range(1, g.D):
        grad_soft = grad_soft + order_ref[k]
    inner = jnp.sum(soft_ref[...] * grad_soft, -1, keepdims=True)
    for k in range(g.C):
        block = lanes_of([grad_soft[:, k * g.JC : (k + 1) * g.JC], inner])
        if k == 0:
            own_ref[...] = block
        else:
            out_refs[k - 1][...] = three_lanes(block)


def pair_kernel(g, e_ref, wl_ref, soft_ref, own_ref, *refs):
    got, pair_ref = refs[: g.C - 1], refs[g.C - 1]
    heads = g.H * g.I
    total = own_ref[...]
    for ref in got:
        total = total + join_three(ref[...], g.JC + 1)
    grad = soft_ref[:, : g.JC] * (total[:, : g.JC] - total[:, g.JC :])
    if g.JC < LANES:
        grad = lanes_of([grad, jnp.zeros((heads, LANES - g.JC), F32)])
    high, low = split_high_low(grad.T[: g.JC])
    grads = lanes_of([high, low])
    pick = (iota((heads, g.H), 0) // g.I == iota((heads, g.H), 1)).astype(BF16)
    base = mm(pick, wl_ref[...]).astype(BF16)
    token = iota((heads, 1), 0) % g.I
    for i in range(0, g.I, 2):
        weights = lanes_of(
            [jnp.where(token == i + k, base, jnp.zeros_like(base)) for k in range(2)]
        )
        upstream = mm(grads, rows_of([weights, weights]))
        for k in range(2):
            pair_ref[i + k] = standardize_backward(
                e_ref[i + k].astype(F32), upstream[:, k * g.Z : (k + 1) * g.Z]
            ).astype(BF16)


def reduce_kernel(g, x_ref, own_ref, *refs):
    got, out_ref = refs[:-1], refs[-1]
    rows = g.SP * g.I
    total = own_ref[...]
    for ref in got:
        total = total + ref[:rows, :].astype(F32)
    total = total.reshape(g.SP, 1, g.I, 2 * g.M)
    upstream = jnp.concatenate([total[..., : g.M], total[..., g.M :]], axis=1)
    upstream = upstream.reshape(g.S, g.I, g.M)[: g.SQ]
    msa = g.fill(standardize_backward(x_ref[...].astype(F32), upstream))
    msa = msa.reshape(g.SP, 2, g.I, g.M)
    msa = jnp.concatenate([msa[:, 0], msa[:, 1]], axis=-1).astype(BF16)
    out_ref[...] = msa.reshape(rows, 2 * g.M)


def across_kernel(g, *refs):
    out_ref = refs[-1]
    row, col = lax.axis_index("row"), lax.axis_index("col")
    for ref, (b, k) in zip(refs[:-1], g.spread, strict=True):
        half = lax.rem(jnp.bitwise_xor(row, b), 2)
        out_ref[lax.rem(col - k + g.C, g.C), half] = ref[...]


def unpack_kernel(g, *refs):
    parts, msa_ref = refs[: g.C], refs[g.C]
    col = lax.axis_index("col")
    for k, ref in enumerate(parts):
        msa = ref[...].astype(F32).reshape(g.SP, 1, g.I, 2 * g.M)
        msa = jnp.concatenate([msa[..., : g.M], msa[..., g.M :]], axis=1)
        msa = msa.reshape(g.S, g.I, g.M)[: g.SQ].astype(BF16)
        msa_ref[pl.ds(lax.rem(col - k + g.C, g.C) * g.SQ, g.SQ)] = msa


def finish_kernel(g, msa_ref, *refs):
    parts, (out_ref, matrix_ref) = refs[: g.D], refs[g.D :]
    depth = lax.axis_index("depth")
    out_ref[...] = msa_ref[...]
    share = g.Q // g.D
    for k in range(g.D):
        first = lax.rem(depth - k + g.D, g.D) * share
        for c in range(g.C):
            block = parts[k][c].astype(F32)
            matrix_ref[pl.ds(first, share), c * g.QL : (c + 1) * g.QL, :] = block


class Sizes:
    def __init__(self, x, e, wl, w1):
        self.R, self.C, self.D = (lax.axis_size(a) for a in ("row", "col", "depth"))
        self.I, self.M = x.shape[1:]
        self.JC, self.Z = e.shape[1:]
        self.H, self.Q = wl.shape[1], w1.shape[1]
        self.QL = self.Q // self.C
        self.SQ = x.shape[0] // self.C
        self.S = -(-self.SQ // 16) * 16
        self.SP, self.N = self.S // 2, self.R * self.I
        self.F = self.R // self.C
        self.NT = -(-self.N // LANES)
        self.G = max(1, LANES // self.JC)
        self.EXTRA = -(-(self.C - 1) * self.S * self.QL // LANES)
        self.carried = 0
        self.spread = [(b, k) for k in range(self.C) for b in range(2)]
        self.order = [*range(1, self.R // 2), *range(self.R // 2 + 1, self.R), self.R // 2]

    def fill(self, rows):
        if self.SQ == self.S:
            return rows
        return rows_of([rows, jnp.zeros((self.S - self.SQ, *rows.shape[1:]), rows.dtype)])

    def place(self, row, col):
        turn = lax.rem(row // self.F - col + self.C, self.C)
        return pl.multiple_of((turn * self.F + lax.rem(row, self.F)) * self.I, self.I)


def shift(array, axis, k):
    count = lax.axis_size(axis)
    return lax.ppermute(array, axis, [(i, (i + k) % count) for i in range(count)])


def swap(array, axis, x):
    return lax.ppermute(array, axis, [(i, i ^ x) for i in range(lax.axis_size(axis))])


def swapped(arrays, axis):
    return [swap(a, axis, k + 1) for k, a in reversed([*enumerate(arrays)])]


def from_near(array, b, k):
    count, wide = lax.axis_size("row"), lax.axis_size("col")
    pairs = [(r * wide + c, (r ^ b) * wide + (c + k) % wide) for r in range(count) for c in range(wide)]
    return lax.ppermute(array, ("row", "col"), pairs)


def shifted_all(array, axis):
    return [array] + [shift(array, axis, k) for k in range(1, lax.axis_size(axis))]


def per_device(
    homolog_ensemble,
    duplex_embedding,
    homolog_present_flags,
    resolved_position_flags,
    payload_weights,
    sigmoid_weights,
    averager_final_weights,
    first_operand_weights,
    second_operand_weights,
    duplex_logit_weights,
    tensor_product_weights,
    averager_upstream_adjoint,
    duplex_upstream_adjoint,
):
    g = Sizes(homolog_ensemble, duplex_embedding, duplex_logit_weights, first_operand_weights)
    shape = jax.ShapeDtypeStruct

    def call(kernel, name, args, outs, scratch=(), far=None, after=(), distant=False, us=1.0):
        size = sum(a.size * a.dtype.itemsize for a in args) + sum(
            math.prod(o.shape) * jnp.dtype(o.dtype).itemsize for o in outs
        )
        single = len(outs) == 1
        near = len(args) if far is None else far
        args = list(args[:near]) + [
            pltpu.with_memory_space_constraint(a, pltpu.HBM) for a in args[near:]
        ]

        if distant:
            after = [pltpu.with_memory_space_constraint(a, pltpu.HBM) for a in after]

        def body(*refs):
            kernel(g, *refs[: len(args)], *refs[len(args) + len(after) :])

        return pl.pallas_call(
            body,
            out_shape=outs[0] if single else tuple(outs),
            in_specs=[VMEM] * near + [FAR] * (len(args) - near) + [FAR if distant else VMEM] * len(after),
            out_specs=VMEM if single else (VMEM,) * len(outs),
            scratch_shapes=list(scratch),
            compiler_params=pltpu.CompilerParams(vmem_limit_bytes=40 * 1024 * 1024),
            cost_estimate=pl.CostEstimate(
                flops=int(us * 1.15e9), bytes_accessed=size, transcendentals=0
            ),
            name=name,
        )(*args, *after)

    heads = g.H * g.I
    rows = g.SP * g.I
    values = 2 * payload_weights.shape[1]
    pairs, tall = g.I * g.JC, heads // g.G
    xn, send, logits, near, x, e, wl, masks, w1, outer_weights, w2 = call(
        normalise_kernel,
        "normalise",
        (
            homolog_ensemble,
            duplex_embedding,
            duplex_upstream_adjoint.reshape(pairs, g.Z),
            resolved_position_flags.reshape(1, g.JC),
            duplex_logit_weights.T,
            homolog_present_flags,
            first_operand_weights.T,
            tensor_product_weights,
            second_operand_weights.T,
            homolog_present_flags.reshape(1, -1),
        ),
        [
            pltpu.VMEM((g.C, g.SP, g.I, 2 * g.M), BF16),
            pltpu.VMEM((rows + g.EXTRA * g.I, 2 * g.M), BF16),
            pltpu.VMEM((tall, g.G * g.JC), F32),
            pltpu.VMEM((pairs + 3 * tall, g.Z), BF16),
            pltpu.VMEM((g.SQ, g.I, g.M), BF16),
            pltpu.VMEM(duplex_embedding.shape, BF16),
            pltpu.VMEM((g.H, g.Z), BF16),
            pltpu.VMEM((g.C * g.SP + 8, 2 * g.M), F32),
            pltpu.VMEM((g.Q, g.M), BF16),
            pltpu.VMEM(tensor_product_weights.shape, BF16),
            pltpu.VMEM((g.Q, g.M), BF16),
        ],
        [
            pltpu.VMEM((1, g.JC), jnp.int32),
            pltpu.SMEM(homolog_present_flags.shape, jnp.int32),
            pltpu.VMEM((1, homolog_present_flags.shape[0]), jnp.int32),
            pltpu.VMEM(homolog_ensemble.shape, BF16),
            pltpu.VMEM(homolog_ensemble.shape, F32),
            pltpu.VMEM((g.I * g.H, LANES), F32),
            pltpu.SemaphoreType.DMA((10,)),
        ],
        far=0,
        us=2.0,
    )
    everyone = [send] + [swap(send, "row", k) for k in g.order]
    nears = shifted_all(near, "col")
    later = (
        sigmoid_weights,
        averager_final_weights.T,
        payload_weights,
    )
    g.carried = len(later)
    left, weights, left_weights, u, sg, wf, p = call(
        prepare_kernel,
        "prepare",
        (xn, w1, outer_weights, masks, averager_upstream_adjoint, *later),
        [
            pltpu.VMEM((g.C * g.I * g.S, g.Q), BF16),
            pltpu.VMEM((g.Q, g.Q, g.Z), BF16),
            pltpu.VMEM((g.I, g.Q * g.S, g.Z), BF16),
            pltpu.VMEM((g.SQ, g.I, g.M), BF16),
        ]
        + [pltpu.VMEM(a.shape, a.dtype) for a in later],
        [
            pltpu.VMEM(tensor_product_weights.shape, F32),
            pltpu.VMEM((2, rows, LANES), F32),
            pltpu.SemaphoreType.DMA,
            pltpu.SemaphoreType.DMA((len(later),)),
        ],
        far=4,
        us=0.01,
    )
    gate_weights, blended, gate_factor = call(
        gate_kernel,
        "gate",
        (xn, u, sg, wf),
        [
            pltpu.VMEM((2 * g.M, values), BF16),
            pltpu.VMEM((rows, values), BF16),
            pltpu.VMEM((rows, values), F32),
        ],
        after=nears[1:],
        us=0.01,
    )
    cotangents, second_term = call(
        right_kernel,
        "right",
        (*nears, left_weights, w2, masks),
        [pltpu.VMEM((g.I, g.N, g.Z), BF16), pltpu.VMEM((g.SP, g.N, 2 * g.M), F32)],
        [pltpu.VMEM((g.NT, g.Q * g.S, LANES), F32)],
        after=(gate_weights,),
        us=0.01,
    )
    share = g.Q * g.QL // g.D
    xall, products, *matrix_parts = call(
        outer_kernel,
        "outer",
        (*everyone, cotangents, left, w2, masks),
        [
            pltpu.VMEM((g.SP, g.N, 2 * g.M), BF16),
            pltpu.VMEM((g.QL, g.C, g.I, g.S, g.Z), BF16),
        ]
        + [pltpu.VMEM((share, g.Z), F32)] * g.D,
        [
            pltpu.VMEM((g.N, max(1, g.EXTRA) * LANES), BF16),
            pltpu.VMEM((g.NT, g.C * g.SP * 2 * g.QL, LANES), F32),
            pltpu.VMEM((g.QL * g.C * g.S, g.N), BF16),
            pltpu.VMEM((g.Q * g.QL, g.Z), F32),
        ],
        after=(second_term,),
        us=0.05,
    )
    matrix_parts = [matrix_parts[0]] + [
        shift(a, "depth", k + 1) for k, a in enumerate(matrix_parts[1:])
    ]
    soft, grad_soft, own, gate_grads, *sums = call(
        attend_kernel,
        "attend",
        (xall, logits, *nears[1:], blended, gate_factor, p, second_term),
        [
            pltpu.VMEM((heads, g.N), F32),
            pltpu.VMEM((heads, g.N), F32),
            pltpu.VMEM((rows, 2 * g.M), F32),
            pltpu.VMEM((rows, values), BF16),
        ]
        + [pltpu.VMEM((rows, 2 * g.M), BF16)] * (g.R - 1),
        [pltpu.VMEM((g.SP, g.N, 2 * g.M), F32)],
        us=3.0,
    )
    *sums, piece = call(
        pack_kernel,
        "pack",
        (*sums, *matrix_parts),
        [pltpu.VMEM((rows + share // 2, 2 * g.M), BF16)] * (g.R - 1)
        + [pltpu.VMEM((share // 2, g.Z), BF16)],
        [pltpu.VMEM((2, share // 2, g.Z), BF16)],
        us=0.2,
    )
    sums = swapped(sums, "row")
    wide = -(-3 * (g.JC + 1) // LANES) * LANES
    scores, *sends = call(
        score_kernel,
        "score",
        (soft, *shifted_all(grad_soft, "depth")),
        [pltpu.VMEM((heads, g.JC + 1), F32)] + [pltpu.VMEM((heads, wide), BF16)] * (g.C - 1),
        [pltpu.VMEM((g.D, heads, g.N), F32)],
        after=(piece,),
        us=0.2,
    )
    arrived = [shift(a, "col", k + 1) for k, a in enumerate(sends)]
    own = call(
        own_kernel,
        "own",
        (xall, products, cotangents, weights, w1, w2, masks, own, gate_grads, gate_weights),
        [pltpu.VMEM((rows, 2 * g.M), F32)],
        [
            pltpu.VMEM((g.NT, g.SP * 2 * g.Q, LANES), F32),
            pltpu.VMEM((g.Q * g.S, g.N), BF16),
            pltpu.VMEM((max(1, g.C - 1), g.QL, g.I, g.S, g.Z), BF16),
            pltpu.VMEM((g.I * g.S, 2 * g.M), F32),
        ],
        after=(scores,),
        us=0.01,
    )
    piece = call(
        piece_kernel,
        "piece",
        (piece, *sums),
        [pltpu.VMEM((share // 2, g.Z), BF16)],
        [pltpu.VMEM((g.R, share // 2, g.Z), BF16)],
        after=(own,),
        us=0.1,
    )
    pieces = [piece] + [from_near(piece, b, k) for b, k in g.spread[1:]]
    part = call(
        reduce_kernel,
        "reduce",
        (x, own, *sums),
        [pltpu.VMEM((rows, 2 * g.M), BF16)],
        after=(piece,),
    )
    pairwise_gradient = call(
        pair_kernel,
        "pair",
        (e, wl, soft, scores, *arrived),
        [shape(duplex_embedding.shape, BF16)],
        after=(part,),
        us=0.01,
    )
    matrix = call(
        across_kernel,
        "across",
        pieces,
        [pltpu.VMEM((g.C, 2, share // 2, g.Z), BF16)],
        after=(pairwise_gradient,),
        distant=True,
        us=0.1,
    ).reshape(g.C, g.Q // g.D, g.QL, g.Z)
    ensemble_derivative = call(
        unpack_kernel,
        "unpack",
        shifted_all(part, "col"),
        [pltpu.VMEM(homolog_ensemble.shape, BF16)],
        after=(matrix,),
    )
    ensemble_derivative, outer_matrix_gradient = call(
        finish_kernel,
        "finish",
        (ensemble_derivative, *shifted_all(matrix, "depth")),
        [shape(homolog_ensemble.shape, BF16), shape((g.Q, g.Q, g.Z), F32)],
    )
    outer_matrix_gradient = outer_matrix_gradient.reshape(tensor_product_weights.shape)
    return (ensemble_derivative, pairwise_gradient, outer_matrix_gradient)


def solution(mesh):
    in_specs = (
        P(("parts", "depth"), "row", None),
        P(("parts", "row"), "col", None),
        P("parts"),
        P(("parts", "col")),
        P(),
        P(),
        P(),
        P(),
        P(),
        P(),
        P(),
        P(("parts", "depth"), "row", None),
        P(("parts", "row"), "col", None),
    )
    out_specs = (
        P(("parts", "depth"), "row", None),
        P(("parts", "row"), "col", None),
        P("parts", None),
    )
    return jax.shard_map(
        per_device, mesh=mesh, in_specs=in_specs, out_specs=out_specs, check_vma=False
    )
```

```python
import functools
import math

import jax
import jax.numpy as jnp
from jax import lax
from jax.experimental import pallas as pl
from jax.experimental.pallas import tpu as pltpu
from jax.sharding import PartitionSpec as P

EPS = 1e-05
PENALTY = 10000.0
F32 = jnp.float32
BF16 = jnp.bfloat16
LANES = 128
NN = (((1,), (0,)), ((), ()))
NT = (((1,), (1,)), ((), ()))
VMEM = pl.BlockSpec(memory_space=pltpu.VMEM)
FAR = pl.BlockSpec(memory_space=pl.ANY)


def mm(a, b, dims=NN):
    return lax.dot_general(a, b, dims, preferred_element_type=F32)


def split_high_low(value):
    high = value.astype(BF16)
    return high, (value - high.astype(F32)).astype(BF16)


def iota(shape, dim):
    return lax.broadcasted_iota(jnp.int32, shape, dim)


def lanes_of(pieces):
    return pieces[0] if len(pieces) == 1 else jnp.concatenate(pieces, axis=-1)


def rows_of(pieces):
    return pieces[0] if len(pieces) == 1 else jnp.concatenate(pieces, axis=0)


def standardize(values):
    centred = values - jnp.mean(values, -1, keepdims=True)
    inverse = lax.rsqrt(jnp.mean(centred * centred, -1, keepdims=True) + EPS)
    return centred * inverse, inverse


def standardize_backward(values, upstream):
    scaled, inverse = standardize(values)
    mean_grad = jnp.mean(upstream, -1, keepdims=True)
    mean_cross = jnp.mean(upstream * scaled, -1, keepdims=True)
    return (upstream - mean_grad - scaled * mean_cross) * inverse


def on_diagonal(block, width):
    rows, lanes = block.shape
    same = iota(block.shape, 0) // (rows // 2) == iota(block.shape, 1) // width
    return jnp.where(same, block, jnp.zeros_like(block))


def split_three(value):
    high = value.astype(BF16)
    rest = value - high.astype(F32)
    middle = rest.astype(BF16)
    return [high, middle, (rest - middle.astype(F32)).astype(BF16)]


def three_lanes(value):
    rows, width = value.shape
    fill = -(3 * width) % LANES
    return lanes_of(split_three(value) + [jnp.zeros((rows, fill), BF16)] * (fill > 0))


def join_three(parts, width):
    wide = parts.astype(F32)
    return (wide[:, :width] + wide[:, width : 2 * width]) + wide[:, 2 * width : 3 * width]


def twice(weights):
    zero = jnp.zeros_like(weights)
    return rows_of([lanes_of([weights, zero]), lanes_of([zero, weights])])


def column_weights(g, w2):
    rows = iota((2 * g.QL, g.Q), 0) % g.QL + lax.axis_index("col") * g.QL
    pick = (iota((2 * g.QL, g.Q), 1) == rows).astype(BF16)
    return on_diagonal(mm(pick, lanes_of([w2, w2])), g.M).astype(BF16)


def normalise_kernel(
    g, x_hbm, e_hbm, dd_hbm, flag_hbm, wl_hbm, live_hbm, w1_hbm, t_hbm, w2_hbm, every_hbm, *refs
):
    xn_ref, send_ref, logit_ref, near_ref, x_ref, e_ref, wl_ref, mask_ref, w1_ref, t_ref, w2_ref = refs[:11]
    flag_in, live_in, every_in, x_in, norm_ref, rows_ref, sem = refs[11:]
    col = lax.axis_index("col")
    pairs = g.I * g.JC
    copies = [
        pltpu.make_async_copy(a, b, sem.at[k])
        for k, (a, b) in enumerate(
            [
                (x_hbm, x_in),
                (e_hbm, e_ref),
                (wl_hbm, wl_ref),
                (flag_hbm, flag_in),
                (dd_hbm, near_ref.at[pl.ds(0, pairs)]),
                (live_hbm, live_in),
                (w1_hbm, w1_ref),
                (t_hbm, t_ref),
                (w2_hbm, w2_ref),
                (every_hbm, every_in),
            ]
        )
    ]
    for copy in copies:
        copy.start()
    for copy in (*copies[:4], copies[5], *copies[8:]):
        copy.wait()
    lane = iota((1, 2 * g.M), 1)
    groups = [lax.rem(col + m, g.C) for m in range(g.C)]
    for m, group in enumerate(groups):
        first = (lax.axis_index("depth") * g.C + group) * g.SQ
        for k in range(g.SP):
            if 2 * k + 1 < g.SQ:
                flags = jnp.where(lane < g.M, live_in[first + 2 * k], live_in[first + 2 * k + 1])
                flags = flags.astype(F32)
            else:
                flags = jnp.zeros((1, 2 * g.M), F32)
            mask_ref[m * g.SP + k : m * g.SP + k + 1, :] = flags
    count = jnp.sum(every_in[...].astype(F32), -1, keepdims=True)
    mask_ref[g.C * g.SP : g.C * g.SP + 1, :] = jnp.broadcast_to(1.0 / (0.001 + count), (1, 2 * g.M))
    norm_ref[...] = standardize(x_in[...].astype(F32))[0]
    x_ref[...] = x_in[pl.ds(col * g.SQ, g.SQ)]
    second = column_weights(g, w2_ref[...])
    rows, blocks = g.SP * g.I, []
    for m, group in enumerate(groups):
        normed = g.fill(norm_ref[pl.ds(group * g.SQ, g.SQ)]).reshape(g.SP, 2, g.I, g.M)
        packed = jnp.concatenate([normed[:, 0], normed[:, 1]], axis=-1).astype(BF16)
        xn_ref[m] = packed
        if m == 0:
            send_ref[:rows, :] = packed.reshape(rows, 2 * g.M)
        else:
            masks = [mask_ref[m * g.SP + k : m * g.SP + k + 1, :] for k in range(g.SP)]
            live = rows_of([(packed[k].astype(F32) * masks[k]).astype(BF16) for k in range(g.SP)])
            factors = mm(live, second, NT)
            blocks += [factors[k * g.I : (k + 1) * g.I] for k in range(g.SP)]
    if blocks:
        wide = lanes_of(blocks)
        fill = -wide.shape[1] % LANES
        if fill:
            wide = lanes_of([wide, jnp.zeros((g.I, fill), F32)])
        for k in range(g.EXTRA):
            block = wide[:, k * LANES : (k + 1) * LANES]
            send_ref[rows + k * g.I : rows + (k + 1) * g.I, :] = block.astype(BF16)
    pair = standardize(e_ref[...].astype(F32).reshape(pairs, g.Z))[0].astype(BF16)
    penalty = (flag_in[...].astype(F32) - 1.0) * PENALTY
    weights = wl_ref[...]
    for i in range(g.I):
        rows_ref[i * g.H : (i + 1) * g.H, : g.JC] = (
            mm(weights, pair[i * g.JC : (i + 1) * g.JC], NT) + penalty
        )
    logits = rows_of([rows_ref[pl.ds(h, g.I, stride=g.H), :][:, : g.JC] for h in range(g.H)])
    tall = g.H * g.I // g.G
    packed = lanes_of([logits[k * tall : (k + 1) * tall] for k in range(g.G)])
    logit_ref[...] = packed
    near_ref[pairs:, :] = rows_of(split_three(packed))
    for copy in (copies[4], *copies[6:8]):
        copy.wait()


def prepare_kernel(g, xn_ref, w1_ref, t_ref, mask_ref, u_hbm, *refs):
    refs = list(refs)
    count = g.carried
    sources, refs = refs[:count], refs[count:]
    left_ref, ts_ref, lt_ref, u_ref, refs = refs[0], refs[1], refs[2], refs[3], refs[4:]
    targets, (wide_ref, half_ref, first_sem, later_sem) = refs[:count], refs[count:]
    first = lax.axis_index("col") * g.SQ
    copies = [pltpu.make_async_copy(u_hbm.at[pl.ds(first, g.SQ)], u_ref, first_sem)]
    copies += [
        pltpu.make_async_copy(a, b, later_sem.at[k])
        for k, (a, b) in enumerate(zip(sources, targets, strict=True))
    ]
    for copy in copies:
        copy.start()
    w1 = rows_of([w1_ref[...], jnp.zeros((LANES - g.Q, g.M), BF16)])
    zero = jnp.zeros_like(w1)
    for m in range(g.C):
        masks = [mask_ref[m * g.SP + k : m * g.SP + k + 1, :] for k in range(g.SP)]
        live_xn = rows_of(
            [(xn_ref[m, k].astype(F32) * masks[k]).astype(BF16) for k in range(g.SP)]
        )
        half_ref[0] = mm(live_xn, lanes_of([w1, zero]), NT)
        half_ref[1] = mm(live_xn, lanes_of([zero, w1]), NT)
        for i in range(g.I):
            halves = [half_ref[half, pl.ds(i, g.SP, stride=g.I), :] for half in range(2)]
            first = (m * g.I + i) * g.S
            left_ref[first : first + g.S, :] = rows_of(halves)[:, : g.Q].astype(BF16)
    wide_ref[...] = t_ref[...].astype(F32)
    for q in range(g.Q):
        ts_ref[q] = wide_ref[pl.ds(q, g.Q, stride=g.Q), :].astype(BF16)
    left = left_ref[: g.I * g.S, :]
    for q in range(0, g.Q, 2):
        product = mm(left, lanes_of([ts_ref[q], ts_ref[q + 1]]))
        for k in range(2):
            block = product[:, k * g.Z : (k + 1) * g.Z].reshape(g.I, g.S, g.Z)
            lt_ref[:, (q + k) * g.S : (q + k + 1) * g.S, :] = block.astype(BF16)
    for copy in copies:
        copy.wait()


def gate_kernel(g, xn_ref, u_ref, sg_ref, wf_ref, gate_weight_ref, gm_ref, gate_ref):
    rows = g.SP * g.I
    xn = xn_ref[0]
    gate_weights = twice(sg_ref[...])
    gate_weight_ref[...] = gate_weights
    gates = jax.nn.sigmoid(mm(xn.reshape(rows, 2 * g.M), gate_weights))
    u = g.fill(u_ref[...]).reshape(g.SP, 2, g.I, g.M)
    packed_u = jnp.concatenate([u[:, 0], u[:, 1]], axis=-1).reshape(rows, 2 * g.M)
    gated = mm(packed_u, twice(wf_ref[...]))
    blended = gated * gates
    gm_ref[...] = blended.astype(BF16)
    gate_ref[...] = blended * (1.0 - gates)


def right_kernel(g, *refs):
    near_refs, (lt_ref, w2_ref, mask_ref, d_ref, go_ref, rg_ref) = refs[: g.C], refs[g.C :]
    for k in range(g.C):
        spot = (g.C - k) % g.C
        block = near_refs[k][: g.I * g.JC, :].reshape(g.I, g.JC, g.Z)
        d_ref[:, spot * g.JC : (spot + 1) * g.JC, :] = block
    masks = [mask_ref[k : k + 1, :] for k in range(g.SP)]
    scale = mask_ref[g.C * g.SP : g.C * g.SP + 1, :]
    right_grad = jnp.zeros((g.Q * g.S, g.N), F32)
    for i in range(0, g.I, 2):
        right_grad = right_grad + mm(
            lanes_of([lt_ref[i], lt_ref[i + 1]]), lanes_of([d_ref[i], d_ref[i + 1]]), NT
        )
    for t in range(g.NT):
        lanes = min(LANES, g.N - t * LANES)
        piece = right_grad[:, t * LANES : t * LANES + lanes]
        if lanes < LANES:
            piece = lanes_of([piece, jnp.zeros((g.Q * g.S, LANES - lanes), F32)])
        rg_ref[t] = piece
    deep = 2 * g.Q
    group = min(g.SP, LANES // deep)
    which = iota((group * deep, g.Q), 0)
    pick = (iota((group * deep, g.Q), 1) == which % deep // 2).astype(BF16)
    w2 = w2_ref[...]
    base = mm(pick, lanes_of([w2, w2]))
    which = iota(base.shape, 0)
    base = jnp.where(which % 2 == iota(base.shape, 1) // g.M, base, 0.0)
    weights = lanes_of([jnp.where(which // deep == k, base, 0.0) for k in range(group)]).astype(BF16)
    for k in range(0, g.SP, group):
        for t in range(g.NT):
            lanes = min(LANES, g.N - t * LANES)
            tall = rows_of(
                [rg_ref[t, pl.ds(k + m, deep, stride=g.SP), :] for m in range(group)]
            )
            tall = (tall * scale).T[:lanes]
            high, low = split_high_low(tall)
            part = mm(high, weights) + mm(low, weights)
            for m in range(group):
                go_ref[k + m, t * LANES : t * LANES + lanes, :] = (
                    part[:, m * 2 * g.M : (m + 1) * 2 * g.M] * masks[k + m]
                )


def outer_kernel(g, *refs):
    refs = list(refs)
    x_refs, refs = refs[: g.R], refs[g.R :]
    d_ref, left_ref, w2_ref, mask_ref, xall_ref, ds_ref, *refs = refs
    w_refs, (others_ref, spread_ref, rt_ref, all_ref) = refs[: g.D], refs[g.D :]
    row, col, depth = (lax.axis_index(a) for a in ("row", "col", "depth"))
    rows, deep = g.SP * g.I, 2 * g.QL
    for k, ref in zip((0, *g.order), x_refs, strict=True):
        place = g.place(jnp.bitwise_xor(row, k), col)
        xall_ref[:, pl.ds(place, g.I), :] = ref[:rows, :].reshape(g.SP, g.I, 2 * g.M)
        for m in range(g.EXTRA):
            block = ref[rows + m * g.I : rows + (m + 1) * g.I, :]
            others_ref[pl.ds(place, g.I), m * LANES : (m + 1) * LANES] = block
    second = column_weights(g, w2_ref[...])
    parts = [
        mm(second, (xall_ref[k].astype(F32) * mask_ref[k : k + 1, :]).astype(BF16), NT)
        for k in range(g.SP)
    ]
    if g.EXTRA:
        lanes = g.EXTRA * LANES
        eye = (iota((lanes, lanes), 0) == iota((lanes, lanes), 1)).astype(BF16)
        parts.append(mm(eye, others_ref[...], NT)[: (g.C - 1) * g.SP * deep])
    first = 0
    for part in parts:
        for t in range(g.NT):
            lanes = min(LANES, g.N - t * LANES)
            piece = part[:, t * LANES : t * LANES + lanes]
            spread_ref[t, first : first + part.shape[0], :lanes] = piece
        first += part.shape[0]
    for q in range(g.QL):
        for m in range(g.C):
            spot = (q * g.C + m) * g.S
            for t in range(g.NT):
                lanes = min(LANES, g.N - t * LANES)
                halves = [
                    spread_ref[t, pl.ds(m * g.SP * deep + half * g.QL + q, g.SP, stride=deep), :]
                    for half in range(2)
                ]
                rt_ref[spot : spot + g.S, t * LANES : t * LANES + lanes] = rows_of(halves)[
                    :, :lanes
                ].astype(BF16)
    rt = rt_ref[...]
    for i in range(0, g.I, 2):
        product = mm(rt, lanes_of([d_ref[i], d_ref[i + 1]]))
        for k in range(2):
            block = product[:, k * g.Z : (k + 1) * g.Z]
            ds_ref[:, :, i + k] = block.reshape(g.QL, g.C, g.S, g.Z).astype(BF16)
    eye = (iota((g.Q, g.Q), 0) == iota((g.Q, g.Q), 1)).astype(BF16)
    left_t = mm(eye, left_ref[...], NT).astype(BF16)
    scale = mask_ref[g.C * g.SP : g.C * g.SP + 1, :]
    entries = g.C * g.S * g.I
    for q in range(0, g.QL, 2):
        both = lanes_of([ds_ref[q].reshape(entries, g.Z), ds_ref[q + 1].reshape(entries, g.Z)])
        part = mm(left_t, both)
        all_ref[pl.ds(q, g.Q, stride=g.QL), :] = part[:, : g.Z] * scale
        all_ref[pl.ds(q + 1, g.Q, stride=g.QL), :] = part[:, g.Z :] * scale
    share = g.Q * g.QL // g.D
    for k in range(g.D):
        first = pl.multiple_of(lax.rem(depth + k, g.D) * share, share)
        w_refs[k][...] = all_ref[pl.ds(first, share), :]


def own_kernel(
    g, xall_ref, near_ref, d_ref, ts_ref, w1_ref, w2_ref, mask_ref, part_ref, gg_ref, gate_weight_ref, own_ref,
    spread_ref, rt_ref, ds_ref, turn_ref,
):
    scale = mask_ref[g.C * g.SP : g.C * g.SP + 1, :]
    masks = [mask_ref[k : k + 1, :] for k in range(g.SP)]
    w2 = w2_ref[...]
    doubled = lanes_of([w2, w2])
    second = on_diagonal(rows_of([doubled, doubled]), g.M)
    for k in range(g.SP):
        live_x = (xall_ref[k].astype(F32) * masks[k]).astype(BF16)
        part = mm(second, live_x, NT)
        for t in range(g.NT):
            lanes = min(LANES, g.N - t * LANES)
            spread_ref[t, k * 2 * g.Q : (k + 1) * 2 * g.Q, :lanes] = part[
                :, t * LANES : t * LANES + lanes
            ]
    for q in range(g.Q):
        for t in range(g.NT):
            lanes = min(LANES, g.N - t * LANES)
            halves = [
                spread_ref[t, pl.ds(half * g.Q + q, g.SP, stride=2 * g.Q), :] for half in range(2)
            ]
            rt_ref[q * g.S : (q + 1) * g.S, t * LANES : t * LANES + lanes] = rows_of(halves)[
                :, :lanes
            ].astype(BF16)
    col = lax.axis_index("col")
    entries = g.S * g.I
    left_grad = jnp.zeros((entries, g.Q), F32)
    for m in range(g.C):
        first = lax.rem(col + m, g.C) * g.QL
        if m > 0:
            rt = rt_ref[pl.ds(pl.multiple_of(first * g.S, g.QL * g.S), g.QL * g.S), :]
            for i in range(0, g.I, 2):
                product = mm(rt, lanes_of([d_ref[i], d_ref[i + 1]]))
                for k in range(2):
                    block = product[:, k * g.Z : (k + 1) * g.Z]
                    ds_ref[m - 1, :, i + k] = block.reshape(g.QL, g.S, g.Z).astype(BF16)
        for q in range(0, g.QL, 2):
            pair = [near_ref[q + k, 0] if m == 0 else ds_ref[m - 1, q + k] for k in range(2)]
            both = lanes_of([part.reshape(entries, g.Z) for part in pair])
            left_grad = left_grad + mm(both, lanes_of([ts_ref[first + q], ts_ref[first + q + 1]]), NT)
    w1 = w1_ref[...]
    first_term = jnp.zeros((entries, 2 * g.M), F32)
    for piece in split_high_low(left_grad * scale[:, : g.Q]):
        first_term = first_term + mm(piece, lanes_of([w1, w1]))
    turn_ref[...] = first_term
    gate_term = mm(gg_ref[...], gate_weight_ref[...], NT)
    lane = iota((1, 2 * g.M), 1)
    for k in range(g.SP):
        rows = slice(k * g.I, (k + 1) * g.I)
        halves = [turn_ref[pl.ds(half * g.SP + k, g.I, stride=g.S), :] for half in range(2)]
        term = jnp.where(lane < g.M, halves[0], halves[1]) * mask_ref[k : k + 1, :]
        own_ref[rows, :] = part_ref[rows, :] + gate_term[rows] + term


def attend_kernel(g, *refs):
    refs = list(refs)
    xall_ref, refs = refs[0], refs[1:]
    logit_ref, near_refs, refs = refs[0], refs[1 : g.C], refs[g.C :]
    gm_ref, gate_ref, p_ref, go_ref, soft_ref, gs_ref, own_ref, gg_ref, *refs = refs
    send_refs, (total_ref,) = refs[: g.R - 1], refs[g.R - 1 :]
    row, col = lax.axis_index("row"), lax.axis_index("col")
    tall, blocks = logit_ref.shape[0], [logit_ref[...]]
    for k in range(1, g.C):
        parts = near_refs[g.C - k - 1][g.I * g.JC :, :].astype(F32)
        blocks.append((parts[:tall] + parts[tall : 2 * tall]) + parts[2 * tall :])
    logits = lanes_of(
        [rows_of([b[:, k * g.JC : (k + 1) * g.JC] for k in range(g.G)]) for b in blocks]
    )
    shifted = jnp.exp(logits - jnp.max(logits, -1, keepdims=True))
    soft = shifted / jnp.sum(shifted, -1, keepdims=True)
    soft_ref[...] = soft
    low = soft.astype(BF16)
    eye = (iota((g.N, g.N), 0) == iota((g.N, g.N), 1)).astype(BF16)
    low_t = mm(eye, low, NT).astype(BF16)
    value_weights = twice(p_ref[...])
    values = mm(xall_ref[...].reshape(g.SP * g.N, 2 * g.M), value_weights).astype(BF16)
    half = value_weights.shape[1] // 2
    width = half // g.H
    group = LANES // width
    count = g.H // group
    tall = group * g.I
    head = iota((1, 2 * LANES), 1) % LANES // width

    def lanes(array, k):
        return lanes_of([array[:, s * half + k * LANES : s * half + (k + 1) * LANES] for s in range(2)])

    group_weights = [lanes(value_weights, k) for k in range(count)]
    low_t = lanes_of([low_t, low_t])
    grad_soft = [jnp.zeros((tall, g.N), F32) for _ in range(count)]
    for k in range(g.SP):
        v = values[k * g.N : (k + 1) * g.N]
        rows = slice(k * g.I, (k + 1) * g.I)
        blended, factor = gm_ref[rows, :], gate_ref[rows, :]
        projected = []
        for m in range(count):
            vm = lanes(v, m)
            crossed = mm(low[m * tall : (m + 1) * tall], vm)
            mixed = crossed[: g.I]
            for h in range(1, group):
                mixed = jnp.where(head == h, crossed[h * g.I : (h + 1) * g.I], mixed)
            gate_grad = (lanes(factor, m) * mixed).astype(BF16)
            for s in range(2):
                first = s * half + m * LANES
                gg_ref[rows, first : first + LANES] = gate_grad[:, s * LANES : (s + 1) * LANES]
            bm = lanes(blended, m)
            by_head = rows_of([jnp.where(head == h, bm, jnp.zeros_like(bm)) for h in range(group)])
            grad_soft[m] = grad_soft[m] + mm(by_head, vm, NT)
            projected.append(mm(by_head, group_weights[m], NT))
        total_ref[k] = go_ref[k] + mm(low_t, rows_of([*split_high_low(rows_of(projected))]))
    gs_ref[...] = rows_of(grad_soft)
    own = total_ref[:, pl.ds(g.place(row, col), g.I), :]
    own_ref[...] = own.reshape(g.SP * g.I, 2 * g.M)
    for x in range(1, g.R):
        block = total_ref[:, pl.ds(g.place(jnp.bitwise_xor(row, x), col), g.I), :]
        send_refs[x - 1][...] = block.reshape(g.SP * g.I, 2 * g.M).astype(BF16)


def pack_kernel(g, *refs):
    refs = list(refs)
    sums, refs = refs[: g.R - 1], refs[g.R - 1 :]
    parts, refs = refs[: g.D], refs[g.D :]
    outs, (own_ref, halves_ref) = refs[: g.R - 1], refs[g.R - 1 :]
    row = lax.axis_index("row")
    total = parts[0][...]
    for ref in parts[1:]:
        total = total + ref[...]
    half, rows = own_ref.shape[0], g.SP * g.I
    for k in range(2):
        halves_ref[k] = total[k * half : (k + 1) * half].astype(BF16)
    own_ref[...] = halves_ref[lax.rem(row, 2)]
    for x in range(1, g.R):
        outs[x - 1][:rows, :] = sums[x - 1][...]
        outs[x - 1][rows:, :] = halves_ref[lax.rem(jnp.bitwise_xor(row, x), 2)]


def piece_kernel(g, own_ref, *refs):
    out_ref, order_ref = refs[-2:]
    row, rows = lax.axis_index("row"), g.SP * g.I
    order_ref[row] = own_ref[...]
    for k in range(1, g.R):
        order_ref[jnp.bitwise_xor(row, g.R - k)] = refs[k - 1][rows:, :]
    total = order_ref[0].astype(F32)
    for r in range(1, g.R):
        total = total + order_ref[r].astype(F32)
    out_ref[...] = total.astype(BF16)


def score_kernel(g, soft_ref, *refs):
    parts, refs = refs[: g.D], refs[g.D :]
    own_ref, out_refs, order_ref = refs[0], refs[1 : g.C], refs[g.C]
    depth = lax.axis_index("depth")
    for k in range(g.D):
        order_ref[lax.rem(depth - k + g.D, g.D)] = parts[k][...]
    grad_soft = order_ref[0]
    for k in range(1, g.D):
        grad_soft = grad_soft + order_ref[k]
    inner = jnp.sum(soft_ref[...] * grad_soft, -1, keepdims=True)
    for k in range(g.C):
        block = lanes_of([grad_soft[:, k * g.JC : (k + 1) * g.JC], inner])
        if k == 0:
            own_ref[...] = block
        else:
            out_refs[k - 1][...] = three_lanes(block)


def pair_kernel(g, e_ref, wl_ref, soft_ref, own_ref, *refs):
    got, pair_ref = refs[: g.C - 1], refs[g.C - 1]
    heads = g.H * g.I
    total = own_ref[...]
    for ref in got:
        total = total + join_three(ref[...], g.JC + 1)
    grad = soft_ref[:, : g.JC] * (total[:, : g.JC] - total[:, g.JC :])
    if g.JC < LANES:
        grad = lanes_of([grad, jnp.zeros((heads, LANES - g.JC), F32)])
    high, low = split_high_low(grad.T[: g.JC])
    grads = lanes_of([high, low])
    pick = (iota((heads, g.H), 0) // g.I == iota((heads, g.H), 1)).astype(BF16)
    base = mm(pick, wl_ref[...]).astype(BF16)
    token = iota((heads, 1), 0) % g.I
    for i in range(0, g.I, 2):
        weights = lanes_of(
            [jnp.where(token == i + k, base, jnp.zeros_like(base)) for k in range(2)]
        )
        upstream = mm(grads, rows_of([weights, weights]))
        for k in range(2):
            pair_ref[i + k] = standardize_backward(
                e_ref[i + k].astype(F32), upstream[:, k * g.Z : (k + 1) * g.Z]
            ).astype(BF16)


def reduce_kernel(g, x_ref, own_ref, *refs):
    got, out_ref = refs[:-1], refs[-1]
    rows = g.SP * g.I
    total = own_ref[...]
    for ref in got:
        total = total + ref[:rows, :].astype(F32)
    total = total.reshape(g.SP, 1, g.I, 2 * g.M)
    upstream = jnp.concatenate([total[..., : g.M], total[..., g.M :]], axis=1)
    upstream = upstream.reshape(g.S, g.I, g.M)[: g.SQ]
    msa = g.fill(standardize_backward(x_ref[...].astype(F32), upstream))
    msa = msa.reshape(g.SP, 2, g.I, g.M)
    msa = jnp.concatenate([msa[:, 0], msa[:, 1]], axis=-1).astype(BF16)
    out_ref[...] = msa.reshape(rows, 2 * g.M)


def across_kernel(g, *refs):
    out_ref = refs[-1]
    row, col = lax.axis_index("row"), lax.axis_index("col")
    for ref, (b, k) in zip(refs[:-1], g.spread, strict=True):
        half = lax.rem(jnp.bitwise_xor(row, b), 2)
        out_ref[lax.rem(col - k + g.C, g.C), half] = ref[...]


def unpack_kernel(g, *refs):
    parts, msa_ref = refs[: g.C], refs[g.C]
    col = lax.axis_index("col")
    for k, ref in enumerate(parts):
        msa = ref[...].astype(F32).reshape(g.SP, 1, g.I, 2 * g.M)
        msa = jnp.concatenate([msa[..., : g.M], msa[..., g.M :]], axis=1)
        msa = msa.reshape(g.S, g.I, g.M)[: g.SQ].astype(BF16)
        msa_ref[pl.ds(lax.rem(col - k + g.C, g.C) * g.SQ, g.SQ)] = msa


def finish_kernel(g, msa_ref, *refs):
    parts, (out_ref, matrix_ref) = refs[: g.D], refs[g.D :]
    depth = lax.axis_index("depth")
    out_ref[...] = msa_ref[...]
    share = g.Q // g.D
    for k in range(g.D):
        first = lax.rem(depth - k + g.D, g.D) * share
        for c in range(g.C):
            block = parts[k][c].astype(F32)
            matrix_ref[pl.ds(first, share), c * g.QL : (c + 1) * g.QL, :] = block


class Sizes:
    def __init__(self, x, e, wl, w1):
        self.R, self.C, self.D = (lax.axis_size(a) for a in ("row", "col", "depth"))
        self.I, self.M = x.shape[1:]
        self.JC, self.Z = e.shape[1:]
        self.H, self.Q = wl.shape[1], w1.shape[1]
        self.QL = self.Q // self.C
        self.SQ = x.shape[0] // self.C
        self.S = -(-self.SQ // 16) * 16
        self.SP, self.N = self.S // 2, self.R * self.I
        self.F = self.R // self.C
        self.NT = -(-self.N // LANES)
        self.G = max(1, LANES // self.JC)
        self.EXTRA = -(-(self.C - 1) * self.S * self.QL // LANES)
        self.carried = 0
        self.spread = [(b, k) for k in range(self.C) for b in range(2)]
        self.order = [*range(1, self.R // 2), *range(self.R // 2 + 1, self.R), self.R // 2]

    def fill(self, rows):
        if self.SQ == self.S:
            return rows
        return rows_of([rows, jnp.zeros((self.S - self.SQ, *rows.shape[1:]), rows.dtype)])

    def place(self, row, col):
        turn = lax.rem(row // self.F - col + self.C, self.C)
        return pl.multiple_of((turn * self.F + lax.rem(row, self.F)) * self.I, self.I)


def shift(array, axis, k):
    count = lax.axis_size(axis)
    return lax.ppermute(array, axis, [(i, (i + k) % count) for i in range(count)])


def swap(array, axis, x):
    return lax.ppermute(array, axis, [(i, i ^ x) for i in range(lax.axis_size(axis))])


def swapped(arrays, axis):
    return [swap(a, axis, k + 1) for k, a in reversed([*enumerate(arrays)])]


def from_near(array, b, k):
    count, wide = lax.axis_size("row"), lax.axis_size("col")
    pairs = [(r * wide + c, (r ^ b) * wide + (c + k) % wide) for r in range(count) for c in range(wide)]
    return lax.ppermute(array, ("row", "col"), pairs)


def shifted_all(array, axis):
    return [array] + [shift(array, axis, k) for k in range(1, lax.axis_size(axis))]


def per_device(
    homolog_ensemble,
    duplex_embedding,
    homolog_present_flags,
    resolved_position_flags,
    payload_weights,
    sigmoid_weights,
    averager_final_weights,
    first_operand_weights,
    second_operand_weights,
    duplex_logit_weights,
    tensor_product_weights,
    averager_upstream_adjoint,
    duplex_upstream_adjoint,
):
    g = Sizes(homolog_ensemble, duplex_embedding, duplex_logit_weights, first_operand_weights)
    shape = jax.ShapeDtypeStruct

    def call(kernel, name, args, outs, scratch=(), far=None, after=(), distant=False, us=1.0):
        size = sum(a.size * a.dtype.itemsize for a in args) + sum(
            math.prod(o.shape) * jnp.dtype(o.dtype).itemsize for o in outs
        )
        single = len(outs) == 1
        near = len(args) if far is None else far
        args = list(args[:near]) + [
            pltpu.with_memory_space_constraint(a, pltpu.HBM) for a in args[near:]
        ]

        if distant:
            after = [pltpu.with_memory_space_constraint(a, pltpu.HBM) for a in after]

        def body(*refs):
            kernel(g, *refs[: len(args)], *refs[len(args) + len(after) :])

        return pl.pallas_call(
            body,
            out_shape=outs[0] if single else tuple(outs),
            in_specs=[VMEM] * near + [FAR] * (len(args) - near) + [FAR if distant else VMEM] * len(after),
            out_specs=VMEM if single else (VMEM,) * len(outs),
            scratch_shapes=list(scratch),
            compiler_params=pltpu.CompilerParams(vmem_limit_bytes=40 * 1024 * 1024),
            cost_estimate=pl.CostEstimate(
                flops=int(us * 1.15e9), bytes_accessed=size, transcendentals=0
            ),
            name=name,
        )(*args, *after)

    heads = g.H * g.I
    rows = g.SP * g.I
    values = 2 * payload_weights.shape[1]
    pairs, tall = g.I * g.JC, heads // g.G
    xn, send, logits, near, x, e, wl, masks, w1, outer_weights, w2 = call(
        normalise_kernel,
        "normalise",
        (
            homolog_ensemble,
            duplex_embedding,
            duplex_upstream_adjoint.reshape(pairs, g.Z),
            resolved_position_flags.reshape(1, g.JC),
            duplex_logit_weights.T,
            homolog_present_flags,
            first_operand_weights.T,
            tensor_product_weights,
            second_operand_weights.T,
            homolog_present_flags.reshape(1, -1),
        ),
        [
            pltpu.VMEM((g.C, g.SP, g.I, 2 * g.M), BF16),
            pltpu.VMEM((rows + g.EXTRA * g.I, 2 * g.M), BF16),
            pltpu.VMEM((tall, g.G * g.JC), F32),
            pltpu.VMEM((pairs + 3 * tall, g.Z), BF16),
            pltpu.VMEM((g.SQ, g.I, g.M), BF16),
            pltpu.VMEM(duplex_embedding.shape, BF16),
            pltpu.VMEM((g.H, g.Z), BF16),
            pltpu.VMEM((g.C * g.SP + 8, 2 * g.M), F32),
            pltpu.VMEM((g.Q, g.M), BF16),
            pltpu.VMEM(tensor_product_weights.shape, BF16),
            pltpu.VMEM((g.Q, g.M), BF16),
        ],
        [
            pltpu.VMEM((1, g.JC), jnp.int32),
            pltpu.SMEM(homolog_present_flags.shape, jnp.int32),
            pltpu.VMEM((1, homolog_present_flags.shape[0]), jnp.int32),
            pltpu.VMEM(homolog_ensemble.shape, BF16),
            pltpu.VMEM(homolog_ensemble.shape, F32),
            pltpu.VMEM((g.I * g.H, LANES), F32),
            pltpu.SemaphoreType.DMA((10,)),
        ],
        far=0,
        us=2.0,
    )
    everyone = [send] + [swap(send, "row", k) for k in g.order]
    nears = shifted_all(near, "col")
    later = (
        sigmoid_weights,
        averager_final_weights.T,
        payload_weights,
    )
    g.carried = len(later)
    left, weights, left_weights, u, sg, wf, p = call(
        prepare_kernel,
        "prepare",
        (xn, w1, outer_weights, masks, averager_upstream_adjoint, *later),
        [
            pltpu.VMEM((g.C * g.I * g.S, g.Q), BF16),
            pltpu.VMEM((g.Q, g.Q, g.Z), BF16),
            pltpu.VMEM((g.I, g.Q * g.S, g.Z), BF16),
            pltpu.VMEM((g.SQ, g.I, g.M), BF16),
        ]
        + [pltpu.VMEM(a.shape, a.dtype) for a in later],
        [
            pltpu.VMEM(tensor_product_weights.shape, F32),
            pltpu.VMEM((2, rows, LANES), F32),
            pltpu.SemaphoreType.DMA,
            pltpu.SemaphoreType.DMA((len(later),)),
        ],
        far=4,
        us=0.01,
    )
    gate_weights, blended, gate_factor = call(
        gate_kernel,
        "gate",
        (xn, u, sg, wf),
        [
            pltpu.VMEM((2 * g.M, values), BF16),
            pltpu.VMEM((rows, values), BF16),
            pltpu.VMEM((rows, values), F32),
        ],
        after=nears[1:],
        us=0.01,
    )
    cotangents, second_term = call(
        right_kernel,
        "right",
        (*nears, left_weights, w2, masks),
        [pltpu.VMEM((g.I, g.N, g.Z), BF16), pltpu.VMEM((g.SP, g.N, 2 * g.M), F32)],
        [pltpu.VMEM((g.NT, g.Q * g.S, LANES), F32)],
        after=(gate_weights,),
        us=0.01,
    )
    share = g.Q * g.QL // g.D
    xall, products, *matrix_parts = call(
        outer_kernel,
        "outer",
        (*everyone, cotangents, left, w2, masks),
        [
            pltpu.VMEM((g.SP, g.N, 2 * g.M), BF16),
            pltpu.VMEM((g.QL, g.C, g.I, g.S, g.Z), BF16),
        ]
        + [pltpu.VMEM((share, g.Z), F32)] * g.D,
        [
            pltpu.VMEM((g.N, max(1, g.EXTRA) * LANES), BF16),
            pltpu.VMEM((g.NT, g.C * g.SP * 2 * g.QL, LANES), F32),
            pltpu.VMEM((g.QL * g.C * g.S, g.N), BF16),
            pltpu.VMEM((g.Q * g.QL, g.Z), F32),
        ],
        after=(second_term,),
        us=0.05,
    )
    matrix_parts = [matrix_parts[0]] + [
        shift(a, "depth", k + 1) for k, a in enumerate(matrix_parts[1:])
    ]
    soft, grad_soft, own, gate_grads, *sums = call(
        attend_kernel,
        "attend",
        (xall, logits, *nears[1:], blended, gate_factor, p, second_term),
        [
            pltpu.VMEM((heads, g.N), F32),
            pltpu.VMEM((heads, g.N), F32),
            pltpu.VMEM((rows, 2 * g.M), F32),
            pltpu.VMEM((rows, values), BF16),
        ]
        + [pltpu.VMEM((rows, 2 * g.M), BF16)] * (g.R - 1),
        [pltpu.VMEM((g.SP, g.N, 2 * g.M), F32)],
        us=3.0,
    )
    *sums, piece = call(
        pack_kernel,
        "pack",
        (*sums, *matrix_parts),
        [pltpu.VMEM((rows + share // 2, 2 * g.M), BF16)] * (g.R - 1)
        + [pltpu.VMEM((share // 2, g.Z), BF16)],
        [pltpu.VMEM((2, share // 2, g.Z), BF16)],
        us=0.2,
    )
    sums = swapped(sums, "row")
    own = call(
        own_kernel,
        "own",
        (xall, products, cotangents, weights, w1, w2, masks, own, gate_grads, gate_weights),
        [pltpu.VMEM((rows, 2 * g.M), F32)],
        [
            pltpu.VMEM((g.NT, g.SP * 2 * g.Q, LANES), F32),
            pltpu.VMEM((g.Q * g.S, g.N), BF16),
            pltpu.VMEM((max(1, g.C - 1), g.QL, g.I, g.S, g.Z), BF16),
            pltpu.VMEM((g.I * g.S, 2 * g.M), F32),
        ],
        after=(piece,),
        us=0.01,
    )
    wide = -(-3 * (g.JC + 1) // LANES) * LANES
    scores, *sends = call(
        score_kernel,
        "score",
        (soft, *shifted_all(grad_soft, "depth")),
        [pltpu.VMEM((heads, g.JC + 1), F32)] + [pltpu.VMEM((heads, wide), BF16)] * (g.C - 1),
        [pltpu.VMEM((g.D, heads, g.N), F32)],
        after=(own,),
        us=0.2,
    )
    arrived = [shift(a, "col", k + 1) for k, a in enumerate(sends)]
    piece = call(
        piece_kernel,
        "piece",
        (piece, *sums),
        [pltpu.VMEM((share // 2, g.Z), BF16)],
        [pltpu.VMEM((g.R, share // 2, g.Z), BF16)],
        after=(scores,),
        us=0.1,
    )
    pieces = [piece] + [from_near(piece, b, k) for b, k in g.spread[1:]]
    part = call(
        reduce_kernel,
        "reduce",
        (x, own, *sums),
        [pltpu.VMEM((rows, 2 * g.M), BF16)],
        after=(piece,),
    )
    pairwise_gradient = call(
        pair_kernel,
        "pair",
        (e, wl, soft, scores, *arrived),
        [shape(duplex_embedding.shape, BF16)],
        after=(part,),
        us=0.01,
    )
    matrix = call(
        across_kernel,
        "across",
        pieces,
        [pltpu.VMEM((g.C, 2, share // 2, g.Z), BF16)],
        after=(pairwise_gradient,),
        distant=True,
        us=0.1,
    ).reshape(g.C, g.Q // g.D, g.QL, g.Z)
    ensemble_derivative = call(
        unpack_kernel,
        "unpack",
        shifted_all(part, "col"),
        [pltpu.VMEM(homolog_ensemble.shape, BF16)],
        after=(matrix,),
    )
    ensemble_derivative, outer_matrix_gradient = call(
        finish_kernel,
        "finish",
        (ensemble_derivative, *shifted_all(matrix, "depth")),
        [shape(homolog_ensemble.shape, BF16), shape((g.Q, g.Q, g.Z), F32)],
    )
    outer_matrix_gradient = outer_matrix_gradient.reshape(tensor_product_weights.shape)
    return (ensemble_derivative, pairwise_gradient, outer_matrix_gradient)


def solution(mesh):
    in_specs = (
        P(("parts", "depth"), "row", None),
        P(("parts", "row"), "col", None),
        P("parts"),
        P(("parts", "col")),
        P(),
        P(),
        P(),
        P(),
        P(),
        P(),
        P(),
        P(("parts", "depth"), "row", None),
        P(("parts", "row"), "col", None),
    )
    out_specs = (
        P(("parts", "depth"), "row", None),
        P(("parts", "row"), "col", None),
        P("parts", None),
    )
    return jax.shard_map(
        per_device, mesh=mesh, in_specs=in_specs, out_specs=out_specs, check_vma=False
    )
```

```python
import functools
import math

import jax
import jax.numpy as jnp
from jax import lax
from jax.experimental import pallas as pl
from jax.experimental.pallas import tpu as pltpu
from jax.sharding import PartitionSpec as P

EPS = 1e-05
PENALTY = 10000.0
F32 = jnp.float32
BF16 = jnp.bfloat16
LANES = 128
NN = (((1,), (0,)), ((), ()))
NT = (((1,), (1,)), ((), ()))
VMEM = pl.BlockSpec(memory_space=pltpu.VMEM)
FAR = pl.BlockSpec(memory_space=pl.ANY)


def mm(a, b, dims=NN):
    return lax.dot_general(a, b, dims, preferred_element_type=F32)


def split_high_low(value):
    high = value.astype(BF16)
    return high, (value - high.astype(F32)).astype(BF16)


def iota(shape, dim):
    return lax.broadcasted_iota(jnp.int32, shape, dim)


def lanes_of(pieces):
    return pieces[0] if len(pieces) == 1 else jnp.concatenate(pieces, axis=-1)


def rows_of(pieces):
    return pieces[0] if len(pieces) == 1 else jnp.concatenate(pieces, axis=0)


def standardize(values):
    centred = values - jnp.mean(values, -1, keepdims=True)
    inverse = lax.rsqrt(jnp.mean(centred * centred, -1, keepdims=True) + EPS)
    return centred * inverse, inverse


def standardize_backward(values, upstream):
    scaled, inverse = standardize(values)
    mean_grad = jnp.mean(upstream, -1, keepdims=True)
    mean_cross = jnp.mean(upstream * scaled, -1, keepdims=True)
    return (upstream - mean_grad - scaled * mean_cross) * inverse


def on_diagonal(block, width):
    rows, lanes = block.shape
    same = iota(block.shape, 0) // (rows // 2) == iota(block.shape, 1) // width
    return jnp.where(same, block, jnp.zeros_like(block))


def split_three(value):
    high = value.astype(BF16)
    rest = value - high.astype(F32)
    middle = rest.astype(BF16)
    return [high, middle, (rest - middle.astype(F32)).astype(BF16)]


def three_lanes(value):
    rows, width = value.shape
    fill = -(3 * width) % LANES
    return lanes_of(split_three(value) + [jnp.zeros((rows, fill), BF16)] * (fill > 0))


def join_three(parts, width):
    wide = parts.astype(F32)
    return (wide[:, :width] + wide[:, width : 2 * width]) + wide[:, 2 * width : 3 * width]


def twice(weights):
    zero = jnp.zeros_like(weights)
    return rows_of([lanes_of([weights, zero]), lanes_of([zero, weights])])


def column_weights(g, w2):
    rows = iota((2 * g.QL, g.Q), 0) % g.QL + lax.axis_index("col") * g.QL
    pick = (iota((2 * g.QL, g.Q), 1) == rows).astype(BF16)
    return on_diagonal(mm(pick, lanes_of([w2, w2])), g.M).astype(BF16)


def normalise_kernel(
    g, x_hbm, e_hbm, dd_hbm, flag_hbm, wl_hbm, live_hbm, w1_hbm, t_hbm, w2_hbm, every_hbm, *refs
):
    xn_ref, send_ref, logit_ref, near_ref, x_ref, e_ref, wl_ref, mask_ref, w1_ref, t_ref, w2_ref, second_ref = refs[:12]
    flag_in, live_in, every_in, x_in, norm_ref, rows_ref, sem = refs[12:]
    col = lax.axis_index("col")
    pairs = g.I * g.JC
    copies = [
        pltpu.make_async_copy(a, b, sem.at[k])
        for k, (a, b) in enumerate(
            [
                (x_hbm, x_in),
                (e_hbm, e_ref),
                (wl_hbm, wl_ref),
                (flag_hbm, flag_in),
                (dd_hbm, near_ref.at[pl.ds(0, pairs)]),
                (live_hbm, live_in),
                (w1_hbm, w1_ref),
                (t_hbm, t_ref),
                (w2_hbm, w2_ref),
                (every_hbm, every_in),
            ]
        )
    ]
    for copy in copies:
        copy.start()
    for copy in (*copies[:4], copies[5], *copies[8:]):
        copy.wait()
    lane = iota((1, 2 * g.M), 1)
    groups = [lax.rem(col + m, g.C) for m in range(g.C)]
    for m, group in enumerate(groups):
        first = (lax.axis_index("depth") * g.C + group) * g.SQ
        for k in range(g.SP):
            if 2 * k + 1 < g.SQ:
                flags = jnp.where(lane < g.M, live_in[first + 2 * k], live_in[first + 2 * k + 1])
                flags = flags.astype(F32)
            else:
                flags = jnp.zeros((1, 2 * g.M), F32)
            mask_ref[m * g.SP + k : m * g.SP + k + 1, :] = flags
    count = jnp.sum(every_in[...].astype(F32), -1, keepdims=True)
    mask_ref[g.C * g.SP : g.C * g.SP + 1, :] = jnp.broadcast_to(1.0 / (0.001 + count), (1, 2 * g.M))
    norm_ref[...] = standardize(x_in[...].astype(F32))[0]
    x_ref[...] = x_in[pl.ds(col * g.SQ, g.SQ)]
    second = column_weights(g, w2_ref[...])
    second_ref[...] = second
    rows, blocks = g.SP * g.I, []
    for m, group in enumerate(groups):
        normed = g.fill(norm_ref[pl.ds(group * g.SQ, g.SQ)]).reshape(g.SP, 2, g.I, g.M)
        packed = jnp.concatenate([normed[:, 0], normed[:, 1]], axis=-1).astype(BF16)
        xn_ref[m] = packed
        if m == 0:
            send_ref[:rows, :] = packed.reshape(rows, 2 * g.M)
        else:
            masks = [mask_ref[m * g.SP + k : m * g.SP + k + 1, :] for k in range(g.SP)]
            live = rows_of([(packed[k].astype(F32) * masks[k]).astype(BF16) for k in range(g.SP)])
            factors = mm(live, second, NT)
            blocks += [factors[k * g.I : (k + 1) * g.I] for k in range(g.SP)]
    if blocks:
        wide = lanes_of(blocks)
        fill = -wide.shape[1] % LANES
        if fill:
            wide = lanes_of([wide, jnp.zeros((g.I, fill), F32)])
        for k in range(g.EXTRA):
            block = wide[:, k * LANES : (k + 1) * LANES]
            send_ref[rows + k * g.I : rows + (k + 1) * g.I, :] = block.astype(BF16)
    pair = standardize(e_ref[...].astype(F32).reshape(pairs, g.Z))[0].astype(BF16)
    penalty = (flag_in[...].astype(F32) - 1.0) * PENALTY
    weights = wl_ref[...]
    for i in range(g.I):
        rows_ref[i * g.H : (i + 1) * g.H, : g.JC] = (
            mm(weights, pair[i * g.JC : (i + 1) * g.JC], NT) + penalty
        )
    logits = rows_of([rows_ref[pl.ds(h, g.I, stride=g.H), :][:, : g.JC] for h in range(g.H)])
    tall = g.H * g.I // g.G
    packed = lanes_of([logits[k * tall : (k + 1) * tall] for k in range(g.G)])
    logit_ref[...] = packed
    near_ref[pairs:, :] = rows_of(split_three(packed))
    for copy in (copies[4], *copies[6:8]):
        copy.wait()


def prepare_kernel(g, xn_ref, w1_ref, t_ref, mask_ref, u_hbm, *refs):
    refs = list(refs)
    count = g.carried
    sources, refs = refs[:count], refs[count:]
    left_ref, ts_ref, lt_ref, u_ref, refs = refs[0], refs[1], refs[2], refs[3], refs[4:]
    targets, (wide_ref, half_ref, first_sem, later_sem) = refs[:count], refs[count:]
    first = lax.axis_index("col") * g.SQ
    copies = [pltpu.make_async_copy(u_hbm.at[pl.ds(first, g.SQ)], u_ref, first_sem)]
    copies += [
        pltpu.make_async_copy(a, b, later_sem.at[k])
        for k, (a, b) in enumerate(zip(sources, targets, strict=True))
    ]
    for copy in copies:
        copy.start()
    w1 = rows_of([w1_ref[...], jnp.zeros((LANES - g.Q, g.M), BF16)])
    zero = jnp.zeros_like(w1)
    for m in range(g.C):
        masks = [mask_ref[m * g.SP + k : m * g.SP + k + 1, :] for k in range(g.SP)]
        live_xn = rows_of(
            [(xn_ref[m, k].astype(F32) * masks[k]).astype(BF16) for k in range(g.SP)]
        )
        half_ref[0] = mm(live_xn, lanes_of([w1, zero]), NT)
        half_ref[1] = mm(live_xn, lanes_of([zero, w1]), NT)
        for i in range(g.I):
            halves = [half_ref[half, pl.ds(i, g.SP, stride=g.I), :] for half in range(2)]
            first = (m * g.I + i) * g.S
            left_ref[first : first + g.S, :] = rows_of(halves)[:, : g.Q].astype(BF16)
    wide_ref[...] = t_ref[...].astype(F32)
    for q in range(g.Q):
        ts_ref[q] = wide_ref[pl.ds(q, g.Q, stride=g.Q), :].astype(BF16)
    left = left_ref[: g.I * g.S, :]
    for q in range(0, g.Q, 2):
        product = mm(left, lanes_of([ts_ref[q], ts_ref[q + 1]]))
        for k in range(2):
            block = product[:, k * g.Z : (k + 1) * g.Z].reshape(g.I, g.S, g.Z)
            lt_ref[:, (q + k) * g.S : (q + k + 1) * g.S, :] = block.astype(BF16)
    for copy in copies:
        copy.wait()


def gate_kernel(g, xn_ref, u_ref, sg_ref, wf_ref, p_ref, logit_ref, *refs):
    near_refs, refs = refs[: g.C - 1], refs[g.C - 1 :]
    gate_weight_ref, gm_ref, gate_ref, value_weight_ref, soft_ref, low_ref, low_t_ref = refs
    value_weight_ref[...] = twice(p_ref[...])
    tall, blocks = logit_ref.shape[0], [logit_ref[...]]
    for k in range(1, g.C):
        parts = near_refs[g.C - k - 1][g.I * g.JC :, :].astype(F32)
        blocks.append((parts[:tall] + parts[tall : 2 * tall]) + parts[2 * tall :])
    logits = lanes_of(
        [rows_of([b[:, k * g.JC : (k + 1) * g.JC] for k in range(g.G)]) for b in blocks]
    )
    shifted = jnp.exp(logits - jnp.max(logits, -1, keepdims=True))
    soft = shifted / jnp.sum(shifted, -1, keepdims=True)
    soft_ref[...] = soft
    low = soft.astype(BF16)
    eye = (iota((g.N, g.N), 0) == iota((g.N, g.N), 1)).astype(BF16)
    low_t = mm(eye, low, NT).astype(BF16)
    low_ref[...] = low
    low_t_ref[...] = lanes_of([low_t, low_t])
    rows = g.SP * g.I
    xn = xn_ref[0]
    gate_weights = twice(sg_ref[...])
    gate_weight_ref[...] = gate_weights
    gates = jax.nn.sigmoid(mm(xn.reshape(rows, 2 * g.M), gate_weights))
    u = g.fill(u_ref[...]).reshape(g.SP, 2, g.I, g.M)
    packed_u = jnp.concatenate([u[:, 0], u[:, 1]], axis=-1).reshape(rows, 2 * g.M)
    gated = mm(packed_u, twice(wf_ref[...]))
    blended = gated * gates
    gm_ref[...] = blended.astype(BF16)
    gate_ref[...] = blended * (1.0 - gates)


def right_kernel(g, *refs):
    near_refs, (lt_ref, w2_ref, mask_ref, d_ref, go_ref, rg_ref) = refs[: g.C], refs[g.C :]
    for k in range(g.C):
        spot = (g.C - k) % g.C
        block = near_refs[k][: g.I * g.JC, :].reshape(g.I, g.JC, g.Z)
        d_ref[:, spot * g.JC : (spot + 1) * g.JC, :] = block
    masks = [mask_ref[k : k + 1, :] for k in range(g.SP)]
    scale = mask_ref[g.C * g.SP : g.C * g.SP + 1, :]
    right_grad = jnp.zeros((g.Q * g.S, g.N), F32)
    for i in range(0, g.I, 2):
        right_grad = right_grad + mm(
            lanes_of([lt_ref[i], lt_ref[i + 1]]), lanes_of([d_ref[i], d_ref[i + 1]]), NT
        )
    for t in range(g.NT):
        lanes = min(LANES, g.N - t * LANES)
        piece = right_grad[:, t * LANES : t * LANES + lanes]
        if lanes < LANES:
            piece = lanes_of([piece, jnp.zeros((g.Q * g.S, LANES - lanes), F32)])
        rg_ref[t] = piece
    deep = 2 * g.Q
    group = min(g.SP, LANES // deep)
    which = iota((group * deep, g.Q), 0)
    pick = (iota((group * deep, g.Q), 1) == which % deep // 2).astype(BF16)
    w2 = w2_ref[...]
    base = mm(pick, lanes_of([w2, w2]))
    which = iota(base.shape, 0)
    base = jnp.where(which % 2 == iota(base.shape, 1) // g.M, base, 0.0)
    weights = lanes_of([jnp.where(which // deep == k, base, 0.0) for k in range(group)]).astype(BF16)
    for k in range(0, g.SP, group):
        for t in range(g.NT):
            lanes = min(LANES, g.N - t * LANES)
            tall = rows_of(
                [rg_ref[t, pl.ds(k + m, deep, stride=g.SP), :] for m in range(group)]
            )
            tall = (tall * scale).T[:lanes]
            high, low = split_high_low(tall)
            part = mm(high, weights) + mm(low, weights)
            for m in range(group):
                go_ref[k + m, t * LANES : t * LANES + lanes, :] = (
                    part[:, m * 2 * g.M : (m + 1) * 2 * g.M] * masks[k + m]
                )


def outer_kernel(g, *refs):
    refs = list(refs)
    x_refs, refs = refs[: g.R], refs[g.R :]
    d_ref, left_ref, second_ref, mask_ref, xall_ref, ds_ref, *refs = refs
    w_refs, (others_ref, spread_ref, rt_ref, all_ref) = refs[: g.D], refs[g.D :]
    row, col, depth = (lax.axis_index(a) for a in ("row", "col", "depth"))
    rows, deep = g.SP * g.I, 2 * g.QL
    for k, ref in zip((0, *g.order), x_refs, strict=True):
        place = g.place(jnp.bitwise_xor(row, k), col)
        xall_ref[:, pl.ds(place, g.I), :] = ref[:rows, :].reshape(g.SP, g.I, 2 * g.M)
        for m in range(g.EXTRA):
            block = ref[rows + m * g.I : rows + (m + 1) * g.I, :]
            others_ref[pl.ds(place, g.I), m * LANES : (m + 1) * LANES] = block
    second = second_ref[...]
    parts = [
        mm(second, (xall_ref[k].astype(F32) * mask_ref[k : k + 1, :]).astype(BF16), NT)
        for k in range(g.SP)
    ]
    if g.EXTRA:
        lanes = g.EXTRA * LANES
        eye = (iota((lanes, lanes), 0) == iota((lanes, lanes), 1)).astype(BF16)
        parts.append(mm(eye, others_ref[...], NT)[: (g.C - 1) * g.SP * deep])
    first = 0
    for part in parts:
        for t in range(g.NT):
            lanes = min(LANES, g.N - t * LANES)
            piece = part[:, t * LANES : t * LANES + lanes]
            spread_ref[t, first : first + part.shape[0], :lanes] = piece
        first += part.shape[0]
    for q in range(g.QL):
        for m in range(g.C):
            spot = (q * g.C + m) * g.S
            for t in range(g.NT):
                lanes = min(LANES, g.N - t * LANES)
                halves = [
                    spread_ref[t, pl.ds(m * g.SP * deep + half * g.QL + q, g.SP, stride=deep), :]
                    for half in range(2)
                ]
                rt_ref[spot : spot + g.S, t * LANES : t * LANES + lanes] = rows_of(halves)[
                    :, :lanes
                ].astype(BF16)
    rt = rt_ref[...]
    for i in range(0, g.I, 2):
        product = mm(rt, lanes_of([d_ref[i], d_ref[i + 1]]))
        for k in range(2):
            block = product[:, k * g.Z : (k + 1) * g.Z]
            ds_ref[:, :, i + k] = block.reshape(g.QL, g.C, g.S, g.Z).astype(BF16)
    eye = (iota((g.Q, g.Q), 0) == iota((g.Q, g.Q), 1)).astype(BF16)
    left_t = mm(eye, left_ref[...], NT).astype(BF16)
    scale = mask_ref[g.C * g.SP : g.C * g.SP + 1, :]
    entries = g.C * g.S * g.I
    for q in range(0, g.QL, 2):
        both = lanes_of([ds_ref[q].reshape(entries, g.Z), ds_ref[q + 1].reshape(entries, g.Z)])
        part = mm(left_t, both)
        all_ref[pl.ds(q, g.Q, stride=g.QL), :] = part[:, : g.Z] * scale
        all_ref[pl.ds(q + 1, g.Q, stride=g.QL), :] = part[:, g.Z :] * scale
    share = g.Q * g.QL // g.D
    for k in range(g.D):
        first = pl.multiple_of(lax.rem(depth + k, g.D) * share, share)
        w_refs[k][...] = all_ref[pl.ds(first, share), :]


def own_kernel(
    g, xall_ref, near_ref, d_ref, ts_ref, w1_ref, w2_ref, mask_ref, part_ref, gg_ref, gate_weight_ref, own_ref,
    spread_ref, rt_ref, ds_ref, turn_ref,
):
    scale = mask_ref[g.C * g.SP : g.C * g.SP + 1, :]
    masks = [mask_ref[k : k + 1, :] for k in range(g.SP)]
    w2 = w2_ref[...]
    doubled = lanes_of([w2, w2])
    second = on_diagonal(rows_of([doubled, doubled]), g.M)
    for k in range(g.SP):
        live_x = (xall_ref[k].astype(F32) * masks[k]).astype(BF16)
        part = mm(second, live_x, NT)
        for t in range(g.NT):
            lanes = min(LANES, g.N - t * LANES)
            spread_ref[t, k * 2 * g.Q : (k + 1) * 2 * g.Q, :lanes] = part[
                :, t * LANES : t * LANES + lanes
            ]
    for q in range(g.Q):
        for t in range(g.NT):
            lanes = min(LANES, g.N - t * LANES)
            halves = [
                spread_ref[t, pl.ds(half * g.Q + q, g.SP, stride=2 * g.Q), :] for half in range(2)
            ]
            rt_ref[q * g.S : (q + 1) * g.S, t * LANES : t * LANES + lanes] = rows_of(halves)[
                :, :lanes
            ].astype(BF16)
    col = lax.axis_index("col")
    entries = g.S * g.I
    left_grad = jnp.zeros((entries, g.Q), F32)
    for m in range(g.C):
        first = lax.rem(col + m, g.C) * g.QL
        if m > 0:
            rt = rt_ref[pl.ds(pl.multiple_of(first * g.S, g.QL * g.S), g.QL * g.S), :]
            for i in range(0, g.I, 2):
                product = mm(rt, lanes_of([d_ref[i], d_ref[i + 1]]))
                for k in range(2):
                    block = product[:, k * g.Z : (k + 1) * g.Z]
                    ds_ref[m - 1, :, i + k] = block.reshape(g.QL, g.S, g.Z).astype(BF16)
        for q in range(0, g.QL, 2):
            pair = [near_ref[q + k, 0] if m == 0 else ds_ref[m - 1, q + k] for k in range(2)]
            both = lanes_of([part.reshape(entries, g.Z) for part in pair])
            left_grad = left_grad + mm(both, lanes_of([ts_ref[first + q], ts_ref[first + q + 1]]), NT)
    w1 = w1_ref[...]
    first_term = jnp.zeros((entries, 2 * g.M), F32)
    for piece in split_high_low(left_grad * scale[:, : g.Q]):
        first_term = first_term + mm(piece, lanes_of([w1, w1]))
    turn_ref[...] = first_term
    gate_term = mm(gg_ref[...], gate_weight_ref[...], NT)
    lane = iota((1, 2 * g.M), 1)
    for k in range(g.SP):
        rows = slice(k * g.I, (k + 1) * g.I)
        halves = [turn_ref[pl.ds(half * g.SP + k, g.I, stride=g.S), :] for half in range(2)]
        term = jnp.where(lane < g.M, halves[0], halves[1]) * mask_ref[k : k + 1, :]
        own_ref[rows, :] = part_ref[rows, :] + gate_term[rows] + term


def attend_kernel(g, *refs):
    xall_ref, low_ref, low_t_ref, gm_ref, gate_ref, value_weight_ref, go_ref, *refs = refs
    gs_ref, own_ref, gg_ref, *refs = refs
    send_refs, (total_ref,) = refs[: g.R - 1], refs[g.R - 1 :]
    row, col = lax.axis_index("row"), lax.axis_index("col")
    value_weights, low, low_t = value_weight_ref[...], low_ref[...], low_t_ref[...]
    values = mm(xall_ref[...].reshape(g.SP * g.N, 2 * g.M), value_weights).astype(BF16)
    half = value_weights.shape[1] // 2
    width = half // g.H
    group = LANES // width
    count = g.H // group
    tall = group * g.I
    head = iota((1, 2 * LANES), 1) % LANES // width

    def lanes(array, k):
        return lanes_of([array[:, s * half + k * LANES : s * half + (k + 1) * LANES] for s in range(2)])

    group_weights = [lanes(value_weights, k) for k in range(count)]
    grad_soft = [jnp.zeros((tall, g.N), F32) for _ in range(count)]
    for k in range(g.SP):
        v = values[k * g.N : (k + 1) * g.N]
        rows = slice(k * g.I, (k + 1) * g.I)
        blended, factor = gm_ref[rows, :], gate_ref[rows, :]
        projected = []
        for m in range(count):
            vm = lanes(v, m)
            crossed = mm(low[m * tall : (m + 1) * tall], vm)
            mixed = crossed[: g.I]
            for h in range(1, group):
                mixed = jnp.where(head == h, crossed[h * g.I : (h + 1) * g.I], mixed)
            gate_grad = (lanes(factor, m) * mixed).astype(BF16)
            for s in range(2):
                first = s * half + m * LANES
                gg_ref[rows, first : first + LANES] = gate_grad[:, s * LANES : (s + 1) * LANES]
            bm = lanes(blended, m)
            by_head = rows_of([jnp.where(head == h, bm, jnp.zeros_like(bm)) for h in range(group)])
            grad_soft[m] = grad_soft[m] + mm(by_head, vm, NT)
            projected.append(mm(by_head, group_weights[m], NT))
        total_ref[k] = go_ref[k] + mm(low_t, rows_of([*split_high_low(rows_of(projected))]))
    gs_ref[...] = rows_of(grad_soft)
    own = total_ref[:, pl.ds(g.place(row, col), g.I), :]
    own_ref[...] = own.reshape(g.SP * g.I, 2 * g.M)
    for x in range(1, g.R):
        block = total_ref[:, pl.ds(g.place(jnp.bitwise_xor(row, x), col), g.I), :]
        send_refs[x - 1][...] = block.reshape(g.SP * g.I, 2 * g.M).astype(BF16)


def pack_kernel(g, *refs):
    refs = list(refs)
    sums, refs = refs[: g.R - 1], refs[g.R - 1 :]
    parts, refs = refs[: g.D], refs[g.D :]
    outs, (own_ref, halves_ref) = refs[: g.R - 1], refs[g.R - 1 :]
    row = lax.axis_index("row")
    total = parts[0][...]
    for ref in parts[1:]:
        total = total + ref[...]
    half, rows = own_ref.shape[0], g.SP * g.I
    for k in range(2):
        halves_ref[k] = total[k * half : (k + 1) * half].astype(BF16)
    own_ref[...] = halves_ref[lax.rem(row, 2)]
    for x in range(1, g.R):
        outs[x - 1][:rows, :] = sums[x - 1][...]
        outs[x - 1][rows:, :] = halves_ref[lax.rem(jnp.bitwise_xor(row, x), 2)]


def piece_kernel(g, own_ref, *refs):
    out_ref, order_ref = refs[-2:]
    row, rows = lax.axis_index("row"), g.SP * g.I
    order_ref[row] = own_ref[...]
    for k in range(1, g.R):
        order_ref[jnp.bitwise_xor(row, g.R - k)] = refs[k - 1][rows:, :]
    total = order_ref[0].astype(F32)
    for r in range(1, g.R):
        total = total + order_ref[r].astype(F32)
    out_ref[...] = total.astype(BF16)


def score_kernel(g, soft_ref, *refs):
    parts, refs = refs[: g.D], refs[g.D :]
    own_ref, out_refs, order_ref = refs[0], refs[1 : g.C], refs[g.C]
    depth = lax.axis_index("depth")
    for k in range(g.D):
        order_ref[lax.rem(depth - k + g.D, g.D)] = parts[k][...]
    grad_soft = order_ref[0]
    for k in range(1, g.D):
        grad_soft = grad_soft + order_ref[k]
    inner = jnp.sum(soft_ref[...] * grad_soft, -1, keepdims=True)
    for k in range(g.C):
        block = lanes_of([grad_soft[:, k * g.JC : (k + 1) * g.JC], inner])
        if k == 0:
            own_ref[...] = block
        else:
            out_refs[k - 1][...] = three_lanes(block)


def pair_kernel(g, e_ref, wl_ref, soft_ref, own_ref, *refs):
    got, pair_ref = refs[: g.C - 1], refs[g.C - 1]
    heads = g.H * g.I
    total = own_ref[...]
    for ref in got:
        total = total + join_three(ref[...], g.JC + 1)
    grad = soft_ref[:, : g.JC] * (total[:, : g.JC] - total[:, g.JC :])
    if g.JC < LANES:
        grad = lanes_of([grad, jnp.zeros((heads, LANES - g.JC), F32)])
    high, low = split_high_low(grad.T[: g.JC])
    grads = lanes_of([high, low])
    pick = (iota((heads, g.H), 0) // g.I == iota((heads, g.H), 1)).astype(BF16)
    base = mm(pick, wl_ref[...]).astype(BF16)
    token = iota((heads, 1), 0) % g.I
    for i in range(0, g.I, 2):
        weights = lanes_of(
            [jnp.where(token == i + k, base, jnp.zeros_like(base)) for k in range(2)]
        )
        upstream = mm(grads, rows_of([weights, weights]))
        for k in range(2):
            pair_ref[i + k] = standardize_backward(
                e_ref[i + k].astype(F32), upstream[:, k * g.Z : (k + 1) * g.Z]
            ).astype(BF16)


def reduce_kernel(g, x_ref, own_ref, *refs):
    got, out_ref = refs[:-1], refs[-1]
    rows = g.SP * g.I
    total = own_ref[...]
    for ref in got:
        total = total + ref[:rows, :].astype(F32)
    total = total.reshape(g.SP, 1, g.I, 2 * g.M)
    upstream = jnp.concatenate([total[..., : g.M], total[..., g.M :]], axis=1)
    upstream = upstream.reshape(g.S, g.I, g.M)[: g.SQ]
    msa = g.fill(standardize_backward(x_ref[...].astype(F32), upstream))
    msa = msa.reshape(g.SP, 2, g.I, g.M)
    msa = jnp.concatenate([msa[:, 0], msa[:, 1]], axis=-1).astype(BF16)
    out_ref[...] = msa.reshape(rows, 2 * g.M)


def across_kernel(g, *refs):
    out_ref = refs[-1]
    row, col = lax.axis_index("row"), lax.axis_index("col")
    for ref, (b, k) in zip(refs[:-1], g.spread, strict=True):
        half = lax.rem(jnp.bitwise_xor(row, b), 2)
        out_ref[lax.rem(col - k + g.C, g.C), half] = ref[...]


def unpack_kernel(g, *refs):
    parts, msa_ref = refs[: g.C], refs[g.C]
    col = lax.axis_index("col")
    for k, ref in enumerate(parts):
        msa = ref[...].astype(F32).reshape(g.SP, 1, g.I, 2 * g.M)
        msa = jnp.concatenate([msa[..., : g.M], msa[..., g.M :]], axis=1)
        msa = msa.reshape(g.S, g.I, g.M)[: g.SQ].astype(BF16)
        msa_ref[pl.ds(lax.rem(col - k + g.C, g.C) * g.SQ, g.SQ)] = msa


def finish_kernel(g, msa_ref, *refs):
    parts, (out_ref, matrix_ref) = refs[: g.D], refs[g.D :]
    depth = lax.axis_index("depth")
    out_ref[...] = msa_ref[...]
    share = g.Q // g.D
    for k in range(g.D):
        first = lax.rem(depth - k + g.D, g.D) * share
        for c in range(g.C):
            block = parts[k][c].astype(F32)
            matrix_ref[pl.ds(first, share), c * g.QL : (c + 1) * g.QL, :] = block


class Sizes:
    def __init__(self, x, e, wl, w1):
        self.R, self.C, self.D = (lax.axis_size(a) for a in ("row", "col", "depth"))
        self.I, self.M = x.shape[1:]
        self.JC, self.Z = e.shape[1:]
        self.H, self.Q = wl.shape[1], w1.shape[1]
        self.QL = self.Q // self.C
        self.SQ = x.shape[0] // self.C
        self.S = -(-self.SQ // 16) * 16
        self.SP, self.N = self.S // 2, self.R * self.I
        self.F = self.R // self.C
        self.NT = -(-self.N // LANES)
        self.G = max(1, LANES // self.JC)
        self.EXTRA = -(-(self.C - 1) * self.S * self.QL // LANES)
        self.carried = 0
        self.spread = [(b, k) for k in range(self.C) for b in range(2)]
        self.order = [*range(1, self.R // 2), *range(self.R // 2 + 1, self.R), self.R // 2]

    def fill(self, rows):
        if self.SQ == self.S:
            return rows
        return rows_of([rows, jnp.zeros((self.S - self.SQ, *rows.shape[1:]), rows.dtype)])

    def place(self, row, col):
        turn = lax.rem(row // self.F - col + self.C, self.C)
        return pl.multiple_of((turn * self.F + lax.rem(row, self.F)) * self.I, self.I)


def shift(array, axis, k):
    count = lax.axis_size(axis)
    return lax.ppermute(array, axis, [(i, (i + k) % count) for i in range(count)])


def swap(array, axis, x):
    return lax.ppermute(array, axis, [(i, i ^ x) for i in range(lax.axis_size(axis))])


def swapped(arrays, axis):
    return [swap(a, axis, k + 1) for k, a in reversed([*enumerate(arrays)])]


def from_near(array, b, k):
    count, wide = lax.axis_size("row"), lax.axis_size("col")
    pairs = [(r * wide + c, (r ^ b) * wide + (c + k) % wide) for r in range(count) for c in range(wide)]
    return lax.ppermute(array, ("row", "col"), pairs)


def shifted_all(array, axis):
    return [array] + [shift(array, axis, k) for k in range(1, lax.axis_size(axis))]


def per_device(
    homolog_ensemble,
    duplex_embedding,
    homolog_present_flags,
    resolved_position_flags,
    payload_weights,
    sigmoid_weights,
    averager_final_weights,
    first_operand_weights,
    second_operand_weights,
    duplex_logit_weights,
    tensor_product_weights,
    averager_upstream_adjoint,
    duplex_upstream_adjoint,
):
    g = Sizes(homolog_ensemble, duplex_embedding, duplex_logit_weights, first_operand_weights)
    shape = jax.ShapeDtypeStruct

    def call(kernel, name, args, outs, scratch=(), far=None, after=(), distant=False, us=1.0):
        size = sum(a.size * a.dtype.itemsize for a in args) + sum(
            math.prod(o.shape) * jnp.dtype(o.dtype).itemsize for o in outs
        )
        single = len(outs) == 1
        near = len(args) if far is None else far
        args = list(args[:near]) + [
            pltpu.with_memory_space_constraint(a, pltpu.HBM) for a in args[near:]
        ]

        if distant:
            after = [pltpu.with_memory_space_constraint(a, pltpu.HBM) for a in after]

        def body(*refs):
            kernel(g, *refs[: len(args)], *refs[len(args) + len(after) :])

        return pl.pallas_call(
            body,
            out_shape=outs[0] if single else tuple(outs),
            in_specs=[VMEM] * near + [FAR] * (len(args) - near) + [FAR if distant else VMEM] * len(after),
            out_specs=VMEM if single else (VMEM,) * len(outs),
            scratch_shapes=list(scratch),
            compiler_params=pltpu.CompilerParams(vmem_limit_bytes=40 * 1024 * 1024),
            cost_estimate=pl.CostEstimate(
                flops=int(us * 1.15e9), bytes_accessed=size, transcendentals=0
            ),
            name=name,
        )(*args, *after)

    heads = g.H * g.I
    rows = g.SP * g.I
    values = 2 * payload_weights.shape[1]
    pairs, tall = g.I * g.JC, heads // g.G
    xn, send, logits, near, x, e, wl, masks, w1, outer_weights, w2, second = call(
        normalise_kernel,
        "normalise",
        (
            homolog_ensemble,
            duplex_embedding,
            duplex_upstream_adjoint.reshape(pairs, g.Z),
            resolved_position_flags.reshape(1, g.JC),
            duplex_logit_weights.T,
            homolog_present_flags,
            first_operand_weights.T,
            tensor_product_weights,
            second_operand_weights.T,
            homolog_present_flags.reshape(1, -1),
        ),
        [
            pltpu.VMEM((g.C, g.SP, g.I, 2 * g.M), BF16),
            pltpu.VMEM((rows + g.EXTRA * g.I, 2 * g.M), BF16),
            pltpu.VMEM((tall, g.G * g.JC), F32),
            pltpu.VMEM((pairs + 3 * tall, g.Z), BF16),
            pltpu.VMEM((g.SQ, g.I, g.M), BF16),
            pltpu.VMEM(duplex_embedding.shape, BF16),
            pltpu.VMEM((g.H, g.Z), BF16),
            pltpu.VMEM((g.C * g.SP + 8, 2 * g.M), F32),
            pltpu.VMEM((g.Q, g.M), BF16),
            pltpu.VMEM(tensor_product_weights.shape, BF16),
            pltpu.VMEM((g.Q, g.M), BF16),
            pltpu.VMEM((2 * g.QL, 2 * g.M), BF16),
        ],
        [
            pltpu.VMEM((1, g.JC), jnp.int32),
            pltpu.SMEM(homolog_present_flags.shape, jnp.int32),
            pltpu.VMEM((1, homolog_present_flags.shape[0]), jnp.int32),
            pltpu.VMEM(homolog_ensemble.shape, BF16),
            pltpu.VMEM(homolog_ensemble.shape, F32),
            pltpu.VMEM((g.I * g.H, LANES), F32),
            pltpu.SemaphoreType.DMA((10,)),
        ],
        far=0,
        us=2.0,
    )
    everyone = [send] + [swap(send, "row", k) for k in g.order]
    nears = shifted_all(near, "col")
    later = (
        sigmoid_weights,
        averager_final_weights.T,
        payload_weights,
    )
    g.carried = len(later)
    left, weights, left_weights, u, sg, wf, p = call(
        prepare_kernel,
        "prepare",
        (xn, w1, outer_weights, masks, averager_upstream_adjoint, *later),
        [
            pltpu.VMEM((g.C * g.I * g.S, g.Q), BF16),
            pltpu.VMEM((g.Q, g.Q, g.Z), BF16),
            pltpu.VMEM((g.I, g.Q * g.S, g.Z), BF16),
            pltpu.VMEM((g.SQ, g.I, g.M), BF16),
        ]
        + [pltpu.VMEM(a.shape, a.dtype) for a in later],
        [
            pltpu.VMEM(tensor_product_weights.shape, F32),
            pltpu.VMEM((2, rows, LANES), F32),
            pltpu.SemaphoreType.DMA,
            pltpu.SemaphoreType.DMA((len(later),)),
        ],
        far=4,
        us=0.01,
    )
    gate_weights, blended, gate_factor, value_weights, soft, low, low_t = call(
        gate_kernel,
        "gate",
        (xn, u, sg, wf, p, logits, *nears[1:]),
        [
            pltpu.VMEM((2 * g.M, values), BF16),
            pltpu.VMEM((rows, values), BF16),
            pltpu.VMEM((rows, values), F32),
            pltpu.VMEM((2 * g.M, values), BF16),
            pltpu.VMEM((heads, g.N), F32),
            pltpu.VMEM((heads, g.N), BF16),
            pltpu.VMEM((g.N, 2 * heads), BF16),
        ],
        us=0.01,
    )
    cotangents, second_term = call(
        right_kernel,
        "right",
        (*nears, left_weights, w2, masks),
        [pltpu.VMEM((g.I, g.N, g.Z), BF16), pltpu.VMEM((g.SP, g.N, 2 * g.M), F32)],
        [pltpu.VMEM((g.NT, g.Q * g.S, LANES), F32)],
        after=(gate_weights,),
        us=0.01,
    )
    share = g.Q * g.QL // g.D
    xall, products, *matrix_parts = call(
        outer_kernel,
        "outer",
        (*everyone, cotangents, left, second, masks),
        [
            pltpu.VMEM((g.SP, g.N, 2 * g.M), BF16),
            pltpu.VMEM((g.QL, g.C, g.I, g.S, g.Z), BF16),
        ]
        + [pltpu.VMEM((share, g.Z), F32)] * g.D,
        [
            pltpu.VMEM((g.N, max(1, g.EXTRA) * LANES), BF16),
            pltpu.VMEM((g.NT, g.C * g.SP * 2 * g.QL, LANES), F32),
            pltpu.VMEM((g.QL * g.C * g.S, g.N), BF16),
            pltpu.VMEM((g.Q * g.QL, g.Z), F32),
        ],
        after=(second_term,),
        us=0.05,
    )
    matrix_parts = [matrix_parts[0]] + [
        shift(a, "depth", k + 1) for k, a in enumerate(matrix_parts[1:])
    ]
    grad_soft, own, gate_grads, *sums = call(
        attend_kernel,
        "attend",
        (xall, low, low_t, blended, gate_factor, value_weights, second_term),
        [
            pltpu.VMEM((heads, g.N), F32),
            pltpu.VMEM((rows, 2 * g.M), F32),
            pltpu.VMEM((rows, values), BF16),
        ]
        + [pltpu.VMEM((rows, 2 * g.M), BF16)] * (g.R - 1),
        [pltpu.VMEM((g.SP, g.N, 2 * g.M), F32)],
        us=3.0,
    )
    *sums, piece = call(
        pack_kernel,
        "pack",
        (*sums, *matrix_parts),
        [pltpu.VMEM((rows + share // 2, 2 * g.M), BF16)] * (g.R - 1)
        + [pltpu.VMEM((share // 2, g.Z), BF16)],
        [pltpu.VMEM((2, share // 2, g.Z), BF16)],
        us=0.2,
    )
    sums = swapped(sums, "row")
    own = call(
        own_kernel,
        "own",
        (xall, products, cotangents, weights, w1, w2, masks, own, gate_grads, gate_weights),
        [pltpu.VMEM((rows, 2 * g.M), F32)],
        [
            pltpu.VMEM((g.NT, g.SP * 2 * g.Q, LANES), F32),
            pltpu.VMEM((g.Q * g.S, g.N), BF16),
            pltpu.VMEM((max(1, g.C - 1), g.QL, g.I, g.S, g.Z), BF16),
            pltpu.VMEM((g.I * g.S, 2 * g.M), F32),
        ],
        after=(piece,),
        us=0.01,
    )
    wide = -(-3 * (g.JC + 1) // LANES) * LANES
    scores, *sends = call(
        score_kernel,
        "score",
        (soft, *shifted_all(grad_soft, "depth")),
        [pltpu.VMEM((heads, g.JC + 1), F32)] + [pltpu.VMEM((heads, wide), BF16)] * (g.C - 1),
        [pltpu.VMEM((g.D, heads, g.N), F32)],
        after=(own,),
        us=0.2,
    )
    arrived = [shift(a, "col", k + 1) for k, a in enumerate(sends)]
    piece = call(
        piece_kernel,
        "piece",
        (piece, *sums),
        [pltpu.VMEM((share // 2, g.Z), BF16)],
        [pltpu.VMEM((g.R, share // 2, g.Z), BF16)],
        after=(scores,),
        us=0.1,
    )
    pieces = [piece] + [from_near(piece, b, k) for b, k in g.spread[1:]]
    part = call(
        reduce_kernel,
        "reduce",
        (x, own, *sums),
        [pltpu.VMEM((rows, 2 * g.M), BF16)],
        after=(piece,),
    )
    pairwise_gradient = call(
        pair_kernel,
        "pair",
        (e, wl, soft, scores, *arrived),
        [shape(duplex_embedding.shape, BF16)],
        after=(part,),
        us=0.01,
    )
    matrix = call(
        across_kernel,
        "across",
        pieces,
        [pltpu.VMEM((g.C, 2, share // 2, g.Z), BF16)],
        after=(pairwise_gradient,),
        distant=True,
        us=0.1,
    ).reshape(g.C, g.Q // g.D, g.QL, g.Z)
    ensemble_derivative = call(
        unpack_kernel,
        "unpack",
        shifted_all(part, "col"),
        [pltpu.VMEM(homolog_ensemble.shape, BF16)],
        after=(matrix,),
    )
    ensemble_derivative, outer_matrix_gradient = call(
        finish_kernel,
        "finish",
        (ensemble_derivative, *shifted_all(matrix, "depth")),
        [shape(homolog_ensemble.shape, BF16), shape((g.Q, g.Q, g.Z), F32)],
    )
    outer_matrix_gradient = outer_matrix_gradient.reshape(tensor_product_weights.shape)
    return (ensemble_derivative, pairwise_gradient, outer_matrix_gradient)


def solution(mesh):
    in_specs = (
        P(("parts", "depth"), "row", None),
        P(("parts", "row"), "col", None),
        P("parts"),
        P(("parts", "col")),
        P(),
        P(),
        P(),
        P(),
        P(),
        P(),
        P(),
        P(("parts", "depth"), "row", None),
        P(("parts", "row"), "col", None),
    )
    out_specs = (
        P(("parts", "depth"), "row", None),
        P(("parts", "row"), "col", None),
        P("parts", None),
    )
    return jax.shard_map(
        per_device, mesh=mesh, in_specs=in_specs, out_specs=out_specs, check_vma=False
    )
```

```python
import functools
import math

import jax
import jax.numpy as jnp
from jax import lax
from jax.experimental import pallas as pl
from jax.experimental.pallas import tpu as pltpu
from jax.sharding import PartitionSpec as P

EPS = 1e-05
PENALTY = 10000.0
F32 = jnp.float32
BF16 = jnp.bfloat16
LANES = 128
NN = (((1,), (0,)), ((), ()))
NT = (((1,), (1,)), ((), ()))
VMEM = pl.BlockSpec(memory_space=pltpu.VMEM)
FAR = pl.BlockSpec(memory_space=pl.ANY)


def mm(a, b, dims=NN):
    return lax.dot_general(a, b, dims, preferred_element_type=F32)


def split_high_low(value):
    high = value.astype(BF16)
    return high, (value - high.astype(F32)).astype(BF16)


def iota(shape, dim):
    return lax.broadcasted_iota(jnp.int32, shape, dim)


def lanes_of(pieces):
    return pieces[0] if len(pieces) == 1 else jnp.concatenate(pieces, axis=-1)


def rows_of(pieces):
    return pieces[0] if len(pieces) == 1 else jnp.concatenate(pieces, axis=0)


def standardize(values):
    centred = values - jnp.mean(values, -1, keepdims=True)
    inverse = lax.rsqrt(jnp.mean(centred * centred, -1, keepdims=True) + EPS)
    return centred * inverse, inverse


def standardize_backward(values, upstream):
    scaled, inverse = standardize(values)
    mean_grad = jnp.mean(upstream, -1, keepdims=True)
    mean_cross = jnp.mean(upstream * scaled, -1, keepdims=True)
    return (upstream - mean_grad - scaled * mean_cross) * inverse


def on_diagonal(block, width):
    rows, lanes = block.shape
    same = iota(block.shape, 0) // (rows // 2) == iota(block.shape, 1) // width
    return jnp.where(same, block, jnp.zeros_like(block))


def split_three(value):
    high = value.astype(BF16)
    rest = value - high.astype(F32)
    middle = rest.astype(BF16)
    return [high, middle, (rest - middle.astype(F32)).astype(BF16)]


def three_lanes(value):
    rows, width = value.shape
    fill = -(3 * width) % LANES
    return lanes_of(split_three(value) + [jnp.zeros((rows, fill), BF16)] * (fill > 0))


def join_three(parts, width):
    wide = parts.astype(F32)
    return (wide[:, :width] + wide[:, width : 2 * width]) + wide[:, 2 * width : 3 * width]


def twice(weights):
    zero = jnp.zeros_like(weights)
    return rows_of([lanes_of([weights, zero]), lanes_of([zero, weights])])


def column_weights(g, w2):
    rows = iota((2 * g.QL, g.Q), 0) % g.QL + lax.axis_index("col") * g.QL
    pick = (iota((2 * g.QL, g.Q), 1) == rows).astype(BF16)
    return on_diagonal(mm(pick, lanes_of([w2, w2])), g.M).astype(BF16)


def normalise_kernel(
    g, x_hbm, e_hbm, dd_hbm, flag_hbm, wl_hbm, live_hbm, w1_hbm, t_hbm, w2_hbm, every_hbm, *refs
):
    xn_ref, send_ref, logit_ref, near_ref, x_ref, e_ref, wl_ref, mask_ref, w1_ref, t_ref, w2_ref, second_ref = refs[:12]
    flag_in, live_in, every_in, x_in, norm_ref, rows_ref, sem = refs[12:]
    col = lax.axis_index("col")
    pairs = g.I * g.JC
    copies = [
        pltpu.make_async_copy(a, b, sem.at[k])
        for k, (a, b) in enumerate(
            [
                (x_hbm, x_in),
                (e_hbm, e_ref),
                (wl_hbm, wl_ref),
                (flag_hbm, flag_in),
                (dd_hbm, near_ref.at[pl.ds(0, pairs)]),
                (live_hbm, live_in),
                (w1_hbm, w1_ref),
                (t_hbm, t_ref),
                (w2_hbm, w2_ref),
                (every_hbm, every_in),
            ]
        )
    ]
    for copy in copies:
        copy.start()
    for copy in (*copies[:4], copies[5], *copies[8:]):
        copy.wait()
    lane = iota((1, 2 * g.M), 1)
    groups = [lax.rem(col + m, g.C) for m in range(g.C)]
    for m, group in enumerate(groups):
        first = (lax.axis_index("depth") * g.C + group) * g.SQ
        for k in range(g.SP):
            if 2 * k + 1 < g.SQ:
                flags = jnp.where(lane < g.M, live_in[first + 2 * k], live_in[first + 2 * k + 1])
                flags = flags.astype(F32)
            else:
                flags = jnp.zeros((1, 2 * g.M), F32)
            mask_ref[m * g.SP + k : m * g.SP + k + 1, :] = flags
    count = jnp.sum(every_in[...].astype(F32), -1, keepdims=True)
    mask_ref[g.C * g.SP : g.C * g.SP + 1, :] = jnp.broadcast_to(1.0 / (0.001 + count), (1, 2 * g.M))
    norm_ref[...] = standardize(x_in[...].astype(F32))[0]
    x_ref[...] = x_in[pl.ds(col * g.SQ, g.SQ)]
    second = column_weights(g, w2_ref[...])
    second_ref[...] = second
    rows, blocks = g.SP * g.I, []
    for m, group in enumerate(groups):
        normed = g.fill(norm_ref[pl.ds(group * g.SQ, g.SQ)]).reshape(g.SP, 2, g.I, g.M)
        packed = jnp.concatenate([normed[:, 0], normed[:, 1]], axis=-1).astype(BF16)
        xn_ref[m] = packed
        if m == 0:
            send_ref[:rows, :] = packed.reshape(rows, 2 * g.M)
        else:
            masks = [mask_ref[m * g.SP + k : m * g.SP + k + 1, :] for k in range(g.SP)]
            live = rows_of([(packed[k].astype(F32) * masks[k]).astype(BF16) for k in range(g.SP)])
            factors = mm(live, second, NT)
            blocks += [factors[k * g.I : (k + 1) * g.I] for k in range(g.SP)]
    if blocks:
        wide = lanes_of(blocks)
        fill = -wide.shape[1] % LANES
        if fill:
            wide = lanes_of([wide, jnp.zeros((g.I, fill), F32)])
        for k in range(g.EXTRA):
            block = wide[:, k * LANES : (k + 1) * LANES]
            send_ref[rows + k * g.I : rows + (k + 1) * g.I, :] = block.astype(BF16)
    pair = standardize(e_ref[...].astype(F32).reshape(pairs, g.Z))[0].astype(BF16)
    penalty = (flag_in[...].astype(F32) - 1.0) * PENALTY
    weights = wl_ref[...]
    for i in range(g.I):
        rows_ref[i * g.H : (i + 1) * g.H, : g.JC] = (
            mm(weights, pair[i * g.JC : (i + 1) * g.JC], NT) + penalty
        )
    logits = rows_of([rows_ref[pl.ds(h, g.I, stride=g.H), :][:, : g.JC] for h in range(g.H)])
    tall = g.H * g.I // g.G
    packed = lanes_of([logits[k * tall : (k + 1) * tall] for k in range(g.G)])
    logit_ref[...] = packed
    near_ref[pairs:, :] = rows_of(split_three(packed))
    for copy in (copies[4], *copies[6:8]):
        copy.wait()


def prepare_kernel(g, xn_ref, w1_ref, t_ref, mask_ref, u_hbm, *refs):
    refs = list(refs)
    count = g.carried
    sources, refs = refs[:count], refs[count:]
    left_ref, ts_ref, lt_ref, u_ref, refs = refs[0], refs[1], refs[2], refs[3], refs[4:]
    targets, (wide_ref, half_ref, first_sem, later_sem) = refs[:count], refs[count:]
    first = lax.axis_index("col") * g.SQ
    copies = [pltpu.make_async_copy(u_hbm.at[pl.ds(first, g.SQ)], u_ref, first_sem)]
    copies += [
        pltpu.make_async_copy(a, b, later_sem.at[k])
        for k, (a, b) in enumerate(zip(sources, targets, strict=True))
    ]
    for copy in copies:
        copy.start()
    w1 = rows_of([w1_ref[...], jnp.zeros((LANES - g.Q, g.M), BF16)])
    zero = jnp.zeros_like(w1)
    for m in range(g.C):
        masks = [mask_ref[m * g.SP + k : m * g.SP + k + 1, :] for k in range(g.SP)]
        live_xn = rows_of(
            [(xn_ref[m, k].astype(F32) * masks[k]).astype(BF16) for k in range(g.SP)]
        )
        half_ref[0] = mm(live_xn, lanes_of([w1, zero]), NT)
        half_ref[1] = mm(live_xn, lanes_of([zero, w1]), NT)
        for i in range(g.I):
            halves = [half_ref[half, pl.ds(i, g.SP, stride=g.I), :] for half in range(2)]
            first = (m * g.I + i) * g.S
            left_ref[first : first + g.S, :] = rows_of(halves)[:, : g.Q].astype(BF16)
    wide_ref[...] = t_ref[...].astype(F32)
    for q in range(g.Q):
        ts_ref[q] = wide_ref[pl.ds(q, g.Q, stride=g.Q), :].astype(BF16)
    left = left_ref[: g.I * g.S, :]
    for q in range(0, g.Q, 2):
        product = mm(left, lanes_of([ts_ref[q], ts_ref[q + 1]]))
        for k in range(2):
            block = product[:, k * g.Z : (k + 1) * g.Z].reshape(g.I, g.S, g.Z)
            lt_ref[:, (q + k) * g.S : (q + k + 1) * g.S, :] = block.astype(BF16)
    for copy in copies:
        copy.wait()


def gate_kernel(g, xn_ref, u_ref, sg_ref, wf_ref, p_ref, logit_ref, *refs):
    near_refs, refs = refs[: g.C - 1], refs[g.C - 1 :]
    gate_weight_ref, gm_ref, gate_ref, value_weight_ref, soft_ref, low_ref, low_t_ref = refs
    value_weight_ref[...] = twice(p_ref[...])
    tall, blocks = logit_ref.shape[0], [logit_ref[...]]
    for k in range(1, g.C):
        parts = near_refs[g.C - k - 1][g.I * g.JC :, :].astype(F32)
        blocks.append((parts[:tall] + parts[tall : 2 * tall]) + parts[2 * tall :])
    logits = lanes_of(
        [rows_of([b[:, k * g.JC : (k + 1) * g.JC] for k in range(g.G)]) for b in blocks]
    )
    shifted = jnp.exp(logits - jnp.max(logits, -1, keepdims=True))
    soft = shifted / jnp.sum(shifted, -1, keepdims=True)
    soft_ref[...] = soft
    low = soft.astype(BF16)
    eye = (iota((g.N, g.N), 0) == iota((g.N, g.N), 1)).astype(BF16)
    low_t = mm(eye, low, NT).astype(BF16)
    low_ref[...] = low
    low_t_ref[...] = lanes_of([low_t, low_t])
    rows = g.SP * g.I
    xn = xn_ref[0]
    gate_weights = twice(sg_ref[...])
    gate_weight_ref[...] = gate_weights
    gates = jax.nn.sigmoid(mm(xn.reshape(rows, 2 * g.M), gate_weights))
    u = g.fill(u_ref[...]).reshape(g.SP, 2, g.I, g.M)
    packed_u = jnp.concatenate([u[:, 0], u[:, 1]], axis=-1).reshape(rows, 2 * g.M)
    gated = mm(packed_u, twice(wf_ref[...]))
    blended = gated * gates
    gm_ref[...] = blended.astype(BF16)
    gate_ref[...] = blended * (1.0 - gates)


def right_kernel(g, *refs):
    near_refs, (lt_ref, w2_ref, mask_ref, d_ref, go_ref, rg_ref) = refs[: g.C], refs[g.C :]
    for k in range(g.C):
        spot = (g.C - k) % g.C
        block = near_refs[k][: g.I * g.JC, :].reshape(g.I, g.JC, g.Z)
        d_ref[:, spot * g.JC : (spot + 1) * g.JC, :] = block
    masks = [mask_ref[k : k + 1, :] for k in range(g.SP)]
    scale = mask_ref[g.C * g.SP : g.C * g.SP + 1, :]
    right_grad = jnp.zeros((g.Q * g.S, g.N), F32)
    for i in range(0, g.I, 2):
        right_grad = right_grad + mm(
            lanes_of([lt_ref[i], lt_ref[i + 1]]), lanes_of([d_ref[i], d_ref[i + 1]]), NT
        )
    for t in range(g.NT):
        lanes = min(LANES, g.N - t * LANES)
        piece = right_grad[:, t * LANES : t * LANES + lanes]
        if lanes < LANES:
            piece = lanes_of([piece, jnp.zeros((g.Q * g.S, LANES - lanes), F32)])
        rg_ref[t] = piece
    deep = 2 * g.Q
    group = min(g.SP, LANES // deep)
    which = iota((group * deep, g.Q), 0)
    pick = (iota((group * deep, g.Q), 1) == which % deep // 2).astype(BF16)
    w2 = w2_ref[...]
    base = mm(pick, lanes_of([w2, w2]))
    which = iota(base.shape, 0)
    base = jnp.where(which % 2 == iota(base.shape, 1) // g.M, base, 0.0)
    weights = lanes_of([jnp.where(which // deep == k, base, 0.0) for k in range(group)]).astype(BF16)
    for k in range(0, g.SP, group):
        for t in range(g.NT):
            lanes = min(LANES, g.N - t * LANES)
            tall = rows_of(
                [rg_ref[t, pl.ds(k + m, deep, stride=g.SP), :] for m in range(group)]
            )
            tall = (tall * scale).T[:lanes]
            high, low = split_high_low(tall)
            part = mm(high, weights) + mm(low, weights)
            for m in range(group):
                go_ref[k + m, t * LANES : t * LANES + lanes, :] = (
                    part[:, m * 2 * g.M : (m + 1) * 2 * g.M] * masks[k + m]
                )


def outer_kernel(g, *refs):
    refs = list(refs)
    x_refs, refs = refs[: g.R], refs[g.R :]
    d_ref, left_ref, second_ref, mask_ref, xall_ref, ds_ref, *refs = refs
    w_refs, (others_ref, spread_ref, rt_ref, all_ref) = refs[: g.D], refs[g.D :]
    row, col, depth = (lax.axis_index(a) for a in ("row", "col", "depth"))
    rows, deep = g.SP * g.I, 2 * g.QL
    for k, ref in zip((0, *g.order), x_refs, strict=True):
        place = g.place(jnp.bitwise_xor(row, k), col)
        xall_ref[:, pl.ds(place, g.I), :] = ref[:rows, :].reshape(g.SP, g.I, 2 * g.M)
        for m in range(g.EXTRA):
            block = ref[rows + m * g.I : rows + (m + 1) * g.I, :]
            others_ref[pl.ds(place, g.I), m * LANES : (m + 1) * LANES] = block
    second = second_ref[...]
    parts = [
        mm(second, (xall_ref[k].astype(F32) * mask_ref[k : k + 1, :]).astype(BF16), NT)
        for k in range(g.SP)
    ]
    if g.EXTRA:
        lanes = g.EXTRA * LANES
        eye = (iota((lanes, lanes), 0) == iota((lanes, lanes), 1)).astype(BF16)
        parts.append(mm(eye, others_ref[...], NT)[: (g.C - 1) * g.SP * deep])
    first = 0
    for part in parts:
        for t in range(g.NT):
            lanes = min(LANES, g.N - t * LANES)
            piece = part[:, t * LANES : t * LANES + lanes]
            spread_ref[t, first : first + part.shape[0], :lanes] = piece
        first += part.shape[0]
    for q in range(g.QL):
        for m in range(g.C):
            spot = (q * g.C + m) * g.S
            for t in range(g.NT):
                lanes = min(LANES, g.N - t * LANES)
                halves = [
                    spread_ref[t, pl.ds(m * g.SP * deep + half * g.QL + q, g.SP, stride=deep), :]
                    for half in range(2)
                ]
                rt_ref[spot : spot + g.S, t * LANES : t * LANES + lanes] = rows_of(halves)[
                    :, :lanes
                ].astype(BF16)
    rt = rt_ref[...]
    for i in range(0, g.I, 2):
        product = mm(rt, lanes_of([d_ref[i], d_ref[i + 1]]))
        for k in range(2):
            block = product[:, k * g.Z : (k + 1) * g.Z]
            ds_ref[:, :, i + k] = block.reshape(g.QL, g.C, g.S, g.Z).astype(BF16)
    eye = (iota((g.Q, g.Q), 0) == iota((g.Q, g.Q), 1)).astype(BF16)
    left_t = mm(eye, left_ref[...], NT).astype(BF16)
    scale = mask_ref[g.C * g.SP : g.C * g.SP + 1, :]
    entries = g.C * g.S * g.I
    for q in range(0, g.QL, 2):
        both = lanes_of([ds_ref[q].reshape(entries, g.Z), ds_ref[q + 1].reshape(entries, g.Z)])
        part = mm(left_t, both)
        all_ref[pl.ds(q, g.Q, stride=g.QL), :] = part[:, : g.Z] * scale
        all_ref[pl.ds(q + 1, g.Q, stride=g.QL), :] = part[:, g.Z :] * scale
    share = g.Q * g.QL // g.D
    for k in range(g.D):
        first = pl.multiple_of(lax.rem(depth + k, g.D) * share, share)
        w_refs[k][...] = all_ref[pl.ds(first, share), :]


def own_kernel(
    g, xall_ref, near_ref, d_ref, ts_ref, w1_ref, w2_ref, mask_ref, part_ref, gg_ref, gate_weight_ref, own_ref,
    spread_ref, rt_ref, ds_ref, turn_ref,
):
    scale = mask_ref[g.C * g.SP : g.C * g.SP + 1, :]
    masks = [mask_ref[k : k + 1, :] for k in range(g.SP)]
    w2 = w2_ref[...]
    doubled = lanes_of([w2, w2])
    second = on_diagonal(rows_of([doubled, doubled]), g.M)
    for k in range(g.SP):
        live_x = (xall_ref[k].astype(F32) * masks[k]).astype(BF16)
        part = mm(second, live_x, NT)
        for t in range(g.NT):
            lanes = min(LANES, g.N - t * LANES)
            spread_ref[t, k * 2 * g.Q : (k + 1) * 2 * g.Q, :lanes] = part[
                :, t * LANES : t * LANES + lanes
            ]
    for q in range(g.Q):
        for t in range(g.NT):
            lanes = min(LANES, g.N - t * LANES)
            halves = [
                spread_ref[t, pl.ds(half * g.Q + q, g.SP, stride=2 * g.Q), :] for half in range(2)
            ]
            rt_ref[q * g.S : (q + 1) * g.S, t * LANES : t * LANES + lanes] = rows_of(halves)[
                :, :lanes
            ].astype(BF16)
    col = lax.axis_index("col")
    entries = g.S * g.I
    left_grad = jnp.zeros((entries, g.Q), F32)
    for m in range(g.C):
        first = lax.rem(col + m, g.C) * g.QL
        if m > 0:
            rt = rt_ref[pl.ds(pl.multiple_of(first * g.S, g.QL * g.S), g.QL * g.S), :]
            for i in range(0, g.I, 2):
                product = mm(rt, lanes_of([d_ref[i], d_ref[i + 1]]))
                for k in range(2):
                    block = product[:, k * g.Z : (k + 1) * g.Z]
                    ds_ref[m - 1, :, i + k] = block.reshape(g.QL, g.S, g.Z).astype(BF16)
        for q in range(0, g.QL, 2):
            pair = [near_ref[q + k, 0] if m == 0 else ds_ref[m - 1, q + k] for k in range(2)]
            both = lanes_of([part.reshape(entries, g.Z) for part in pair])
            left_grad = left_grad + mm(both, lanes_of([ts_ref[first + q], ts_ref[first + q + 1]]), NT)
    w1 = w1_ref[...]
    first_term = jnp.zeros((entries, 2 * g.M), F32)
    for piece in split_high_low(left_grad * scale[:, : g.Q]):
        first_term = first_term + mm(piece, lanes_of([w1, w1]))
    turn_ref[...] = first_term
    gate_term = mm(gg_ref[...], gate_weight_ref[...], NT)
    lane = iota((1, 2 * g.M), 1)
    for k in range(g.SP):
        rows = slice(k * g.I, (k + 1) * g.I)
        halves = [turn_ref[pl.ds(half * g.SP + k, g.I, stride=g.S), :] for half in range(2)]
        term = jnp.where(lane < g.M, halves[0], halves[1]) * mask_ref[k : k + 1, :]
        own_ref[rows, :] = part_ref[rows, :] + gate_term[rows] + term


def send_kernel(g, low_t_ref, gm_ref, value_weight_ref, go_ref, own_ref, *refs):
    send_refs, (total_ref,) = refs[: g.R - 1], refs[g.R - 1 :]
    row, col = lax.axis_index("row"), lax.axis_index("col")
    value_weights, low_t = value_weight_ref[...], low_t_ref[...]
    half = value_weights.shape[1] // 2
    width = half // g.H
    group = LANES // width
    count = g.H // group
    tall = group * g.I
    head = iota((1, 2 * LANES), 1) % LANES // width

    def lanes(array, k):
        return lanes_of([array[:, s * half + k * LANES : s * half + (k + 1) * LANES] for s in range(2)])

    group_weights = [lanes(value_weights, k) for k in range(count)]
    for k in range(g.SP):
        blended = gm_ref[k * g.I : (k + 1) * g.I, :]
        projected = []
        for m in range(count):
            bm = lanes(blended, m)
            by_head = rows_of([jnp.where(head == h, bm, jnp.zeros_like(bm)) for h in range(group)])
            projected.append(mm(by_head, group_weights[m], NT))
        total_ref[k] = go_ref[k] + mm(low_t, rows_of([*split_high_low(rows_of(projected))]))
    own = total_ref[:, pl.ds(g.place(row, col), g.I), :]
    own_ref[...] = own.reshape(g.SP * g.I, 2 * g.M)
    for x in range(1, g.R):
        block = total_ref[:, pl.ds(g.place(jnp.bitwise_xor(row, x), col), g.I), :]
        send_refs[x - 1][...] = block.reshape(g.SP * g.I, 2 * g.M).astype(BF16)


def attend_kernel(g, xall_ref, low_ref, gm_ref, gate_ref, value_weight_ref, gs_ref, gg_ref):
    value_weights, low = value_weight_ref[...], low_ref[...]
    values = mm(xall_ref[...].reshape(g.SP * g.N, 2 * g.M), value_weights).astype(BF16)
    half = value_weights.shape[1] // 2
    width = half // g.H
    group = LANES // width
    count = g.H // group
    tall = group * g.I
    head = iota((1, 2 * LANES), 1) % LANES // width

    def lanes(array, k):
        return lanes_of([array[:, s * half + k * LANES : s * half + (k + 1) * LANES] for s in range(2)])

    grad_soft = [jnp.zeros((tall, g.N), F32) for _ in range(count)]
    for k in range(g.SP):
        v = values[k * g.N : (k + 1) * g.N]
        rows = slice(k * g.I, (k + 1) * g.I)
        blended, factor = gm_ref[rows, :], gate_ref[rows, :]
        for m in range(count):
            vm = lanes(v, m)
            crossed = mm(low[m * tall : (m + 1) * tall], vm)
            mixed = crossed[: g.I]
            for h in range(1, group):
                mixed = jnp.where(head == h, crossed[h * g.I : (h + 1) * g.I], mixed)
            gate_grad = (lanes(factor, m) * mixed).astype(BF16)
            for s in range(2):
                first = s * half + m * LANES
                gg_ref[rows, first : first + LANES] = gate_grad[:, s * LANES : (s + 1) * LANES]
            bm = lanes(blended, m)
            by_head = rows_of([jnp.where(head == h, bm, jnp.zeros_like(bm)) for h in range(group)])
            grad_soft[m] = grad_soft[m] + mm(by_head, vm, NT)
    gs_ref[...] = rows_of(grad_soft)


def pack_kernel(g, *refs):
    refs = list(refs)
    sums, refs = refs[: g.R - 1], refs[g.R - 1 :]
    parts, refs = refs[: g.D], refs[g.D :]
    outs, (own_ref, halves_ref) = refs[: g.R - 1], refs[g.R - 1 :]
    row = lax.axis_index("row")
    total = parts[0][...]
    for ref in parts[1:]:
        total = total + ref[...]
    half, rows = own_ref.shape[0], g.SP * g.I
    for k in range(2):
        halves_ref[k] = total[k * half : (k + 1) * half].astype(BF16)
    own_ref[...] = halves_ref[lax.rem(row, 2)]
    for x in range(1, g.R):
        outs[x - 1][:rows, :] = sums[x - 1][...]
        outs[x - 1][rows:, :] = halves_ref[lax.rem(jnp.bitwise_xor(row, x), 2)]


def piece_kernel(g, own_ref, *refs):
    out_ref, order_ref = refs[-2:]
    row, rows = lax.axis_index("row"), g.SP * g.I
    order_ref[row] = own_ref[...]
    for k in range(1, g.R):
        order_ref[jnp.bitwise_xor(row, g.R - k)] = refs[k - 1][rows:, :]
    total = order_ref[0].astype(F32)
    for r in range(1, g.R):
        total = total + order_ref[r].astype(F32)
    out_ref[...] = total.astype(BF16)


def score_kernel(g, soft_ref, *refs):
    parts, refs = refs[: g.D], refs[g.D :]
    own_ref, out_refs, order_ref = refs[0], refs[1 : g.C], refs[g.C]
    depth = lax.axis_index("depth")
    for k in range(g.D):
        order_ref[lax.rem(depth - k + g.D, g.D)] = parts[k][...]
    grad_soft = order_ref[0]
    for k in range(1, g.D):
        grad_soft = grad_soft + order_ref[k]
    inner = jnp.sum(soft_ref[...] * grad_soft, -1, keepdims=True)
    for k in range(g.C):
        block = lanes_of([grad_soft[:, k * g.JC : (k + 1) * g.JC], inner])
        if k == 0:
            own_ref[...] = block
        else:
            out_refs[k - 1][...] = three_lanes(block)


def pair_kernel(g, e_ref, wl_ref, soft_ref, own_ref, *refs):
    got, pair_ref = refs[: g.C - 1], refs[g.C - 1]
    heads = g.H * g.I
    total = own_ref[...]
    for ref in got:
        total = total + join_three(ref[...], g.JC + 1)
    grad = soft_ref[:, : g.JC] * (total[:, : g.JC] - total[:, g.JC :])
    if g.JC < LANES:
        grad = lanes_of([grad, jnp.zeros((heads, LANES - g.JC), F32)])
    high, low = split_high_low(grad.T[: g.JC])
    grads = lanes_of([high, low])
    pick = (iota((heads, g.H), 0) // g.I == iota((heads, g.H), 1)).astype(BF16)
    base = mm(pick, wl_ref[...]).astype(BF16)
    token = iota((heads, 1), 0) % g.I
    for i in range(0, g.I, 2):
        weights = lanes_of(
            [jnp.where(token == i + k, base, jnp.zeros_like(base)) for k in range(2)]
        )
        upstream = mm(grads, rows_of([weights, weights]))
        for k in range(2):
            pair_ref[i + k] = standardize_backward(
                e_ref[i + k].astype(F32), upstream[:, k * g.Z : (k + 1) * g.Z]
            ).astype(BF16)


def reduce_kernel(g, x_ref, own_ref, *refs):
    got, out_ref = refs[:-1], refs[-1]
    rows = g.SP * g.I
    total = own_ref[...]
    for ref in got:
        total = total + ref[:rows, :].astype(F32)
    total = total.reshape(g.SP, 1, g.I, 2 * g.M)
    upstream = jnp.concatenate([total[..., : g.M], total[..., g.M :]], axis=1)
    upstream = upstream.reshape(g.S, g.I, g.M)[: g.SQ]
    msa = g.fill(standardize_backward(x_ref[...].astype(F32), upstream))
    msa = msa.reshape(g.SP, 2, g.I, g.M)
    msa = jnp.concatenate([msa[:, 0], msa[:, 1]], axis=-1).astype(BF16)
    out_ref[...] = msa.reshape(rows, 2 * g.M)


def across_kernel(g, *refs):
    out_ref = refs[-1]
    row, col = lax.axis_index("row"), lax.axis_index("col")
    for ref, (b, k) in zip(refs[:-1], g.spread, strict=True):
        half = lax.rem(jnp.bitwise_xor(row, b), 2)
        out_ref[lax.rem(col - k + g.C, g.C), half] = ref[...]


def unpack_kernel(g, *refs):
    parts, msa_ref = refs[: g.C], refs[g.C]
    col = lax.axis_index("col")
    for k, ref in enumerate(parts):
        msa = ref[...].astype(F32).reshape(g.SP, 1, g.I, 2 * g.M)
        msa = jnp.concatenate([msa[..., : g.M], msa[..., g.M :]], axis=1)
        msa = msa.reshape(g.S, g.I, g.M)[: g.SQ].astype(BF16)
        msa_ref[pl.ds(lax.rem(col - k + g.C, g.C) * g.SQ, g.SQ)] = msa


def finish_kernel(g, msa_ref, *refs):
    parts, (out_ref, matrix_ref) = refs[: g.D], refs[g.D :]
    depth = lax.axis_index("depth")
    out_ref[...] = msa_ref[...]
    share = g.Q // g.D
    for k in range(g.D):
        first = lax.rem(depth - k + g.D, g.D) * share
        for c in range(g.C):
            block = parts[k][c].astype(F32)
            matrix_ref[pl.ds(first, share), c * g.QL : (c + 1) * g.QL, :] = block


class Sizes:
    def __init__(self, x, e, wl, w1):
        self.R, self.C, self.D = (lax.axis_size(a) for a in ("row", "col", "depth"))
        self.I, self.M = x.shape[1:]
        self.JC, self.Z = e.shape[1:]
        self.H, self.Q = wl.shape[1], w1.shape[1]
        self.QL = self.Q // self.C
        self.SQ = x.shape[0] // self.C
        self.S = -(-self.SQ // 16) * 16
        self.SP, self.N = self.S // 2, self.R * self.I
        self.F = self.R // self.C
        self.NT = -(-self.N // LANES)
        self.G = max(1, LANES // self.JC)
        self.EXTRA = -(-(self.C - 1) * self.S * self.QL // LANES)
        self.carried = 0
        self.spread = [(b, k) for k in range(self.C) for b in range(2)]
        self.order = [*range(1, self.R // 2), *range(self.R // 2 + 1, self.R), self.R // 2]

    def fill(self, rows):
        if self.SQ == self.S:
            return rows
        return rows_of([rows, jnp.zeros((self.S - self.SQ, *rows.shape[1:]), rows.dtype)])

    def place(self, row, col):
        turn = lax.rem(row // self.F - col + self.C, self.C)
        return pl.multiple_of((turn * self.F + lax.rem(row, self.F)) * self.I, self.I)


def shift(array, axis, k):
    count = lax.axis_size(axis)
    return lax.ppermute(array, axis, [(i, (i + k) % count) for i in range(count)])


def swap(array, axis, x):
    return lax.ppermute(array, axis, [(i, i ^ x) for i in range(lax.axis_size(axis))])


def swapped(arrays, axis):
    return [swap(a, axis, k + 1) for k, a in reversed([*enumerate(arrays)])]


def from_near(array, b, k):
    count, wide = lax.axis_size("row"), lax.axis_size("col")
    pairs = [(r * wide + c, (r ^ b) * wide + (c + k) % wide) for r in range(count) for c in range(wide)]
    return lax.ppermute(array, ("row", "col"), pairs)


def shifted_all(array, axis):
    return [array] + [shift(array, axis, k) for k in range(1, lax.axis_size(axis))]


def per_device(
    homolog_ensemble,
    duplex_embedding,
    homolog_present_flags,
    resolved_position_flags,
    payload_weights,
    sigmoid_weights,
    averager_final_weights,
    first_operand_weights,
    second_operand_weights,
    duplex_logit_weights,
    tensor_product_weights,
    averager_upstream_adjoint,
    duplex_upstream_adjoint,
):
    g = Sizes(homolog_ensemble, duplex_embedding, duplex_logit_weights, first_operand_weights)
    shape = jax.ShapeDtypeStruct

    def call(kernel, name, args, outs, scratch=(), far=None, after=(), distant=False, us=1.0):
        size = sum(a.size * a.dtype.itemsize for a in args) + sum(
            math.prod(o.shape) * jnp.dtype(o.dtype).itemsize for o in outs
        )
        single = len(outs) == 1
        near = len(args) if far is None else far
        args = list(args[:near]) + [
            pltpu.with_memory_space_constraint(a, pltpu.HBM) for a in args[near:]
        ]

        if distant:
            after = [pltpu.with_memory_space_constraint(a, pltpu.HBM) for a in after]

        def body(*refs):
            kernel(g, *refs[: len(args)], *refs[len(args) + len(after) :])

        return pl.pallas_call(
            body,
            out_shape=outs[0] if single else tuple(outs),
            in_specs=[VMEM] * near + [FAR] * (len(args) - near) + [FAR if distant else VMEM] * len(after),
            out_specs=VMEM if single else (VMEM,) * len(outs),
            scratch_shapes=list(scratch),
            compiler_params=pltpu.CompilerParams(vmem_limit_bytes=40 * 1024 * 1024),
            cost_estimate=pl.CostEstimate(
                flops=int(us * 1.15e9), bytes_accessed=size, transcendentals=0
            ),
            name=name,
        )(*args, *after)

    heads = g.H * g.I
    rows = g.SP * g.I
    values = 2 * payload_weights.shape[1]
    pairs, tall = g.I * g.JC, heads // g.G
    xn, send, logits, near, x, e, wl, masks, w1, outer_weights, w2, second = call(
        normalise_kernel,
        "normalise",
        (
            homolog_ensemble,
            duplex_embedding,
            duplex_upstream_adjoint.reshape(pairs, g.Z),
            resolved_position_flags.reshape(1, g.JC),
            duplex_logit_weights.T,
            homolog_present_flags,
            first_operand_weights.T,
            tensor_product_weights,
            second_operand_weights.T,
            homolog_present_flags.reshape(1, -1),
        ),
        [
            pltpu.VMEM((g.C, g.SP, g.I, 2 * g.M), BF16),
            pltpu.VMEM((rows + g.EXTRA * g.I, 2 * g.M), BF16),
            pltpu.VMEM((tall, g.G * g.JC), F32),
            pltpu.VMEM((pairs + 3 * tall, g.Z), BF16),
            pltpu.VMEM((g.SQ, g.I, g.M), BF16),
            pltpu.VMEM(duplex_embedding.shape, BF16),
            pltpu.VMEM((g.H, g.Z), BF16),
            pltpu.VMEM((g.C * g.SP + 8, 2 * g.M), F32),
            pltpu.VMEM((g.Q, g.M), BF16),
            pltpu.VMEM(tensor_product_weights.shape, BF16),
            pltpu.VMEM((g.Q, g.M), BF16),
            pltpu.VMEM((2 * g.QL, 2 * g.M), BF16),
        ],
        [
            pltpu.VMEM((1, g.JC), jnp.int32),
            pltpu.SMEM(homolog_present_flags.shape, jnp.int32),
            pltpu.VMEM((1, homolog_present_flags.shape[0]), jnp.int32),
            pltpu.VMEM(homolog_ensemble.shape, BF16),
            pltpu.VMEM(homolog_ensemble.shape, F32),
            pltpu.VMEM((g.I * g.H, LANES), F32),
            pltpu.SemaphoreType.DMA((10,)),
        ],
        far=0,
        us=2.0,
    )
    everyone = [send] + [swap(send, "row", k) for k in g.order]
    nears = shifted_all(near, "col")
    later = (
        sigmoid_weights,
        averager_final_weights.T,
        payload_weights,
    )
    g.carried = len(later)
    left, weights, left_weights, u, sg, wf, p = call(
        prepare_kernel,
        "prepare",
        (xn, w1, outer_weights, masks, averager_upstream_adjoint, *later),
        [
            pltpu.VMEM((g.C * g.I * g.S, g.Q), BF16),
            pltpu.VMEM((g.Q, g.Q, g.Z), BF16),
            pltpu.VMEM((g.I, g.Q * g.S, g.Z), BF16),
            pltpu.VMEM((g.SQ, g.I, g.M), BF16),
        ]
        + [pltpu.VMEM(a.shape, a.dtype) for a in later],
        [
            pltpu.VMEM(tensor_product_weights.shape, F32),
            pltpu.VMEM((2, rows, LANES), F32),
            pltpu.SemaphoreType.DMA,
            pltpu.SemaphoreType.DMA((len(later),)),
        ],
        far=4,
        us=0.01,
    )
    gate_weights, blended, gate_factor, value_weights, soft, low, low_t = call(
        gate_kernel,
        "gate",
        (xn, u, sg, wf, p, logits, *nears[1:]),
        [
            pltpu.VMEM((2 * g.M, values), BF16),
            pltpu.VMEM((rows, values), BF16),
            pltpu.VMEM((rows, values), F32),
            pltpu.VMEM((2 * g.M, values), BF16),
            pltpu.VMEM((heads, g.N), F32),
            pltpu.VMEM((heads, g.N), BF16),
            pltpu.VMEM((g.N, 2 * heads), BF16),
        ],
        us=0.01,
    )
    cotangents, second_term = call(
        right_kernel,
        "right",
        (*nears, left_weights, w2, masks),
        [pltpu.VMEM((g.I, g.N, g.Z), BF16), pltpu.VMEM((g.SP, g.N, 2 * g.M), F32)],
        [pltpu.VMEM((g.NT, g.Q * g.S, LANES), F32)],
        after=(gate_weights,),
        us=0.01,
    )
    share = g.Q * g.QL // g.D
    xall, products, *matrix_parts = call(
        outer_kernel,
        "outer",
        (*everyone, cotangents, left, second, masks),
        [
            pltpu.VMEM((g.SP, g.N, 2 * g.M), BF16),
            pltpu.VMEM((g.QL, g.C, g.I, g.S, g.Z), BF16),
        ]
        + [pltpu.VMEM((share, g.Z), F32)] * g.D,
        [
            pltpu.VMEM((g.N, max(1, g.EXTRA) * LANES), BF16),
            pltpu.VMEM((g.NT, g.C * g.SP * 2 * g.QL, LANES), F32),
            pltpu.VMEM((g.QL * g.C * g.S, g.N), BF16),
            pltpu.VMEM((g.Q * g.QL, g.Z), F32),
        ],
        after=(second_term,),
        us=0.05,
    )
    matrix_parts = [matrix_parts[0]] + [
        shift(a, "depth", k + 1) for k, a in enumerate(matrix_parts[1:])
    ]
    own, *sums = call(
        send_kernel,
        "send",
        (low_t, blended, value_weights, second_term),
        [pltpu.VMEM((rows, 2 * g.M), F32)] + [pltpu.VMEM((rows, 2 * g.M), BF16)] * (g.R - 1),
        [pltpu.VMEM((g.SP, g.N, 2 * g.M), F32)],
        after=(xall,),
        us=3.0,
    )
    *sums, piece = call(
        pack_kernel,
        "pack",
        (*sums, *matrix_parts),
        [pltpu.VMEM((rows + share // 2, 2 * g.M), BF16)] * (g.R - 1)
        + [pltpu.VMEM((share // 2, g.Z), BF16)],
        [pltpu.VMEM((2, share // 2, g.Z), BF16)],
        us=0.2,
    )
    sums = swapped(sums, "row")
    grad_soft, gate_grads = call(
        attend_kernel,
        "attend",
        (xall, low, blended, gate_factor, value_weights),
        [pltpu.VMEM((heads, g.N), F32), pltpu.VMEM((rows, values), BF16)],
        after=(piece,),
        us=0.01,
    )
    own = call(
        own_kernel,
        "own",
        (xall, products, cotangents, weights, w1, w2, masks, own, gate_grads, gate_weights),
        [pltpu.VMEM((rows, 2 * g.M), F32)],
        [
            pltpu.VMEM((g.NT, g.SP * 2 * g.Q, LANES), F32),
            pltpu.VMEM((g.Q * g.S, g.N), BF16),
            pltpu.VMEM((max(1, g.C - 1), g.QL, g.I, g.S, g.Z), BF16),
            pltpu.VMEM((g.I * g.S, 2 * g.M), F32),
        ],
        after=(piece,),
        us=0.01,
    )
    wide = -(-3 * (g.JC + 1) // LANES) * LANES
    scores, *sends = call(
        score_kernel,
        "score",
        (soft, *shifted_all(grad_soft, "depth")),
        [pltpu.VMEM((heads, g.JC + 1), F32)] + [pltpu.VMEM((heads, wide), BF16)] * (g.C - 1),
        [pltpu.VMEM((g.D, heads, g.N), F32)],
        after=(own,),
        us=0.2,
    )
    arrived = [shift(a, "col", k + 1) for k, a in enumerate(sends)]
    piece = call(
        piece_kernel,
        "piece",
        (piece, *sums),
        [pltpu.VMEM((share // 2, g.Z), BF16)],
        [pltpu.VMEM((g.R, share // 2, g.Z), BF16)],
        after=(scores,),
        us=0.1,
    )
    pieces = [piece] + [from_near(piece, b, k) for b, k in g.spread[1:]]
    part = call(
        reduce_kernel,
        "reduce",
        (x, own, *sums),
        [pltpu.VMEM((rows, 2 * g.M), BF16)],
        after=(piece,),
    )
    pairwise_gradient = call(
        pair_kernel,
        "pair",
        (e, wl, soft, scores, *arrived),
        [shape(duplex_embedding.shape, BF16)],
        after=(part,),
        us=0.01,
    )
    matrix = call(
        across_kernel,
        "across",
        pieces,
        [pltpu.VMEM((g.C, 2, share // 2, g.Z), BF16)],
        after=(pairwise_gradient,),
        distant=True,
        us=0.1,
    ).reshape(g.C, g.Q // g.D, g.QL, g.Z)
    ensemble_derivative = call(
        unpack_kernel,
        "unpack",
        shifted_all(part, "col"),
        [pltpu.VMEM(homolog_ensemble.shape, BF16)],
        after=(matrix,),
    )
    ensemble_derivative, outer_matrix_gradient = call(
        finish_kernel,
        "finish",
        (ensemble_derivative, *shifted_all(matrix, "depth")),
        [shape(homolog_ensemble.shape, BF16), shape((g.Q, g.Q, g.Z), F32)],
    )
    outer_matrix_gradient = outer_matrix_gradient.reshape(tensor_product_weights.shape)
    return (ensemble_derivative, pairwise_gradient, outer_matrix_gradient)


def solution(mesh):
    in_specs = (
        P(("parts", "depth"), "row", None),
        P(("parts", "row"), "col", None),
        P("parts"),
        P(("parts", "col")),
        P(),
        P(),
        P(),
        P(),
        P(),
        P(),
        P(),
        P(("parts", "depth"), "row", None),
        P(("parts", "row"), "col", None),
    )
    out_specs = (
        P(("parts", "depth"), "row", None),
        P(("parts", "row"), "col", None),
        P("parts", None),
    )
    return jax.shard_map(
        per_device, mesh=mesh, in_specs=in_specs, out_specs=out_specs, check_vma=False
    )
```

```python
import functools
import math

import jax
import jax.numpy as jnp
from jax import lax
from jax.experimental import pallas as pl
from jax.experimental.pallas import tpu as pltpu
from jax.sharding import PartitionSpec as P

EPS = 1e-05
PENALTY = 10000.0
F32 = jnp.float32
BF16 = jnp.bfloat16
LANES = 128
NN = (((1,), (0,)), ((), ()))
NT = (((1,), (1,)), ((), ()))
VMEM = pl.BlockSpec(memory_space=pltpu.VMEM)
FAR = pl.BlockSpec(memory_space=pl.ANY)


def mm(a, b, dims=NN):
    return lax.dot_general(a, b, dims, preferred_element_type=F32)


def split_high_low(value):
    high = value.astype(BF16)
    return high, (value - high.astype(F32)).astype(BF16)


def iota(shape, dim):
    return lax.broadcasted_iota(jnp.int32, shape, dim)


def lanes_of(pieces):
    return pieces[0] if len(pieces) == 1 else jnp.concatenate(pieces, axis=-1)


def rows_of(pieces):
    return pieces[0] if len(pieces) == 1 else jnp.concatenate(pieces, axis=0)


def standardize(values):
    centred = values - jnp.mean(values, -1, keepdims=True)
    inverse = lax.rsqrt(jnp.mean(centred * centred, -1, keepdims=True) + EPS)
    return centred * inverse, inverse


def standardize_backward(values, upstream):
    scaled, inverse = standardize(values)
    mean_grad = jnp.mean(upstream, -1, keepdims=True)
    mean_cross = jnp.mean(upstream * scaled, -1, keepdims=True)
    return (upstream - mean_grad - scaled * mean_cross) * inverse


def on_diagonal(block, width):
    rows, lanes = block.shape
    same = iota(block.shape, 0) // (rows // 2) == iota(block.shape, 1) // width
    return jnp.where(same, block, jnp.zeros_like(block))


def split_three(value):
    high = value.astype(BF16)
    rest = value - high.astype(F32)
    middle = rest.astype(BF16)
    return [high, middle, (rest - middle.astype(F32)).astype(BF16)]


def three_lanes(value):
    rows, width = value.shape
    fill = -(3 * width) % LANES
    return lanes_of(split_three(value) + [jnp.zeros((rows, fill), BF16)] * (fill > 0))


def join_three(parts, width):
    wide = parts.astype(F32)
    return (wide[:, :width] + wide[:, width : 2 * width]) + wide[:, 2 * width : 3 * width]


def twice(weights):
    zero = jnp.zeros_like(weights)
    return rows_of([lanes_of([weights, zero]), lanes_of([zero, weights])])


def column_weights(g, w2):
    rows = iota((2 * g.QL, g.Q), 0) % g.QL + lax.axis_index("col") * g.QL
    pick = (iota((2 * g.QL, g.Q), 1) == rows).astype(BF16)
    return on_diagonal(mm(pick, lanes_of([w2, w2])), g.M).astype(BF16)


def normalise_kernel(
    g, x_hbm, e_hbm, dd_hbm, flag_hbm, wl_hbm, live_hbm, w1_hbm, t_hbm, w2_hbm, every_hbm, *refs
):
    xn_ref, send_ref, logit_ref, near_ref, x_ref, e_ref, wl_ref, mask_ref, w1_ref, t_ref, w2_ref, second_ref = refs[:12]
    flag_in, live_in, every_in, x_in, norm_ref, rows_ref, sem = refs[12:]
    col = lax.axis_index("col")
    pairs = g.I * g.JC
    copies = [
        pltpu.make_async_copy(a, b, sem.at[k])
        for k, (a, b) in enumerate(
            [
                (x_hbm, x_in),
                (e_hbm, e_ref),
                (wl_hbm, wl_ref),
                (flag_hbm, flag_in),
                (dd_hbm, near_ref.at[pl.ds(0, pairs)]),
                (live_hbm, live_in),
                (w1_hbm, w1_ref),
                (t_hbm, t_ref),
                (w2_hbm, w2_ref),
                (every_hbm, every_in),
            ]
        )
    ]
    for copy in copies:
        copy.start()
    for copy in (*copies[:4], copies[5], *copies[8:]):
        copy.wait()
    lane = iota((1, 2 * g.M), 1)
    groups = [lax.rem(col + m, g.C) for m in range(g.C)]
    for m, group in enumerate(groups):
        first = (lax.axis_index("depth") * g.C + group) * g.SQ
        for k in range(g.SP):
            if 2 * k + 1 < g.SQ:
                flags = jnp.where(lane < g.M, live_in[first + 2 * k], live_in[first + 2 * k + 1])
                flags = flags.astype(F32)
            else:
                flags = jnp.zeros((1, 2 * g.M), F32)
            mask_ref[m * g.SP + k : m * g.SP + k + 1, :] = flags
    count = jnp.sum(every_in[...].astype(F32), -1, keepdims=True)
    mask_ref[g.C * g.SP : g.C * g.SP + 1, :] = jnp.broadcast_to(1.0 / (0.001 + count), (1, 2 * g.M))
    norm_ref[...] = standardize(x_in[...].astype(F32))[0]
    x_ref[...] = x_in[pl.ds(col * g.SQ, g.SQ)]
    second = column_weights(g, w2_ref[...])
    second_ref[...] = second
    rows, blocks = g.SP * g.I, []
    for m, group in enumerate(groups):
        normed = g.fill(norm_ref[pl.ds(group * g.SQ, g.SQ)]).reshape(g.SP, 2, g.I, g.M)
        packed = jnp.concatenate([normed[:, 0], normed[:, 1]], axis=-1).astype(BF16)
        xn_ref[m] = packed
        if m == 0:
            send_ref[:rows, :] = packed.reshape(rows, 2 * g.M)
        else:
            masks = [mask_ref[m * g.SP + k : m * g.SP + k + 1, :] for k in range(g.SP)]
            live = rows_of([(packed[k].astype(F32) * masks[k]).astype(BF16) for k in range(g.SP)])
            factors = mm(live, second, NT)
            blocks += [factors[k * g.I : (k + 1) * g.I] for k in range(g.SP)]
    if blocks:
        wide = lanes_of(blocks)
        fill = -wide.shape[1] % LANES
        if fill:
            wide = lanes_of([wide, jnp.zeros((g.I, fill), F32)])
        for k in range(g.EXTRA):
            block = wide[:, k * LANES : (k + 1) * LANES]
            send_ref[rows + k * g.I : rows + (k + 1) * g.I, :] = block.astype(BF16)
    pair = standardize(e_ref[...].astype(F32).reshape(pairs, g.Z))[0].astype(BF16)
    penalty = (flag_in[...].astype(F32) - 1.0) * PENALTY
    weights = wl_ref[...]
    for i in range(g.I):
        rows_ref[i * g.H : (i + 1) * g.H, : g.JC] = (
            mm(weights, pair[i * g.JC : (i + 1) * g.JC], NT) + penalty
        )
    logits = rows_of([rows_ref[pl.ds(h, g.I, stride=g.H), :][:, : g.JC] for h in range(g.H)])
    tall = g.H * g.I // g.G
    packed = lanes_of([logits[k * tall : (k + 1) * tall] for k in range(g.G)])
    logit_ref[...] = packed
    near_ref[pairs:, :] = rows_of(split_three(packed))
    for copy in (copies[4], *copies[6:8]):
        copy.wait()


def prepare_kernel(g, xn_ref, w1_ref, t_ref, mask_ref, u_hbm, *refs):
    refs = list(refs)
    count = g.carried
    sources, refs = refs[:count], refs[count:]
    left_ref, ts_ref, lt_ref, u_ref, refs = refs[0], refs[1], refs[2], refs[3], refs[4:]
    targets, (wide_ref, half_ref, first_sem, later_sem) = refs[:count], refs[count:]
    first = lax.axis_index("col") * g.SQ
    copies = [pltpu.make_async_copy(u_hbm.at[pl.ds(first, g.SQ)], u_ref, first_sem)]
    copies += [
        pltpu.make_async_copy(a, b, later_sem.at[k])
        for k, (a, b) in enumerate(zip(sources, targets, strict=True))
    ]
    for copy in copies:
        copy.start()
    w1 = rows_of([w1_ref[...], jnp.zeros((LANES - g.Q, g.M), BF16)])
    zero = jnp.zeros_like(w1)
    for m in range(g.C):
        masks = [mask_ref[m * g.SP + k : m * g.SP + k + 1, :] for k in range(g.SP)]
        live_xn = rows_of(
            [(xn_ref[m, k].astype(F32) * masks[k]).astype(BF16) for k in range(g.SP)]
        )
        half_ref[0] = mm(live_xn, lanes_of([w1, zero]), NT)
        half_ref[1] = mm(live_xn, lanes_of([zero, w1]), NT)
        for i in range(g.I):
            halves = [half_ref[half, pl.ds(i, g.SP, stride=g.I), :] for half in range(2)]
            first = (m * g.I + i) * g.S
            left_ref[first : first + g.S, :] = rows_of(halves)[:, : g.Q].astype(BF16)
    wide_ref[...] = t_ref[...].astype(F32)
    for q in range(g.Q):
        ts_ref[q] = wide_ref[pl.ds(q, g.Q, stride=g.Q), :].astype(BF16)
    left = left_ref[: g.I * g.S, :]
    for q in range(0, g.Q, 2):
        product = mm(left, lanes_of([ts_ref[q], ts_ref[q + 1]]))
        for k in range(2):
            block = product[:, k * g.Z : (k + 1) * g.Z].reshape(g.I, g.S, g.Z)
            lt_ref[:, (q + k) * g.S : (q + k + 1) * g.S, :] = block.astype(BF16)
    for copy in copies:
        copy.wait()


def gate_kernel(g, xn_ref, u_ref, sg_ref, wf_ref, p_ref, logit_ref, *refs):
    near_refs, refs = refs[: g.C - 1], refs[g.C - 1 :]
    gate_weight_ref, gm_ref, gate_ref, value_weight_ref, soft_ref, low_ref, low_t_ref = refs
    value_weight_ref[...] = twice(p_ref[...])
    tall, blocks = logit_ref.shape[0], [logit_ref[...]]
    for k in range(1, g.C):
        parts = near_refs[g.C - k - 1][g.I * g.JC :, :].astype(F32)
        blocks.append((parts[:tall] + parts[tall : 2 * tall]) + parts[2 * tall :])
    logits = lanes_of(
        [rows_of([b[:, k * g.JC : (k + 1) * g.JC] for k in range(g.G)]) for b in blocks]
    )
    shifted = jnp.exp(logits - jnp.max(logits, -1, keepdims=True))
    soft = shifted / jnp.sum(shifted, -1, keepdims=True)
    soft_ref[...] = soft
    low = soft.astype(BF16)
    eye = (iota((g.N, g.N), 0) == iota((g.N, g.N), 1)).astype(BF16)
    low_t = mm(eye, low, NT).astype(BF16)
    low_ref[...] = low
    low_t_ref[...] = lanes_of([low_t, low_t])
    rows = g.SP * g.I
    xn = xn_ref[0]
    gate_weights = twice(sg_ref[...])
    gate_weight_ref[...] = gate_weights
    gates = jax.nn.sigmoid(mm(xn.reshape(rows, 2 * g.M), gate_weights))
    u = g.fill(u_ref[...]).reshape(g.SP, 2, g.I, g.M)
    packed_u = jnp.concatenate([u[:, 0], u[:, 1]], axis=-1).reshape(rows, 2 * g.M)
    gated = mm(packed_u, twice(wf_ref[...]))
    blended = gated * gates
    gm_ref[...] = blended.astype(BF16)
    gate_ref[...] = blended * (1.0 - gates)


def right_kernel(g, *refs):
    near_refs, (lt_ref, w2_ref, mask_ref, d_ref, go_ref, rg_ref) = refs[: g.C], refs[g.C :]
    for k in range(g.C):
        spot = (g.C - k) % g.C
        block = near_refs[k][: g.I * g.JC, :].reshape(g.I, g.JC, g.Z)
        d_ref[:, spot * g.JC : (spot + 1) * g.JC, :] = block
    masks = [mask_ref[k : k + 1, :] for k in range(g.SP)]
    scale = mask_ref[g.C * g.SP : g.C * g.SP + 1, :]
    right_grad = jnp.zeros((g.Q * g.S, g.N), F32)
    for i in range(0, g.I, 2):
        right_grad = right_grad + mm(
            lanes_of([lt_ref[i], lt_ref[i + 1]]), lanes_of([d_ref[i], d_ref[i + 1]]), NT
        )
    for t in range(g.NT):
        lanes = min(LANES, g.N - t * LANES)
        piece = right_grad[:, t * LANES : t * LANES + lanes]
        if lanes < LANES:
            piece = lanes_of([piece, jnp.zeros((g.Q * g.S, LANES - lanes), F32)])
        rg_ref[t] = piece
    deep = 2 * g.Q
    group = min(g.SP, LANES // deep)
    which = iota((group * deep, g.Q), 0)
    pick = (iota((group * deep, g.Q), 1) == which % deep // 2).astype(BF16)
    w2 = w2_ref[...]
    base = mm(pick, lanes_of([w2, w2]))
    which = iota(base.shape, 0)
    base = jnp.where(which % 2 == iota(base.shape, 1) // g.M, base, 0.0)
    weights = lanes_of([jnp.where(which // deep == k, base, 0.0) for k in range(group)]).astype(BF16)
    for k in range(0, g.SP, group):
        for t in range(g.NT):
            lanes = min(LANES, g.N - t * LANES)
            tall = rows_of(
                [rg_ref[t, pl.ds(k + m, deep, stride=g.SP), :] for m in range(group)]
            )
            tall = (tall * scale).T[:lanes]
            high, low = split_high_low(tall)
            part = mm(high, weights) + mm(low, weights)
            for m in range(group):
                go_ref[k + m, t * LANES : t * LANES + lanes, :] = (
                    part[:, m * 2 * g.M : (m + 1) * 2 * g.M] * masks[k + m]
                )


def outer_kernel(g, *refs):
    refs = list(refs)
    x_refs, refs = refs[: g.R], refs[g.R :]
    d_ref, left_ref, second_ref, mask_ref, xall_ref, ds_ref, *refs = refs
    w_refs, (others_ref, spread_ref, rt_ref, all_ref) = refs[: g.D], refs[g.D :]
    row, col, depth = (lax.axis_index(a) for a in ("row", "col", "depth"))
    rows, deep = g.SP * g.I, 2 * g.QL
    for k, ref in zip((0, *g.order), x_refs, strict=True):
        place = g.place(jnp.bitwise_xor(row, k), col)
        xall_ref[:, pl.ds(place, g.I), :] = ref[:rows, :].reshape(g.SP, g.I, 2 * g.M)
        for m in range(g.EXTRA):
            block = ref[rows + m * g.I : rows + (m + 1) * g.I, :]
            others_ref[pl.ds(place, g.I), m * LANES : (m + 1) * LANES] = block
    second = second_ref[...]
    parts = [
        mm(second, (xall_ref[k].astype(F32) * mask_ref[k : k + 1, :]).astype(BF16), NT)
        for k in range(g.SP)
    ]
    if g.EXTRA:
        lanes = g.EXTRA * LANES
        eye = (iota((lanes, lanes), 0) == iota((lanes, lanes), 1)).astype(BF16)
        parts.append(mm(eye, others_ref[...], NT)[: (g.C - 1) * g.SP * deep])
    first = 0
    for part in parts:
        for t in range(g.NT):
            lanes = min(LANES, g.N - t * LANES)
            piece = part[:, t * LANES : t * LANES + lanes]
            spread_ref[t, first : first + part.shape[0], :lanes] = piece
        first += part.shape[0]
    for q in range(g.QL):
        for m in range(g.C):
            spot = (q * g.C + m) * g.S
            for t in range(g.NT):
                lanes = min(LANES, g.N - t * LANES)
                halves = [
                    spread_ref[t, pl.ds(m * g.SP * deep + half * g.QL + q, g.SP, stride=deep), :]
                    for half in range(2)
                ]
                rt_ref[spot : spot + g.S, t * LANES : t * LANES + lanes] = rows_of(halves)[
                    :, :lanes
                ].astype(BF16)
    rt = rt_ref[...]
    for i in range(0, g.I, 2):
        product = mm(rt, lanes_of([d_ref[i], d_ref[i + 1]]))
        for k in range(2):
            block = product[:, k * g.Z : (k + 1) * g.Z]
            ds_ref[:, :, i + k] = block.reshape(g.QL, g.C, g.S, g.Z).astype(BF16)
    eye = (iota((g.Q, g.Q), 0) == iota((g.Q, g.Q), 1)).astype(BF16)
    left_t = mm(eye, left_ref[...], NT).astype(BF16)
    scale = mask_ref[g.C * g.SP : g.C * g.SP + 1, :]
    entries = g.C * g.S * g.I
    for q in range(0, g.QL, 2):
        both = lanes_of([ds_ref[q].reshape(entries, g.Z), ds_ref[q + 1].reshape(entries, g.Z)])
        part = mm(left_t, both)
        all_ref[pl.ds(q, g.Q, stride=g.QL), :] = part[:, : g.Z] * scale
        all_ref[pl.ds(q + 1, g.Q, stride=g.QL), :] = part[:, g.Z :] * scale
    share = g.Q * g.QL // g.D
    for k in range(g.D):
        first = pl.multiple_of(lax.rem(depth + k, g.D) * share, share)
        w_refs[k][...] = all_ref[pl.ds(first, share), :]


def own_kernel(
    g, xall_ref, near_ref, d_ref, ts_ref, w1_ref, w2_ref, mask_ref, part_ref, gg_ref, gate_weight_ref, own_ref,
    spread_ref, rt_ref, ds_ref, turn_ref,
):
    scale = mask_ref[g.C * g.SP : g.C * g.SP + 1, :]
    masks = [mask_ref[k : k + 1, :] for k in range(g.SP)]
    w2 = w2_ref[...]
    doubled = lanes_of([w2, w2])
    second = on_diagonal(rows_of([doubled, doubled]), g.M)
    for k in range(g.SP):
        live_x = (xall_ref[k].astype(F32) * masks[k]).astype(BF16)
        part = mm(second, live_x, NT)
        for t in range(g.NT):
            lanes = min(LANES, g.N - t * LANES)
            spread_ref[t, k * 2 * g.Q : (k + 1) * 2 * g.Q, :lanes] = part[
                :, t * LANES : t * LANES + lanes
            ]
    for q in range(g.Q):
        for t in range(g.NT):
            lanes = min(LANES, g.N - t * LANES)
            halves = [
                spread_ref[t, pl.ds(half * g.Q + q, g.SP, stride=2 * g.Q), :] for half in range(2)
            ]
            rt_ref[q * g.S : (q + 1) * g.S, t * LANES : t * LANES + lanes] = rows_of(halves)[
                :, :lanes
            ].astype(BF16)
    col = lax.axis_index("col")
    entries = g.S * g.I
    left_grad = jnp.zeros((entries, g.Q), F32)
    for m in range(g.C):
        first = lax.rem(col + m, g.C) * g.QL
        if m > 0:
            rt = rt_ref[pl.ds(pl.multiple_of(first * g.S, g.QL * g.S), g.QL * g.S), :]
            for i in range(0, g.I, 2):
                product = mm(rt, lanes_of([d_ref[i], d_ref[i + 1]]))
                for k in range(2):
                    block = product[:, k * g.Z : (k + 1) * g.Z]
                    ds_ref[m - 1, :, i + k] = block.reshape(g.QL, g.S, g.Z).astype(BF16)
        for q in range(0, g.QL, 2):
            pair = [near_ref[q + k, 0] if m == 0 else ds_ref[m - 1, q + k] for k in range(2)]
            both = lanes_of([part.reshape(entries, g.Z) for part in pair])
            left_grad = left_grad + mm(both, lanes_of([ts_ref[first + q], ts_ref[first + q + 1]]), NT)
    w1 = w1_ref[...]
    first_term = jnp.zeros((entries, 2 * g.M), F32)
    for piece in split_high_low(left_grad * scale[:, : g.Q]):
        first_term = first_term + mm(piece, lanes_of([w1, w1]))
    turn_ref[...] = first_term
    gate_term = mm(gg_ref[...], gate_weight_ref[...], NT)
    lane = iota((1, 2 * g.M), 1)
    for k in range(g.SP):
        rows = slice(k * g.I, (k + 1) * g.I)
        halves = [turn_ref[pl.ds(half * g.SP + k, g.I, stride=g.S), :] for half in range(2)]
        term = jnp.where(lane < g.M, halves[0], halves[1]) * mask_ref[k : k + 1, :]
        own_ref[rows, :] = part_ref[rows, :] + gate_term[rows] + term


def send_kernel(g, low_t_ref, gm_ref, value_weight_ref, go_ref, own_ref, *refs):
    send_refs, (total_ref,) = refs[: g.R - 1], refs[g.R - 1 :]
    row, col = lax.axis_index("row"), lax.axis_index("col")
    value_weights, low_t = value_weight_ref[...], low_t_ref[...]
    half = value_weights.shape[1] // 2
    width = half // g.H
    group = LANES // width
    count = g.H // group
    tall = group * g.I
    head = iota((1, 2 * LANES), 1) % LANES // width

    def lanes(array, k):
        return lanes_of([array[:, s * half + k * LANES : s * half + (k + 1) * LANES] for s in range(2)])

    group_weights = [lanes(value_weights, k) for k in range(count)]
    for k in range(g.SP):
        blended = gm_ref[k * g.I : (k + 1) * g.I, :]
        projected = []
        for m in range(count):
            bm = lanes(blended, m)
            by_head = rows_of([jnp.where(head == h, bm, jnp.zeros_like(bm)) for h in range(group)])
            projected.append(mm(by_head, group_weights[m], NT))
        total_ref[k] = go_ref[k] + mm(low_t, rows_of([*split_high_low(rows_of(projected))]))
    own = total_ref[:, pl.ds(g.place(row, col), g.I), :]
    own_ref[...] = own.reshape(g.SP * g.I, 2 * g.M)
    for x in range(1, g.R):
        block = total_ref[:, pl.ds(g.place(jnp.bitwise_xor(row, x), col), g.I), :]
        send_refs[x - 1][...] = block.reshape(g.SP * g.I, 2 * g.M).astype(BF16)


def attend_kernel(g, xall_ref, low_ref, gm_ref, gate_ref, value_weight_ref, gs_ref, gg_ref):
    value_weights, low = value_weight_ref[...], low_ref[...]
    values = mm(xall_ref[...].reshape(g.SP * g.N, 2 * g.M), value_weights).astype(BF16)
    half = value_weights.shape[1] // 2
    width = half // g.H
    group = LANES // width
    count = g.H // group
    tall = group * g.I
    head = iota((1, 2 * LANES), 1) % LANES // width

    def lanes(array, k):
        return lanes_of([array[:, s * half + k * LANES : s * half + (k + 1) * LANES] for s in range(2)])

    grad_soft = [jnp.zeros((tall, g.N), F32) for _ in range(count)]
    for k in range(g.SP):
        v = values[k * g.N : (k + 1) * g.N]
        rows = slice(k * g.I, (k + 1) * g.I)
        blended, factor = gm_ref[rows, :], gate_ref[rows, :]
        for m in range(count):
            vm = lanes(v, m)
            crossed = mm(low[m * tall : (m + 1) * tall], vm)
            mixed = crossed[: g.I]
            for h in range(1, group):
                mixed = jnp.where(head == h, crossed[h * g.I : (h + 1) * g.I], mixed)
            gate_grad = (lanes(factor, m) * mixed).astype(BF16)
            for s in range(2):
                first = s * half + m * LANES
                gg_ref[rows, first : first + LANES] = gate_grad[:, s * LANES : (s + 1) * LANES]
            bm = lanes(blended, m)
            by_head = rows_of([jnp.where(head == h, bm, jnp.zeros_like(bm)) for h in range(group)])
            grad_soft[m] = grad_soft[m] + mm(by_head, vm, NT)
    gs_ref[...] = rows_of(grad_soft)


def pack_kernel(g, *refs):
    refs = list(refs)
    sums, refs = refs[: g.R - 1], refs[g.R - 1 :]
    parts, refs = refs[: g.D], refs[g.D :]
    outs, (own_ref, halves_ref) = refs[: g.R - 1], refs[g.R - 1 :]
    row = lax.axis_index("row")
    total = parts[0][...]
    for ref in parts[1:]:
        total = total + ref[...]
    half, rows = own_ref.shape[0], g.SP * g.I
    for k in range(2):
        halves_ref[k] = total[k * half : (k + 1) * half].astype(BF16)
    own_ref[...] = halves_ref[lax.rem(row, 2)]
    for x in range(1, g.R):
        outs[x - 1][:rows, :] = sums[x - 1][...]
        outs[x - 1][rows:, :] = halves_ref[lax.rem(jnp.bitwise_xor(row, x), 2)]


def piece_kernel(g, own_ref, *refs):
    out_ref, order_ref = refs[-2:]
    row, rows = lax.axis_index("row"), g.SP * g.I
    order_ref[row] = own_ref[...]
    for k in range(1, g.R):
        order_ref[jnp.bitwise_xor(row, g.R - k)] = refs[k - 1][rows:, :]
    total = order_ref[0].astype(F32)
    for r in range(1, g.R):
        total = total + order_ref[r].astype(F32)
    out_ref[...] = total.astype(BF16)


def score_kernel(g, soft_ref, *refs):
    parts, refs = refs[: g.D], refs[g.D :]
    own_ref, out_refs, order_ref = refs[0], refs[1 : g.C], refs[g.C]
    depth = lax.axis_index("depth")
    for k in range(g.D):
        order_ref[lax.rem(depth - k + g.D, g.D)] = parts[k][...]
    grad_soft = order_ref[0]
    for k in range(1, g.D):
        grad_soft = grad_soft + order_ref[k]
    inner = jnp.sum(soft_ref[...] * grad_soft, -1, keepdims=True)
    for k in range(g.C):
        block = lanes_of([grad_soft[:, k * g.JC : (k + 1) * g.JC], inner])
        if k == 0:
            own_ref[...] = block
        else:
            out_refs[k - 1][...] = three_lanes(block)


def pair_kernel(g, e_ref, wl_ref, soft_ref, own_ref, *refs):
    got, pair_ref = refs[: g.C - 1], refs[g.C - 1]
    heads = g.H * g.I
    total = own_ref[...]
    for ref in got:
        total = total + join_three(ref[...], g.JC + 1)
    grad = soft_ref[:, : g.JC] * (total[:, : g.JC] - total[:, g.JC :])
    if g.JC < LANES:
        grad = lanes_of([grad, jnp.zeros((heads, LANES - g.JC), F32)])
    high, low = split_high_low(grad.T[: g.JC])
    grads = lanes_of([high, low])
    pick = (iota((heads, g.H), 0) // g.I == iota((heads, g.H), 1)).astype(BF16)
    base = mm(pick, wl_ref[...]).astype(BF16)
    token = iota((heads, 1), 0) % g.I
    for i in range(0, g.I, 2):
        weights = lanes_of(
            [jnp.where(token == i + k, base, jnp.zeros_like(base)) for k in range(2)]
        )
        upstream = mm(grads, rows_of([weights, weights]))
        for k in range(2):
            pair_ref[i + k] = standardize_backward(
                e_ref[i + k].astype(F32), upstream[:, k * g.Z : (k + 1) * g.Z]
            ).astype(BF16)


def reduce_kernel(g, x_ref, own_ref, *refs):
    got, out_ref = refs[:-1], refs[-1]
    rows = g.SP * g.I
    total = own_ref[...]
    for ref in got:
        total = total + ref[:rows, :].astype(F32)
    total = total.reshape(g.SP, 1, g.I, 2 * g.M)
    upstream = jnp.concatenate([total[..., : g.M], total[..., g.M :]], axis=1)
    upstream = upstream.reshape(g.S, g.I, g.M)[: g.SQ]
    msa = g.fill(standardize_backward(x_ref[...].astype(F32), upstream))
    msa = msa.reshape(g.SP, 2, g.I, g.M)
    msa = jnp.concatenate([msa[:, 0], msa[:, 1]], axis=-1).astype(BF16)
    out_ref[...] = msa.reshape(rows, 2 * g.M)


def across_kernel(g, *refs):
    out_ref = refs[-1]
    row, col = lax.axis_index("row"), lax.axis_index("col")
    for ref, (b, k) in zip(refs[:-1], g.spread, strict=True):
        half = lax.rem(jnp.bitwise_xor(row, b), 2)
        out_ref[lax.rem(col - k + g.C, g.C), half] = ref[...]


def unpack_kernel(g, *refs):
    parts, msa_ref = refs[: g.C], refs[g.C]
    col = lax.axis_index("col")
    for k, ref in enumerate(parts):
        msa = ref[...].astype(F32).reshape(g.SP, 1, g.I, 2 * g.M)
        msa = jnp.concatenate([msa[..., : g.M], msa[..., g.M :]], axis=1)
        msa = msa.reshape(g.S, g.I, g.M)[: g.SQ].astype(BF16)
        msa_ref[pl.ds(lax.rem(col - k + g.C, g.C) * g.SQ, g.SQ)] = msa


def finish_kernel(g, msa_ref, *refs):
    parts, (out_ref, matrix_ref) = refs[: g.D], refs[g.D :]
    depth = lax.axis_index("depth")
    out_ref[...] = msa_ref[...]
    share = g.Q // g.D
    for k in range(g.D):
        first = lax.rem(depth - k + g.D, g.D) * share
        for c in range(g.C):
            block = parts[k][c].astype(F32)
            matrix_ref[pl.ds(first, share), c * g.QL : (c + 1) * g.QL, :] = block


class Sizes:
    def __init__(self, x, e, wl, w1):
        self.R, self.C, self.D = (lax.axis_size(a) for a in ("row", "col", "depth"))
        self.I, self.M = x.shape[1:]
        self.JC, self.Z = e.shape[1:]
        self.H, self.Q = wl.shape[1], w1.shape[1]
        self.QL = self.Q // self.C
        self.SQ = x.shape[0] // self.C
        self.S = -(-self.SQ // 16) * 16
        self.SP, self.N = self.S // 2, self.R * self.I
        self.F = self.R // self.C
        self.NT = -(-self.N // LANES)
        self.G = max(1, LANES // self.JC)
        self.EXTRA = -(-(self.C - 1) * self.S * self.QL // LANES)
        self.carried = 0
        self.spread = [(b, k) for b in range(2) for k in range(self.C)]
        self.order = [*range(1, self.R // 2), *range(self.R // 2 + 1, self.R), self.R // 2]

    def fill(self, rows):
        if self.SQ == self.S:
            return rows
        return rows_of([rows, jnp.zeros((self.S - self.SQ, *rows.shape[1:]), rows.dtype)])

    def place(self, row, col):
        turn = lax.rem(row // self.F - col + self.C, self.C)
        return pl.multiple_of((turn * self.F + lax.rem(row, self.F)) * self.I, self.I)


def shift(array, axis, k):
    count = lax.axis_size(axis)
    return lax.ppermute(array, axis, [(i, (i + k) % count) for i in range(count)])


def swap(array, axis, x):
    return lax.ppermute(array, axis, [(i, i ^ x) for i in range(lax.axis_size(axis))])


def swapped(arrays, axis):
    return [swap(a, axis, k + 1) for k, a in reversed([*enumerate(arrays)])]


def from_near(array, b, k):
    count, wide = lax.axis_size("row"), lax.axis_size("col")
    pairs = [(r * wide + c, (r ^ b) * wide + (c + k) % wide) for r in range(count) for c in range(wide)]
    return lax.ppermute(array, ("row", "col"), pairs)


def shifted_all(array, axis):
    return [array] + [shift(array, axis, k) for k in range(1, lax.axis_size(axis))]


def per_device(
    homolog_ensemble,
    duplex_embedding,
    homolog_present_flags,
    resolved_position_flags,
    payload_weights,
    sigmoid_weights,
    averager_final_weights,
    first_operand_weights,
    second_operand_weights,
    duplex_logit_weights,
    tensor_product_weights,
    averager_upstream_adjoint,
    duplex_upstream_adjoint,
):
    g = Sizes(homolog_ensemble, duplex_embedding, duplex_logit_weights, first_operand_weights)
    shape = jax.ShapeDtypeStruct

    def call(kernel, name, args, outs, scratch=(), far=None, after=(), distant=False, us=1.0):
        size = sum(a.size * a.dtype.itemsize for a in args) + sum(
            math.prod(o.shape) * jnp.dtype(o.dtype).itemsize for o in outs
        )
        single = len(outs) == 1
        near = len(args) if far is None else far
        args = list(args[:near]) + [
            pltpu.with_memory_space_constraint(a, pltpu.HBM) for a in args[near:]
        ]

        if distant:
            after = [pltpu.with_memory_space_constraint(a, pltpu.HBM) for a in after]

        def body(*refs):
            kernel(g, *refs[: len(args)], *refs[len(args) + len(after) :])

        return pl.pallas_call(
            body,
            out_shape=outs[0] if single else tuple(outs),
            in_specs=[VMEM] * near + [FAR] * (len(args) - near) + [FAR if distant else VMEM] * len(after),
            out_specs=VMEM if single else (VMEM,) * len(outs),
            scratch_shapes=list(scratch),
            compiler_params=pltpu.CompilerParams(vmem_limit_bytes=40 * 1024 * 1024),
            cost_estimate=pl.CostEstimate(
                flops=int(us * 1.15e9), bytes_accessed=size, transcendentals=0
            ),
            name=name,
        )(*args, *after)

    heads = g.H * g.I
    rows = g.SP * g.I
    values = 2 * payload_weights.shape[1]
    pairs, tall = g.I * g.JC, heads // g.G
    xn, send, logits, near, x, e, wl, masks, w1, outer_weights, w2, second = call(
        normalise_kernel,
        "normalise",
        (
            homolog_ensemble,
            duplex_embedding,
            duplex_upstream_adjoint.reshape(pairs, g.Z),
            resolved_position_flags.reshape(1, g.JC),
            duplex_logit_weights.T,
            homolog_present_flags,
            first_operand_weights.T,
            tensor_product_weights,
            second_operand_weights.T,
            homolog_present_flags.reshape(1, -1),
        ),
        [
            pltpu.VMEM((g.C, g.SP, g.I, 2 * g.M), BF16),
            pltpu.VMEM((rows + g.EXTRA * g.I, 2 * g.M), BF16),
            pltpu.VMEM((tall, g.G * g.JC), F32),
            pltpu.VMEM((pairs + 3 * tall, g.Z), BF16),
            pltpu.VMEM((g.SQ, g.I, g.M), BF16),
            pltpu.VMEM(duplex_embedding.shape, BF16),
            pltpu.VMEM((g.H, g.Z), BF16),
            pltpu.VMEM((g.C * g.SP + 8, 2 * g.M), F32),
            pltpu.VMEM((g.Q, g.M), BF16),
            pltpu.VMEM(tensor_product_weights.shape, BF16),
            pltpu.VMEM((g.Q, g.M), BF16),
            pltpu.VMEM((2 * g.QL, 2 * g.M), BF16),
        ],
        [
            pltpu.VMEM((1, g.JC), jnp.int32),
            pltpu.SMEM(homolog_present_flags.shape, jnp.int32),
            pltpu.VMEM((1, homolog_present_flags.shape[0]), jnp.int32),
            pltpu.VMEM(homolog_ensemble.shape, BF16),
            pltpu.VMEM(homolog_ensemble.shape, F32),
            pltpu.VMEM((g.I * g.H, LANES), F32),
            pltpu.SemaphoreType.DMA((10,)),
        ],
        far=0,
        us=2.0,
    )
    everyone = [send] + [swap(send, "row", k) for k in g.order]
    nears = shifted_all(near, "col")
    later = (
        sigmoid_weights,
        averager_final_weights.T,
        payload_weights,
    )
    g.carried = len(later)
    left, weights, left_weights, u, sg, wf, p = call(
        prepare_kernel,
        "prepare",
        (xn, w1, outer_weights, masks, averager_upstream_adjoint, *later),
        [
            pltpu.VMEM((g.C * g.I * g.S, g.Q), BF16),
            pltpu.VMEM((g.Q, g.Q, g.Z), BF16),
            pltpu.VMEM((g.I, g.Q * g.S, g.Z), BF16),
            pltpu.VMEM((g.SQ, g.I, g.M), BF16),
        ]
        + [pltpu.VMEM(a.shape, a.dtype) for a in later],
        [
            pltpu.VMEM(tensor_product_weights.shape, F32),
            pltpu.VMEM((2, rows, LANES), F32),
            pltpu.SemaphoreType.DMA,
            pltpu.SemaphoreType.DMA((len(later),)),
        ],
        far=4,
        us=0.01,
    )
    gate_weights, blended, gate_factor, value_weights, soft, low, low_t = call(
        gate_kernel,
        "gate",
        (xn, u, sg, wf, p, logits, *nears[1:]),
        [
            pltpu.VMEM((2 * g.M, values), BF16),
            pltpu.VMEM((rows, values), BF16),
            pltpu.VMEM((rows, values), F32),
            pltpu.VMEM((2 * g.M, values), BF16),
            pltpu.VMEM((heads, g.N), F32),
            pltpu.VMEM((heads, g.N), BF16),
            pltpu.VMEM((g.N, 2 * heads), BF16),
        ],
        us=0.01,
    )
    cotangents, second_term = call(
        right_kernel,
        "right",
        (*nears, left_weights, w2, masks),
        [pltpu.VMEM((g.I, g.N, g.Z), BF16), pltpu.VMEM((g.SP, g.N, 2 * g.M), F32)],
        [pltpu.VMEM((g.NT, g.Q * g.S, LANES), F32)],
        after=(gate_weights,),
        us=0.01,
    )
    share = g.Q * g.QL // g.D
    xall, products, *matrix_parts = call(
        outer_kernel,
        "outer",
        (*everyone, cotangents, left, second, masks),
        [
            pltpu.VMEM((g.SP, g.N, 2 * g.M), BF16),
            pltpu.VMEM((g.QL, g.C, g.I, g.S, g.Z), BF16),
        ]
        + [pltpu.VMEM((share, g.Z), F32)] * g.D,
        [
            pltpu.VMEM((g.N, max(1, g.EXTRA) * LANES), BF16),
            pltpu.VMEM((g.NT, g.C * g.SP * 2 * g.QL, LANES), F32),
            pltpu.VMEM((g.QL * g.C * g.S, g.N), BF16),
            pltpu.VMEM((g.Q * g.QL, g.Z), F32),
        ],
        after=(second_term,),
        us=0.05,
    )
    matrix_parts = [matrix_parts[0]] + [
        shift(a, "depth", k + 1) for k, a in enumerate(matrix_parts[1:])
    ]
    own, *sums = call(
        send_kernel,
        "send",
        (low_t, blended, value_weights, second_term),
        [pltpu.VMEM((rows, 2 * g.M), F32)] + [pltpu.VMEM((rows, 2 * g.M), BF16)] * (g.R - 1),
        [pltpu.VMEM((g.SP, g.N, 2 * g.M), F32)],
        after=(xall,),
        us=3.0,
    )
    *sums, piece = call(
        pack_kernel,
        "pack",
        (*sums, *matrix_parts),
        [pltpu.VMEM((rows + share // 2, 2 * g.M), BF16)] * (g.R - 1)
        + [pltpu.VMEM((share // 2, g.Z), BF16)],
        [pltpu.VMEM((2, share // 2, g.Z), BF16)],
        us=0.2,
    )
    sums = swapped(sums, "row")
    grad_soft, gate_grads = call(
        attend_kernel,
        "attend",
        (xall, low, blended, gate_factor, value_weights),
        [pltpu.VMEM((heads, g.N), F32), pltpu.VMEM((rows, values), BF16)],
        after=(piece,),
        us=0.01,
    )
    own = call(
        own_kernel,
        "own",
        (xall, products, cotangents, weights, w1, w2, masks, own, gate_grads, gate_weights),
        [pltpu.VMEM((rows, 2 * g.M), F32)],
        [
            pltpu.VMEM((g.NT, g.SP * 2 * g.Q, LANES), F32),
            pltpu.VMEM((g.Q * g.S, g.N), BF16),
            pltpu.VMEM((max(1, g.C - 1), g.QL, g.I, g.S, g.Z), BF16),
            pltpu.VMEM((g.I * g.S, 2 * g.M), F32),
        ],
        after=(piece,),
        us=0.01,
    )
    wide = -(-3 * (g.JC + 1) // LANES) * LANES
    scores, *sends = call(
        score_kernel,
        "score",
        (soft, *shifted_all(grad_soft, "depth")),
        [pltpu.VMEM((heads, g.JC + 1), F32)] + [pltpu.VMEM((heads, wide), BF16)] * (g.C - 1),
        [pltpu.VMEM((g.D, heads, g.N), F32)],
        after=(own,),
        us=0.2,
    )
    arrived = [shift(a, "col", k + 1) for k, a in enumerate(sends)]
    piece = call(
        piece_kernel,
        "piece",
        (piece, *sums),
        [pltpu.VMEM((share // 2, g.Z), BF16)],
        [pltpu.VMEM((g.R, share // 2, g.Z), BF16)],
        after=(scores,),
        us=0.1,
    )
    pieces = [piece] + [from_near(piece, b, k) for b, k in g.spread[1:]]
    part = call(
        reduce_kernel,
        "reduce",
        (x, own, *sums),
        [pltpu.VMEM((rows, 2 * g.M), BF16)],
        after=(piece,),
    )
    pairwise_gradient = call(
        pair_kernel,
        "pair",
        (e, wl, soft, scores, *arrived),
        [shape(duplex_embedding.shape, BF16)],
        after=(part,),
        us=0.01,
    )
    matrix = call(
        across_kernel,
        "across",
        pieces,
        [pltpu.VMEM((g.C, 2, share // 2, g.Z), BF16)],
        after=(pairwise_gradient,),
        distant=True,
        us=0.1,
    ).reshape(g.C, g.Q // g.D, g.QL, g.Z)
    ensemble_derivative = call(
        unpack_kernel,
        "unpack",
        shifted_all(part, "col"),
        [pltpu.VMEM(homolog_ensemble.shape, BF16)],
        after=(matrix,),
    )
    ensemble_derivative, outer_matrix_gradient = call(
        finish_kernel,
        "finish",
        (ensemble_derivative, *shifted_all(matrix, "depth")),
        [shape(homolog_ensemble.shape, BF16), shape((g.Q, g.Q, g.Z), F32)],
    )
    outer_matrix_gradient = outer_matrix_gradient.reshape(tensor_product_weights.shape)
    return (ensemble_derivative, pairwise_gradient, outer_matrix_gradient)


def solution(mesh):
    in_specs = (
        P(("parts", "depth"), "row", None),
        P(("parts", "row"), "col", None),
        P("parts"),
        P(("parts", "col")),
        P(),
        P(),
        P(),
        P(),
        P(),
        P(),
        P(),
        P(("parts", "depth"), "row", None),
        P(("parts", "row"), "col", None),
    )
    out_specs = (
        P(("parts", "depth"), "row", None),
        P(("parts", "row"), "col", None),
        P("parts", None),
    )
    return jax.shard_map(
        per_device, mesh=mesh, in_specs=in_specs, out_specs=out_specs, check_vma=False
    )
```
